32 devices in a mesh: cores: 2 (over y), gz: 4 (over z), gy: 2 (over x), col: 2 (over core).
Axes of the slice: x: 2, y: 2, z: 4, core: 2. Of those that a mesh axis runs over, the one named last changes fastest.
Arguments:
- density: bfloat16 [32, 64, 512], P(('cores', 'gz'), 'gy', 'col'), parts along dimension 0, may hold values from -6 to 6
- first_kernel: bfloat16 [27, 8, 1], replicated, may hold values from -1.25 to 1.25
- first_bias: float32 [8], replicated, may hold values from -3 to 3
- second_kernel: bfloat16 [27, 2, 8], replicated, may hold values from -0.625 to 0.625
- second_bias: float32 [2], replicated, may hold values from -3 to 3
- owners: int32 [8, 2, 2, 16, 1], P(('cores', 'gz'), 'gy', 'col'), parts along dimension 0, may hold values from 0 to 3; in each aligned block of 16 rows (0 to 15, 16 to 31, ..., all dimensions but the last counted through in order) at most 8 rows name the same one
- solutes: float32 [8, 2, 2, 32, 2, 4, 4, 128], P(('cores', 'gz'), 'gy', 'col'), parts along dimension 0, may hold values from 0.2 to 2
- biomass: bfloat16 [8, 2, 2, 32, 4, 4, 128], P(('cores', 'gz'), 'gy', 'col'), parts along dimension 0, may hold values from 0.099609375 to 1
Outputs:
- fractions: bfloat16 [2, 32, 64, 512], P(None, ('cores', 'gz'), 'gy', 'col'), parts along dimension 1
- solutes_next: float32 [8, 2, 2, 32, 2, 4, 4, 128], P(('cores', 'gz'), 'gy', 'col'), parts along dimension 0
The draws below stay inside these ranges and needn't reach their ends.
There are 2 independent parts, one for each index of `cores`. The reference program is written for one: setup_inputs(seed, part) draws one part's arguments, and reference() takes and returns one part's arrays. A program takes and returns all parts, laid end to end along the dimension named above; an argument that names none is the same for every part. Nothing has to cross between parts.
Inputs may be any that keep to these rules, and one draw needn't show every extreme that they name: `owners`: among the 16 bricks of one device at most 8 name the same owner, and some device reaches 8.
All inputs are finite; a program needn't handle non-finite values.
Results may differ from the reference program's by a relative error of at most 0.0034.
Values may be sent and summed in bfloat16 or wider, within the bound.
No kernel may reach another device: no remote copies, remote signals or barrier semaphores. Data moves between devices by JAX's collectives and lax.ppermute only.
A program may use at most 64 MiB of HBM per device.

```python
import math
import jax
import jax.numpy as jnp
import numpy as np

CH = 8
CZ = 4
CY = 32
CX = 256
BY = 4
BX = 128
STEPS = 4
NB = 16
CAP = 8
SLOTS = 32
NZ = 16
NY = 64
NX = 512
N_GZ = 4
N_GY = 2
N_COL = 2


def block_levels(own_key, dims, pieces, least, largest):
    gain = 1.0
    for position, blocks in pieces:
        steps = jax.random.uniform(jax.random.fold_in(jax.random.fold_in(own_key, 6), position), (blocks,), jnp.float32, least / len(pieces), largest / len(pieces))
        gain = gain * jnp.repeat(jnp.exp(steps), dims[position] // blocks).reshape((-1,) + (1,) * (len(dims) - 1 - position))
    return gain


def routed_block(own_key, own, number, rows, number_of, top, bound, slope):
    sequence = jax.random.permutation(own_key, number_of)
    heavy_load, ordinary = shares(number_of, rows * top, bound, slope, True), shares(number_of, rows * top, bound, slope, False)
    places = jnp.arange(number_of)

    def named(sizes, offset_by):
        used = int((sizes > 0).sum())
        fixed = max(1, used // 4)
        passed = fixed + (places - fixed + offset_by * (used - fixed)) % max(1, number_of - fixed)
        return jnp.zeros((number_of,), jnp.int32).at[sequence[jnp.where(places < fixed, places, passed)]].set(jnp.asarray(sizes, jnp.int32))

    sizes = jnp.where(number % 4 == 0, named(heavy_load, number // 4), named(ordinary, number - number // 4 - 1))
    mixed = jax.random.permutation(jax.random.fold_in(own, 3), number_of)
    donor, taker = mixed[0:number_of // 2 * 2:2], mixed[1:number_of // 2 * 2:2]
    slack = jnp.minimum(sizes[donor] - 1, bound - sizes[taker]) // 2
    slack = jnp.where((donor == sequence[0]) | (taker == sequence[0]) | (sizes[taker] == 0), 0, jnp.maximum(slack, 0))
    passed = jax.random.randint(jax.random.fold_in(own, 4), (number_of // 2,), 0, 1 << 20) % (slack + 1)
    sizes = sizes.at[donor].add(-passed).at[taker].add(passed)
    items = jnp.searchsorted(jnp.cumsum(sizes), jnp.arange(rows * top), side="right").astype(jnp.int32)
    table = items.reshape(top, rows).T
    table = table[jax.random.permutation(jax.random.fold_in(own, 1), rows)]
    offset_by = jax.random.randint(jax.random.fold_in(own, 2), (rows, 1), 0, top)
    return jnp.take_along_axis(table, (jnp.arange(top)[None, :] + offset_by) % top, axis=1)


def shares(count, total, reach, lean, full):
    loads = [(1 << 20) // math.isqrt(grade ** lean) + 1 for grade in range(1, count + 1)]
    largest = reach if full else min(reach, max(-(-total // count), total * loads[0] // sum(loads)))
    least = 1 if total - largest >= count - 1 else 0
    holding, spare = [largest] + [least] * (count - 1), total - largest - least * (count - 1)
    while spare > 0:
        candidates = [i for i in range(1, count) if holding[i] < largest] or [i for i in range(1, count) if holding[i] < reach]
        pool, remaining = sum([loads[i] for i in candidates]), spare
        for i in candidates:
            more = min(reach - holding[i], max(1, remaining * loads[i] // pool), spare)
            holding[i] = holding[i] + more
            spare = spare - more
    return np.array(holding)


def bell_draw(own_key, dims, scale, reach, pieces=(), held_as=jnp.bfloat16):
    loudness = block_levels(own_key, dims, pieces, -0.22, 0.18) if pieces else 1.0
    result = jax.random.normal(own_key, dims, jnp.float32) * scale * loudness
    return jnp.minimum(jnp.maximum(result, -reach), reach).astype(held_as)


def setup_inputs(seed: int = 0, part: int = 0) -> dict:
    keys = jax.random.split(jax.random.key(seed), 9)
    part_keys = jax.random.split(jax.random.fold_in(keys[8], part), 9)
    density = bell_draw(part_keys[0], (NZ, NY, NX), 1.0, 6.0, ((0, 4), (1, 2), (2, 2)))
    first_kernel = bell_draw(keys[1], (27, CH, 1), 27 ** -0.5, 1.25)
    first_bias = bell_draw(keys[2], (CH,), 1.0, 3.0, (), jnp.float32)
    second_kernel = bell_draw(keys[3], (27, 2, CH), (27 * CH // 2) ** -0.5, 0.625)
    second_bias = bell_draw(keys[4], (2,), 1.0, 3.0, (), jnp.float32)
    owners_keys = jax.random.split(jax.random.fold_in(part_keys[5], 1), N_GZ * N_GY * N_COL * NB // NB)
    owners_turns = jax.random.permutation(jax.random.fold_in(part_keys[5], 3), N_GZ * N_GY * N_COL * NB // NB)
    owners = jax.vmap(lambda own, number: routed_block(jax.random.fold_in(part_keys[5], 2), own, number, NB, N_GZ, 1, CAP, 2))(owners_keys, owners_turns).reshape((N_GZ, N_GY, N_COL, NB, 1))
    solutes = jnp.clip(jnp.exp(math.log(2.0) - 2.3025851 * jax.random.uniform(part_keys[6], (N_GZ, N_GY, N_COL, SLOTS, 2, CZ, BY, BX), jnp.float32) ** block_levels(part_keys[6], (N_GZ, N_GY, N_COL, SLOTS, 2, CZ, BY, BX), ((0, 4), (1, 2), (2, 2)), -0.2, 0.2)), 0.2, 2.0)
    biomass = jnp.clip(jnp.exp(math.log(1.0) - 2.306499 * jax.random.uniform(part_keys[7], (N_GZ, N_GY, N_COL, SLOTS, CZ, BY, BX), jnp.float32) ** block_levels(part_keys[7], (N_GZ, N_GY, N_COL, SLOTS, CZ, BY, BX), ((0, 4), (1, 2), (2, 2)), -0.2, 0.2)), 0.099609375, 1.0).astype(jnp.bfloat16)
    return dict(density=density, first_kernel=first_kernel, first_bias=first_bias, second_kernel=second_kernel, second_bias=second_bias, owners=owners, solutes=solutes, biomass=biomass)


def conv_layer(padded, weights, depth, rows, columns):
    total = jnp.zeros((weights.shape[1], depth, rows, columns), jnp.float32)
    for offset in range(27):
        shift_z = offset // 9
        shift_y = (offset // 3) % 3
        shift_x = offset % 3
        window = padded[:, shift_z:shift_z + depth, shift_y:shift_y + rows, shift_x:shift_x + columns]
        total = total + jnp.einsum("oc,czyx->ozyx", weights[offset].astype(jnp.float32), window.astype(jnp.float32))
    return total


def laplace(field):
    padded = jnp.pad(field, [(0, 0)] * (field.ndim - 3) + [(1, 1), (1, 1), (1, 1)], mode="edge")
    centre = padded[..., 1:-1, 1:-1, 1:-1]
    beside_all = padded[..., 2:, 1:-1, 1:-1] + padded[..., :-2, 1:-1, 1:-1]
    beside_all = beside_all + padded[..., 1:-1, 2:, 1:-1] + padded[..., 1:-1, :-2, 1:-1]
    beside_all = beside_all + padded[..., 1:-1, 1:-1, 2:] + padded[..., 1:-1, 1:-1, :-2]
    return beside_all - 6.0 * centre


def advance(state, arrived, biomass):
    pore = arrived[..., 0, :, :, :].astype(jnp.float32)
    organic = arrived[..., 1, :, :, :].astype(jnp.float32)
    mass = biomass.astype(jnp.float32)
    carbon = state[..., 0, :, :, :]
    oxygen = state[..., 1, :, :, :]
    for step in range(STEPS):
        uptake = 0.25 * mass * carbon / (0.5 + jnp.abs(carbon)) * oxygen / (0.3 + jnp.abs(oxygen))
        carbon_new = carbon + 0.12 * pore * laplace(carbon) + 0.3 * organic - uptake
        oxygen_new = oxygen + 0.16 * pore * laplace(oxygen) - uptake
        carbon, oxygen = carbon_new, oxygen_new
    return jnp.stack([carbon, oxygen], axis=-4)


def reference(density, first_kernel, first_bias, second_kernel, second_bias, owners, solutes, biomass):
    padded = jnp.pad(density[None], ((0, 0), (1, 1), (1, 1), (1, 1)))
    first = conv_layer(padded, first_kernel, NZ, NY, NX)
    hidden = jnp.maximum(first + first_bias[:, None, None, None], 0.0).astype(jnp.bfloat16)
    padded = jnp.pad(hidden, ((0, 0), (1, 1), (1, 1), (1, 1)))
    second = conv_layer(padded, second_kernel, NZ, NY, NX)
    fractions = jax.nn.sigmoid(second + second_bias[:, None, None, None]).astype(jnp.bfloat16)
    bricks = fractions.reshape(2, N_GZ, CZ, N_GY, CY // BY, BY, N_COL, CX // BX, BX)
    bricks = bricks.transpose(1, 3, 6, 4, 7, 0, 2, 5, 8).reshape(N_GZ, N_GY, N_COL, NB, 2, CZ, BY, BX)
    target = owners[..., 0].astype(jnp.int32)
    onehot = (target[..., None] == jnp.arange(N_GZ, dtype=jnp.int32)).astype(jnp.int32)
    before = jnp.cumsum(onehot, axis=3) - onehot
    rank = jnp.sum(before * onehot, axis=-1).astype(jnp.int32)
    source = jnp.broadcast_to(jnp.arange(N_GZ, dtype=jnp.int32)[:, None, None, None], target.shape)
    row_index = jnp.broadcast_to(jnp.arange(N_GY, dtype=jnp.int32)[None, :, None, None], target.shape)
    col_index = jnp.broadcast_to(jnp.arange(N_COL, dtype=jnp.int32)[None, None, :, None], target.shape)
    slot_index = source * CAP + rank
    arrived = jnp.zeros((N_GZ, N_GY, N_COL, SLOTS, 2, CZ, BY, BX), jnp.bfloat16)
    arrived = arrived.at[target, row_index, col_index, slot_index].set(bricks)
    solutes_next = advance(solutes, arrived, biomass)
    return fractions, solutes_next
```

```python
import functools

import jax
import jax.numpy as jnp
from jax import lax
from jax.experimental import pallas as pl
from jax.experimental.pallas import tpu as pltpu
from jax.sharding import PartitionSpec as P

BY = 4
BX = 128
STEPS = 4
TILE = 16
OUTSIDE = -3e38


def step_index(values, width, count):
    index = jnp.zeros(values.shape, jnp.int32)
    for k in range(1, count):
        index = index + (values >= k * width).astype(jnp.int32)
    return index


def one_hot(condition):
    return jnp.where(condition, 1.0, 0.0).astype(jnp.bfloat16)


def iotas(shape):
    return (
        lax.broadcasted_iota(jnp.int32, shape, 0),
        lax.broadcasted_iota(jnp.int32, shape, 1),
    )


def banded_kernel(dims, w1_ref, b1_ref, w2_ref, t1_ref, bias_ref, t2_ref):
    rows, window, edges, count_gy, channels = dims
    g = lax.axis_index("gy")
    part = rows + TILE * edges
    tall = (rows + 2) * channels
    row, _ = iotas((tall, channels))
    _, channel = iotas((tall, channels))
    spread = one_hot((row & (channels - 1)) == channel)
    w1 = lax.dot_general(
        spread, w1_ref[...], (((1,), (1,)), ((), ())), preferred_element_type=jnp.float32
    ).astype(jnp.bfloat16)
    tap, column = iotas((27, 9 * part))
    block = step_index(column, part, 9)
    dz = step_index(block, 3, 3)
    dx = block - 3 * dz
    row, column = iotas((tall, 9 * part))
    place = column - part * step_index(column, part, 9)
    below = jnp.where(g < count_gy - 1, place, 1000)
    above = jnp.where(g > 0, place - part, 1000)
    if edges == 1:
        outer = jnp.where(g == 0, below, above)
    else:
        outer = jnp.where(place < rows + TILE, below, above)
    input_row = jnp.where(place < rows, place, outer)
    distance = input_row - (row >> (channels.bit_length() - 1)) + 2
    total = jnp.zeros((tall, 9 * part), jnp.float32)
    for dy in range(3):
        pick = one_hot(tap == 9 * dz + 3 * dy + dx)
        values = jnp.dot(w1, pick, preferred_element_type=jnp.float32)
        total = jnp.where(distance == dy, values, total)
    t1_ref[...] = total.astype(jnp.bfloat16)
    row, _ = iotas((tall, window))
    bias = jnp.zeros((tall, window), jnp.float32)
    for k in range(channels):
        bias = jnp.where((row & (channels - 1)) == k, b1_ref[k], bias)
    outside = ((row < channels) & (g == 0)) | (
        (row >= tall - channels) & (g == count_gy - 1)
    )
    bias_ref[...] = jnp.where(outside, OUTSIDE, bias)
    channel, column = iotas((channels, 3 * tall))
    spread = one_hot((column & (channels - 1)) == channel)
    wide = jnp.dot(w2_ref[...], spread, preferred_element_type=jnp.float32)
    tap, column = iotas((54, 3 * tall))
    wide = jnp.where(
        step_index(tap, 18, 3) == step_index(column, tall, 3), wide, 0.0
    ).astype(jnp.bfloat16)
    row, tap = iotas((6 * rows, 54))
    tap_z = step_index(tap, 18, 3)
    tap_y = step_index(tap - 18 * tap_z, 6, 3)
    inside = tap - 18 * tap_z - 6 * tap_y
    tap_x, tap_o = inside >> 1, inside & 1
    row_x = step_index(row, 2 * rows, 3)
    same = (row_x == tap_x) & (((row >> 2) & 1) == tap_o)
    row, column = iotas((6 * rows, 3 * tall))
    local = row - 2 * rows * step_index(row, 2 * rows, 3)
    y = (local >> 3) * BY + (local & 3)
    hidden_row = (column - tall * step_index(column, tall, 3)) >> (channels.bit_length() - 1)
    total = jnp.zeros((6 * rows, 3 * tall), jnp.float32)
    for dy in range(3):
        values = jnp.dot(
            one_hot(same & (tap_y == dy)), wide, preferred_element_type=jnp.float32
        )
        total = jnp.where(hidden_row - y == dy, values, total)
    t2_ref[...] = total.astype(jnp.bfloat16)


def column_kernel(
    dims,
    b2_ref,
    gathered_ref,
    t1_ref,
    bias_ref,
    t2_ref,
    solutes_ref,
    biomass_ref,
    fractions_ref,
    next_ref,
    tiles,
    shifted,
    hidden,
    bricks,
    arrived,
    mass,
    owner_rows,
    owner_table,
    brick_of_slot,
    tile_sems,
    owner_sem,
):
    count_gz, count_gy, depth, rows, columns, channels, edges, segment, slots = dims
    z_index = lax.axis_index("gz")
    g = lax.axis_index("gy")
    c = lax.axis_index("col")
    window = columns + BX
    part = rows + TILE * edges
    tall = (rows + 2) * channels
    brick_rows = rows // BY
    brick_columns = columns // BX
    capacity = slots // count_gz
    segments = count_gz // segment
    single = segments == 1
    lead = 0 if single else 1
    held = segment + 2 * lead
    below, above = jnp.minimum(g + 1, count_gy - 1), jnp.maximum(g - 1, 0)
    if edges == 1:
        sides = [(g, c), (g, 1 - c), (1 - g, c), (1 - g, 1 - c)]
    else:
        sides = [(g, c), (g, 1 - c), (below, c), (below, 1 - c), (above, c), (above, 1 - c)]

    lane = lax.broadcasted_iota(jnp.int32, (TILE, window), 1)
    zero_slice = jnp.zeros((3 * part, window), jnp.bfloat16)
    zero_hidden = jnp.zeros((tall, window), jnp.bfloat16)

    def one_segment(q):
        copies = []
        for t in range(held):
            tile = jnp.clip(q * segment + t - lead, 0, count_gz - 1)
            for k, (gy, col) in enumerate(sides):
                copy = pltpu.make_async_copy(
                    gathered_ref.at[tile, gy, col], tiles.at[t, k], tile_sems.at[t, k]
                )
                copy.start()
                copies.append(copy)
        for copy in copies:
            copy.wait()

        for t in range(segment):
            row = tiles[t + lead, 0, depth * rows : depth * rows + TILE, 0:BX]
            owner_rows[t] = row[0:8].astype(jnp.float32).astype(jnp.int32)
        table = pltpu.make_async_copy(owner_rows, owner_table, owner_sem)
        table.start()

        def shifts(z, valid):
            t, zz = z // depth, z % depth
            for r in range(part // TILE):
                if r < rows // TILE:
                    side, start = 0, zz * rows + r * TILE
                elif edges == 1:
                    side, start = 2, zz * rows + jnp.where(g == 0, 0, rows - TILE)
                elif r == rows // TILE:
                    side, start = 2, zz * rows
                else:
                    side, start = 4, zz * rows + rows - TILE
                pieces = []
                for j in range(window // BX):
                    from_other = jnp.where(c == 0, int(j == window // BX - 1), int(j == 0))
                    offset = jnp.where(
                        c == 0,
                        j * BX if j < window // BX - 1 else 0,
                        (j - 1) * BX if j > 0 else columns - BX,
                    )
                    pieces.append(
                        tiles[
                            t,
                            side + from_other,
                            pl.ds(pl.multiple_of(start, TILE), TILE),
                            pl.ds(pl.multiple_of(offset, BX), BX),
                        ]
                    )
                centre = jnp.concatenate(pieces, axis=1).astype(jnp.float32)
                if valid is not None:
                    centre = centre * valid
                left = jnp.where(lane == 0, 0.0, pltpu.roll(centre, 1, 1))
                right = jnp.where(lane == window - 1, 0.0, pltpu.roll(centre, window - 1, 1))
                slot = z - depth * lead + 2
                for dx, value in enumerate((left, centre, right)):
                    at = slot * (3 * part) + dx * part + r * TILE
                    shifted[pl.ds(pl.multiple_of(at, TILE), TILE), :] = value.astype(jnp.bfloat16)

        if single:
            shifted[3 * part : 6 * part, :] = zero_slice
            at = (segment * depth + 2) * 3 * part
            shifted[at : at + 3 * part, :] = zero_slice

            @pl.loop(0, segment * depth, unroll=4)
            def _(z):
                shifts(z, None)
        else:

            @pl.loop(depth - 2, depth + segment * depth + 2)
            def _(z):
                at = q * segment * depth + z - depth
                valid = ((at >= 0) & (at < count_gz * depth)).astype(jnp.float32)
                shifts(z, valid)

        def first(z, valid):
            at = pl.multiple_of((z + 1) * (3 * part), TILE)
            total = jnp.dot(
                t1_ref[...], shifted[pl.ds(at, 9 * part), :], preferred_element_type=jnp.float32
            )
            values = jnp.maximum(total + bias_ref[...], 0.0)
            if valid is not None:
                values = values * valid
            at = pl.multiple_of((z + 1) * tall, TILE)
            hidden[pl.ds(at, tall), :] = values.astype(jnp.bfloat16)

        if single:
            hidden[0:tall, :] = zero_hidden
            at = (segment * depth + 1) * tall
            hidden[at : at + tall, :] = zero_hidden

            @pl.loop(0, segment * depth, unroll=2)
            def _(z):
                first(z, None)
        else:

            @pl.loop(-1, segment * depth + 1)
            def _(z):
                at = q * segment * depth + z
                first(z, ((at >= 0) & (at < count_gz * depth)).astype(jnp.float32))

        height = 2 * rows
        wide_lane = lax.broadcasted_iota(jnp.int32, (height, window), 1)
        fraction = (lax.broadcasted_iota(jnp.int32, (height, columns), 0) >> 2) & 1
        second_bias = jnp.where(fraction == 0, b2_ref[0], b2_ref[1])

        @pl.loop(0, segment * depth, unroll=2)
        def _(z):
            at = pl.multiple_of(z * tall, TILE)
            total = jnp.dot(
                t2_ref[...], hidden[pl.ds(at, 3 * tall), :], preferred_element_type=jnp.float32
            )
            before = pltpu.roll(total[0:height], 1, 1)
            after = pltpu.roll(total[2 * height :], window - 1, 1)
            total = total[height : 2 * height]
            total = total + jnp.where(wide_lane == 0, 0.0, before)
            total = total + jnp.where(wide_lane == window - 1, 0.0, after)
            own = jnp.where(c == 0, total[:, 0:columns], total[:, BX:window])
            values = 0.5 + 0.5 * jnp.tanh(0.5 * (own + second_bias))
            values = values.astype(jnp.bfloat16).astype(jnp.float32)
            t, zz = q * segment + z // depth, z % depth
            for yb in range(brick_rows):
                for xb in range(brick_columns):
                    bricks[t, yb * brick_columns + xb, zz] = values[
                        yb * 8 : yb * 8 + 8, xb * BX : (xb + 1) * BX
                    ]

        table.wait()

        @pl.loop(0, segment * capacity)
        def _(k):
            brick_of_slot[q * segment * capacity + k] = -1

        @pl.loop(0, segment)
        def _(t):
            rank = jnp.int32(0)
            for b in range(brick_rows * brick_columns):
                mine = owner_table[t, 0, b] == z_index

                @pl.when(mine)
                def _():
                    brick_of_slot[(q * segment + t) * capacity + rank] = b

                rank = rank + mine.astype(jnp.int32)

    if single:
        one_segment(0)
    else:

        @pl.loop(0, segments)
        def _(q):
            one_segment(q)

    for zz in range(depth):
        for xb in range(brick_columns):
            own = [bricks[z_index, yb * brick_columns + xb, zz] for yb in range(brick_rows)]
            for o in range(2):
                values = jnp.concatenate([v[o * BY : o * BY + BY] for v in own], axis=0)
                fractions_ref[o, zz, :, xb * BX : (xb + 1) * BX] = values.astype(jnp.bfloat16)

    size = depth * BY

    @pl.loop(0, slots)
    def _(j):
        brick = brick_of_slot[j]
        values = bricks[j // capacity, jnp.maximum(brick, 0)]
        values = jnp.where(brick >= 0, values, 0.0)
        at = pl.multiple_of(j * (2 * size), 8)
        arrived[pl.ds(at, 2 * size), :] = values.reshape(2 * size, BX)
        at = pl.multiple_of(j * size, size)
        mass[pl.ds(at, size), :] = 0.25 * biomass_ref[pl.ds(at, size), :].astype(jnp.float32)

    last = lax.broadcasted_iota(jnp.int32, (8, BX), 1) == BX - 1

    def laplace(field, z, y):
        centre = field[z][y]
        ahead = jnp.where(last, 0.0, pltpu.roll(centre, BX - 1, 1) - centre)
        result = ahead - pltpu.roll(ahead, 1, 1)
        beside = [
            field[zz][yy]
            for zz, yy in ((z - 1, y), (z + 1, y), (z, y - 1), (z, y + 1))
            if 0 <= zz < depth and 0 <= yy < BY
        ]
        return result + (functools.reduce(jnp.add, beside) - float(len(beside)) * centre)

    @pl.loop(0, slots // 8)
    def _(group):
        def load(ref, pitch, offset):
            return ref[pl.ds(group * 8 * pitch + offset, 8, stride=pitch), :]

        grid = [(z, y) for z in range(depth) for y in range(BY)]
        carbon = [[load(solutes_ref, 2 * size, z * BY + y) for y in range(BY)] for z in range(depth)]
        oxygen = [
            [load(solutes_ref, 2 * size, size + z * BY + y) for y in range(BY)]
            for z in range(depth)
        ]
        for _ in range(STEPS):
            carbon_new = [[None] * BY for _ in range(depth)]
            oxygen_new = [[None] * BY for _ in range(depth)]
            for z, y in grid:
                doc, oxy = carbon[z][y], oxygen[z][y]
                pore = load(arrived, 2 * size, z * 8 + y)
                organic = load(arrived, 2 * size, z * 8 + BY + y)
                quarter = load(mass, size, z * BY + y)
                uptake = (quarter * doc * oxy) / ((0.5 + jnp.abs(doc)) * (0.3 + jnp.abs(oxy)))
                carbon_new[z][y] = doc + (0.12 * pore) * laplace(carbon, z, y) + (
                    0.3 * organic - uptake
                )
                oxygen_new[z][y] = oxy + (0.16 * pore) * laplace(oxygen, z, y) - uptake
            carbon, oxygen = carbon_new, oxygen_new
        for z, y in grid:
            at = group * 16 * size + z * BY + y
            next_ref[pl.ds(at, 8, stride=2 * size), :] = carbon[z][y]
            next_ref[pl.ds(at + size, 8, stride=2 * size), :] = oxygen[z][y]


def vmem(shape, dtype):
    return pltpu.VMEM(shape, dtype)


def per_device(
    sizes, density, first_kernel, first_bias, second_kernel, second_bias, owners, solutes, biomass
):
    count_gz, count_gy, count_col = sizes
    depth, rows, columns = density.shape
    channels = first_kernel.shape[1]
    slots = solutes.shape[3]
    window = columns + BX
    edges = 1 if count_gy == 2 else 2
    part = rows + TILE * edges
    tall = (rows + 2) * channels
    segment = min(count_gz, 4)
    held = segment if segment == count_gz else segment + 2
    brick_count = (rows // BY) * (columns // BX)
    height = depth * rows

    named = jnp.zeros((TILE, columns), jnp.bfloat16)
    named = named.at[0, 0:brick_count].set(owners.reshape(brick_count).astype(jnp.bfloat16))
    payload = jnp.concatenate([density.reshape(height, columns), named], axis=0)
    gathered = lax.all_gather(payload, ("gz", "gy", "col"), axis=0, tiled=False)
    gathered = gathered.reshape(count_gz, count_gy, count_col, height + TILE, columns)

    in_vmem = pl.BlockSpec(memory_space=pltpu.VMEM)
    in_smem = pl.BlockSpec(memory_space=pltpu.SMEM)
    t1, bias, t2 = pl.pallas_call(
        functools.partial(banded_kernel, (rows, window, edges, count_gy, channels)),
        out_shape=(
            jax.ShapeDtypeStruct((tall, 9 * part), jnp.bfloat16),
            jax.ShapeDtypeStruct((tall, window), jnp.float32),
            jax.ShapeDtypeStruct((6 * rows, 3 * tall), jnp.bfloat16),
        ),
        in_specs=[in_vmem, in_smem, in_vmem],
        out_specs=(in_vmem, in_vmem, in_vmem),
        compiler_params=pltpu.CompilerParams(vmem_limit_bytes=24 * 2**20),
        cost_estimate=pl.CostEstimate(
            flops=2 * tall * 9 * part * 27 * 4, bytes_accessed=4 * 2**20, transcendentals=0
        ),
        name="banded",
    )(
        first_kernel.reshape(27, channels),
        first_bias,
        second_kernel.reshape(54, channels),
    )

    cells = depth * BY
    fractions, solutes_next = pl.pallas_call(
        functools.partial(
            column_kernel,
            (count_gz, count_gy, depth, rows, columns, channels, edges, segment, slots),
        ),
        out_shape=(
            jax.ShapeDtypeStruct((2, depth, rows, columns), jnp.bfloat16),
            jax.ShapeDtypeStruct((slots * 2 * cells, BX), jnp.float32),
        ),
        in_specs=[in_smem, pl.BlockSpec(memory_space=pl.ANY)] + [in_vmem] * 5,
        out_specs=(in_vmem, in_vmem),
        scratch_shapes=[
            vmem((held, 2 + 2 * edges, height + TILE, columns), jnp.bfloat16),
            vmem(((segment * depth + 4) * 3 * part, window), jnp.bfloat16),
            vmem(((segment * depth + 2) * tall, window), jnp.bfloat16),
            vmem((count_gz, brick_count, depth, 8, BX), jnp.float32),
            vmem((slots * 2 * cells, BX), jnp.float32),
            vmem((slots * cells, BX), jnp.float32),
            vmem((segment, 8, BX), jnp.int32),
            pltpu.SMEM((segment, 8, BX), jnp.int32),
            pltpu.SMEM((slots,), jnp.int32),
            pltpu.SemaphoreType.DMA((held, 2 + 2 * edges)),
            pltpu.SemaphoreType.DMA,
        ],
        compiler_params=pltpu.CompilerParams(vmem_limit_bytes=40 * 2**20),
        cost_estimate=pl.CostEstimate(
            flops=2 * count_gz * depth * window * tall * 9 * part,
            bytes_accessed=4 * 2**20,
            transcendentals=0,
        ),
        name="column",
    )(
        second_bias,
        gathered,
        t1,
        bias,
        t2,
        solutes.reshape(slots * 2 * cells, BX),
        biomass.reshape(slots * cells, BX),
    )
    return fractions, solutes_next.reshape(solutes.shape)


def solution(mesh):
    sizes = (mesh.shape["gz"], mesh.shape["gy"], mesh.shape["col"])
    assert sizes[2] == 2
    return jax.shard_map(
        functools.partial(per_device, sizes),
        mesh=mesh,
        in_specs=(
            P(("cores", "gz"), "gy", "col"),
            P(),
            P(),
            P(),
            P(),
            P(("cores", "gz"), "gy", "col", None, None),
            P(("cores", "gz"), "gy", "col", None, None, None, None, None),
            P(("cores", "gz"), "gy", "col", None, None, None, None),
        ),
        out_specs=(
            P(None, ("cores", "gz"), "gy", "col"),
            P(("cores", "gz"), "gy", "col", None, None, None, None, None),
        ),
        check_vma=False,
    )
```

```python
import functools

import jax
import jax.numpy as jnp
from jax import lax
from jax.experimental import pallas as pl
from jax.experimental.pallas import tpu as pltpu
from jax.sharding import PartitionSpec as P

BY = 4
BX = 128
STEPS = 4
TILE = 16
HALF = 16
CHANNELS = 8
REACH = HALF + 2
PART = 3 * HALF + TILE
TALL = REACH * CHANNELS
OUTSIDE = -3e38

VMEM = pl.BlockSpec(memory_space=pltpu.VMEM)
SMEM = pl.BlockSpec(memory_space=pltpu.SMEM)
HBM = pl.BlockSpec(memory_space=pltpu.HBM)


def step_index(values, width, count):
    index = jnp.zeros(values.shape, jnp.int32)
    for k in range(1, count):
        index = index + (values >= k * width).astype(jnp.int32)
    return index


def one_hot(condition):
    return jnp.where(condition, 1.0, 0.0).astype(jnp.bfloat16)


def iotas(shape):
    return (
        lax.broadcasted_iota(jnp.int32, shape, 0),
        lax.broadcasted_iota(jnp.int32, shape, 1),
    )


def tap_parts(tap):
    dz = step_index(tap, 9, 3)
    dy = step_index(tap - 9 * dz, 3, 3)
    return dz, dy, tap - 9 * dz - 3 * dy


def pack_kernel(density_ref, owners_ref, payload_ref, sem):
    height, columns = density_ref.shape
    copy = pltpu.make_async_copy(density_ref, payload_ref.at[0:height], sem)
    copy.start()
    named = owners_ref[...].astype(jnp.float32)
    count = named.shape[1]
    payload_ref[height : height + TILE, 0:BX] = jnp.concatenate(
        [
            jnp.broadcast_to(named, (TILE, count)),
            jnp.zeros((TILE, BX - count), jnp.float32),
        ],
        axis=1,
    ).astype(jnp.bfloat16)
    payload_ref[height : height + TILE, BX:columns] = jnp.zeros(
        (TILE, columns - BX), jnp.bfloat16
    )
    copy.wait()


def banded_kernel(dims, w1_ref, b1_ref, w2_ref, b2_ref, t1_ref, bias_ref, t2_ref, bias2_ref):
    window, count_gy = dims
    g = lax.axis_index("gy")
    row, channel = iotas((TALL, CHANNELS))
    spread = one_hot((row & (CHANNELS - 1)) == channel)
    w1 = jnp.dot(spread, w1_ref[...], preferred_element_type=jnp.float32).astype(jnp.bfloat16)
    tap, column = iotas((27, 3 * PART))
    dz = step_index(column, PART, 3)
    place = column - PART * dz
    dx = jnp.where(place < 3 * HALF, place >> 4, (place - 3 * HALF) >> 2)
    base = 9 * dz + dx
    row, column = iotas((TALL, 3 * PART))
    place = column & (PART - 1)
    seam = (place - 3 * HALF) & 3
    seam_row = jnp.where(seam < 2, seam - 2, seam + HALF - 2)
    input_row = jnp.where(place < 3 * HALF, place & (HALF - 1), seam_row)
    distance = jnp.where(place < 3 * HALF + 12, input_row - (row >> 3) + 2, -1)
    total = jnp.zeros((TALL, 3 * PART), jnp.float32)
    for dy in range(3):
        values = jnp.dot(w1, one_hot(tap == base + 3 * dy), preferred_element_type=jnp.float32)
        total = jnp.where(distance == dy, values, total)
    t1_ref[...] = total.astype(jnp.bfloat16)
    row, column = iotas((TALL, 2 * window))
    bias = jnp.zeros((TALL, 2 * window), jnp.float32)
    for k in range(CHANNELS):
        bias = jnp.where((row & (CHANNELS - 1)) == k, b1_ref[k], bias)
    outside = ((row < CHANNELS) & (column < window) & (g == 0)) | (
        (row >= TALL - CHANNELS) & (column >= window) & (g == count_gy - 1)
    )
    bias_ref[...] = jnp.where(outside, OUTSIDE, bias)
    channel, column = iotas((CHANNELS, 3 * TALL))
    spread = one_hot((column & (CHANNELS - 1)) == channel)
    tap, column = iotas((27, 3 * TALL))
    same_z = tap_parts(tap)[0] == step_index(column, TALL, 3)
    row, tap = iotas((6 * HALF, 27))
    _, tap_y, tap_x = tap_parts(tap)
    same_x = (row >> 5) == tap_x
    wide = []
    for o in range(2):
        values = lax.dot_general(
            w2_ref[o * CHANNELS : (o + 1) * CHANNELS, :],
            spread,
            (((0,), (0,)), ((), ())),
            preferred_element_type=jnp.float32,
        )
        wide.append(jnp.where(same_z, values, 0.0).astype(jnp.bfloat16))
    out_row, column = iotas((6 * HALF, 3 * TALL))
    y = ((out_row >> 3) & 3) * BY + (out_row & 3)
    hidden_row = (column - TALL * step_index(column, TALL, 3)) >> 3
    total = jnp.zeros((6 * HALF, 3 * TALL), jnp.float32)
    for dy in range(3):
        values = 0.0
        for o in range(2):
            pick = one_hot(same_x & (tap_y == dy) & (((row >> 2) & 1) == o))
            values = values + jnp.dot(pick, wide[o], preferred_element_type=jnp.float32)
        total = jnp.where(hidden_row - y == dy, values, total)
    t2_ref[...] = total.astype(jnp.bfloat16)
    row, _ = iotas((2 * HALF, 2 * window))
    bias2_ref[...] = jnp.where(((row >> 2) & 1) == 0, b2_ref[0], b2_ref[1])


def edges_kernel(dims, *refs):
    count_gy, depth, rows, columns, few, count = dims
    tiles, outs = refs[:few], refs[few:]
    g = lax.axis_index("gy")
    c = lax.axis_index("col")
    block = pl.multiple_of((1 - c) * BX, BX)

    def take(i, start, size, lanes):
        if few > 1:
            return tiles[i][pl.ds(start, size), lanes]
        return tiles[0][i, pl.ds(start, size), lanes]

    def pair(i):
        whole = pl.ds(0, columns)
        some = pl.ds(block, BX)
        for k in range(2):
            height = depth * rows
            at = (2 * i + k) * height
            if not isinstance(at, int):
                at = pl.multiple_of(at, TILE)
            outs[0][pl.ds(at, height), :] = take(2 * i + k, 0, height, some)
        low, high = ([], []), ([], [])
        for k in range(2):
            for zz in range(depth):
                for n, lanes in enumerate((whole, some)):
                    first = take(2 * i + k, zz * rows, TILE, lanes).astype(jnp.float32)
                    last = take(2 * i + k, (zz + 1) * rows - TILE, TILE, lanes).astype(jnp.float32)
                    low[n].append(first[0:2])
                    high[n].append(last[TILE - 2 :])
        at = 2 * i * 2 * depth
        if not isinstance(at, int):
            at = pl.multiple_of(at, TILE)
        for n in range(2):
            first = jnp.concatenate(low[n], axis=0)
            last = jnp.concatenate(high[n], axis=0)
            if count_gy == 2:
                send = jnp.where(g == 0, last, first)
                outs[1 + n][pl.ds(at, TILE), :] = send.astype(jnp.bfloat16)
            else:
                outs[1 + n][pl.ds(at, TILE), :] = last.astype(jnp.bfloat16)
                outs[3 + n][pl.ds(at, TILE), :] = first.astype(jnp.bfloat16)

    if few > 1:
        for i in range(count // 2):
            pair(i)
    else:
        pl.loop(0, count // 2)(pair)


def column_kernel(dims, few, *refs):
    count_gz, count_gy, depth, rows, columns, segment, slots = dims
    tiles, refs = refs[:few], refs[few:]
    x_ref, refs = refs[0], refs[1:]
    top_refs, refs = refs[:2], refs[2:]
    if count_gy == 2:
        bottom_refs = top_refs
    else:
        bottom_refs, refs = refs[:2], refs[2:]
    t1_ref, bias_ref, t2_ref, bias2_ref, solutes_ref, biomass_ref, *refs = refs
    fractions_ref, next_ref, *refs = refs
    (
        edge_rows,
        shifted,
        hidden,
        bricks,
        arrived,
        state,
        biomass,
        mass,
        fractions,
        owner_rows,
        owner_table,
        brick_of_slot,
        sems,
        group_sems,
    ) = refs
    z_index = lax.axis_index("gz")
    g = lax.axis_index("gy")
    c = lax.axis_index("col")
    window = columns + BX
    brick_rows = HALF // BY
    brick_columns = columns // BX
    brick_count = rows // BY * brick_columns
    capacity = slots // count_gz
    single = segment == count_gz
    first_tile = z_index if few > 1 else 0
    size = depth * BY

    state_copy = pltpu.make_async_copy(solutes_ref, state, sems.at[0])
    state_copy.start()
    biomass_copy = pltpu.make_async_copy(biomass_ref, biomass, sems.at[1])
    biomass_copy.start()

    def tile_rows(i, start, size, lanes):
        if not isinstance(start, int):
            start = pl.multiple_of(start, TILE)
        if few > 1:
            return tiles[i][pl.ds(start, size), lanes]
        return tiles[0][i, pl.ds(start, size), lanes]

    def read_owners(i):
        row = tile_rows(i, depth * rows, TILE, pl.ds(0, BX))
        owner_rows[i] = row.astype(jnp.float32)[0:8].astype(jnp.int32)

    if few > 1:
        for i in range(count_gz):
            read_owners(i)
    else:
        pl.loop(0, count_gz)(read_owners)
    table_copy = pltpu.make_async_copy(owner_rows, owner_table, sems.at[2])
    table_copy.start()

    def arrange(own, other):
        left, right = own[:, 0:BX], own[:, BX:columns]
        return jnp.concatenate(
            [
                jnp.where(c == 0, left, other),
                jnp.where(c == 0, right, left),
                jnp.where(c == 0, other, right),
            ],
            axis=1,
        )

    for k, pair in enumerate((top_refs, bottom_refs)):
        exists = (g > 0) if k == 0 else (g < count_gy - 1)
        values = arrange(pair[0][...].astype(jnp.float32), pair[1][...].astype(jnp.float32))
        edge_rows[k] = values * exists.astype(jnp.float32)

    def moved(values):
        lane = lax.broadcasted_iota(jnp.int32, values.shape, 1)
        return (
            jnp.where(lane == 0, 0.0, pltpu.roll(values, 1, 1)),
            values,
            jnp.where(lane == window - 1, 0.0, pltpu.roll(values, window - 1, 1)),
        )

    def edge_pair(k, at):
        if isinstance(at, int):
            return edge_rows[k, at : at + 2, :]
        group = edge_rows[k, pl.ds(pl.multiple_of(at // 8 * 8, 8), 8), :]
        return pltpu.roll(group, lax.rem(8 - at % 8, 8), 0)[0:2]

    def shifts(i, zz, slot, valid):
        z = i * depth + zz
        halves = []
        for h in range(2):
            own = tile_rows(i, zz * rows + h * HALF, HALF, pl.ds(0, columns))
            at = z * rows + h * HALF
            if not isinstance(at, int):
                at = pl.multiple_of(at, TILE)
            values = arrange(own, x_ref[pl.ds(at, HALF), :]).astype(jnp.float32)
            halves.append(values if valid is None else values * valid)
        top, bottom = edge_pair(0, 2 * z), edge_pair(1, 2 * z)
        if valid is not None:
            top, bottom = top * valid, bottom * valid
        seams = [
            jnp.concatenate([top, halves[1][0:2]], axis=0),
            jnp.concatenate([halves[0][HALF - 2 :], bottom], axis=0),
        ]
        for h in range(2):
            lanes = slice(h * window, (h + 1) * window)
            for dx, values in enumerate(moved(halves[h])):
                shifted[slot, dx * HALF : (dx + 1) * HALF, lanes] = values.astype(jnp.bfloat16)
            values = jnp.concatenate(
                [*moved(seams[h]), jnp.zeros((4, window), jnp.float32)], axis=0
            )
            shifted[slot, 3 * HALF : PART, lanes] = values.astype(jnp.bfloat16)

    def first(z, valid):
        total = jnp.dot(
            t1_ref[...],
            shifted[pl.ds(z + 1, 3)].reshape(3 * PART, 2 * window),
            preferred_element_type=jnp.float32,
        )
        values = jnp.maximum(total + bias_ref[...], 0.0)
        if valid is not None:
            values = values * valid
        hidden[z + 1] = values.astype(jnp.bfloat16)

    height = 2 * HALF
    lane = lax.broadcasted_iota(jnp.int32, (height, 2 * window), 1)
    left_edge = (lane == 0) | (lane == window)
    right_edge = (lane == window - 1) | (lane == 2 * window - 1)

    def second(z, t, zz):
        total = jnp.dot(
            t2_ref[...],
            hidden[pl.ds(z, 3)].reshape(3 * TALL, 2 * window),
            preferred_element_type=jnp.float32,
        )
        before = pltpu.roll(total[0:height], 1, 1)
        after = pltpu.roll(total[2 * height :], 2 * window - 1, 1)
        total = total[height : 2 * height] + bias2_ref[...]
        total = total + jnp.where(left_edge, 0.0, before)
        total = total + jnp.where(right_edge, 0.0, after)
        for h in range(2):
            at = h * window
            own = jnp.where(
                c == 0, total[:, at : at + columns], total[:, at + BX : at + window]
            )
            values = 0.5 + 0.5 * jnp.tanh(0.5 * own)
            values = values.astype(jnp.bfloat16).astype(jnp.float32)
            for yb in range(brick_rows):
                for xb in range(brick_columns):
                    b = (h * brick_rows + yb) * brick_columns + xb
                    bricks[t, b, zz] = values[yb * 8 : yb * 8 + 8, xb * BX : (xb + 1) * BX]

    def valid_slice(z):
        return ((z >= 0) & (z < count_gz * depth)).astype(jnp.float32)

    depths = segment * depth
    if single:
        shifted[1] = jnp.zeros((PART, 2 * window), jnp.bfloat16)
        shifted[depths + 2] = jnp.zeros((PART, 2 * window), jnp.bfloat16)
        hidden[0] = jnp.zeros((TALL, 2 * window), jnp.bfloat16)
        hidden[depths + 1] = jnp.zeros((TALL, 2 * window), jnp.bfloat16)
        for i in range(count_gz):
            tile = lax.rem(first_tile + i, count_gz)
            for zz in range(depth):
                shifts(i, zz, tile * depth + zz + 2, None)

        @pl.loop(0, depths, unroll=4)
        def _(z):
            first(z, None)

        @pl.loop(0, depths, unroll=4)
        def _(z):
            second(z, z // depth, z % depth)
    else:

        @pl.loop(0, count_gz // segment)
        def _(q):
            @pl.loop(-2, depths + 2)
            def _(z):
                at = q * depths + z
                inside = jnp.clip(at, 0, count_gz * depth - 1)
                shifts(inside // depth, inside % depth, z + 2, valid_slice(at))

            @pl.loop(-1, depths + 1)
            def _(z):
                first(z, valid_slice(q * depths + z))

            @pl.loop(0, depths)
            def _(z):
                second(z, q * segment + z // depth, z % depth)

    for zz in range(depth):
        for xb in range(brick_columns):
            own = [
                bricks[z_index, yb * brick_columns + xb, zz] for yb in range(rows // BY)
            ]
            for o in range(2):
                values = jnp.concatenate([v[o * BY : o * BY + BY] for v in own], axis=0)
                fractions[o, zz, :, xb * BX : (xb + 1) * BX] = values.astype(jnp.bfloat16)
    fractions_copy = pltpu.make_async_copy(fractions, fractions_ref, sems.at[3])
    fractions_copy.start()

    table_copy.wait()

    @pl.loop(0, slots)
    def _(j):
        brick_of_slot[j] = -1

    @pl.loop(0, count_gz)
    def _(i):
        tile = lax.rem(first_tile + i, count_gz)
        rank = jnp.int32(0)
        for b in range(brick_count):
            mine = owner_table[i, 0, b] == z_index

            @pl.when(mine)
            def _():
                brick_of_slot[tile * capacity + rank] = b

            rank = rank + mine.astype(jnp.int32)

    biomass_copy.wait()

    @pl.loop(0, slots)
    def _(j):
        brick = brick_of_slot[j]
        values = bricks[j // capacity, jnp.maximum(brick, 0)]
        values = jnp.where(brick >= 0, values, 0.0)
        at = pl.multiple_of(j * (2 * size), 8)
        arrived[pl.ds(at, 2 * size), :] = values.reshape(2 * size, BX)
        at = pl.multiple_of(j * size, size)
        mass[pl.ds(at, size), :] = 0.25 * biomass[pl.ds(at, size), :].astype(jnp.float32)

    last = lax.broadcasted_iota(jnp.int32, (8, BX), 1) == BX - 1

    def laplace(field, z, y):
        centre = field[z][y]
        ahead = jnp.where(last, 0.0, pltpu.roll(centre, BX - 1, 1) - centre)
        result = ahead - pltpu.roll(ahead, 1, 1)
        beside = [
            field[zz][yy]
            for zz, yy in ((z - 1, y), (z + 1, y), (z, y - 1), (z, y + 1))
            if 0 <= zz < depth and 0 <= yy < BY
        ]
        return result + (functools.reduce(jnp.add, beside) - float(len(beside)) * centre)

    state_copy.wait()

    def next_copy(group):
        at = pl.ds(pl.multiple_of(group * 16 * size, 16 * size), 16 * size)
        return pltpu.make_async_copy(state.at[at], next_ref.at[at], group_sems.at[group])

    @pl.loop(0, slots // 8)
    def _(group):
        def rows_of(pitch, offset):
            return pl.ds(group * 8 * pitch + offset, 8, stride=pitch)

        grid = [(z, y) for z in range(depth) for y in range(BY)]
        carbon = [
            [state[rows_of(2 * size, z * BY + y), :] for y in range(BY)] for z in range(depth)
        ]
        oxygen = [
            [state[rows_of(2 * size, size + z * BY + y), :] for y in range(BY)]
            for z in range(depth)
        ]
        for _ in range(STEPS):
            carbon_new = [[None] * BY for _ in range(depth)]
            oxygen_new = [[None] * BY for _ in range(depth)]
            for z, y in grid:
                doc, oxy = carbon[z][y], oxygen[z][y]
                pore = arrived[rows_of(2 * size, z * 8 + y), :]
                organic = arrived[rows_of(2 * size, z * 8 + BY + y), :]
                quarter = mass[rows_of(size, z * BY + y), :]
                uptake = (quarter * doc * oxy) / ((0.5 + jnp.abs(doc)) * (0.3 + jnp.abs(oxy)))
                carbon_new[z][y] = doc + (0.12 * pore) * laplace(carbon, z, y) + (
                    0.3 * organic - uptake
                )
                oxygen_new[z][y] = oxy + (0.16 * pore) * laplace(oxygen, z, y) - uptake
            carbon, oxygen = carbon_new, oxygen_new
        for z, y in grid:
            state[rows_of(2 * size, z * BY + y), :] = carbon[z][y]
            state[rows_of(2 * size, size + z * BY + y), :] = oxygen[z][y]
        next_copy(group).start()

    @pl.loop(0, slots // 8)
    def _(group):
        next_copy(group).wait()

    fractions_copy.wait()


def per_device(
    sizes, density, first_kernel, first_bias, second_kernel, second_bias, owners, solutes, biomass
):
    count_gz, count_gy, count_col = sizes
    depth, rows, columns = density.shape
    slots = solutes.shape[3]
    window = columns + BX
    segment = min(count_gz, 4)
    brick_count = (rows // BY) * (columns // BX)
    height = depth * rows
    depths = count_gz * depth
    bf16, f32 = jnp.bfloat16, jnp.float32
    shape = jax.ShapeDtypeStruct

    payload = pl.pallas_call(
        pack_kernel,
        out_shape=shape((height + TILE, columns), bf16),
        in_specs=[HBM, VMEM],
        out_specs=VMEM,
        scratch_shapes=[pltpu.SemaphoreType.DMA],
        compiler_params=pltpu.CompilerParams(vmem_limit_bytes=4 * 2**20),
        name="pack",
    )(density.reshape(height, columns), owners.reshape(1, brick_count))

    few = count_gz if count_gz == segment else 1
    if few > 1:
        tiles = [payload] + [
            lax.ppermute(payload, "gz", [((i + s) % count_gz, i) for i in range(count_gz)])
            for s in range(1, count_gz)
        ]
    else:
        tiles = [lax.all_gather(payload, "gz", axis=0, tiled=False)]

    t1, bias, t2, bias2 = pl.pallas_call(
        functools.partial(banded_kernel, (window, count_gy)),
        out_shape=(
            shape((TALL, 3 * PART), bf16),
            shape((TALL, 2 * window), f32),
            shape((6 * HALF, 3 * TALL), bf16),
            shape((2 * HALF, 2 * window), f32),
        ),
        in_specs=[VMEM, SMEM, VMEM, SMEM],
        out_specs=(VMEM, VMEM, VMEM, VMEM),
        compiler_params=pltpu.CompilerParams(vmem_limit_bytes=16 * 2**20),
        cost_estimate=pl.CostEstimate(
            flops=20 * 2**20, bytes_accessed=4 * 2**20, transcendentals=0
        ),
        name="banded",
    )(
        first_kernel.transpose(2, 1, 0).reshape(CHANNELS, 27),
        first_bias,
        second_kernel.transpose(1, 2, 0).reshape(2 * CHANNELS, 27),
        second_bias,
    )

    edge_shapes = [shape((2 * depths, columns), bf16), shape((2 * depths, BX), bf16)]
    sent = pl.pallas_call(
        functools.partial(edges_kernel, (count_gy, depth, rows, columns, few, count_gz)),
        out_shape=[shape((depths * rows, BX), bf16)] + edge_shapes * (1 if count_gy == 2 else 2),
        in_specs=[VMEM] * few,
        out_specs=[VMEM] * (3 if count_gy == 2 else 5),
        compiler_params=pltpu.CompilerParams(vmem_limit_bytes=16 * 2**20),
        name="edges",
    )(*tiles)

    def over(pairs):
        return [
            (gy * count_col + col, to * count_col + 1 - col)
            for gy, to in pairs
            for col in range(count_col)
        ]

    beside = lax.ppermute(sent[0], "col", [(0, 1), (1, 0)])
    if count_gy == 2:
        directions = [[(0, 1), (1, 0)]]
    else:
        up = [(i, i + 1) for i in range(count_gy - 1)]
        directions = [up, [(j, i) for i, j in up]]
    edges = []
    for k, pairs in enumerate(directions):
        edges.append(lax.ppermute(sent[1 + 2 * k], "gy", pairs))
        edges.append(lax.ppermute(sent[2 + 2 * k], ("gy", "col"), over(pairs)))

    cells = depth * BY
    fractions, solutes_next = pl.pallas_call(
        functools.partial(
            column_kernel, (count_gz, count_gy, depth, rows, columns, segment, slots), few
        ),
        out_shape=(
            shape((2, depth, rows, columns), bf16),
            shape((slots * 2 * cells, BX), f32),
        ),
        in_specs=[VMEM] * (few + 1 + len(edges) + 4) + [HBM, HBM],
        out_specs=(HBM, HBM),
        scratch_shapes=[
            pltpu.VMEM((2, 2 * depths, window), f32),
            pltpu.VMEM((segment * depth + 4, PART, 2 * window), bf16),
            pltpu.VMEM((segment * depth + 2, TALL, 2 * window), bf16),
            pltpu.VMEM((count_gz, brick_count, depth, 8, BX), f32),
            pltpu.VMEM((slots * 2 * cells, BX), f32),
            pltpu.VMEM((slots * 2 * cells, BX), f32),
            pltpu.VMEM((slots * cells, BX), bf16),
            pltpu.VMEM((slots * cells, BX), f32),
            pltpu.VMEM((2, depth, rows, columns), bf16),
            pltpu.VMEM((count_gz, 8, BX), jnp.int32),
            pltpu.SMEM((count_gz, 8, BX), jnp.int32),
            pltpu.SMEM((slots,), jnp.int32),
            pltpu.SemaphoreType.DMA((4,)),
            pltpu.SemaphoreType.DMA((slots // 8,)),
        ],
        compiler_params=pltpu.CompilerParams(vmem_limit_bytes=40 * 2**20),
        cost_estimate=pl.CostEstimate(
            flops=2 * depths * 2 * window * TALL * (3 * PART + 3 * 6 * HALF),
            bytes_accessed=4 * 2**20,
            transcendentals=0,
        ),
        name="column",
    )(
        *tiles,
        beside,
        *edges,
        t1,
        bias,
        t2,
        bias2,
        solutes.reshape(slots * 2 * cells, BX),
        biomass.reshape(slots * cells, BX),
    )
    return fractions, solutes_next.reshape(solutes.shape)


def solution(mesh):
    sizes = (mesh.shape["gz"], mesh.shape["gy"], mesh.shape["col"])
    assert sizes[2] == 2
    return jax.shard_map(
        functools.partial(per_device, sizes),
        mesh=mesh,
        in_specs=(
            P(("cores", "gz"), "gy", "col"),
            P(),
            P(),
            P(),
            P(),
            P(("cores", "gz"), "gy", "col", None, None),
            P(("cores", "gz"), "gy", "col", None, None, None, None, None),
            P(("cores", "gz"), "gy", "col", None, None, None, None),
        ),
        out_specs=(
            P(None, ("cores", "gz"), "gy", "col"),
            P(("cores", "gz"), "gy", "col", None, None, None, None, None),
        ),
        check_vma=False,
    )
```

```python
import functools

import jax
import jax.numpy as jnp
from jax import lax
from jax.experimental import pallas as pl
from jax.experimental.pallas import tpu as pltpu
from jax.sharding import PartitionSpec as P

BY = 4
BX = 128
STEPS = 4
TILE = 16
HALF = 16
CHANNELS = 8
REACH = HALF + 2
PART = 3 * HALF + TILE
TALL = REACH * CHANNELS
OUTSIDE = -3e38

VMEM = pl.BlockSpec(memory_space=pltpu.VMEM)
SMEM = pl.BlockSpec(memory_space=pltpu.SMEM)
HBM = pl.BlockSpec(memory_space=pltpu.HBM)


def in_hbm(array):
    return pltpu.with_memory_space_constraint(array, pltpu.HBM)


def step_index(values, width, count):
    index = jnp.zeros(values.shape, jnp.int32)
    for k in range(1, count):
        index = index + (values >= k * width).astype(jnp.int32)
    return index


def one_hot(condition):
    return jnp.where(condition, 1.0, 0.0).astype(jnp.bfloat16)


def iotas(shape):
    return (
        lax.broadcasted_iota(jnp.int32, shape, 0),
        lax.broadcasted_iota(jnp.int32, shape, 1),
    )


def tap_parts(tap):
    dz = step_index(tap, 9, 3)
    dy = step_index(tap - 9 * dz, 3, 3)
    return dz, dy, tap - 9 * dz - 3 * dy


def pack_kernel(density_ref, owners_ref, payload_ref, named_ref, sems):
    height, columns = density_ref.shape
    blocks = columns // BX
    copies = [pltpu.make_async_copy(owners_ref, named_ref, sems.at[blocks])]
    for k in range(blocks):
        copies.append(
            pltpu.make_async_copy(
                density_ref.at[:, k * BX : (k + 1) * BX],
                payload_ref.at[k * height : (k + 1) * height],
                sems.at[k],
            )
        )
    for copy in copies:
        copy.start()
    copies[0].wait()
    named = named_ref[...].astype(jnp.float32)
    count = named.shape[1]
    payload_ref[blocks * height : blocks * height + TILE, :] = jnp.concatenate(
        [
            jnp.broadcast_to(named, (TILE, count)),
            jnp.zeros((TILE, BX - count), jnp.float32),
        ],
        axis=1,
    ).astype(jnp.bfloat16)
    for copy in copies[1:]:
        copy.wait()


def banded_kernel(dims, *refs):
    window, count_gy = dims
    sources, refs = refs[:4], refs[5:]
    t1_ref, bias_ref, t2_ref, bias2_ref, *local, sems = refs
    copies = [
        pltpu.make_async_copy(source, target, sems.at[k])
        for k, (source, target) in enumerate(zip(sources, local))
    ]
    for copy in copies:
        copy.start()
    for copy in copies:
        copy.wait()
    w1_ref, b1_ref, w2_ref, b2_ref = local
    g = lax.axis_index("gy")
    row, channel = iotas((TALL, CHANNELS))
    spread = one_hot((row & (CHANNELS - 1)) == channel)
    w1 = jnp.dot(spread, w1_ref[...], preferred_element_type=jnp.float32).astype(jnp.bfloat16)
    tap, column = iotas((27, 3 * PART))
    dz = step_index(column, PART, 3)
    place = column - PART * dz
    dx = jnp.where(place < 3 * HALF, place >> 4, (place - 3 * HALF) >> 2)
    base = 9 * dz + dx
    row, column = iotas((TALL, 3 * PART))
    place = column & (PART - 1)
    seam = (place - 3 * HALF) & 3
    seam_row = jnp.where(seam < 2, seam - 2, seam + HALF - 2)
    input_row = jnp.where(place < 3 * HALF, place & (HALF - 1), seam_row)
    distance = jnp.where(place < 3 * HALF + 12, input_row - (row >> 3) + 2, -1)
    total = jnp.zeros((TALL, 3 * PART), jnp.float32)
    for dy in range(3):
        values = jnp.dot(w1, one_hot(tap == base + 3 * dy), preferred_element_type=jnp.float32)
        total = jnp.where(distance == dy, values, total)
    t1_ref[...] = total.astype(jnp.bfloat16)
    row, column = iotas((TALL, 2 * window))
    bias = jnp.zeros((TALL, 2 * window), jnp.float32)
    for k in range(CHANNELS):
        bias = jnp.where((row & (CHANNELS - 1)) == k, b1_ref[k], bias)
    outside = ((row < CHANNELS) & (column < window) & (g == 0)) | (
        (row >= TALL - CHANNELS) & (column >= window) & (g == count_gy - 1)
    )
    bias_ref[...] = jnp.where(outside, OUTSIDE, bias)
    channel, column = iotas((CHANNELS, 3 * TALL))
    spread = one_hot((column & (CHANNELS - 1)) == channel)
    tap, column = iotas((27, 3 * TALL))
    same_z = tap_parts(tap)[0] == step_index(column, TALL, 3)
    row, tap = iotas((6 * HALF, 27))
    _, tap_y, tap_x = tap_parts(tap)
    same_x = (row >> 5) == tap_x
    wide = []
    for o in range(2):
        values = lax.dot_general(
            w2_ref[o * CHANNELS : (o + 1) * CHANNELS, :],
            spread,
            (((0,), (0,)), ((), ())),
            preferred_element_type=jnp.float32,
        )
        wide.append(jnp.where(same_z, values, 0.0).astype(jnp.bfloat16))
    out_row, column = iotas((6 * HALF, 3 * TALL))
    y = ((out_row >> 3) & 3) * BY + (out_row & 3)
    hidden_row = (column - TALL * step_index(column, TALL, 3)) >> 3
    total = jnp.zeros((6 * HALF, 3 * TALL), jnp.float32)
    for dy in range(3):
        values = 0.0
        for o in range(2):
            pick = one_hot(same_x & (tap_y == dy) & (((row >> 2) & 1) == o))
            values = values + jnp.dot(pick, wide[o], preferred_element_type=jnp.float32)
        total = jnp.where(hidden_row - y == dy, values, total)
    t2_ref[...] = total.astype(jnp.bfloat16)
    row, _ = iotas((2 * HALF, 2 * window))
    bias2_ref[...] = jnp.where(((row >> 2) & 1) == 0, b2_ref[0], b2_ref[1])


def edges_kernel(dims, *refs):
    count_gy, depth, rows, columns, few, count = dims
    tiles, outs = refs[:few], refs[few + 1 :]
    g = lax.axis_index("gy")
    c = lax.axis_index("col")
    height = depth * rows
    block = (1 - c) * height

    def take(i, start, size):
        start = pl.ds(pl.multiple_of(start, TILE), size)
        if few > 1:
            return tiles[i][start, :]
        return tiles[0][i, start, :]

    def pair(i):
        for k in range(2):
            at = pl.multiple_of((2 * i + k) * height, TILE)
            outs[0][pl.ds(at, height), :] = take(2 * i + k, block, height)
        low, high = [], []
        for k in range(2):
            for zz in range(depth):
                first, last = [], []
                for base in (0, height):
                    at = base + zz * rows
                    first.append(take(2 * i + k, at, TILE).astype(jnp.float32)[0:2])
                    at = at + rows - TILE
                    last.append(take(2 * i + k, at, TILE).astype(jnp.float32)[TILE - 2 :])
                low.append(jnp.concatenate(first, axis=1))
                high.append(jnp.concatenate(last, axis=1))
        at = pl.multiple_of(2 * i * 2 * depth, TILE)
        first, last = jnp.concatenate(low, axis=0), jnp.concatenate(high, axis=0)
        sends = [jnp.where(g == 0, last, first)] if count_gy == 2 else [last, first]
        for n, send in enumerate(sends):
            send = send.astype(jnp.bfloat16)
            outs[1 + 2 * n][pl.ds(at, TILE), :] = send
            outs[2 + 2 * n][pl.ds(at, TILE), :] = jnp.where(
                c == 0, send[:, BX:columns], send[:, 0:BX]
            )

    if few > 1:
        for i in range(count // 2):
            pair(i)
    else:
        pl.loop(0, count // 2)(pair)


def column_kernel(dims, few, *refs):
    count_gz, count_gy, depth, rows, columns, segment, slots = dims
    tiles, refs = refs[:few], refs[few:]
    x_ref, refs = refs[0], refs[1:]
    top_refs, refs = refs[:2], refs[2:]
    if count_gy == 2:
        bottom_refs = top_refs
    else:
        bottom_refs, refs = refs[:2], refs[2:]
    t1_ref, bias_ref, t2_ref, bias2_ref, solutes_ref, biomass_ref, *refs = refs
    fractions_ref, next_ref, *refs = refs
    (
        edge_rows,
        shifted,
        hidden,
        bricks,
        arrived,
        state,
        biomass,
        mass,
        fractions,
        owner_rows,
        owner_table,
        brick_of_slot,
        sems,
        group_sems,
    ) = refs
    z_index = lax.axis_index("gz")
    g = lax.axis_index("gy")
    c = lax.axis_index("col")
    window = columns + BX
    brick_rows = HALF // BY
    brick_columns = columns // BX
    brick_count = rows // BY * brick_columns
    capacity = slots // count_gz
    single = segment == count_gz
    first_tile = z_index if few > 1 else 0
    size = depth * BY

    state_copy = pltpu.make_async_copy(solutes_ref, state, sems.at[0])
    state_copy.start()
    biomass_copy = pltpu.make_async_copy(biomass_ref, biomass, sems.at[1])
    biomass_copy.start()

    def tile_rows(i, start, size):
        if not isinstance(start, int):
            start = pl.multiple_of(start, TILE)
        if few > 1:
            return tiles[i][pl.ds(start, size), :]
        return tiles[0][i, pl.ds(start, size), :]

    def read_owners(i):
        row = tile_rows(i, brick_columns * depth * rows, TILE)
        owner_rows[i] = row.astype(jnp.float32)[0:8].astype(jnp.int32)

    if few > 1:
        for i in range(count_gz):
            read_owners(i)
    else:
        pl.loop(0, count_gz)(read_owners)
    table_copy = pltpu.make_async_copy(owner_rows, owner_table, sems.at[2])
    table_copy.start()

    def arrange(left, right, other):
        return jnp.concatenate(
            [
                jnp.where(c == 0, left, other),
                jnp.where(c == 0, right, left),
                jnp.where(c == 0, other, right),
            ],
            axis=1,
        )

    for k, pair in enumerate((top_refs, bottom_refs)):
        exists = (g > 0) if k == 0 else (g < count_gy - 1)
        own, other = pair[0][...].astype(jnp.float32), pair[1][...].astype(jnp.float32)
        values = arrange(own[:, 0:BX], own[:, BX:columns], other)
        edge_rows[k] = values * exists.astype(jnp.float32)

    def moved(values):
        lane = lax.broadcasted_iota(jnp.int32, values.shape, 1)
        return (
            jnp.where(lane == 0, 0.0, pltpu.roll(values, 1, 1)),
            values,
            jnp.where(lane == window - 1, 0.0, pltpu.roll(values, window - 1, 1)),
        )

    def edge_pair(k, at):
        if isinstance(at, int):
            return edge_rows[k, at : at + 2, :]
        group = edge_rows[k, pl.ds(pl.multiple_of(at // 8 * 8, 8), 8), :]
        return pltpu.roll(group, lax.rem(8 - at % 8, 8), 0)[0:2]

    def shifts(i, zz, slot, valid):
        z = i * depth + zz
        halves = []
        for h in range(2):
            at = zz * rows + h * HALF
            own = [tile_rows(i, k * depth * rows + at, HALF) for k in range(2)]
            at = z * rows + h * HALF
            if not isinstance(at, int):
                at = pl.multiple_of(at, TILE)
            values = arrange(*own, x_ref[pl.ds(at, HALF), :]).astype(jnp.float32)
            halves.append(values if valid is None else values * valid)
        top, bottom = edge_pair(0, 2 * z), edge_pair(1, 2 * z)
        if valid is not None:
            top, bottom = top * valid, bottom * valid
        seams = [
            jnp.concatenate([top, halves[1][0:2]], axis=0),
            jnp.concatenate([halves[0][HALF - 2 :], bottom], axis=0),
        ]
        for h in range(2):
            lanes = slice(h * window, (h + 1) * window)
            for dx, values in enumerate(moved(halves[h])):
                shifted[slot, dx * HALF : (dx + 1) * HALF, lanes] = values.astype(jnp.bfloat16)
            values = jnp.concatenate(
                [*moved(seams[h]), jnp.zeros((4, window), jnp.float32)], axis=0
            )
            shifted[slot, 3 * HALF : PART, lanes] = values.astype(jnp.bfloat16)

    def first(z, valid):
        total = jnp.dot(
            t1_ref[...],
            shifted[pl.ds(z + 1, 3)].reshape(3 * PART, 2 * window),
            preferred_element_type=jnp.float32,
        )
        values = jnp.maximum(total + bias_ref[...], 0.0)
        if valid is not None:
            values = values * valid
        hidden[z + 1] = values.astype(jnp.bfloat16)

    height = 2 * HALF
    lane = lax.broadcasted_iota(jnp.int32, (height, 2 * window), 1)
    left_edge = (lane == 0) | (lane == window)
    right_edge = (lane == window - 1) | (lane == 2 * window - 1)

    def second(z, t, zz):
        total = jnp.dot(
            t2_ref[...],
            hidden[pl.ds(z, 3)].reshape(3 * TALL, 2 * window),
            preferred_element_type=jnp.float32,
        )
        before = pltpu.roll(total[0:height], 1, 1)
        after = pltpu.roll(total[2 * height :], 2 * window - 1, 1)
        total = total[height : 2 * height] + bias2_ref[...]
        total = total + jnp.where(left_edge, 0.0, before)
        total = total + jnp.where(right_edge, 0.0, after)
        for h in range(2):
            at = h * window
            own = jnp.where(
                c == 0, total[:, at : at + columns], total[:, at + BX : at + window]
            )
            values = 0.5 + 0.5 * jnp.tanh(0.5 * own)
            values = values.astype(jnp.bfloat16).astype(jnp.float32)
            for yb in range(brick_rows):
                for xb in range(brick_columns):
                    b = (h * brick_rows + yb) * brick_columns + xb
                    bricks[t, b, zz] = values[yb * 8 : yb * 8 + 8, xb * BX : (xb + 1) * BX]

    def valid_slice(z):
        return ((z >= 0) & (z < count_gz * depth)).astype(jnp.float32)

    depths = segment * depth
    if single:
        shifted[1] = jnp.zeros((PART, 2 * window), jnp.bfloat16)
        shifted[depths + 2] = jnp.zeros((PART, 2 * window), jnp.bfloat16)
        hidden[0] = jnp.zeros((TALL, 2 * window), jnp.bfloat16)
        hidden[depths + 1] = jnp.zeros((TALL, 2 * window), jnp.bfloat16)
        for i in range(count_gz):
            tile = lax.rem(first_tile + i, count_gz)
            for zz in range(depth):
                shifts(i, zz, tile * depth + zz + 2, None)

        @pl.loop(0, depths, unroll=4)
        def _(z):
            first(z, None)

        @pl.loop(0, depths, unroll=4)
        def _(z):
            second(z, z // depth, z % depth)
    else:

        @pl.loop(0, count_gz // segment)
        def _(q):
            @pl.loop(-2, depths + 2)
            def _(z):
                at = q * depths + z
                inside = jnp.clip(at, 0, count_gz * depth - 1)
                shifts(inside // depth, inside % depth, z + 2, valid_slice(at))

            @pl.loop(-1, depths + 1)
            def _(z):
                first(z, valid_slice(q * depths + z))

            @pl.loop(0, depths)
            def _(z):
                second(z, q * segment + z // depth, z % depth)

    for zz in range(depth):
        for xb in range(brick_columns):
            own = [
                bricks[z_index, yb * brick_columns + xb, zz] for yb in range(rows // BY)
            ]
            for o in range(2):
                values = jnp.concatenate([v[o * BY : o * BY + BY] for v in own], axis=0)
                fractions[o, zz, :, xb * BX : (xb + 1) * BX] = values.astype(jnp.bfloat16)
    fractions_copy = pltpu.make_async_copy(fractions, fractions_ref, sems.at[3])
    fractions_copy.start()

    table_copy.wait()

    @pl.loop(0, slots)
    def _(j):
        brick_of_slot[j] = -1

    @pl.loop(0, count_gz)
    def _(i):
        tile = lax.rem(first_tile + i, count_gz)
        rank = jnp.int32(0)
        for b in range(brick_count):
            mine = owner_table[i, 0, b] == z_index

            @pl.when(mine)
            def _():
                brick_of_slot[tile * capacity + rank] = b

            rank = rank + mine.astype(jnp.int32)

    biomass_copy.wait()

    @pl.loop(0, slots)
    def _(j):
        brick = brick_of_slot[j]
        values = bricks[j // capacity, jnp.maximum(brick, 0)]
        values = jnp.where(brick >= 0, values, 0.0)
        at = pl.multiple_of(j * (2 * size), 8)
        arrived[pl.ds(at, 2 * size), :] = values.reshape(2 * size, BX)
        at = pl.multiple_of(j * size, size)
        mass[pl.ds(at, size), :] = 0.25 * biomass[pl.ds(at, size), :].astype(jnp.float32)

    last = lax.broadcasted_iota(jnp.int32, (8, BX), 1) == BX - 1

    def laplace(field, z, y):
        centre = field[z][y]
        ahead = jnp.where(last, 0.0, pltpu.roll(centre, BX - 1, 1) - centre)
        result = ahead - pltpu.roll(ahead, 1, 1)
        beside = [
            field[zz][yy]
            for zz, yy in ((z - 1, y), (z + 1, y), (z, y - 1), (z, y + 1))
            if 0 <= zz < depth and 0 <= yy < BY
        ]
        return result + (functools.reduce(jnp.add, beside) - float(len(beside)) * centre)

    state_copy.wait()

    def next_copy(group):
        at = pl.ds(pl.multiple_of(group * 16 * size, 16 * size), 16 * size)
        return pltpu.make_async_copy(state.at[at], next_ref.at[at], group_sems.at[group])

    @pl.loop(0, slots // 8)
    def _(group):
        def rows_of(pitch, offset):
            return pl.ds(group * 8 * pitch + offset, 8, stride=pitch)

        grid = [(z, y) for z in range(depth) for y in range(BY)]
        carbon = [
            [state[rows_of(2 * size, z * BY + y), :] for y in range(BY)] for z in range(depth)
        ]
        oxygen = [
            [state[rows_of(2 * size, size + z * BY + y), :] for y in range(BY)]
            for z in range(depth)
        ]
        pore = [[arrived[rows_of(2 * size, z * 8 + y), :] for y in range(BY)] for z in range(depth)]
        organic = [
            [0.3 * arrived[rows_of(2 * size, z * 8 + BY + y), :] for y in range(BY)]
            for z in range(depth)
        ]
        quarter = [[mass[rows_of(size, z * BY + y), :] for y in range(BY)] for z in range(depth)]
        slow = [[0.12 * p for p in row] for row in pore]
        fast = [[0.16 * p for p in row] for row in pore]
        for _ in range(STEPS):
            carbon_new = [[None] * BY for _ in range(depth)]
            oxygen_new = [[None] * BY for _ in range(depth)]
            for z, y in grid:
                doc, oxy = carbon[z][y], oxygen[z][y]
                uptake = quarter[z][y] * doc * oxy
                uptake = uptake / ((0.5 + jnp.abs(doc)) * (0.3 + jnp.abs(oxy)))
                gain = organic[z][y] - uptake
                carbon_new[z][y] = doc + slow[z][y] * laplace(carbon, z, y) + gain
                oxygen_new[z][y] = oxy + fast[z][y] * laplace(oxygen, z, y) - uptake
            carbon, oxygen = carbon_new, oxygen_new
        for z, y in grid:
            state[rows_of(2 * size, z * BY + y), :] = carbon[z][y]
            state[rows_of(2 * size, size + z * BY + y), :] = oxygen[z][y]
        next_copy(group).start()

    @pl.loop(0, slots // 8)
    def _(group):
        next_copy(group).wait()

    fractions_copy.wait()


def per_device(
    sizes, density, first_kernel, first_bias, second_kernel, second_bias, owners, solutes, biomass
):
    count_gz, count_gy, count_col = sizes
    depth, rows, columns = density.shape
    slots = solutes.shape[3]
    window = columns + BX
    segment = min(count_gz, 4)
    brick_count = (rows // BY) * (columns // BX)
    height = depth * rows
    depths = count_gz * depth
    bf16, f32 = jnp.bfloat16, jnp.float32
    shape = jax.ShapeDtypeStruct

    payload = pl.pallas_call(
        pack_kernel,
        out_shape=shape((columns // BX * height + TILE, BX), bf16),
        in_specs=[HBM, HBM],
        out_specs=VMEM,
        scratch_shapes=[
            pltpu.VMEM((1, brick_count), jnp.int32),
            pltpu.SemaphoreType.DMA((columns // BX + 1,)),
        ],
        compiler_params=pltpu.CompilerParams(vmem_limit_bytes=4 * 2**20),
        name="pack",
    )(in_hbm(density.reshape(height, columns)), in_hbm(owners.reshape(1, brick_count)))

    few = count_gz if count_gz == segment else 1
    if few > 1:
        tiles = [payload] + [
            lax.ppermute(payload, "gz", [((i + s) % count_gz, i) for i in range(count_gz)])
            for s in range(1, count_gz)
        ]
    else:
        tiles = [lax.all_gather(payload, "gz", axis=0, tiled=False)]

    t1, bias, t2, bias2 = pl.pallas_call(
        functools.partial(banded_kernel, (window, count_gy)),
        out_shape=(
            shape((TALL, 3 * PART), bf16),
            shape((TALL, 2 * window), f32),
            shape((6 * HALF, 3 * TALL), bf16),
            shape((2 * HALF, 2 * window), f32),
        ),
        in_specs=[HBM, HBM, HBM, HBM, pl.BlockSpec(memory_space=pl.ANY)],
        out_specs=(VMEM, VMEM, VMEM, VMEM),
        scratch_shapes=[
            pltpu.VMEM((CHANNELS, 27), bf16),
            pltpu.SMEM((CHANNELS,), f32),
            pltpu.VMEM((2 * CHANNELS, 27), bf16),
            pltpu.SMEM((2,), f32),
            pltpu.SemaphoreType.DMA((4,)),
        ],
        compiler_params=pltpu.CompilerParams(vmem_limit_bytes=16 * 2**20),
        cost_estimate=pl.CostEstimate(
            flops=20 * 2**20, bytes_accessed=4 * 2**20, transcendentals=0
        ),
        name="banded",
    )(
        in_hbm(first_kernel.transpose(2, 1, 0).reshape(CHANNELS, 27)),
        in_hbm(first_bias),
        in_hbm(second_kernel.transpose(1, 2, 0).reshape(2 * CHANNELS, 27)),
        in_hbm(second_bias),
        payload,
    )

    edge_shapes = [shape((2 * depths, columns), bf16), shape((2 * depths, BX), bf16)]
    sent = pl.pallas_call(
        functools.partial(edges_kernel, (count_gy, depth, rows, columns, few, count_gz)),
        out_shape=[shape((depths * rows, BX), bf16)] + edge_shapes * (1 if count_gy == 2 else 2),
        in_specs=[VMEM] * few + [pl.BlockSpec(memory_space=pl.ANY)],
        out_specs=[VMEM] * (3 if count_gy == 2 else 5),
        compiler_params=pltpu.CompilerParams(vmem_limit_bytes=16 * 2**20),
        name="edges",
    )(*tiles, bias2)

    def over(pairs):
        return [
            (gy * count_col + col, to * count_col + 1 - col)
            for gy, to in pairs
            for col in range(count_col)
        ]

    beside = lax.ppermute(sent[0], "col", [(0, 1), (1, 0)])
    if count_gy == 2:
        directions = [[(0, 1), (1, 0)]]
    else:
        up = [(i, i + 1) for i in range(count_gy - 1)]
        directions = [up, [(j, i) for i, j in up]]
    edges = []
    for k, pairs in enumerate(directions):
        edges.append(lax.ppermute(sent[1 + 2 * k], "gy", pairs))
        edges.append(lax.ppermute(sent[2 + 2 * k], ("gy", "col"), over(pairs)))

    cells = depth * BY
    fractions, solutes_next = pl.pallas_call(
        functools.partial(
            column_kernel, (count_gz, count_gy, depth, rows, columns, segment, slots), few
        ),
        out_shape=(
            shape((2, depth, rows, columns), bf16),
            shape((slots * 2 * cells, BX), f32),
        ),
        in_specs=[VMEM] * (few + 1 + len(edges) + 4) + [HBM, HBM],
        out_specs=(HBM, HBM),
        scratch_shapes=[
            pltpu.VMEM((2, 2 * depths, window), f32),
            pltpu.VMEM((segment * depth + 4, PART, 2 * window), bf16),
            pltpu.VMEM((segment * depth + 2, TALL, 2 * window), bf16),
            pltpu.VMEM((count_gz, brick_count, depth, 8, BX), f32),
            pltpu.VMEM((slots * 2 * cells, BX), f32),
            pltpu.VMEM((slots * 2 * cells, BX), f32),
            pltpu.VMEM((slots * cells, BX), bf16),
            pltpu.VMEM((slots * cells, BX), f32),
            pltpu.VMEM((2, depth, rows, columns), bf16),
            pltpu.VMEM((count_gz, 8, BX), jnp.int32),
            pltpu.SMEM((count_gz, 8, BX), jnp.int32),
            pltpu.SMEM((slots,), jnp.int32),
            pltpu.SemaphoreType.DMA((4,)),
            pltpu.SemaphoreType.DMA((slots // 8,)),
        ],
        compiler_params=pltpu.CompilerParams(vmem_limit_bytes=40 * 2**20),
        cost_estimate=pl.CostEstimate(
            flops=2 * depths * 2 * window * TALL * (3 * PART + 3 * 6 * HALF),
            bytes_accessed=4 * 2**20,
            transcendentals=0,
        ),
        name="column",
    )(
        *tiles,
        beside,
        *edges,
        t1,
        bias,
        t2,
        bias2,
        in_hbm(solutes.reshape(slots * 2 * cells, BX)),
        in_hbm(biomass.reshape(slots * cells, BX)),
    )
    return fractions, solutes_next.reshape(solutes.shape)


def solution(mesh):
    sizes = (mesh.shape["gz"], mesh.shape["gy"], mesh.shape["col"])
    assert sizes[2] == 2
    return jax.shard_map(
        functools.partial(per_device, sizes),
        mesh=mesh,
        in_specs=(
            P(("cores", "gz"), "gy", "col"),
            P(),
            P(),
            P(),
            P(),
            P(("cores", "gz"), "gy", "col", None, None),
            P(("cores", "gz"), "gy", "col", None, None, None, None, None),
            P(("cores", "gz"), "gy", "col", None, None, None, None),
        ),
        out_specs=(
            P(None, ("cores", "gz"), "gy", "col"),
            P(("cores", "gz"), "gy", "col", None, None, None, None, None),
        ),
        check_vma=False,
    )
```

```python
import functools

import jax
import jax.numpy as jnp
from jax import lax
from jax.experimental import pallas as pl
from jax.experimental.pallas import tpu as pltpu
from jax.sharding import PartitionSpec as P

BY = 4
BX = 128
STEPS = 4
TILE = 16
HALF = 16
CHANNELS = 8
REACH = HALF + 2
PART = 3 * HALF + TILE
TALL = REACH * CHANNELS
OUTSIDE = -3e38
OWNER_ROW = 6

VMEM = pl.BlockSpec(memory_space=pltpu.VMEM)
SMEM = pl.BlockSpec(memory_space=pltpu.SMEM)
HBM = pl.BlockSpec(memory_space=pltpu.HBM)


def in_hbm(array):
    return pltpu.with_memory_space_constraint(array, pltpu.HBM)


def step_index(values, width, count):
    index = jnp.zeros(values.shape, jnp.int32)
    for k in range(1, count):
        index = index + (values >= k * width).astype(jnp.int32)
    return index


def one_hot(condition):
    return jnp.where(condition, 1.0, 0.0).astype(jnp.bfloat16)


def iotas(shape):
    return (
        lax.broadcasted_iota(jnp.int32, shape, 0),
        lax.broadcasted_iota(jnp.int32, shape, 1),
    )


def tap_parts(tap):
    dz = step_index(tap, 9, 3)
    dy = step_index(tap - 9 * dz, 3, 3)
    return dz, dy, tap - 9 * dz - 3 * dy


def swap_lanes(c, row, lane, first, sender):
    low = (c != 0) if sender else (c == 0)
    place = row - first
    return (place >= 0) & (place < 2) & (lane == jnp.where(low, place, BX - 2 + place))


def edges_kernel(dims, density_ref, owners_ref, own_ref, misc_ref, x_ref, *refs):
    count_gy, depth, rows, directions = dims
    sends, (named_ref, sems) = refs[: 2 * directions], refs[2 * directions :]
    g = lax.axis_index("gy")
    c = lax.axis_index("col")
    height, columns = density_ref.shape
    blocks = columns // BX
    copies = [pltpu.make_async_copy(owners_ref, named_ref, sems.at[blocks])]
    for k in range(blocks):
        copies.append(
            pltpu.make_async_copy(
                density_ref.at[:, k * BX : (k + 1) * BX],
                own_ref.at[k * height : (k + 1) * height],
                sems.at[k],
            )
        )
    for copy in copies:
        copy.start()
    row, lane = iotas((TILE, BX))
    copies[0].wait()
    named = named_ref[...].astype(jnp.float32)
    count = named.shape[1]
    named = jnp.concatenate(
        [
            jnp.broadcast_to(named, (TILE, count)),
            jnp.zeros((TILE, BX - count), jnp.float32),
        ],
        axis=1,
    )
    misc_ref[...] = jnp.where(row == OWNER_ROW, named, 0.0).astype(jnp.bfloat16)
    for copy in copies[1:]:
        copy.wait()

    def columns_of(first, values):
        pick = one_hot(swap_lanes(c, row, lane, first, True))
        return lax.dot_general(
            pick, values, (((1,), (1,)), ((), ())), preferred_element_type=jnp.float32
        ).astype(jnp.bfloat16)

    x_ref[...] = columns_of(
        0, own_ref[pl.ds(pl.multiple_of((1 - c) * height, TILE), height), :]
    )
    first, last = [], []
    for k in range(blocks):
        ends = ([], [])
        for zz in range(depth):
            at = k * height + zz * rows
            ends[0].append(own_ref[at : at + TILE, :].astype(jnp.float32)[0:2])
            at = at + rows - TILE
            ends[1].append(own_ref[at : at + TILE, :].astype(jnp.float32)[TILE - 2 :])
        first.append(jnp.concatenate(ends[0], axis=0))
        last.append(jnp.concatenate(ends[1], axis=0))
    if directions == 1:
        chosen = [[jnp.where(g == 0, low, high) for low, high in zip(last, first)]]
    else:
        chosen = [last, first]
    for d, pair in enumerate(chosen):
        sends[2 * d][...] = jnp.concatenate(pair, axis=0).astype(jnp.bfloat16)
        near = jnp.where(c == 0, pair[1], pair[0])
        near = jnp.concatenate([near, jnp.zeros((BX - near.shape[0], BX), jnp.float32)], axis=0)
        sends[2 * d + 1][...] = columns_of(2 + 2 * d, near.astype(jnp.bfloat16))


def pack_kernel(directions, own_ref, misc_ref, x_ref, *refs):
    received, (payload_ref, edge_ref) = refs[: 2 * directions], refs[2 * directions :]
    height = own_ref.shape[0]
    payload_ref[0:height, :] = own_ref[...]
    misc = misc_ref[...] + x_ref[...]
    for d in range(directions):
        misc = misc + received[2 * d + 1][...]
    for d, value in enumerate([received[2 * k][...] for k in range(directions)] + [misc]):
        at = d * TILE
        edge_ref[at : at + TILE, :] = value
        payload_ref[height + at : height + at + TILE, :] = value


def banded_kernel(dims, *refs):
    window, count_gy = dims
    sources, refs = refs[:4], refs[5:]
    t1_ref, bias_ref, t2_ref, bias2_ref, *local, sems = refs
    copies = [
        pltpu.make_async_copy(source, target, sems.at[k])
        for k, (source, target) in enumerate(zip(sources, local))
    ]
    for copy in copies:
        copy.start()
    for copy in copies:
        copy.wait()
    w1_ref, b1_ref, w2_ref, b2_ref = local
    g = lax.axis_index("gy")
    row, channel = iotas((TALL, CHANNELS))
    spread = one_hot((row & (CHANNELS - 1)) == channel)
    w1 = jnp.dot(spread, w1_ref[...], preferred_element_type=jnp.float32).astype(jnp.bfloat16)
    tap, column = iotas((27, 3 * PART))
    dz = step_index(column, PART, 3)
    place = column - PART * dz
    dx = jnp.where(place < 3 * HALF, place >> 4, (place - 3 * HALF) >> 2)
    base = 9 * dz + dx
    row, column = iotas((TALL, 3 * PART))
    place = column & (PART - 1)
    seam = (place - 3 * HALF) & 3
    seam_row = jnp.where(seam < 2, seam - 2, seam + HALF - 2)
    input_row = jnp.where(place < 3 * HALF, place & (HALF - 1), seam_row)
    distance = jnp.where(place < 3 * HALF + 12, input_row - (row >> 3) + 2, -1)
    total = jnp.zeros((TALL, 3 * PART), jnp.float32)
    for dy in range(3):
        values = jnp.dot(w1, one_hot(tap == base + 3 * dy), preferred_element_type=jnp.float32)
        total = jnp.where(distance == dy, values, total)
    t1_ref[...] = total.astype(jnp.bfloat16)
    row, column = iotas((TALL, 2 * window))
    bias = jnp.zeros((TALL, 2 * window), jnp.float32)
    for k in range(CHANNELS):
        bias = jnp.where((row & (CHANNELS - 1)) == k, b1_ref[k], bias)
    outside = ((row < CHANNELS) & (column < window) & (g == 0)) | (
        (row >= TALL - CHANNELS) & (column >= window) & (g == count_gy - 1)
    )
    bias_ref[...] = jnp.where(outside, OUTSIDE, bias)
    channel, column = iotas((CHANNELS, 3 * TALL))
    spread = one_hot((column & (CHANNELS - 1)) == channel)
    tap, column = iotas((27, 3 * TALL))
    same_z = tap_parts(tap)[0] == step_index(column, TALL, 3)
    row, tap = iotas((6 * HALF, 27))
    _, tap_y, tap_x = tap_parts(tap)
    same_x = (row >> 5) == tap_x
    wide = []
    for o in range(2):
        values = lax.dot_general(
            w2_ref[o * CHANNELS : (o + 1) * CHANNELS, :],
            spread,
            (((0,), (0,)), ((), ())),
            preferred_element_type=jnp.float32,
        )
        wide.append(jnp.where(same_z, values, 0.0).astype(jnp.bfloat16))
    out_row, column = iotas((6 * HALF, 3 * TALL))
    y = ((out_row >> 3) & 3) * BY + (out_row & 3)
    hidden_row = (column - TALL * step_index(column, TALL, 3)) >> 3
    total = jnp.zeros((6 * HALF, 3 * TALL), jnp.float32)
    for dy in range(3):
        values = 0.0
        for o in range(2):
            pick = one_hot(same_x & (tap_y == dy) & (((row >> 2) & 1) == o))
            values = values + jnp.dot(pick, wide[o], preferred_element_type=jnp.float32)
        total = jnp.where(hidden_row - y == dy, values, total)
    t2_ref[...] = total.astype(jnp.bfloat16)
    row, _ = iotas((2 * HALF, 2 * window))
    bias2_ref[...] = jnp.where(((row >> 2) & 1) == 0, b2_ref[0], b2_ref[1])


def column_kernel(dims, few, *refs):
    count_gz, count_gy, depth, rows, columns, segment, slots, directions = dims
    count = few + 1 if few > 1 else 1
    tiles, refs = refs[:count], refs[count:]
    t1_ref, bias_ref, t2_ref, bias2_ref, solutes_ref, biomass_ref, *refs = refs
    fractions_ref, next_ref, *refs = refs
    (
        edge_rows,
        beside,
        shifted,
        hidden,
        bricks,
        arrived,
        state,
        biomass,
        mass,
        fractions,
        owner_rows,
        owner_table,
        brick_of_slot,
        sems,
        group_sems,
    ) = refs
    z_index = lax.axis_index("gz")
    g = lax.axis_index("gy")
    c = lax.axis_index("col")
    window = columns + BX
    brick_rows = HALF // BY
    brick_columns = columns // BX
    brick_count = rows // BY * brick_columns
    capacity = slots // count_gz
    single = segment == count_gz
    first_tile = z_index if few > 1 else 0
    size = depth * BY

    state_copy = pltpu.make_async_copy(solutes_ref, state, sems.at[0])
    state_copy.start()
    biomass_copy = pltpu.make_async_copy(biomass_ref, biomass, sems.at[1])
    biomass_copy.start()

    def tile_rows(i, start, size):
        if not isinstance(start, int):
            start = pl.multiple_of(start, TILE)
        if few > 1:
            return tiles[i][pl.ds(start, size), :]
        return tiles[0][i, pl.ds(start, size), :]

    def edge_tile(i, k):
        at = brick_columns * depth * rows + k * TILE
        if few > 1 and tiles[i].shape[0] <= at:
            return tiles[count_gz][k * TILE : (k + 1) * TILE, :]
        return tile_rows(i, at, TILE)

    def arrange(left, right, other):
        return jnp.concatenate(
            [
                jnp.where(c == 0, left, other),
                jnp.where(c == 0, right, left),
                jnp.where(c == 0, other, right),
            ],
            axis=1,
        )

    small_row, small_lane = iotas((TILE, BX))

    def unpack(i):
        misc = edge_tile(i, directions)
        owner_rows[i] = misc.astype(jnp.float32)[0:8].astype(jnp.int32)

        def columns_of(first):
            pick = one_hot(swap_lanes(c, small_row, small_lane, first, False))
            return lax.dot_general(
                misc, pick, (((0,), (0,)), ((), ())), preferred_element_type=jnp.float32
            )

        at = i * (depth * rows)
        if not isinstance(at, int):
            at = pl.multiple_of(at, TILE)
        beside[pl.ds(at, depth * rows), :] = columns_of(0).astype(jnp.bfloat16)
        at = i * (2 * depth)
        if not isinstance(at, int):
            at = pl.multiple_of(at, 8)
        sides = []
        for d in range(directions):
            pair = edge_tile(i, d).astype(jnp.float32)
            corner = columns_of(2 + 2 * d)[0 : 2 * depth]
            sides.append(arrange(pair[0 : 2 * depth], pair[2 * depth :], corner))
        edge_rows[0, pl.ds(at, 2 * depth), :] = jnp.where(g > 0, sides[0], 0.0)
        edge_rows[1, pl.ds(at, 2 * depth), :] = jnp.where(g < count_gy - 1, sides[-1], 0.0)

    if few > 1:
        for i in range(count_gz):
            unpack(i)
    else:
        pl.loop(0, count_gz)(unpack)
    table_copy = pltpu.make_async_copy(owner_rows, owner_table, sems.at[2])
    table_copy.start()

    def moved(values):
        lane = lax.broadcasted_iota(jnp.int32, values.shape, 1)
        return (
            jnp.where(lane == 0, 0.0, pltpu.roll(values, 1, 1)),
            values,
            jnp.where(lane == window - 1, 0.0, pltpu.roll(values, window - 1, 1)),
        )

    def edge_pair(k, at):
        if isinstance(at, int):
            return edge_rows[k, at : at + 2, :]
        group = edge_rows[k, pl.ds(pl.multiple_of(at // 8 * 8, 8), 8), :]
        return pltpu.roll(group, lax.rem(8 - at % 8, 8), 0)[0:2]

    def shifts(i, zz, slot, valid):
        z = i * depth + zz
        halves = []
        for h in range(2):
            at = zz * rows + h * HALF
            own = [tile_rows(i, k * depth * rows + at, HALF) for k in range(2)]
            at = z * rows + h * HALF
            if not isinstance(at, int):
                at = pl.multiple_of(at, TILE)
            values = arrange(*own, beside[pl.ds(at, HALF), :]).astype(jnp.float32)
            halves.append(values if valid is None else values * valid)
        top, bottom = edge_pair(0, 2 * z), edge_pair(1, 2 * z)
        if valid is not None:
            top, bottom = top * valid, bottom * valid
        seams = [
            jnp.concatenate([top, halves[1][0:2]], axis=0),
            jnp.concatenate([halves[0][HALF - 2 :], bottom], axis=0),
        ]
        for h in range(2):
            lanes = slice(h * window, (h + 1) * window)
            for dx, values in enumerate(moved(halves[h])):
                shifted[slot, dx * HALF : (dx + 1) * HALF, lanes] = values.astype(jnp.bfloat16)
            values = jnp.concatenate(
                [*moved(seams[h]), jnp.zeros((4, window), jnp.float32)], axis=0
            )
            shifted[slot, 3 * HALF : PART, lanes] = values.astype(jnp.bfloat16)

    def first(z, valid):
        total = jnp.dot(
            t1_ref[...],
            shifted[pl.ds(z + 1, 3)].reshape(3 * PART, 2 * window),
            preferred_element_type=jnp.float32,
        )
        values = jnp.maximum(total + bias_ref[...], 0.0)
        if valid is not None:
            values = values * valid
        hidden[z + 1] = values.astype(jnp.bfloat16)

    height = 2 * HALF
    lane = lax.broadcasted_iota(jnp.int32, (height, 2 * window), 1)
    left_edge = (lane == 0) | (lane == window)
    right_edge = (lane == window - 1) | (lane == 2 * window - 1)

    def second(z, t, zz):
        total = jnp.dot(
            t2_ref[...],
            hidden[pl.ds(z, 3)].reshape(3 * TALL, 2 * window),
            preferred_element_type=jnp.float32,
        )
        before = pltpu.roll(total[0:height], 1, 1)
        after = pltpu.roll(total[2 * height :], 2 * window - 1, 1)
        total = total[height : 2 * height] + bias2_ref[...]
        total = total + jnp.where(left_edge, 0.0, before)
        total = total + jnp.where(right_edge, 0.0, after)
        for h in range(2):
            at = h * window
            own = jnp.where(
                c == 0, total[:, at : at + columns], total[:, at + BX : at + window]
            )
            values = 0.5 + 0.5 * jnp.tanh(0.5 * own)
            values = values.astype(jnp.bfloat16).astype(jnp.float32)
            for yb in range(brick_rows):
                for xb in range(brick_columns):
                    b = (h * brick_rows + yb) * brick_columns + xb
                    bricks[t, b, zz] = values[yb * 8 : yb * 8 + 8, xb * BX : (xb + 1) * BX]

    def valid_slice(z):
        return ((z >= 0) & (z < count_gz * depth)).astype(jnp.float32)

    depths = segment * depth
    if single:
        shifted[1] = jnp.zeros((PART, 2 * window), jnp.bfloat16)
        shifted[depths + 2] = jnp.zeros((PART, 2 * window), jnp.bfloat16)
        hidden[0] = jnp.zeros((TALL, 2 * window), jnp.bfloat16)
        hidden[depths + 1] = jnp.zeros((TALL, 2 * window), jnp.bfloat16)
        for i in range(count_gz):
            tile = lax.rem(first_tile + i, count_gz)
            for zz in range(depth):
                shifts(i, zz, tile * depth + zz + 2, None)

        @pl.loop(0, depths, unroll=4)
        def _(z):
            first(z, None)

        @pl.loop(0, depths, unroll=4)
        def _(z):
            second(z, z // depth, z % depth)
    else:

        @pl.loop(0, count_gz // segment)
        def _(q):
            @pl.loop(-2, depths + 2)
            def _(z):
                at = q * depths + z
                inside = jnp.clip(at, 0, count_gz * depth - 1)
                shifts(inside // depth, inside % depth, z + 2, valid_slice(at))

            @pl.loop(-1, depths + 1)
            def _(z):
                first(z, valid_slice(q * depths + z))

            @pl.loop(0, depths)
            def _(z):
                second(z, q * segment + z // depth, z % depth)

    for zz in range(depth):
        for xb in range(brick_columns):
            own = [
                bricks[z_index, yb * brick_columns + xb, zz] for yb in range(rows // BY)
            ]
            for o in range(2):
                values = jnp.concatenate([v[o * BY : o * BY + BY] for v in own], axis=0)
                fractions[o, zz, :, xb * BX : (xb + 1) * BX] = values.astype(jnp.bfloat16)
    fractions_copy = pltpu.make_async_copy(fractions, fractions_ref, sems.at[3])
    fractions_copy.start()

    table_copy.wait()

    @pl.loop(0, slots)
    def _(j):
        brick_of_slot[j] = -1

    @pl.loop(0, count_gz)
    def _(i):
        tile = lax.rem(first_tile + i, count_gz)
        rank = jnp.int32(0)
        for b in range(brick_count):
            mine = owner_table[i, OWNER_ROW, b] == z_index

            @pl.when(mine)
            def _():
                brick_of_slot[tile * capacity + rank] = b

            rank = rank + mine.astype(jnp.int32)

    biomass_copy.wait()

    @pl.loop(0, slots)
    def _(j):
        brick = brick_of_slot[j]
        values = bricks[j // capacity, jnp.maximum(brick, 0)]
        values = jnp.where(brick >= 0, values, 0.0)
        at = pl.multiple_of(j * (2 * size), 8)
        arrived[pl.ds(at, 2 * size), :] = values.reshape(2 * size, BX)
        at = pl.multiple_of(j * size, size)
        mass[pl.ds(at, size), :] = 0.25 * biomass[pl.ds(at, size), :].astype(jnp.float32)

    last = lax.broadcasted_iota(jnp.int32, (8, BX), 1) == BX - 1

    def laplace(field, z, y):
        centre = field[z][y]
        ahead = jnp.where(last, 0.0, pltpu.roll(centre, BX - 1, 1) - centre)
        result = ahead - pltpu.roll(ahead, 1, 1)
        beside = [
            field[zz][yy]
            for zz, yy in ((z - 1, y), (z + 1, y), (z, y - 1), (z, y + 1))
            if 0 <= zz < depth and 0 <= yy < BY
        ]
        return result + (functools.reduce(jnp.add, beside) - float(len(beside)) * centre)

    state_copy.wait()

    def next_copy(group):
        at = pl.ds(pl.multiple_of(group * 16 * size, 16 * size), 16 * size)
        return pltpu.make_async_copy(state.at[at], next_ref.at[at], group_sems.at[group])

    @pl.loop(0, slots // 8)
    def _(group):
        def rows_of(pitch, offset):
            return pl.ds(group * 8 * pitch + offset, 8, stride=pitch)

        grid = [(z, y) for z in range(depth) for y in range(BY)]
        carbon = [
            [state[rows_of(2 * size, z * BY + y), :] for y in range(BY)] for z in range(depth)
        ]
        oxygen = [
            [state[rows_of(2 * size, size + z * BY + y), :] for y in range(BY)]
            for z in range(depth)
        ]
        pore = [[arrived[rows_of(2 * size, z * 8 + y), :] for y in range(BY)] for z in range(depth)]
        organic = [
            [0.3 * arrived[rows_of(2 * size, z * 8 + BY + y), :] for y in range(BY)]
            for z in range(depth)
        ]
        quarter = [[mass[rows_of(size, z * BY + y), :] for y in range(BY)] for z in range(depth)]
        slow = [[0.12 * p for p in row] for row in pore]
        fast = [[0.16 * p for p in row] for row in pore]
        for _ in range(STEPS):
            carbon_new = [[None] * BY for _ in range(depth)]
            oxygen_new = [[None] * BY for _ in range(depth)]
            for z, y in grid:
                doc, oxy = carbon[z][y], oxygen[z][y]
                uptake = quarter[z][y] * doc * oxy
                uptake = uptake / ((0.5 + jnp.abs(doc)) * (0.3 + jnp.abs(oxy)))
                gain = organic[z][y] - uptake
                carbon_new[z][y] = doc + slow[z][y] * laplace(carbon, z, y) + gain
                oxygen_new[z][y] = oxy + fast[z][y] * laplace(oxygen, z, y) - uptake
            carbon, oxygen = carbon_new, oxygen_new
        for z, y in grid:
            state[rows_of(2 * size, z * BY + y), :] = carbon[z][y]
            state[rows_of(2 * size, size + z * BY + y), :] = oxygen[z][y]
        next_copy(group).start()

    @pl.loop(0, slots // 8)
    def _(group):
        next_copy(group).wait()

    fractions_copy.wait()


def per_device(
    sizes, density, first_kernel, first_bias, second_kernel, second_bias, owners, solutes, biomass
):
    count_gz, count_gy, count_col = sizes
    depth, rows, columns = density.shape
    slots = solutes.shape[3]
    window = columns + BX
    segment = min(count_gz, 4)
    brick_count = (rows // BY) * (columns // BX)
    height = depth * rows
    depths = count_gz * depth
    bf16, f32 = jnp.bfloat16, jnp.float32
    shape = jax.ShapeDtypeStruct

    def over(pairs):
        return [
            (gy * count_col + col, to * count_col + 1 - col)
            for gy, to in pairs
            for col in range(count_col)
        ]

    if count_gy == 2:
        ways = [[(0, 1), (1, 0)]]
    else:
        up = [(i, i + 1) for i in range(count_gy - 1)]
        ways = [up, [(j, i) for i, j in up]]
    directions = len(ways)
    blocks = columns // BX
    own, misc, near, *sent = pl.pallas_call(
        functools.partial(edges_kernel, (count_gy, depth, rows, directions)),
        out_shape=[shape((blocks * height, BX), bf16)] + [shape((TILE, BX), bf16)] * (2 + 2 * directions),
        in_specs=[HBM, HBM],
        out_specs=[VMEM] * (3 + 2 * directions),
        scratch_shapes=[
            pltpu.VMEM((1, brick_count), jnp.int32),
            pltpu.SemaphoreType.DMA((blocks + 1,)),
        ],
        compiler_params=pltpu.CompilerParams(vmem_limit_bytes=4 * 2**20),
        name="edges",
    )(in_hbm(density.reshape(height, columns)), in_hbm(owners.reshape(1, brick_count)))

    received = []
    for d, pairs in enumerate(ways):
        received.append(lax.ppermute(sent[2 * d], "gy", pairs))
        received.append(lax.ppermute(sent[2 * d + 1], ("gy", "col"), over(pairs)))
    near = lax.ppermute(near, "col", [(0, 1), (1, 0)])
    payload, cells_around = pl.pallas_call(
        functools.partial(pack_kernel, directions),
        out_shape=[
            shape((blocks * height + (directions + 1) * TILE, BX), bf16),
            shape(((directions + 1) * TILE, BX), bf16),
        ],
        in_specs=[VMEM] * (3 + 2 * directions),
        out_specs=[VMEM] * 2,
        compiler_params=pltpu.CompilerParams(vmem_limit_bytes=4 * 2**20),
        name="pack",
    )(own, misc, near, *received)

    def turned(array, s):
        return lax.ppermute(array, "gz", [((i + s) % count_gz, i) for i in range(count_gz)])

    few = count_gz if count_gz == 4 else 1
    if few > 1:
        tiles = [payload, turned(payload, 1), turned(own, 2), turned(payload, 3)]
        tiles.append(turned(cells_around, 2))
    else:
        tiles = [lax.all_gather(payload, "gz", axis=0, tiled=False)]

    t1, bias, t2, bias2 = pl.pallas_call(
        functools.partial(banded_kernel, (window, count_gy)),
        out_shape=(
            shape((TALL, 3 * PART), bf16),
            shape((TALL, 2 * window), f32),
            shape((6 * HALF, 3 * TALL), bf16),
            shape((2 * HALF, 2 * window), f32),
        ),
        in_specs=[HBM, HBM, HBM, HBM, pl.BlockSpec(memory_space=pl.ANY)],
        out_specs=(VMEM, VMEM, VMEM, VMEM),
        scratch_shapes=[
            pltpu.VMEM((CHANNELS, 27), bf16),
            pltpu.SMEM((CHANNELS,), f32),
            pltpu.VMEM((2 * CHANNELS, 27), bf16),
            pltpu.SMEM((2,), f32),
            pltpu.SemaphoreType.DMA((4,)),
        ],
        compiler_params=pltpu.CompilerParams(vmem_limit_bytes=16 * 2**20),
        cost_estimate=pl.CostEstimate(
            flops=20 * 2**20, bytes_accessed=4 * 2**20, transcendentals=0
        ),
        name="banded",
    )(
        in_hbm(first_kernel.transpose(2, 1, 0).reshape(CHANNELS, 27)),
        in_hbm(first_bias),
        in_hbm(second_kernel.transpose(1, 2, 0).reshape(2 * CHANNELS, 27)),
        in_hbm(second_bias),
        payload,
    )

    cells = depth * BY
    fractions, solutes_next = pl.pallas_call(
        functools.partial(
            column_kernel,
            (count_gz, count_gy, depth, rows, columns, segment, slots, directions),
            few,
        ),
        out_shape=(
            shape((2, depth, rows, columns), bf16),
            shape((slots * 2 * cells, BX), f32),
        ),
        in_specs=[VMEM] * (len(tiles) + 4) + [HBM, HBM],
        out_specs=(HBM, HBM),
        scratch_shapes=[
            pltpu.VMEM((2, 2 * depths, window), f32),
            pltpu.VMEM((depths * rows, BX), bf16),
            pltpu.VMEM((segment * depth + 4, PART, 2 * window), bf16),
            pltpu.VMEM((segment * depth + 2, TALL, 2 * window), bf16),
            pltpu.VMEM((count_gz, brick_count, depth, 8, BX), f32),
            pltpu.VMEM((slots * 2 * cells, BX), f32),
            pltpu.VMEM((slots * 2 * cells, BX), f32),
            pltpu.VMEM((slots * cells, BX), bf16),
            pltpu.VMEM((slots * cells, BX), f32),
            pltpu.VMEM((2, depth, rows, columns), bf16),
            pltpu.VMEM((count_gz, 8, BX), jnp.int32),
            pltpu.SMEM((count_gz, 8, BX), jnp.int32),
            pltpu.SMEM((slots,), jnp.int32),
            pltpu.SemaphoreType.DMA((4,)),
            pltpu.SemaphoreType.DMA((slots // 8,)),
        ],
        compiler_params=pltpu.CompilerParams(vmem_limit_bytes=40 * 2**20),
        cost_estimate=pl.CostEstimate(
            flops=2 * depths * 2 * window * TALL * (3 * PART + 3 * 6 * HALF),
            bytes_accessed=4 * 2**20,
            transcendentals=0,
        ),
        name="column",
    )(
        *tiles,
        t1,
        bias,
        t2,
        bias2,
        in_hbm(solutes.reshape(slots * 2 * cells, BX)),
        in_hbm(biomass.reshape(slots * cells, BX)),
    )
    return fractions, solutes_next.reshape(solutes.shape)


def solution(mesh):
    sizes = (mesh.shape["gz"], mesh.shape["gy"], mesh.shape["col"])
    assert sizes[2] == 2
    return jax.shard_map(
        functools.partial(per_device, sizes),
        mesh=mesh,
        in_specs=(
            P(("cores", "gz"), "gy", "col"),
            P(),
            P(),
            P(),
            P(),
            P(("cores", "gz"), "gy", "col", None, None),
            P(("cores", "gz"), "gy", "col", None, None, None, None, None),
            P(("cores", "gz"), "gy", "col", None, None, None, None),
        ),
        out_specs=(
            P(None, ("cores", "gz"), "gy", "col"),
            P(("cores", "gz"), "gy", "col", None, None, None, None, None),
        ),
        check_vma=False,
    )
```

```python
import functools

import jax
import jax.numpy as jnp
from jax import lax
from jax.experimental import pallas as pl
from jax.experimental.pallas import tpu as pltpu
from jax.sharding import PartitionSpec as P

BY = 4
BX = 128
STEPS = 4
TILE = 16
HALF = 16
CHANNELS = 8
REACH = HALF + 2
PART = 3 * HALF + TILE
TALL = REACH * CHANNELS
OUTSIDE = -3e38
OWNER_ROW = 6

VMEM = pl.BlockSpec(memory_space=pltpu.VMEM)
SMEM = pl.BlockSpec(memory_space=pltpu.SMEM)
ANY = pl.BlockSpec(memory_space=pl.ANY)
HBM = pl.BlockSpec(memory_space=pltpu.HBM)


def in_hbm(array):
    return pltpu.with_memory_space_constraint(array, pltpu.HBM)


def step_index(values, width, count):
    index = jnp.zeros(values.shape, jnp.int32)
    for k in range(1, count):
        index = index + (values >= k * width).astype(jnp.int32)
    return index


def one_hot(condition):
    return jnp.where(condition, 1.0, 0.0).astype(jnp.bfloat16)


def iotas(shape):
    return (
        lax.broadcasted_iota(jnp.int32, shape, 0),
        lax.broadcasted_iota(jnp.int32, shape, 1),
    )


def tap_parts(tap):
    dz = step_index(tap, 9, 3)
    dy = step_index(tap - 9 * dz, 3, 3)
    return dz, dy, tap - 9 * dz - 3 * dy


def swap_lanes(c, row, lane, first, sender):
    low = (c != 0) if sender else (c == 0)
    place = row - first
    return (place >= 0) & (place < 2) & (lane == jnp.where(low, place, BX - 2 + place))


def edges_kernel(dims, density_ref, owners_ref, own_ref, misc_ref, x_ref, *refs):
    count_gy, depth, rows, directions = dims
    sends, (named_ref, sems) = refs[: 2 * directions], refs[2 * directions :]
    g = lax.axis_index("gy")
    c = lax.axis_index("col")
    height, columns = density_ref.shape
    blocks = columns // BX
    copies = [pltpu.make_async_copy(owners_ref, named_ref, sems.at[blocks])]
    for k in range(blocks):
        copies.append(
            pltpu.make_async_copy(
                density_ref.at[:, k * BX : (k + 1) * BX],
                own_ref.at[k * height : (k + 1) * height],
                sems.at[k],
            )
        )
    for copy in copies:
        copy.start()
    row, lane = iotas((TILE, BX))
    copies[0].wait()
    named = named_ref[...].astype(jnp.float32)
    count = named.shape[1]
    named = jnp.concatenate(
        [
            jnp.broadcast_to(named, (TILE, count)),
            jnp.zeros((TILE, BX - count), jnp.float32),
        ],
        axis=1,
    )
    misc_ref[...] = jnp.where(row == OWNER_ROW, named, 0.0).astype(jnp.bfloat16)
    for copy in copies[1:]:
        copy.wait()

    def columns_of(first, values):
        pick = one_hot(swap_lanes(c, row, lane, first, True))
        return lax.dot_general(
            pick, values, (((1,), (1,)), ((), ())), preferred_element_type=jnp.float32
        ).astype(jnp.bfloat16)

    x_ref[...] = columns_of(
        0, own_ref[pl.ds(pl.multiple_of((1 - c) * height, TILE), height), :]
    )
    first, last = [], []
    for k in range(blocks):
        ends = ([], [])
        for zz in range(depth):
            at = k * height + zz * rows
            ends[0].append(own_ref[at : at + TILE, :].astype(jnp.float32)[0:2])
            at = at + rows - TILE
            ends[1].append(own_ref[at : at + TILE, :].astype(jnp.float32)[TILE - 2 :])
        first.append(jnp.concatenate(ends[0], axis=0))
        last.append(jnp.concatenate(ends[1], axis=0))
    if directions == 1:
        chosen = [[jnp.where(g == 0, low, high) for low, high in zip(last, first)]]
    else:
        chosen = [last, first]
    for d, pair in enumerate(chosen):
        sends[2 * d][...] = jnp.concatenate(pair, axis=0).astype(jnp.bfloat16)
        near = jnp.where(c == 0, pair[1], pair[0])
        near = jnp.concatenate([near, jnp.zeros((BX - near.shape[0], BX), jnp.float32)], axis=0)
        sends[2 * d + 1][...] = columns_of(2 + 2 * d, near.astype(jnp.bfloat16))


def pack_kernel(directions, own_ref, misc_ref, x_ref, _, *refs):
    received, (payload_ref, edge_ref) = refs[: 2 * directions], refs[2 * directions :]
    height = own_ref.shape[0]
    payload_ref[0:height, :] = own_ref[...]
    misc = misc_ref[...] + x_ref[...]
    for d in range(directions):
        misc = misc + received[2 * d + 1][...]
    for d, value in enumerate([received[2 * k][...] for k in range(directions)] + [misc]):
        at = d * TILE
        edge_ref[at : at + TILE, :] = value
        payload_ref[height + at : height + at + TILE, :] = value


def banded_kernel(dims, *refs):
    window, count_gy = dims
    sources, refs = refs[:4], refs[5:]
    t1_ref, bias_ref, t2_ref, bias2_ref, *local, sems = refs
    copies = [
        pltpu.make_async_copy(source, target, sems.at[k])
        for k, (source, target) in enumerate(zip(sources, local))
    ]
    for copy in copies:
        copy.start()
    for copy in copies:
        copy.wait()
    w1_ref, b1_ref, w2_ref, b2_ref = local
    g = lax.axis_index("gy")
    row, channel = iotas((TALL, CHANNELS))
    spread = one_hot((row & (CHANNELS - 1)) == channel)
    w1 = jnp.dot(spread, w1_ref[...], preferred_element_type=jnp.float32).astype(jnp.bfloat16)
    tap, column = iotas((27, 3 * PART))
    dz = step_index(column, PART, 3)
    place = column - PART * dz
    dx = jnp.where(place < 3 * HALF, place >> 4, (place - 3 * HALF) >> 2)
    base = 9 * dz + dx
    row, column = iotas((TALL, 3 * PART))
    place = column & (PART - 1)
    seam = (place - 3 * HALF) & 3
    seam_row = jnp.where(seam < 2, seam - 2, seam + HALF - 2)
    input_row = jnp.where(place < 3 * HALF, place & (HALF - 1), seam_row)
    distance = jnp.where(place < 3 * HALF + 12, input_row - (row >> 3) + 2, -1)
    total = jnp.zeros((TALL, 3 * PART), jnp.float32)
    for dy in range(3):
        values = jnp.dot(w1, one_hot(tap == base + 3 * dy), preferred_element_type=jnp.float32)
        total = jnp.where(distance == dy, values, total)
    t1_ref[...] = total.astype(jnp.bfloat16)
    row, column = iotas((TALL, 2 * window))
    bias = jnp.zeros((TALL, 2 * window), jnp.float32)
    for k in range(CHANNELS):
        bias = jnp.where((row & (CHANNELS - 1)) == k, b1_ref[k], bias)
    outside = ((row < CHANNELS) & (column < window) & (g == 0)) | (
        (row >= TALL - CHANNELS) & (column >= window) & (g == count_gy - 1)
    )
    bias_ref[...] = jnp.where(outside, OUTSIDE, bias)
    channel, column = iotas((CHANNELS, 3 * TALL))
    spread = one_hot((column & (CHANNELS - 1)) == channel)
    tap, column = iotas((27, 3 * TALL))
    same_z = tap_parts(tap)[0] == step_index(column, TALL, 3)
    row, tap = iotas((6 * HALF, 27))
    _, tap_y, tap_x = tap_parts(tap)
    same_x = (row >> 5) == tap_x
    wide = []
    for o in range(2):
        values = lax.dot_general(
            w2_ref[o * CHANNELS : (o + 1) * CHANNELS, :],
            spread,
            (((0,), (0,)), ((), ())),
            preferred_element_type=jnp.float32,
        )
        wide.append(jnp.where(same_z, values, 0.0).astype(jnp.bfloat16))
    out_row, column = iotas((6 * HALF, 3 * TALL))
    y = ((out_row >> 3) & 3) * BY + (out_row & 3)
    hidden_row = (column - TALL * step_index(column, TALL, 3)) >> 3
    total = jnp.zeros((6 * HALF, 3 * TALL), jnp.float32)
    for dy in range(3):
        values = 0.0
        for o in range(2):
            pick = one_hot(same_x & (tap_y == dy) & (((row >> 2) & 1) == o))
            values = values + jnp.dot(pick, wide[o], preferred_element_type=jnp.float32)
        total = jnp.where(hidden_row - y == dy, values, total)
    t2_ref[...] = total.astype(jnp.bfloat16)
    row, _ = iotas((2 * HALF, 2 * window))
    bias2_ref[...] = jnp.where(((row >> 2) & 1) == 0, b2_ref[0], b2_ref[1])


def laplace(field, z, y):
    centre = field[z][y]
    last = lax.broadcasted_iota(jnp.int32, centre.shape, 1) == BX - 1
    ahead = jnp.where(last, 0.0, pltpu.roll(centre, BX - 1, 1) - centre)
    result = ahead - pltpu.roll(ahead, 1, 1)
    beside = [
        field[zz][yy]
        for zz, yy in ((z - 1, y), (z + 1, y), (z, y - 1), (z, y + 1))
        if 0 <= zz < len(field) and 0 <= yy < BY
    ]
    return result + (functools.reduce(jnp.add, beside) - float(len(beside)) * centre)


def uptake_of(quarter, doc, oxy):
    return quarter * doc * oxy / ((0.5 + jnp.abs(doc)) * (0.3 + jnp.abs(oxy)))


def prepare_kernel(dims, solutes_ref, biomass_ref, _, *refs):
    depth, slots = dims
    outs, (state, biomass, mass, sems) = refs[:5], refs[5:]
    size = depth * BY
    copies = []
    for group in range(slots // 8):
        for k, (source, target) in enumerate(((solutes_ref, state), (biomass_ref, biomass))):
            rows = (2 - k) * 8 * size
            at = pl.ds(group * rows, rows)
            copies.append(
                pltpu.make_async_copy(source.at[at], target.at[at], sems.at[group, k])
            )
    for copy in copies:
        copy.start()
    for group in range(slots // 8):
        copies[2 * group].wait()
        copies[2 * group + 1].wait()
        at = slice(group * 8 * size, (group + 1) * 8 * size)
        mass[at, :] = biomass[at, :].astype(jnp.float32)

        def rows_of(pitch, offset):
            return pl.ds(group * 8 * pitch + offset, 8, stride=pitch)

        grid = [(z, y) for z in range(depth) for y in range(BY)]
        carbon, oxygen = [
            [
                [state[rows_of(2 * size, k * size + z * BY + y), :] for y in range(BY)]
                for z in range(depth)
            ]
            for k in range(2)
        ]
        for z, y in grid:
            at = group * 8 * size + (z * BY + y) * 8
            at = slice(at, at + 8)
            doc, oxy = carbon[z][y], oxygen[z][y]
            quarter = 0.25 * mass[rows_of(size, z * BY + y), :]
            uptake = uptake_of(quarter, doc, oxy)
            values = (
                doc - uptake,
                oxy - uptake,
                laplace(carbon, z, y),
                laplace(oxygen, z, y),
                quarter,
            )
            for out, value in zip(outs, values):
                out[at, :] = value


def column_kernel(dims, few, *refs):
    count_gz, count_gy, depth, rows, columns, segment, slots, directions = dims
    count = few + 1 if few > 1 else 1
    tiles, refs = refs[:count], refs[count:]
    t1_ref, bias_ref, t2_ref, bias2_ref, *refs = refs
    carbon_ref, oxygen_ref, carbon_around_ref, oxygen_around_ref, quarter_ref, *refs = refs
    fractions_ref, next_ref, *refs = refs
    (
        edge_rows,
        beside,
        shifted,
        hidden,
        bricks,
        arrived,
        state,
        fractions,
        owner_rows,
        owner_table,
        brick_of_slot,
        sems,
        group_sems,
    ) = refs
    z_index = lax.axis_index("gz")
    g = lax.axis_index("gy")
    c = lax.axis_index("col")
    window = columns + BX
    brick_rows = HALF // BY
    brick_columns = columns // BX
    brick_count = rows // BY * brick_columns
    capacity = slots // count_gz
    single = segment == count_gz
    first_tile = z_index if few > 1 else 0
    size = depth * BY

    def tile_rows(i, start, size):
        if not isinstance(start, int):
            start = pl.multiple_of(start, TILE)
        if few > 1:
            return tiles[i][pl.ds(start, size), :]
        return tiles[0][i, pl.ds(start, size), :]

    def edge_tile(i, k):
        at = brick_columns * depth * rows + k * TILE
        if few > 1 and tiles[i].shape[0] <= at:
            return tiles[count_gz][k * TILE : (k + 1) * TILE, :]
        return tile_rows(i, at, TILE)

    def arrange(left, right, other):
        return jnp.concatenate(
            [
                jnp.where(c == 0, left, other),
                jnp.where(c == 0, right, left),
                jnp.where(c == 0, other, right),
            ],
            axis=1,
        )

    small_row, small_lane = iotas((TILE, BX))

    def unpack(i):
        misc = edge_tile(i, directions)
        owner_rows[i] = misc.astype(jnp.float32)[0:8].astype(jnp.int32)

        def columns_of(first):
            pick = one_hot(swap_lanes(c, small_row, small_lane, first, False))
            return lax.dot_general(
                misc, pick, (((0,), (0,)), ((), ())), preferred_element_type=jnp.float32
            )

        at = i * (depth * rows)
        if not isinstance(at, int):
            at = pl.multiple_of(at, TILE)
        beside[pl.ds(at, depth * rows), :] = columns_of(0).astype(jnp.bfloat16)
        at = i * (2 * depth)
        if not isinstance(at, int):
            at = pl.multiple_of(at, 8)
        sides = []
        for d in range(directions):
            pair = edge_tile(i, d).astype(jnp.float32)
            corner = columns_of(2 + 2 * d)[0 : 2 * depth]
            sides.append(arrange(pair[0 : 2 * depth], pair[2 * depth :], corner))
        edge_rows[0, pl.ds(at, 2 * depth), :] = jnp.where(g > 0, sides[0], 0.0)
        edge_rows[1, pl.ds(at, 2 * depth), :] = jnp.where(g < count_gy - 1, sides[-1], 0.0)

    if few > 1:
        for i in range(count_gz):
            unpack(i)
    else:
        pl.loop(0, count_gz)(unpack)
    table_copy = pltpu.make_async_copy(owner_rows, owner_table, sems.at[0])
    table_copy.start()

    def moved(values):
        lane = lax.broadcasted_iota(jnp.int32, values.shape, 1)
        return (
            jnp.where(lane == 0, 0.0, pltpu.roll(values, 1, 1)),
            values,
            jnp.where(lane == window - 1, 0.0, pltpu.roll(values, window - 1, 1)),
        )

    def edge_pair(k, at):
        if isinstance(at, int):
            return edge_rows[k, at : at + 2, :]
        group = edge_rows[k, pl.ds(pl.multiple_of(at // 8 * 8, 8), 8), :]
        return pltpu.roll(group, lax.rem(8 - at % 8, 8), 0)[0:2]

    def shifts(i, zz, slot, valid):
        z = i * depth + zz
        halves = []
        for h in range(2):
            at = zz * rows + h * HALF
            own = [tile_rows(i, k * depth * rows + at, HALF) for k in range(2)]
            at = z * rows + h * HALF
            if not isinstance(at, int):
                at = pl.multiple_of(at, TILE)
            values = arrange(*own, beside[pl.ds(at, HALF), :]).astype(jnp.float32)
            halves.append(values if valid is None else values * valid)
        top, bottom = edge_pair(0, 2 * z), edge_pair(1, 2 * z)
        if valid is not None:
            top, bottom = top * valid, bottom * valid
        seams = [
            jnp.concatenate([top, halves[1][0:2]], axis=0),
            jnp.concatenate([halves[0][HALF - 2 :], bottom], axis=0),
        ]
        for h in range(2):
            lanes = slice(h * window, (h + 1) * window)
            for dx, values in enumerate(moved(halves[h])):
                shifted[slot, dx * HALF : (dx + 1) * HALF, lanes] = values.astype(jnp.bfloat16)
            values = jnp.concatenate(
                [*moved(seams[h]), jnp.zeros((4, window), jnp.float32)], axis=0
            )
            shifted[slot, 3 * HALF : PART, lanes] = values.astype(jnp.bfloat16)

    def first(z, valid):
        total = jnp.dot(
            t1_ref[...],
            shifted[pl.ds(z + 1, 3)].reshape(3 * PART, 2 * window),
            preferred_element_type=jnp.float32,
        )
        values = jnp.maximum(total + bias_ref[...], 0.0)
        if valid is not None:
            values = values * valid
        hidden[z + 1] = values.astype(jnp.bfloat16)

    height = 2 * HALF
    lane = lax.broadcasted_iota(jnp.int32, (height, 2 * window), 1)
    left_edge = (lane == 0) | (lane == window)
    right_edge = (lane == window - 1) | (lane == 2 * window - 1)

    def second(z, t, zz):
        total = jnp.dot(
            t2_ref[...],
            hidden[pl.ds(z, 3)].reshape(3 * TALL, 2 * window),
            preferred_element_type=jnp.float32,
        )
        before = pltpu.roll(total[0:height], 1, 1)
        after = pltpu.roll(total[2 * height :], 2 * window - 1, 1)
        total = total[height : 2 * height] + bias2_ref[...]
        total = total + jnp.where(left_edge, 0.0, before)
        total = total + jnp.where(right_edge, 0.0, after)
        for h in range(2):
            at = h * window
            own = jnp.where(
                c == 0, total[:, at : at + columns], total[:, at + BX : at + window]
            )
            values = 0.5 + 0.5 * jnp.tanh(0.5 * own)
            values = values.astype(jnp.bfloat16).astype(jnp.float32)
            for yb in range(brick_rows):
                for xb in range(brick_columns):
                    b = (h * brick_rows + yb) * brick_columns + xb
                    bricks[t, b, zz] = values[yb * 8 : yb * 8 + 8, xb * BX : (xb + 1) * BX]

    def valid_slice(z):
        return ((z >= 0) & (z < count_gz * depth)).astype(jnp.float32)

    depths = segment * depth
    if single:
        shifted[1] = jnp.zeros((PART, 2 * window), jnp.bfloat16)
        shifted[depths + 2] = jnp.zeros((PART, 2 * window), jnp.bfloat16)
        hidden[0] = jnp.zeros((TALL, 2 * window), jnp.bfloat16)
        hidden[depths + 1] = jnp.zeros((TALL, 2 * window), jnp.bfloat16)
        for i in range(count_gz):
            tile = lax.rem(first_tile + i, count_gz)
            for zz in range(depth):
                shifts(i, zz, tile * depth + zz + 2, None)

        @pl.loop(0, depths, unroll=4)
        def _(z):
            first(z, None)

        @pl.loop(0, depths, unroll=4)
        def _(z):
            second(z, z // depth, z % depth)
    else:

        @pl.loop(0, count_gz // segment)
        def _(q):
            @pl.loop(-2, depths + 2)
            def _(z):
                at = q * depths + z
                inside = jnp.clip(at, 0, count_gz * depth - 1)
                shifts(inside // depth, inside % depth, z + 2, valid_slice(at))

            @pl.loop(-1, depths + 1)
            def _(z):
                first(z, valid_slice(q * depths + z))

            @pl.loop(0, depths)
            def _(z):
                second(z, q * segment + z // depth, z % depth)

    for zz in range(depth):
        for xb in range(brick_columns):
            own = [
                bricks[z_index, yb * brick_columns + xb, zz] for yb in range(rows // BY)
            ]
            for o in range(2):
                values = jnp.concatenate([v[o * BY : o * BY + BY] for v in own], axis=0)
                fractions[o, zz, :, xb * BX : (xb + 1) * BX] = values.astype(jnp.bfloat16)
    fractions_copy = pltpu.make_async_copy(fractions, fractions_ref, sems.at[1])
    fractions_copy.start()

    table_copy.wait()
    for j in range(slots):
        brick_of_slot[j] = -1

    @pl.loop(0, count_gz)
    def _(i):
        first = lax.rem(first_tile + i, count_gz) * capacity
        rank = jnp.int32(0)
        for b in range(brick_count):
            mine = owner_table[i, OWNER_ROW, b] == z_index
            brick_of_slot[jnp.where(mine, first + rank, slots)] = b
            rank = rank + mine.astype(jnp.int32)

    @pl.loop(0, slots, unroll=8)
    def _(j):
        brick = brick_of_slot[j]
        values = bricks[j // capacity, jnp.maximum(brick, 0)]
        values = jnp.where(brick >= 0, values, 0.0)
        at = pl.multiple_of(j * (2 * size), 8)
        arrived[pl.ds(at, 2 * size), :] = values.reshape(2 * size, BX)

    def next_copy(group):
        at = pl.ds(pl.multiple_of(group * 16 * size, 16 * size), 16 * size)
        return pltpu.make_async_copy(state.at[at], next_ref.at[at], group_sems.at[group])

    @pl.loop(0, slots // 8)
    def _(group):
        grid = [(z, y) for z in range(depth) for y in range(BY)]

        def load(ref):
            base = group * (8 * size)
            return [
                [
                    ref[pl.ds(pl.multiple_of(base + (z * BY + y) * 8, 8), 8), :]
                    for y in range(BY)
                ]
                for z in range(depth)
            ]

        def rows_of(offset):
            return pl.ds(group * 16 * size + offset, 8, stride=2 * size)

        quarter = load(quarter_ref)
        pore = [[arrived[rows_of(z * 8 + y), :] for y in range(BY)] for z in range(depth)]
        organic = [
            [0.3 * arrived[rows_of(z * 8 + BY + y), :] for y in range(BY)] for z in range(depth)
        ]
        slow = [[0.12 * p for p in row] for row in pore]
        fast = [[0.16 * p for p in row] for row in pore]
        carbon, oxygen = load(carbon_ref), load(oxygen_ref)
        around = load(carbon_around_ref), load(oxygen_around_ref)
        for z, y in grid:
            carbon[z][y] += slow[z][y] * around[0][z][y] + organic[z][y]
            oxygen[z][y] += fast[z][y] * around[1][z][y]
        for _ in range(STEPS - 1):
            carbon_new = [[None] * BY for _ in range(depth)]
            oxygen_new = [[None] * BY for _ in range(depth)]
            for z, y in grid:
                doc, oxy = carbon[z][y], oxygen[z][y]
                uptake = uptake_of(quarter[z][y], doc, oxy)
                gain = organic[z][y] - uptake
                carbon_new[z][y] = doc + slow[z][y] * laplace(carbon, z, y) + gain
                oxygen_new[z][y] = oxy + fast[z][y] * laplace(oxygen, z, y) - uptake
            carbon, oxygen = carbon_new, oxygen_new
        for z, y in grid:
            state[rows_of(z * BY + y), :] = carbon[z][y]
            state[rows_of(size + z * BY + y), :] = oxygen[z][y]
        next_copy(group).start()

    @pl.loop(0, slots // 8)
    def _(group):
        next_copy(group).wait()

    fractions_copy.wait()


def per_device(
    sizes, density, first_kernel, first_bias, second_kernel, second_bias, owners, solutes, biomass
):
    count_gz, count_gy, count_col = sizes
    depth, rows, columns = density.shape
    slots = solutes.shape[3]
    window = columns + BX
    segment = min(count_gz, 4)
    brick_count = (rows // BY) * (columns // BX)
    height = depth * rows
    depths = count_gz * depth
    bf16, f32 = jnp.bfloat16, jnp.float32
    shape = jax.ShapeDtypeStruct

    def over(pairs):
        return [
            (gy * count_col + col, to * count_col + 1 - col)
            for gy, to in pairs
            for col in range(count_col)
        ]

    if count_gy == 2:
        ways = [[(0, 1), (1, 0)]]
    else:
        up = [(i, i + 1) for i in range(count_gy - 1)]
        ways = [up, [(j, i) for i, j in up]]
    directions = len(ways)
    blocks = columns // BX
    own, misc, near, *sent = pl.pallas_call(
        functools.partial(edges_kernel, (count_gy, depth, rows, directions)),
        out_shape=[shape((blocks * height, BX), bf16)] + [shape((TILE, BX), bf16)] * (2 + 2 * directions),
        in_specs=[HBM, HBM],
        out_specs=[VMEM] * (3 + 2 * directions),
        scratch_shapes=[
            pltpu.VMEM((1, brick_count), jnp.int32),
            pltpu.SemaphoreType.DMA((blocks + 1,)),
        ],
        compiler_params=pltpu.CompilerParams(vmem_limit_bytes=4 * 2**20),
        name="edges",
    )(in_hbm(density.reshape(height, columns)), in_hbm(owners.reshape(1, brick_count)))

    received = []
    for d, pairs in enumerate(ways):
        received.append(lax.ppermute(sent[2 * d], "gy", pairs))
        received.append(lax.ppermute(sent[2 * d + 1], ("gy", "col"), over(pairs)))
    near = lax.ppermute(near, "col", [(0, 1), (1, 0)])
    cells = depth * BY
    prepared = pl.pallas_call(
        functools.partial(prepare_kernel, (depth, slots)),
        out_shape=[shape((slots * cells, BX), f32)] * 5,
        in_specs=[HBM, HBM, ANY],
        out_specs=[VMEM] * 5,
        scratch_shapes=[
            pltpu.VMEM((slots * 2 * cells, BX), f32),
            pltpu.VMEM((slots * cells, BX), bf16),
            pltpu.VMEM((slots * cells, BX), f32),
            pltpu.SemaphoreType.DMA((slots // 8, 2)),
        ],
        compiler_params=pltpu.CompilerParams(vmem_limit_bytes=12 * 2**20),
        cost_estimate=pl.CostEstimate(
            flops=60 * slots * cells * BX, bytes_accessed=2**20, transcendentals=0
        ),
        name="prepare",
    )(
        in_hbm(solutes.reshape(slots * 2 * cells, BX)),
        in_hbm(biomass.reshape(slots * cells, BX)),
        misc,
    )
    payload, cells_around = pl.pallas_call(
        functools.partial(pack_kernel, directions),
        out_shape=[
            shape((blocks * height + (directions + 1) * TILE, BX), bf16),
            shape(((directions + 1) * TILE, BX), bf16),
        ],
        in_specs=[VMEM] * 3 + [ANY] + [VMEM] * (2 * directions),
        out_specs=[VMEM] * 2,
        compiler_params=pltpu.CompilerParams(vmem_limit_bytes=4 * 2**20),
        name="pack",
    )(own, misc, near, prepared[-1], *received)

    def turned(array, s):
        return lax.ppermute(array, "gz", [((i + s) % count_gz, i) for i in range(count_gz)])

    few = count_gz if count_gz == 4 else 1
    if few > 1:
        opposite = turned(own, 2)
        tiles = [payload, turned(payload, 1), opposite, turned(payload, 3)]
        cells_around, _ = lax.optimization_barrier((cells_around, opposite))
        tiles.append(turned(cells_around, 2))
    else:
        tiles = [lax.all_gather(payload, "gz", axis=0, tiled=False)]

    t1, bias, t2, bias2 = pl.pallas_call(
        functools.partial(banded_kernel, (window, count_gy)),
        out_shape=(
            shape((TALL, 3 * PART), bf16),
            shape((TALL, 2 * window), f32),
            shape((6 * HALF, 3 * TALL), bf16),
            shape((2 * HALF, 2 * window), f32),
        ),
        in_specs=[HBM, HBM, HBM, HBM, ANY],
        out_specs=(VMEM, VMEM, VMEM, VMEM),
        scratch_shapes=[
            pltpu.VMEM((CHANNELS, 27), bf16),
            pltpu.SMEM((CHANNELS,), f32),
            pltpu.VMEM((2 * CHANNELS, 27), bf16),
            pltpu.SMEM((2,), f32),
            pltpu.SemaphoreType.DMA((4,)),
        ],
        compiler_params=pltpu.CompilerParams(vmem_limit_bytes=16 * 2**20),
        cost_estimate=pl.CostEstimate(
            flops=20 * 2**20, bytes_accessed=4 * 2**20, transcendentals=0
        ),
        name="banded",
    )(
        in_hbm(first_kernel.transpose(2, 1, 0).reshape(CHANNELS, 27)),
        in_hbm(first_bias),
        in_hbm(second_kernel.transpose(1, 2, 0).reshape(2 * CHANNELS, 27)),
        in_hbm(second_bias),
        payload,
    )

    fractions, solutes_next = pl.pallas_call(
        functools.partial(
            column_kernel,
            (count_gz, count_gy, depth, rows, columns, segment, slots, directions),
            few,
        ),
        out_shape=(
            shape((2, depth, rows, columns), bf16),
            shape((slots * 2 * cells, BX), f32),
        ),
        in_specs=[VMEM] * (len(tiles) + 9),
        out_specs=(HBM, HBM),
        scratch_shapes=[
            pltpu.VMEM((2, 2 * depths, window), f32),
            pltpu.VMEM((depths * rows, BX), bf16),
            pltpu.VMEM((segment * depth + 4, PART, 2 * window), bf16),
            pltpu.VMEM((segment * depth + 2, TALL, 2 * window), bf16),
            pltpu.VMEM((count_gz, brick_count, depth, 8, BX), f32),
            pltpu.VMEM((slots * 2 * cells, BX), f32),
            pltpu.VMEM((slots * 2 * cells, BX), f32),
            pltpu.VMEM((2, depth, rows, columns), bf16),
            pltpu.VMEM((count_gz, 8, BX), jnp.int32),
            pltpu.SMEM((count_gz, 8, BX), jnp.int32),
            pltpu.SMEM((slots + 1,), jnp.int32),
            pltpu.SemaphoreType.DMA((2,)),
            pltpu.SemaphoreType.DMA((slots // 8,)),
        ],
        compiler_params=pltpu.CompilerParams(vmem_limit_bytes=40 * 2**20),
        cost_estimate=pl.CostEstimate(
            flops=2 * depths * 2 * window * TALL * (3 * PART + 3 * 6 * HALF),
            bytes_accessed=4 * 2**20,
            transcendentals=0,
        ),
        name="column",
    )(
        *tiles,
        t1,
        bias,
        t2,
        bias2,
        *prepared,
    )
    return fractions, solutes_next.reshape(solutes.shape)


def solution(mesh):
    sizes = (mesh.shape["gz"], mesh.shape["gy"], mesh.shape["col"])
    assert sizes[2] == 2
    return jax.shard_map(
        functools.partial(per_device, sizes),
        mesh=mesh,
        in_specs=(
            P(("cores", "gz"), "gy", "col"),
            P(),
            P(),
            P(),
            P(),
            P(("cores", "gz"), "gy", "col", None, None),
            P(("cores", "gz"), "gy", "col", None, None, None, None, None),
            P(("cores", "gz"), "gy", "col", None, None, None, None),
        ),
        out_specs=(
            P(None, ("cores", "gz"), "gy", "col"),
            P(("cores", "gz"), "gy", "col", None, None, None, None, None),
        ),
        check_vma=False,
    )
```

```python
import functools

import jax
import jax.numpy as jnp
from jax import lax
from jax.experimental import pallas as pl
from jax.experimental.pallas import tpu as pltpu
from jax.sharding import PartitionSpec as P

BY = 4
BX = 128
STEPS = 4
TILE = 16
HALF = 16
CHANNELS = 8
REACH = HALF + 2
PART = 3 * HALF + TILE
TALL = REACH * CHANNELS
OUTSIDE = -3e38

VMEM = pl.BlockSpec(memory_space=pltpu.VMEM)
SMEM = pl.BlockSpec(memory_space=pltpu.SMEM)
ANY = pl.BlockSpec(memory_space=pl.ANY)
HBM = pl.BlockSpec(memory_space=pltpu.HBM)


def in_hbm(array):
    return pltpu.with_memory_space_constraint(array, pltpu.HBM)


def step_index(values, width, count):
    index = jnp.zeros(values.shape, jnp.int32)
    for k in range(1, count):
        index = index + (values >= k * width).astype(jnp.int32)
    return index


def one_hot(condition):
    return jnp.where(condition, 1.0, 0.0).astype(jnp.bfloat16)


def iotas(shape):
    return (
        lax.broadcasted_iota(jnp.int32, shape, 0),
        lax.broadcasted_iota(jnp.int32, shape, 1),
    )


def tap_parts(tap):
    dz = step_index(tap, 9, 3)
    dy = step_index(tap - 9 * dz, 3, 3)
    return dz, dy, tap - 9 * dz - 3 * dy


def pack_kernel(density_ref, owners_ref, payload_ref, named_ref, sems):
    height, columns = density_ref.shape
    blocks = columns // BX
    copies = [pltpu.make_async_copy(owners_ref, named_ref, sems.at[blocks])]
    for k in range(blocks):
        copies.append(
            pltpu.make_async_copy(
                density_ref.at[:, k * BX : (k + 1) * BX],
                payload_ref.at[k * height : (k + 1) * height],
                sems.at[k],
            )
        )
    for copy in copies:
        copy.start()
    copies[0].wait()
    named = named_ref[...].astype(jnp.float32)
    count = named.shape[1]
    payload_ref[blocks * height : blocks * height + TILE, :] = jnp.concatenate(
        [
            jnp.broadcast_to(named, (TILE, count)),
            jnp.zeros((TILE, BX - count), jnp.float32),
        ],
        axis=1,
    ).astype(jnp.bfloat16)
    for copy in copies[1:]:
        copy.wait()


def banded_kernel(dims, *refs):
    window, count_gy = dims
    sources, refs = refs[:4], refs[5:]
    t1_ref, bias_ref, t2_ref, bias2_ref, *local, sems = refs
    copies = [
        pltpu.make_async_copy(source, target, sems.at[k])
        for k, (source, target) in enumerate(zip(sources, local))
    ]
    for copy in copies:
        copy.start()
    for copy in copies:
        copy.wait()
    w1_ref, b1_ref, w2_ref, b2_ref = local
    g = lax.axis_index("gy")
    row, channel = iotas((TALL, CHANNELS))
    spread = one_hot((row & (CHANNELS - 1)) == channel)
    w1 = jnp.dot(spread, w1_ref[...], preferred_element_type=jnp.float32).astype(jnp.bfloat16)
    tap, column = iotas((27, 3 * PART))
    dz = step_index(column, PART, 3)
    place = column - PART * dz
    dx = jnp.where(place < 3 * HALF, place >> 4, (place - 3 * HALF) >> 2)
    base = 9 * dz + dx
    row, column = iotas((TALL, 3 * PART))
    place = column & (PART - 1)
    seam = (place - 3 * HALF) & 3
    seam_row = jnp.where(seam < 2, seam - 2, seam + HALF - 2)
    input_row = jnp.where(place < 3 * HALF, place & (HALF - 1), seam_row)
    distance = jnp.where(place < 3 * HALF + 12, input_row - (row >> 3) + 2, -1)
    total = jnp.zeros((TALL, 3 * PART), jnp.float32)
    for dy in range(3):
        values = jnp.dot(w1, one_hot(tap == base + 3 * dy), preferred_element_type=jnp.float32)
        total = jnp.where(distance == dy, values, total)
    t1_ref[...] = total.astype(jnp.bfloat16)
    row, column = iotas((TALL, 2 * window))
    bias = jnp.zeros((TALL, 2 * window), jnp.float32)
    for k in range(CHANNELS):
        bias = jnp.where((row & (CHANNELS - 1)) == k, b1_ref[k], bias)
    outside = ((row < CHANNELS) & (column < window) & (g == 0)) | (
        (row >= TALL - CHANNELS) & (column >= window) & (g == count_gy - 1)
    )
    bias_ref[...] = jnp.where(outside, OUTSIDE, bias)
    channel, column = iotas((CHANNELS, 3 * TALL))
    spread = one_hot((column & (CHANNELS - 1)) == channel)
    tap, column = iotas((27, 3 * TALL))
    same_z = tap_parts(tap)[0] == step_index(column, TALL, 3)
    row, tap = iotas((6 * HALF, 27))
    _, tap_y, tap_x = tap_parts(tap)
    same_x = (row >> 5) == tap_x
    wide = []
    for o in range(2):
        values = lax.dot_general(
            w2_ref[o * CHANNELS : (o + 1) * CHANNELS, :],
            spread,
            (((0,), (0,)), ((), ())),
            preferred_element_type=jnp.float32,
        )
        wide.append(jnp.where(same_z, values, 0.0).astype(jnp.bfloat16))
    out_row, column = iotas((6 * HALF, 3 * TALL))
    y = ((out_row >> 3) & 3) * BY + (out_row & 3)
    hidden_row = (column - TALL * step_index(column, TALL, 3)) >> 3
    total = jnp.zeros((6 * HALF, 3 * TALL), jnp.float32)
    for dy in range(3):
        values = 0.0
        for o in range(2):
            pick = one_hot(same_x & (tap_y == dy) & (((row >> 2) & 1) == o))
            values = values + jnp.dot(pick, wide[o], preferred_element_type=jnp.float32)
        total = jnp.where(hidden_row - y == dy, values, total)
    t2_ref[...] = total.astype(jnp.bfloat16)
    row, _ = iotas((2 * HALF, 2 * window))
    bias2_ref[...] = jnp.where(((row >> 2) & 1) == 0, b2_ref[0], b2_ref[1])


def edges_kernel(dims, *refs):
    count_gy, depth, rows, columns, few, count = dims
    tiles, outs = refs[:few], refs[few + 2 :]
    g = lax.axis_index("gy")
    c = lax.axis_index("col")
    height = depth * rows
    block = (1 - c) * height

    def take(i, start, size):
        start = pl.ds(pl.multiple_of(start, TILE), size)
        if few > 1:
            return tiles[i][start, :]
        return tiles[0][i, start, :]

    def pair(i):
        for k in range(2):
            at = pl.multiple_of((2 * i + k) * height, TILE)
            outs[0][pl.ds(at, height), :] = take(2 * i + k, block, height)
        low, high = [], []
        for k in range(2):
            for zz in range(depth):
                first, last = [], []
                for base in (0, height):
                    at = base + zz * rows
                    first.append(take(2 * i + k, at, TILE).astype(jnp.float32)[0:2])
                    at = at + rows - TILE
                    last.append(take(2 * i + k, at, TILE).astype(jnp.float32)[TILE - 2 :])
                low.append(jnp.concatenate(first, axis=1))
                high.append(jnp.concatenate(last, axis=1))
        at = pl.multiple_of(2 * i * 2 * depth, TILE)
        first, last = jnp.concatenate(low, axis=0), jnp.concatenate(high, axis=0)
        sends = [jnp.where(g == 0, last, first)] if count_gy == 2 else [last, first]
        for n, send in enumerate(sends):
            send = send.astype(jnp.bfloat16)
            outs[1 + n][pl.ds(at, TILE), :] = send

    if few > 1:
        for i in range(count // 2):
            pair(i)
    else:
        pl.loop(0, count // 2)(pair)


def corner_kernel(edge_ref, corner_ref):
    c = lax.axis_index("col")
    corner_ref[...] = jnp.where(c == 0, edge_ref[:, BX:], edge_ref[:, 0:BX])


def laplace(field, z, y):
    centre = field[z][y]
    last = lax.broadcasted_iota(jnp.int32, centre.shape, 1) == BX - 1
    ahead = jnp.where(last, 0.0, pltpu.roll(centre, BX - 1, 1) - centre)
    result = ahead - pltpu.roll(ahead, 1, 1)
    beside = [
        field[zz][yy]
        for zz, yy in ((z - 1, y), (z + 1, y), (z, y - 1), (z, y + 1))
        if 0 <= zz < len(field) and 0 <= yy < BY
    ]
    return result + (functools.reduce(jnp.add, beside) - float(len(beside)) * centre)


def uptake_of(quarter, doc, oxy):
    return quarter * doc * oxy / ((0.5 + jnp.abs(doc)) * (0.3 + jnp.abs(oxy)))


def prepare_kernel(dims, solutes_ref, biomass_ref, _, *refs):
    depth, slots = dims
    outs, (state, biomass, mass, sems) = refs[:5], refs[5:]
    size = depth * BY
    copies = []
    for group in range(slots // 8):
        for k, (source, target) in enumerate(((solutes_ref, state), (biomass_ref, biomass))):
            rows = (2 - k) * 8 * size
            at = pl.ds(group * rows, rows)
            copies.append(
                pltpu.make_async_copy(source.at[at], target.at[at], sems.at[group, k])
            )
    for copy in copies:
        copy.start()
    for group in range(slots // 8):
        copies[2 * group].wait()
        copies[2 * group + 1].wait()
        at = slice(group * 8 * size, (group + 1) * 8 * size)
        mass[at, :] = biomass[at, :].astype(jnp.float32)

        def rows_of(pitch, offset):
            return pl.ds(group * 8 * pitch + offset, 8, stride=pitch)

        grid = [(z, y) for z in range(depth) for y in range(BY)]
        carbon, oxygen = [
            [
                [state[rows_of(2 * size, k * size + z * BY + y), :] for y in range(BY)]
                for z in range(depth)
            ]
            for k in range(2)
        ]
        for z, y in grid:
            at = group * 8 * size + (z * BY + y) * 8
            at = slice(at, at + 8)
            doc, oxy = carbon[z][y], oxygen[z][y]
            quarter = 0.25 * mass[rows_of(size, z * BY + y), :]
            uptake = uptake_of(quarter, doc, oxy)
            values = (
                doc - uptake,
                oxy - uptake,
                laplace(carbon, z, y),
                laplace(oxygen, z, y),
                quarter,
            )
            for out, value in zip(outs, values):
                out[at, :] = value


def column_kernel(dims, few, *refs):
    count_gz, count_gy, depth, rows, columns, segment, slots, directions = dims
    tiles, refs = refs[:few], refs[few:]
    x_ref, refs = refs[0], refs[1:]
    top_refs, refs = refs[:2], refs[2:]
    if directions == 1:
        bottom_refs = top_refs
    else:
        bottom_refs, refs = refs[:2], refs[2:]
    t1_ref, bias_ref, t2_ref, bias2_ref, *refs = refs
    carbon_ref, oxygen_ref, carbon_around_ref, oxygen_around_ref, quarter_ref, *refs = refs
    fractions_ref, next_ref, *refs = refs
    (
        edge_rows,
        shifted,
        hidden,
        bricks,
        arrived,
        state,
        fractions,
        owner_rows,
        owner_table,
        brick_of_slot,
        sems,
        group_sems,
    ) = refs
    z_index = lax.axis_index("gz")
    g = lax.axis_index("gy")
    c = lax.axis_index("col")
    window = columns + BX
    brick_rows = HALF // BY
    brick_columns = columns // BX
    brick_count = rows // BY * brick_columns
    capacity = slots // count_gz
    single = segment == count_gz
    first_tile = z_index if few > 1 else 0
    size = depth * BY

    def tile_rows(i, start, size):
        if not isinstance(start, int):
            start = pl.multiple_of(start, TILE)
        if few > 1:
            return tiles[i][pl.ds(start, size), :]
        return tiles[0][i, pl.ds(start, size), :]

    def read_owners(i):
        row = tile_rows(i, brick_columns * depth * rows, TILE)
        owner_rows[i] = row.astype(jnp.float32)[0:8].astype(jnp.int32)

    if few > 1:
        for i in range(count_gz):
            read_owners(i)
    else:
        pl.loop(0, count_gz)(read_owners)
    table_copy = pltpu.make_async_copy(owner_rows, owner_table, sems.at[0])
    table_copy.start()

    def arrange(left, right, other):
        return jnp.concatenate(
            [
                jnp.where(c == 0, left, other),
                jnp.where(c == 0, right, left),
                jnp.where(c == 0, other, right),
            ],
            axis=1,
        )

    for k, pair in enumerate((top_refs, bottom_refs)):
        exists = (g > 0) if k == 0 else (g < count_gy - 1)
        own, other = pair[0][...].astype(jnp.float32), pair[1][...].astype(jnp.float32)
        values = arrange(own[:, 0:BX], own[:, BX:columns], other)
        edge_rows[k] = values * exists.astype(jnp.float32)

    def moved(values):
        lane = lax.broadcasted_iota(jnp.int32, values.shape, 1)
        return (
            jnp.where(lane == 0, 0.0, pltpu.roll(values, 1, 1)),
            values,
            jnp.where(lane == window - 1, 0.0, pltpu.roll(values, window - 1, 1)),
        )

    def edge_pair(k, at):
        if isinstance(at, int):
            return edge_rows[k, at : at + 2, :]
        group = edge_rows[k, pl.ds(pl.multiple_of(at // 8 * 8, 8), 8), :]
        return pltpu.roll(group, lax.rem(8 - at % 8, 8), 0)[0:2]

    def shifts(i, zz, slot, valid):
        z = i * depth + zz
        halves = []
        for h in range(2):
            at = zz * rows + h * HALF
            own = [tile_rows(i, k * depth * rows + at, HALF) for k in range(2)]
            at = z * rows + h * HALF
            if not isinstance(at, int):
                at = pl.multiple_of(at, TILE)
            values = arrange(*own, x_ref[pl.ds(at, HALF), :]).astype(jnp.float32)
            halves.append(values if valid is None else values * valid)
        top, bottom = edge_pair(0, 2 * z), edge_pair(1, 2 * z)
        if valid is not None:
            top, bottom = top * valid, bottom * valid
        seams = [
            jnp.concatenate([top, halves[1][0:2]], axis=0),
            jnp.concatenate([halves[0][HALF - 2 :], bottom], axis=0),
        ]
        for h in range(2):
            lanes = slice(h * window, (h + 1) * window)
            for dx, values in enumerate(moved(halves[h])):
                shifted[slot, dx * HALF : (dx + 1) * HALF, lanes] = values.astype(jnp.bfloat16)
            values = jnp.concatenate(
                [*moved(seams[h]), jnp.zeros((4, window), jnp.float32)], axis=0
            )
            shifted[slot, 3 * HALF : PART, lanes] = values.astype(jnp.bfloat16)

    def first(z, valid):
        total = jnp.dot(
            t1_ref[...],
            shifted[pl.ds(z + 1, 3)].reshape(3 * PART, 2 * window),
            preferred_element_type=jnp.float32,
        )
        values = jnp.maximum(total + bias_ref[...], 0.0)
        if valid is not None:
            values = values * valid
        hidden[z + 1] = values.astype(jnp.bfloat16)

    height = 2 * HALF
    lane = lax.broadcasted_iota(jnp.int32, (height, 2 * window), 1)
    left_edge = (lane == 0) | (lane == window)
    right_edge = (lane == window - 1) | (lane == 2 * window - 1)

    def second(z, t, zz):
        total = jnp.dot(
            t2_ref[...],
            hidden[pl.ds(z, 3)].reshape(3 * TALL, 2 * window),
            preferred_element_type=jnp.float32,
        )
        before = pltpu.roll(total[0:height], 1, 1)
        after = pltpu.roll(total[2 * height :], 2 * window - 1, 1)
        total = total[height : 2 * height] + bias2_ref[...]
        total = total + jnp.where(left_edge, 0.0, before)
        total = total + jnp.where(right_edge, 0.0, after)
        for h in range(2):
            at = h * window
            own = jnp.where(
                c == 0, total[:, at : at + columns], total[:, at + BX : at + window]
            )
            values = 0.5 + 0.5 * jnp.tanh(0.5 * own)
            values = values.astype(jnp.bfloat16).astype(jnp.float32)
            for yb in range(brick_rows):
                for xb in range(brick_columns):
                    b = (h * brick_rows + yb) * brick_columns + xb
                    bricks[t, b, zz] = values[yb * 8 : yb * 8 + 8, xb * BX : (xb + 1) * BX]

    def valid_slice(z):
        return ((z >= 0) & (z < count_gz * depth)).astype(jnp.float32)

    depths = segment * depth
    if single:
        shifted[1] = jnp.zeros((PART, 2 * window), jnp.bfloat16)
        shifted[depths + 2] = jnp.zeros((PART, 2 * window), jnp.bfloat16)
        hidden[0] = jnp.zeros((TALL, 2 * window), jnp.bfloat16)
        hidden[depths + 1] = jnp.zeros((TALL, 2 * window), jnp.bfloat16)
        for i in range(count_gz):
            tile = lax.rem(first_tile + i, count_gz)
            for zz in range(depth):
                shifts(i, zz, tile * depth + zz + 2, None)

        first(0, None)
        for z in range(depths):
            if z + 1 < depths:
                first(z + 1, None)
            second(z, z // depth, z % depth)
    else:

        @pl.loop(0, count_gz // segment)
        def _(q):
            @pl.loop(-2, depths + 2)
            def _(z):
                at = q * depths + z
                inside = jnp.clip(at, 0, count_gz * depth - 1)
                shifts(inside // depth, inside % depth, z + 2, valid_slice(at))

            @pl.loop(-1, depths + 1)
            def _(z):
                first(z, valid_slice(q * depths + z))

            @pl.loop(0, depths)
            def _(z):
                second(z, q * segment + z // depth, z % depth)

    for zz in range(depth):
        for xb in range(brick_columns):
            own = [
                bricks[z_index, yb * brick_columns + xb, zz] for yb in range(rows // BY)
            ]
            for o in range(2):
                values = jnp.concatenate([v[o * BY : o * BY + BY] for v in own], axis=0)
                fractions[o, zz, :, xb * BX : (xb + 1) * BX] = values.astype(jnp.bfloat16)
    fractions_copy = pltpu.make_async_copy(fractions, fractions_ref, sems.at[1])
    fractions_copy.start()

    table_copy.wait()
    for j in range(slots):
        brick_of_slot[j] = -1

    @pl.loop(0, count_gz)
    def _(i):
        first = lax.rem(first_tile + i, count_gz) * capacity
        rank = jnp.int32(0)
        for b in range(brick_count):
            mine = owner_table[i, 0, b] == z_index
            brick_of_slot[jnp.where(mine, first + rank, slots)] = b
            rank = rank + mine.astype(jnp.int32)

    @pl.loop(0, slots, unroll=8)
    def _(j):
        brick = brick_of_slot[j]
        values = bricks[j // capacity, jnp.maximum(brick, 0)]
        values = jnp.where(brick >= 0, values, 0.0)
        at = pl.multiple_of(j * (2 * size), 8)
        arrived[pl.ds(at, 2 * size), :] = values.reshape(2 * size, BX)

    def next_copy(group):
        at = pl.ds(pl.multiple_of(group * 16 * size, 16 * size), 16 * size)
        return pltpu.make_async_copy(state.at[at], next_ref.at[at], group_sems.at[group])

    @pl.loop(0, slots // 8)
    def _(group):
        grid = [(z, y) for z in range(depth) for y in range(BY)]

        def load(ref):
            base = group * (8 * size)
            return [
                [
                    ref[pl.ds(pl.multiple_of(base + (z * BY + y) * 8, 8), 8), :]
                    for y in range(BY)
                ]
                for z in range(depth)
            ]

        def rows_of(offset):
            return pl.ds(group * 16 * size + offset, 8, stride=2 * size)

        quarter = load(quarter_ref)
        pore = [[arrived[rows_of(z * 8 + y), :] for y in range(BY)] for z in range(depth)]
        organic = [
            [0.3 * arrived[rows_of(z * 8 + BY + y), :] for y in range(BY)] for z in range(depth)
        ]
        slow = [[0.12 * p for p in row] for row in pore]
        fast = [[0.16 * p for p in row] for row in pore]
        carbon, oxygen = load(carbon_ref), load(oxygen_ref)
        around = load(carbon_around_ref), load(oxygen_around_ref)
        for z, y in grid:
            carbon[z][y] += slow[z][y] * around[0][z][y] + organic[z][y]
            oxygen[z][y] += fast[z][y] * around[1][z][y]
        for _ in range(STEPS - 1):
            carbon_new = [[None] * BY for _ in range(depth)]
            oxygen_new = [[None] * BY for _ in range(depth)]
            for z, y in grid:
                doc, oxy = carbon[z][y], oxygen[z][y]
                uptake = uptake_of(quarter[z][y], doc, oxy)
                gain = organic[z][y] - uptake
                carbon_new[z][y] = doc + slow[z][y] * laplace(carbon, z, y) + gain
                oxygen_new[z][y] = oxy + fast[z][y] * laplace(oxygen, z, y) - uptake
            carbon, oxygen = carbon_new, oxygen_new
        for z, y in grid:
            state[rows_of(z * BY + y), :] = carbon[z][y]
            state[rows_of(size + z * BY + y), :] = oxygen[z][y]
        next_copy(group).start()

    @pl.loop(0, slots // 8)
    def _(group):
        next_copy(group).wait()

    fractions_copy.wait()


def per_device(
    sizes, density, first_kernel, first_bias, second_kernel, second_bias, owners, solutes, biomass
):
    count_gz, count_gy, count_col = sizes
    depth, rows, columns = density.shape
    slots = solutes.shape[3]
    window = columns + BX
    segment = min(count_gz, 4)
    brick_count = (rows // BY) * (columns // BX)
    height = depth * rows
    depths = count_gz * depth
    bf16, f32 = jnp.bfloat16, jnp.float32
    shape = jax.ShapeDtypeStruct

    payload = pl.pallas_call(
        pack_kernel,
        out_shape=shape((columns // BX * height + TILE, BX), bf16),
        in_specs=[HBM, HBM],
        out_specs=VMEM,
        scratch_shapes=[
            pltpu.VMEM((1, brick_count), jnp.int32),
            pltpu.SemaphoreType.DMA((columns // BX + 1,)),
        ],
        compiler_params=pltpu.CompilerParams(vmem_limit_bytes=4 * 2**20),
        name="pack",
    )(in_hbm(density.reshape(height, columns)), in_hbm(owners.reshape(1, brick_count)))

    few = count_gz if count_gz == segment else 1
    if few > 1:
        tiles = [payload] + [
            lax.ppermute(payload, "gz", [((i + s) % count_gz, i) for i in range(count_gz)])
            for s in range(1, count_gz)
        ]
    else:
        tiles = [lax.all_gather(payload, "gz", axis=0, tiled=False)]

    cells = depth * BY
    prepared = pl.pallas_call(
        functools.partial(prepare_kernel, (depth, slots)),
        out_shape=[shape((slots * cells, BX), f32)] * 5,
        in_specs=[HBM, HBM, ANY],
        out_specs=[VMEM] * 5,
        scratch_shapes=[
            pltpu.VMEM((slots * 2 * cells, BX), f32),
            pltpu.VMEM((slots * cells, BX), bf16),
            pltpu.VMEM((slots * cells, BX), f32),
            pltpu.SemaphoreType.DMA((slots // 8, 2)),
        ],
        compiler_params=pltpu.CompilerParams(vmem_limit_bytes=12 * 2**20),
        cost_estimate=pl.CostEstimate(
            flops=60 * slots * cells * BX, bytes_accessed=2**20, transcendentals=0
        ),
        name="prepare",
    )(
        in_hbm(solutes.reshape(slots * 2 * cells, BX)),
        in_hbm(biomass.reshape(slots * cells, BX)),
        payload,
    )
    t1, bias, t2, bias2 = pl.pallas_call(
        functools.partial(banded_kernel, (window, count_gy)),
        out_shape=(
            shape((TALL, 3 * PART), bf16),
            shape((TALL, 2 * window), f32),
            shape((6 * HALF, 3 * TALL), bf16),
            shape((2 * HALF, 2 * window), f32),
        ),
        in_specs=[HBM, HBM, HBM, HBM, ANY],
        out_specs=(VMEM, VMEM, VMEM, VMEM),
        scratch_shapes=[
            pltpu.VMEM((CHANNELS, 27), bf16),
            pltpu.SMEM((CHANNELS,), f32),
            pltpu.VMEM((2 * CHANNELS, 27), bf16),
            pltpu.SMEM((2,), f32),
            pltpu.SemaphoreType.DMA((4,)),
        ],
        compiler_params=pltpu.CompilerParams(vmem_limit_bytes=16 * 2**20),
        cost_estimate=pl.CostEstimate(
            flops=20 * 2**20, bytes_accessed=4 * 2**20, transcendentals=0
        ),
        name="banded",
    )(
        in_hbm(first_kernel.transpose(2, 1, 0).reshape(CHANNELS, 27)),
        in_hbm(first_bias),
        in_hbm(second_kernel.transpose(1, 2, 0).reshape(2 * CHANNELS, 27)),
        in_hbm(second_bias),
        payload,
    )

    if count_gy == 2:
        ways = [[(0, 1), (1, 0)]]
    else:
        up = [(i, i + 1) for i in range(count_gy - 1)]
        ways = [up, [(j, i) for i, j in up]]
    directions = len(ways)
    swap = [(0, 1), (1, 0)]
    near, *sent = pl.pallas_call(
        functools.partial(edges_kernel, (count_gy, depth, rows, columns, few, count_gz)),
        out_shape=[shape((depths * rows, BX), bf16)]
        + [shape((2 * depths, columns), bf16)] * directions,
        in_specs=[VMEM] * few + [ANY, ANY],
        out_specs=[VMEM] * (1 + directions),
        compiler_params=pltpu.CompilerParams(vmem_limit_bytes=16 * 2**20),
        name="edges",
    )(*tiles, bias2, prepared[-1])
    edges = []
    for pairs, edge in zip(ways, sent):
        edge = lax.ppermute(edge, "gy", pairs)
        corner = pl.pallas_call(
            corner_kernel,
            out_shape=shape((2 * depths, BX), bf16),
            in_specs=[VMEM],
            out_specs=VMEM,
            compiler_params=pltpu.CompilerParams(vmem_limit_bytes=4 * 2**20),
            name="corner",
        )(edge)
        edges += [edge, lax.ppermute(corner, "col", swap)]
    near = lax.ppermute(near, "col", swap)

    fractions, solutes_next = pl.pallas_call(
        functools.partial(
            column_kernel,
            (count_gz, count_gy, depth, rows, columns, segment, slots, directions),
            few,
        ),
        out_shape=(
            shape((2, depth, rows, columns), bf16),
            shape((slots * 2 * cells, BX), f32),
        ),
        in_specs=[VMEM] * (few + 1 + len(edges) + 9),
        out_specs=(HBM, HBM),
        scratch_shapes=[
            pltpu.VMEM((2, 2 * depths, window), f32),
            pltpu.VMEM((segment * depth + 4, PART, 2 * window), bf16),
            pltpu.VMEM((segment * depth + 2, TALL, 2 * window), bf16),
            pltpu.VMEM((count_gz, brick_count, depth, 8, BX), f32),
            pltpu.VMEM((slots * 2 * cells, BX), f32),
            pltpu.VMEM((slots * 2 * cells, BX), f32),
            pltpu.VMEM((2, depth, rows, columns), bf16),
            pltpu.VMEM((count_gz, 8, BX), jnp.int32),
            pltpu.SMEM((count_gz, 8, BX), jnp.int32),
            pltpu.SMEM((slots + 1,), jnp.int32),
            pltpu.SemaphoreType.DMA((2,)),
            pltpu.SemaphoreType.DMA((slots // 8,)),
        ],
        compiler_params=pltpu.CompilerParams(vmem_limit_bytes=40 * 2**20),
        cost_estimate=pl.CostEstimate(
            flops=2 * depths * 2 * window * TALL * (3 * PART + 3 * 6 * HALF),
            bytes_accessed=4 * 2**20,
            transcendentals=0,
        ),
        name="column",
    )(
        *tiles,
        near,
        *edges,
        t1,
        bias,
        t2,
        bias2,
        *prepared,
    )
    return fractions, solutes_next.reshape(solutes.shape)


def solution(mesh):
    sizes = (mesh.shape["gz"], mesh.shape["gy"], mesh.shape["col"])
    assert sizes[2] == 2
    return jax.shard_map(
        functools.partial(per_device, sizes),
        mesh=mesh,
        in_specs=(
            P(("cores", "gz"), "gy", "col"),
            P(),
            P(),
            P(),
            P(),
            P(("cores", "gz"), "gy", "col", None, None),
            P(("cores", "gz"), "gy", "col", None, None, None, None, None),
            P(("cores", "gz"), "gy", "col", None, None, None, None),
        ),
        out_specs=(
            P(None, ("cores", "gz"), "gy", "col"),
            P(("cores", "gz"), "gy", "col", None, None, None, None, None),
        ),
        check_vma=False,
    )
```

```python
import functools

import jax
import jax.numpy as jnp
from jax import lax
from jax.experimental import pallas as pl
from jax.experimental.pallas import tpu as pltpu
from jax.sharding import PartitionSpec as P

BY = 4
BX = 128
STEPS = 4
TILE = 16
HALF = 16
CHANNELS = 8
REACH = HALF + 2
PART = 3 * HALF + TILE
TALL = REACH * CHANNELS
OUTSIDE = -3e38

VMEM = pl.BlockSpec(memory_space=pltpu.VMEM)
SMEM = pl.BlockSpec(memory_space=pltpu.SMEM)
ANY = pl.BlockSpec(memory_space=pl.ANY)
HBM = pl.BlockSpec(memory_space=pltpu.HBM)


def in_hbm(array):
    return pltpu.with_memory_space_constraint(array, pltpu.HBM)


def step_index(values, width, count):
    index = jnp.zeros(values.shape, jnp.int32)
    for k in range(1, count):
        index = index + (values >= k * width).astype(jnp.int32)
    return index


def one_hot(condition):
    return jnp.where(condition, 1.0, 0.0).astype(jnp.bfloat16)


def iotas(shape):
    return (
        lax.broadcasted_iota(jnp.int32, shape, 0),
        lax.broadcasted_iota(jnp.int32, shape, 1),
    )


def tap_parts(tap):
    dz = step_index(tap, 9, 3)
    dy = step_index(tap - 9 * dz, 3, 3)
    return dz, dy, tap - 9 * dz - 3 * dy


def pack_kernel(density_ref, owners_ref, payload_ref, named_ref, sems):
    height, columns = density_ref.shape
    blocks = columns // BX
    copies = [pltpu.make_async_copy(owners_ref, named_ref, sems.at[blocks])]
    for k in range(blocks):
        copies.append(
            pltpu.make_async_copy(
                density_ref.at[:, k * BX : (k + 1) * BX],
                payload_ref.at[k * height : (k + 1) * height],
                sems.at[k],
            )
        )
    for copy in copies:
        copy.start()
    copies[0].wait()
    named = named_ref[...].astype(jnp.float32)
    count = named.shape[1]
    payload_ref[blocks * height : blocks * height + TILE, :] = jnp.concatenate(
        [
            jnp.broadcast_to(named, (TILE, count)),
            jnp.zeros((TILE, BX - count), jnp.float32),
        ],
        axis=1,
    ).astype(jnp.bfloat16)
    for copy in copies[1:]:
        copy.wait()


def upper_lanes(first):
    half = BX // 2
    start = first + jnp.where(lax.axis_index("col") == 0, 0, half)
    return start, start + half


def banded_kernel(dims, *refs):
    columns, count_gy = dims
    lanes = 2 * columns + BX
    sources, refs = refs[:4], refs[5:]
    t1_ref, bias_ref, t2_ref, bias2_ref, *local, sems = refs
    copies = [
        pltpu.make_async_copy(source, target, sems.at[k])
        for k, (source, target) in enumerate(zip(sources, local))
    ]
    for copy in copies:
        copy.start()
    for copy in copies:
        copy.wait()
    w1_ref, b1_ref, w2_ref, b2_ref = local
    g = lax.axis_index("gy")
    row, channel = iotas((TALL, CHANNELS))
    spread = one_hot((row & (CHANNELS - 1)) == channel)
    w1 = jnp.dot(spread, w1_ref[...], preferred_element_type=jnp.float32).astype(jnp.bfloat16)
    tap, column = iotas((27, 3 * PART))
    dz = step_index(column, PART, 3)
    place = column - PART * dz
    dx = jnp.where(place < 3 * HALF, place >> 4, (place - 3 * HALF) >> 2)
    base = 9 * dz + dx
    row, column = iotas((TALL, 3 * PART))
    place = column & (PART - 1)
    seam = (place - 3 * HALF) & 3
    seam_row = jnp.where(seam < 2, seam - 2, seam + HALF - 2)
    input_row = jnp.where(place < 3 * HALF, place & (HALF - 1), seam_row)
    distance = jnp.where(place < 3 * HALF + 12, input_row - (row >> 3) + 2, -1)
    total = jnp.zeros((TALL, 3 * PART), jnp.float32)
    for dy in range(3):
        values = jnp.dot(w1, one_hot(tap == base + 3 * dy), preferred_element_type=jnp.float32)
        total = jnp.where(distance == dy, values, total)
    t1_ref[...] = total.astype(jnp.bfloat16)
    row, column = iotas((TALL, lanes))
    bias = jnp.zeros((TALL, lanes), jnp.float32)
    for k in range(CHANNELS):
        bias = jnp.where((row & (CHANNELS - 1)) == k, b1_ref[k], bias)
    start, stop = upper_lanes(2 * columns)
    upper = (column < columns) | ((column >= start) & (column < stop))
    outside = ((row < CHANNELS) & upper & (g == 0)) | (
        (row >= TALL - CHANNELS) & jnp.logical_not(upper) & (g == count_gy - 1)
    )
    bias_ref[...] = jnp.where(outside, OUTSIDE, bias)
    channel, column = iotas((CHANNELS, 3 * TALL))
    spread = one_hot((column & (CHANNELS - 1)) == channel)
    tap, column = iotas((27, 3 * TALL))
    same_z = tap_parts(tap)[0] == step_index(column, TALL, 3)
    row, tap = iotas((6 * HALF, 27))
    _, tap_y, tap_x = tap_parts(tap)
    same_x = (row >> 5) == tap_x
    wide = []
    for o in range(2):
        values = lax.dot_general(
            w2_ref[o * CHANNELS : (o + 1) * CHANNELS, :],
            spread,
            (((0,), (0,)), ((), ())),
            preferred_element_type=jnp.float32,
        )
        wide.append(jnp.where(same_z, values, 0.0).astype(jnp.bfloat16))
    out_row, column = iotas((6 * HALF, 3 * TALL))
    y = ((out_row >> 3) & 3) * BY + (out_row & 3)
    hidden_row = (column - TALL * step_index(column, TALL, 3)) >> 3
    total = jnp.zeros((6 * HALF, 3 * TALL), jnp.float32)
    for dy in range(3):
        values = 0.0
        for o in range(2):
            pick = one_hot(same_x & (tap_y == dy) & (((row >> 2) & 1) == o))
            values = values + jnp.dot(pick, wide[o], preferred_element_type=jnp.float32)
        total = jnp.where(hidden_row - y == dy, values, total)
    t2_ref[...] = total.astype(jnp.bfloat16)
    row, _ = iotas((2 * HALF, columns))
    bias2_ref[...] = jnp.where(((row >> 2) & 1) == 0, b2_ref[0], b2_ref[1])


def edges_kernel(dims, *refs):
    count_gy, depth, rows, columns, few, count = dims
    tiles, outs = refs[:few], refs[few + 2 :]
    g = lax.axis_index("gy")
    c = lax.axis_index("col")
    height = depth * rows
    block = (1 - c) * height

    def take(i, start, size):
        start = pl.ds(pl.multiple_of(start, TILE), size)
        if few > 1:
            return tiles[i][start, :]
        return tiles[0][i, start, :]

    def pair(i):
        for k in range(2):
            at = pl.multiple_of((2 * i + k) * height, TILE)
            outs[0][pl.ds(at, height), :] = take(2 * i + k, block, height)
        low, high = [], []
        for k in range(2):
            for zz in range(depth):
                first, last = [], []
                for base in (0, height):
                    at = base + zz * rows
                    first.append(take(2 * i + k, at, TILE).astype(jnp.float32)[0:2])
                    at = at + rows - TILE
                    last.append(take(2 * i + k, at, TILE).astype(jnp.float32)[TILE - 2 :])
                low.append(jnp.concatenate(first, axis=1))
                high.append(jnp.concatenate(last, axis=1))
        at = pl.multiple_of(2 * i * 2 * depth, TILE)
        first, last = jnp.concatenate(low, axis=0), jnp.concatenate(high, axis=0)
        sends = [jnp.where(g == 0, last, first)] if count_gy == 2 else [last, first]
        for n, send in enumerate(sends):
            send = send.astype(jnp.bfloat16)
            outs[1 + n][pl.ds(at, TILE), :] = send

    if few > 1:
        for i in range(count // 2):
            pair(i)
    else:
        pl.loop(0, count // 2)(pair)


def corner_kernel(edge_ref, corner_ref):
    c = lax.axis_index("col")
    corner_ref[...] = jnp.where(c == 0, edge_ref[:, BX:], edge_ref[:, 0:BX])


def laplace(field, z, y):
    centre = field[z][y]
    last = lax.broadcasted_iota(jnp.int32, centre.shape, 1) == BX - 1
    ahead = jnp.where(last, 0.0, pltpu.roll(centre, BX - 1, 1) - centre)
    result = ahead - pltpu.roll(ahead, 1, 1)
    beside = [
        field[zz][yy]
        for zz, yy in ((z - 1, y), (z + 1, y), (z, y - 1), (z, y + 1))
        if 0 <= zz < len(field) and 0 <= yy < BY
    ]
    return result + (functools.reduce(jnp.add, beside) - float(len(beside)) * centre)


def uptake_of(quarter, doc, oxy):
    divisor = (0.5 + jnp.abs(doc)) * (0.3 + jnp.abs(oxy))
    inverse = pl.reciprocal(divisor, approx=True)
    return quarter * doc * oxy * (inverse * (2.0 - divisor * inverse))


def prepare_kernel(dims, solutes_ref, biomass_ref, _, *refs):
    depth, slots = dims
    outs, (state, biomass, mass, sems) = refs[:5], refs[5:]
    size = depth * BY
    copies = []
    for group in range(slots // 8):
        for k, (source, target) in enumerate(((solutes_ref, state), (biomass_ref, biomass))):
            rows = (2 - k) * 8 * size
            at = pl.ds(group * rows, rows)
            copies.append(
                pltpu.make_async_copy(source.at[at], target.at[at], sems.at[group, k])
            )
    for copy in copies:
        copy.start()
    for group in range(slots // 8):
        copies[2 * group].wait()
        copies[2 * group + 1].wait()
        at = slice(group * 8 * size, (group + 1) * 8 * size)
        mass[at, :] = biomass[at, :].astype(jnp.float32)

        def rows_of(pitch, offset):
            return pl.ds(group * 8 * pitch + offset, 8, stride=pitch)

        grid = [(z, y) for z in range(depth) for y in range(BY)]
        carbon, oxygen = [
            [
                [state[rows_of(2 * size, k * size + z * BY + y), :] for y in range(BY)]
                for z in range(depth)
            ]
            for k in range(2)
        ]
        for z, y in grid:
            at = group * 8 * size + (z * BY + y) * 8
            at = slice(at, at + 8)
            doc, oxy = carbon[z][y], oxygen[z][y]
            quarter = 0.25 * mass[rows_of(size, z * BY + y), :]
            uptake = uptake_of(quarter, doc, oxy)
            values = (
                doc - uptake,
                oxy - uptake,
                laplace(carbon, z, y),
                laplace(oxygen, z, y),
                quarter,
            )
            for out, value in zip(outs, values):
                out[at, :] = value


def column_kernel(dims, few, *refs):
    count_gz, count_gy, depth, rows, columns, segment, slots, directions = dims
    tiles, refs = refs[:few], refs[few:]
    x_ref, refs = refs[0], refs[1:]
    top_refs, refs = refs[:2], refs[2:]
    if directions == 1:
        bottom_refs = top_refs
    else:
        bottom_refs, refs = refs[:2], refs[2:]
    t1_ref, bias_ref, t2_ref, bias2_ref, *refs = refs
    carbon_ref, oxygen_ref, carbon_around_ref, oxygen_around_ref, quarter_ref, *refs = refs
    fractions_ref, next_ref, *refs = refs
    (
        edge_rows,
        shifted,
        hidden,
        bricks,
        arrived,
        state,
        fractions,
        owner_rows,
        owner_table,
        brick_of_slot,
        sems,
        group_sems,
    ) = refs
    z_index = lax.axis_index("gz")
    g = lax.axis_index("gy")
    c = lax.axis_index("col")
    window = columns + BX
    lanes = 2 * columns + BX
    brick_rows = HALF // BY
    brick_columns = columns // BX
    brick_count = rows // BY * brick_columns
    capacity = slots // count_gz
    single = segment == count_gz
    first_tile = z_index if few > 1 else 0
    size = depth * BY

    def tile_rows(i, start, size):
        if not isinstance(start, int):
            start = pl.multiple_of(start, TILE)
        if few > 1:
            return tiles[i][pl.ds(start, size), :]
        return tiles[0][i, pl.ds(start, size), :]

    def read_owners(i):
        row = tile_rows(i, brick_columns * depth * rows, TILE)
        owner_rows[i] = row.astype(jnp.float32)[0:8].astype(jnp.int32)

    if few > 1:
        for i in range(count_gz):
            read_owners(i)
    else:
        pl.loop(0, count_gz)(read_owners)
    table_copy = pltpu.make_async_copy(owner_rows, owner_table, sems.at[0])
    table_copy.start()

    def arrange(left, right, other):
        lane = lax.broadcasted_iota(jnp.int32, other.shape, 1)
        near = jnp.where(c == 0, 0, BX - 2)
        other = jnp.where((lane >= near) & (lane < near + 2), other, 0.0).astype(other.dtype)
        return jnp.concatenate([left, right, other], axis=1)

    for k, pair in enumerate((top_refs, bottom_refs)):
        exists = (g > 0) if k == 0 else (g < count_gy - 1)
        own, other = pair[0][...].astype(jnp.float32), pair[1][...].astype(jnp.float32)
        values = arrange(own[:, 0:BX], own[:, BX:columns], other)
        edge_rows[k] = values * exists.astype(jnp.float32)

    def moved(values):
        return pltpu.roll(values, 1, 1), values, pltpu.roll(values, window - 1, 1)

    def shared(upper, lower):
        lane = lax.broadcasted_iota(jnp.int32, upper.shape, 1)
        start, stop = upper_lanes(0)
        return jnp.where(
            (lane >= start) & (lane < stop), upper, pltpu.roll(lower, BX // 2, 1)
        )

    def keep(slot, rows_at, upper, lower):
        parts = (upper[:, 0:columns], lower[:, 0:columns])
        for h, part in enumerate(parts):
            shifted[slot, rows_at, h * columns : (h + 1) * columns] = part.astype(jnp.bfloat16)
        part = shared(upper[:, columns:], lower[:, columns:])
        shifted[slot, rows_at, 2 * columns : lanes] = part.astype(jnp.bfloat16)

    def edge_pair(k, at):
        if isinstance(at, int):
            return edge_rows[k, at : at + 2, :]
        group = edge_rows[k, pl.ds(pl.multiple_of(at // 8 * 8, 8), 8), :]
        return pltpu.roll(group, lax.rem(8 - at % 8, 8), 0)[0:2]

    def shifts(i, zz, slot, valid):
        z = i * depth + zz
        halves = []
        for h in range(2):
            at = zz * rows + h * HALF
            own = [tile_rows(i, k * depth * rows + at, HALF) for k in range(2)]
            at = z * rows + h * HALF
            if not isinstance(at, int):
                at = pl.multiple_of(at, TILE)
            values = arrange(*own, x_ref[pl.ds(at, HALF), :]).astype(jnp.float32)
            halves.append(values if valid is None else values * valid)
        top, bottom = edge_pair(0, 2 * z), edge_pair(1, 2 * z)
        if valid is not None:
            top, bottom = top * valid, bottom * valid
        seams = [
            jnp.concatenate([top, halves[1][0:2]], axis=0),
            jnp.concatenate([halves[0][HALF - 2 :], bottom], axis=0),
        ]
        for dx, (upper, lower) in enumerate(zip(moved(halves[0]), moved(halves[1]))):
            keep(slot, slice(dx * HALF, (dx + 1) * HALF), upper, lower)
        rest = jnp.zeros((4, window), jnp.float32)
        upper, lower = [jnp.concatenate([*moved(seam), rest], axis=0) for seam in seams]
        keep(slot, slice(3 * HALF, PART), upper, lower)

    def first(z, valid):
        total = jnp.dot(
            t1_ref[...],
            shifted[pl.ds(z + 1, 3)].reshape(3 * PART, lanes),
            preferred_element_type=jnp.float32,
        )
        values = jnp.maximum(total + bias_ref[...], 0.0)
        if valid is not None:
            values = values * valid
        hidden[z + 1] = values.astype(jnp.bfloat16)

    height = 2 * HALF
    lane = lax.broadcasted_iota(jnp.int32, (height, columns), 1)

    def second(z, t, zz):
        total = jnp.dot(
            t2_ref[...],
            hidden[pl.ds(z, 3)].reshape(3 * TALL, lanes),
            preferred_element_type=jnp.float32,
        )
        before = jnp.where(c == 0, 0.0, total[0:height, 2 * columns :])
        after = jnp.where(c == 0, total[2 * height :, 2 * columns :], 0.0)
        for h in range(2):
            at = slice(h * columns, (h + 1) * columns)
            left = pltpu.roll(before, 1 + h * BX // 2, 1)
            left = jnp.concatenate([left] * brick_columns, axis=1)
            left = jnp.where(lane == 0, left, pltpu.roll(total[0:height, at], 1, 1))
            right = pltpu.roll(after, BX - 1 - h * BX // 2, 1)
            right = jnp.concatenate([right] * brick_columns, axis=1)
            right = jnp.where(
                lane == columns - 1,
                right,
                pltpu.roll(total[2 * height :, at], columns - 1, 1),
            )
            own = total[height : 2 * height, at] + bias2_ref[...] + (left + right)
            values = 0.5 + 0.5 * jnp.tanh(0.5 * own)
            values = values.astype(jnp.bfloat16).astype(jnp.float32)
            for yb in range(brick_rows):
                for xb in range(brick_columns):
                    b = (h * brick_rows + yb) * brick_columns + xb
                    bricks[t, b, zz] = values[yb * 8 : yb * 8 + 8, xb * BX : (xb + 1) * BX]

    def valid_slice(z):
        return ((z >= 0) & (z < count_gz * depth)).astype(jnp.float32)

    depths = segment * depth
    if single:
        shifted[1] = jnp.zeros((PART, lanes), jnp.bfloat16)
        shifted[depths + 2] = jnp.zeros((PART, lanes), jnp.bfloat16)
        hidden[0] = jnp.zeros((TALL, lanes), jnp.bfloat16)
        hidden[depths + 1] = jnp.zeros((TALL, lanes), jnp.bfloat16)
        for i in range(count_gz):
            tile = lax.rem(first_tile + i, count_gz)
            for zz in range(depth):
                shifts(i, zz, tile * depth + zz + 2, None)

        @pl.loop(0, depths, unroll=4)
        def _(z):
            first(z, None)

        @pl.loop(0, depths, unroll=4)
        def _(z):
            second(z, z // depth, z % depth)

    else:

        @pl.loop(0, count_gz // segment)
        def _(q):
            @pl.loop(-2, depths + 2)
            def _(z):
                at = q * depths + z
                inside = jnp.clip(at, 0, count_gz * depth - 1)
                shifts(inside // depth, inside % depth, z + 2, valid_slice(at))

            @pl.loop(-1, depths + 1)
            def _(z):
                first(z, valid_slice(q * depths + z))

            @pl.loop(0, depths)
            def _(z):
                second(z, q * segment + z // depth, z % depth)

    for zz in range(depth):
        for xb in range(brick_columns):
            own = [
                bricks[z_index, yb * brick_columns + xb, zz] for yb in range(rows // BY)
            ]
            for o in range(2):
                values = jnp.concatenate([v[o * BY : o * BY + BY] for v in own], axis=0)
                fractions[o, zz, :, xb * BX : (xb + 1) * BX] = values.astype(jnp.bfloat16)
    fractions_copy = pltpu.make_async_copy(fractions, fractions_ref, sems.at[1])
    fractions_copy.start()

    table_copy.wait()
    for j in range(slots):
        brick_of_slot[j] = -1

    @pl.loop(0, count_gz)
    def _(i):
        first = lax.rem(first_tile + i, count_gz) * capacity
        rank = jnp.int32(0)
        for b in range(brick_count):
            mine = owner_table[i, 0, b] == z_index
            brick_of_slot[jnp.where(mine, first + rank, slots)] = b
            rank = rank + mine.astype(jnp.int32)

    @pl.loop(0, slots, unroll=8)
    def _(j):
        brick = brick_of_slot[j]
        values = bricks[j // capacity, jnp.maximum(brick, 0)]
        values = jnp.where(brick >= 0, values, 0.0)
        at = pl.multiple_of(j * (2 * size), 8)
        arrived[pl.ds(at, 2 * size), :] = values.reshape(2 * size, BX)

    def next_copy(group):
        at = pl.ds(pl.multiple_of(group * 16 * size, 16 * size), 16 * size)
        return pltpu.make_async_copy(state.at[at], next_ref.at[at], group_sems.at[group])

    @pl.loop(0, slots // 8)
    def _(group):
        grid = [(z, y) for z in range(depth) for y in range(BY)]

        def load(ref):
            base = group * (8 * size)
            return [
                [
                    ref[pl.ds(pl.multiple_of(base + (z * BY + y) * 8, 8), 8), :]
                    for y in range(BY)
                ]
                for z in range(depth)
            ]

        def rows_of(offset):
            return pl.ds(group * 16 * size + offset, 8, stride=2 * size)

        quarter = load(quarter_ref)
        pore = [[arrived[rows_of(z * 8 + y), :] for y in range(BY)] for z in range(depth)]
        organic = [
            [0.3 * arrived[rows_of(z * 8 + BY + y), :] for y in range(BY)] for z in range(depth)
        ]
        slow = [[0.12 * p for p in row] for row in pore]
        fast = [[0.16 * p for p in row] for row in pore]
        carbon, oxygen = load(carbon_ref), load(oxygen_ref)
        around = load(carbon_around_ref), load(oxygen_around_ref)
        for z, y in grid:
            carbon[z][y] += slow[z][y] * around[0][z][y] + organic[z][y]
            oxygen[z][y] += fast[z][y] * around[1][z][y]
        for _ in range(STEPS - 1):
            carbon_new = [[None] * BY for _ in range(depth)]
            oxygen_new = [[None] * BY for _ in range(depth)]
            for z, y in grid:
                doc, oxy = carbon[z][y], oxygen[z][y]
                uptake = uptake_of(quarter[z][y], doc, oxy)
                gain = organic[z][y] - uptake
                carbon_new[z][y] = doc + slow[z][y] * laplace(carbon, z, y) + gain
                oxygen_new[z][y] = oxy + fast[z][y] * laplace(oxygen, z, y) - uptake
            carbon, oxygen = carbon_new, oxygen_new
        for z, y in grid:
            state[rows_of(z * BY + y), :] = carbon[z][y]
            state[rows_of(size + z * BY + y), :] = oxygen[z][y]
        next_copy(group).start()

    @pl.loop(0, slots // 8)
    def _(group):
        next_copy(group).wait()

    fractions_copy.wait()


def per_device(
    sizes, density, first_kernel, first_bias, second_kernel, second_bias, owners, solutes, biomass
):
    count_gz, count_gy, count_col = sizes
    depth, rows, columns = density.shape
    slots = solutes.shape[3]
    window = columns + BX
    lanes = 2 * columns + BX
    segment = min(count_gz, 4)
    brick_count = (rows // BY) * (columns // BX)
    height = depth * rows
    depths = count_gz * depth
    bf16, f32 = jnp.bfloat16, jnp.float32
    shape = jax.ShapeDtypeStruct

    payload = pl.pallas_call(
        pack_kernel,
        out_shape=shape((columns // BX * height + TILE, BX), bf16),
        in_specs=[HBM, HBM],
        out_specs=VMEM,
        scratch_shapes=[
            pltpu.VMEM((1, brick_count), jnp.int32),
            pltpu.SemaphoreType.DMA((columns // BX + 1,)),
        ],
        compiler_params=pltpu.CompilerParams(vmem_limit_bytes=4 * 2**20),
        name="pack",
    )(in_hbm(density.reshape(height, columns)), in_hbm(owners.reshape(1, brick_count)))

    few = count_gz if count_gz == segment else 1
    if few > 1:
        tiles = [payload] + [
            lax.ppermute(payload, "gz", [((i + s) % count_gz, i) for i in range(count_gz)])
            for s in range(1, count_gz)
        ]
    else:
        tiles = [lax.all_gather(payload, "gz", axis=0, tiled=False)]

    cells = depth * BY
    prepared = pl.pallas_call(
        functools.partial(prepare_kernel, (depth, slots)),
        out_shape=[shape((slots * cells, BX), f32)] * 5,
        in_specs=[HBM, HBM, ANY],
        out_specs=[VMEM] * 5,
        scratch_shapes=[
            pltpu.VMEM((slots * 2 * cells, BX), f32),
            pltpu.VMEM((slots * cells, BX), bf16),
            pltpu.VMEM((slots * cells, BX), f32),
            pltpu.SemaphoreType.DMA((slots // 8, 2)),
        ],
        compiler_params=pltpu.CompilerParams(vmem_limit_bytes=12 * 2**20),
        cost_estimate=pl.CostEstimate(
            flops=60 * slots * cells * BX, bytes_accessed=2**20, transcendentals=0
        ),
        name="prepare",
    )(
        in_hbm(solutes.reshape(slots * 2 * cells, BX)),
        in_hbm(biomass.reshape(slots * cells, BX)),
        payload,
    )
    t1, bias, t2, bias2 = pl.pallas_call(
        functools.partial(banded_kernel, (columns, count_gy)),
        out_shape=(
            shape((TALL, 3 * PART), bf16),
            shape((TALL, lanes), f32),
            shape((6 * HALF, 3 * TALL), bf16),
            shape((2 * HALF, columns), f32),
        ),
        in_specs=[HBM, HBM, HBM, HBM, ANY],
        out_specs=(VMEM, VMEM, VMEM, VMEM),
        scratch_shapes=[
            pltpu.VMEM((CHANNELS, 27), bf16),
            pltpu.SMEM((CHANNELS,), f32),
            pltpu.VMEM((2 * CHANNELS, 27), bf16),
            pltpu.SMEM((2,), f32),
            pltpu.SemaphoreType.DMA((4,)),
        ],
        compiler_params=pltpu.CompilerParams(vmem_limit_bytes=16 * 2**20),
        cost_estimate=pl.CostEstimate(
            flops=20 * 2**20, bytes_accessed=4 * 2**20, transcendentals=0
        ),
        name="banded",
    )(
        in_hbm(first_kernel.transpose(2, 1, 0).reshape(CHANNELS, 27)),
        in_hbm(first_bias),
        in_hbm(second_kernel.transpose(1, 2, 0).reshape(2 * CHANNELS, 27)),
        in_hbm(second_bias),
        payload,
    )

    if count_gy == 2:
        ways = [[(0, 1), (1, 0)]]
    else:
        up = [(i, i + 1) for i in range(count_gy - 1)]
        ways = [up, [(j, i) for i, j in up]]
    directions = len(ways)
    swap = [(0, 1), (1, 0)]
    near, *sent = pl.pallas_call(
        functools.partial(edges_kernel, (count_gy, depth, rows, columns, few, count_gz)),
        out_shape=[shape((depths * rows, BX), bf16)]
        + [shape((2 * depths, columns), bf16)] * directions,
        in_specs=[VMEM] * few + [ANY, ANY],
        out_specs=[VMEM] * (1 + directions),
        compiler_params=pltpu.CompilerParams(vmem_limit_bytes=16 * 2**20),
        name="edges",
    )(*tiles, bias2, prepared[-1])
    edges = []
    for pairs, edge in zip(ways, sent):
        edge = lax.ppermute(edge, "gy", pairs)
        corner = pl.pallas_call(
            corner_kernel,
            out_shape=shape((2 * depths, BX), bf16),
            in_specs=[VMEM],
            out_specs=VMEM,
            compiler_params=pltpu.CompilerParams(vmem_limit_bytes=4 * 2**20),
            name="corner",
        )(edge)
        edges += [edge, lax.ppermute(corner, "col", swap)]
    near = lax.ppermute(near, "col", swap)

    fractions, solutes_next = pl.pallas_call(
        functools.partial(
            column_kernel,
            (count_gz, count_gy, depth, rows, columns, segment, slots, directions),
            few,
        ),
        out_shape=(
            shape((2, depth, rows, columns), bf16),
            shape((slots * 2 * cells, BX), f32),
        ),
        in_specs=[VMEM] * (few + 1 + len(edges) + 9),
        out_specs=(HBM, HBM),
        scratch_shapes=[
            pltpu.VMEM((2, 2 * depths, window), f32),
            pltpu.VMEM((segment * depth + 4, PART, lanes), bf16),
            pltpu.VMEM((segment * depth + 2, TALL, lanes), bf16),
            pltpu.VMEM((count_gz, brick_count, depth, 8, BX), f32),
            pltpu.VMEM((slots * 2 * cells, BX), f32),
            pltpu.VMEM((slots * 2 * cells, BX), f32),
            pltpu.VMEM((2, depth, rows, columns), bf16),
            pltpu.VMEM((count_gz, 8, BX), jnp.int32),
            pltpu.SMEM((count_gz, 8, BX), jnp.int32),
            pltpu.SMEM((slots + 1,), jnp.int32),
            pltpu.SemaphoreType.DMA((2,)),
            pltpu.SemaphoreType.DMA((slots // 8,)),
        ],
        compiler_params=pltpu.CompilerParams(vmem_limit_bytes=40 * 2**20),
        cost_estimate=pl.CostEstimate(
            flops=2 * depths * lanes * TALL * (3 * PART + 3 * 6 * HALF),
            bytes_accessed=4 * 2**20,
            transcendentals=0,
        ),
        name="column",
    )(
        *tiles,
        near,
        *edges,
        t1,
        bias,
        t2,
        bias2,
        *prepared,
    )
    return fractions, solutes_next.reshape(solutes.shape)


def solution(mesh):
    sizes = (mesh.shape["gz"], mesh.shape["gy"], mesh.shape["col"])
    assert sizes[2] == 2
    return jax.shard_map(
        functools.partial(per_device, sizes),
        mesh=mesh,
        in_specs=(
            P(("cores", "gz"), "gy", "col"),
            P(),
            P(),
            P(),
            P(),
            P(("cores", "gz"), "gy", "col", None, None),
            P(("cores", "gz"), "gy", "col", None, None, None, None, None),
            P(("cores", "gz"), "gy", "col", None, None, None, None),
        ),
        out_specs=(
            P(None, ("cores", "gz"), "gy", "col"),
            P(("cores", "gz"), "gy", "col", None, None, None, None, None),
        ),
        check_vma=False,
    )
```

```python
import functools

import jax
import jax.numpy as jnp
from jax import lax
from jax.experimental import pallas as pl
from jax.experimental.pallas import tpu as pltpu
from jax.sharding import PartitionSpec as P

BY = 4
BX = 128
STEPS = 4
TILE = 16
HALF = 16
CHANNELS = 8
REACH = HALF + 2
PART = 3 * HALF + TILE
TALL = REACH * CHANNELS
OUTSIDE = -3e38

VMEM = pl.BlockSpec(memory_space=pltpu.VMEM)
SMEM = pl.BlockSpec(memory_space=pltpu.SMEM)
ANY = pl.BlockSpec(memory_space=pl.ANY)
HBM = pl.BlockSpec(memory_space=pltpu.HBM)


def in_hbm(array):
    return pltpu.with_memory_space_constraint(array, pltpu.HBM)


def step_index(values, width, count):
    index = jnp.zeros(values.shape, jnp.int32)
    for k in range(1, count):
        index = index + (values >= k * width).astype(jnp.int32)
    return index


def one_hot(condition):
    return jnp.where(condition, 1.0, 0.0).astype(jnp.bfloat16)


def iotas(shape):
    return (
        lax.broadcasted_iota(jnp.int32, shape, 0),
        lax.broadcasted_iota(jnp.int32, shape, 1),
    )


def tap_parts(tap):
    dz = step_index(tap, 9, 3)
    dy = step_index(tap - 9 * dz, 3, 3)
    return dz, dy, tap - 9 * dz - 3 * dy


def pack_kernel(density_ref, owners_ref, payload_ref, named_ref, sems):
    height, columns = density_ref.shape
    blocks = columns // BX
    copies = [pltpu.make_async_copy(owners_ref, named_ref, sems.at[blocks])]
    for k in range(blocks):
        copies.append(
            pltpu.make_async_copy(
                density_ref.at[:, k * BX : (k + 1) * BX],
                payload_ref.at[k * height : (k + 1) * height],
                sems.at[k],
            )
        )
    for copy in copies:
        copy.start()
    copies[0].wait()
    named = named_ref[...].astype(jnp.float32)
    count = named.shape[1]
    payload_ref[blocks * height : blocks * height + TILE, :] = jnp.concatenate(
        [
            jnp.broadcast_to(named, (TILE, count)),
            jnp.zeros((TILE, BX - count), jnp.float32),
        ],
        axis=1,
    ).astype(jnp.bfloat16)
    for copy in copies[1:]:
        copy.wait()


def banded_kernel(dims, *refs):
    window, count_gy = dims
    sources, refs = refs[:4], refs[5:]
    t1_ref, bias_ref, t2_ref, bias2_ref, *local, sems = refs
    copies = [
        pltpu.make_async_copy(source, target, sems.at[k])
        for k, (source, target) in enumerate(zip(sources, local))
    ]
    for copy in copies:
        copy.start()
    for copy in copies:
        copy.wait()
    w1_ref, b1_ref, w2_ref, b2_ref = local
    g = lax.axis_index("gy")
    row, channel = iotas((TALL, CHANNELS))
    spread = one_hot((row & (CHANNELS - 1)) == channel)
    w1 = jnp.dot(spread, w1_ref[...], preferred_element_type=jnp.float32).astype(jnp.bfloat16)
    tap, column = iotas((27, 4 * PART))
    dz = column >> 6
    place = column & (PART - 1)
    dx = jnp.where(place < 3 * HALF, place >> 4, (place - 3 * HALF) >> 2)
    base = 9 * dz + dx
    row, column = iotas((TALL, 4 * PART))
    place = column & (PART - 1)
    seam = (place - 3 * HALF) & 3
    seam_row = jnp.where(seam < 2, seam - 2, seam + HALF - 2)
    input_row = jnp.where(place < 3 * HALF, place & (HALF - 1), seam_row)
    distance = jnp.where(place < 3 * HALF + 12, input_row - (row >> 3) + 2, -1)
    for out in range(2):
        total = jnp.zeros((TALL, 4 * PART), jnp.float32)
        for dy in range(3):
            pick = one_hot(tap == base - 9 * out + 3 * dy)
            values = jnp.dot(w1, pick, preferred_element_type=jnp.float32)
            total = jnp.where(distance == dy, values, total)
        t1_ref[out * TALL : (out + 1) * TALL, :] = total.astype(jnp.bfloat16)
    row, column = iotas((TALL, 2 * window))
    bias = jnp.zeros((TALL, 2 * window), jnp.float32)
    for k in range(CHANNELS):
        bias = jnp.where((row & (CHANNELS - 1)) == k, b1_ref[k], bias)
    outside = ((row < CHANNELS) & (column < window) & (g == 0)) | (
        (row >= TALL - CHANNELS) & (column >= window) & (g == count_gy - 1)
    )
    bias_ref[...] = jnp.where(outside, OUTSIDE, bias)
    channel, column = iotas((CHANNELS, 4 * TALL))
    spread = one_hot((column & (CHANNELS - 1)) == channel)
    tap, column = iotas((27, 4 * TALL))
    tap_z, slice_z = tap_parts(tap)[0], step_index(column, TALL, 4)
    row, tap = iotas((6 * HALF, 27))
    _, tap_y, tap_x = tap_parts(tap)
    same_x = (row >> 5) == tap_x
    wide = [
        lax.dot_general(
            w2_ref[o * CHANNELS : (o + 1) * CHANNELS, :],
            spread,
            (((0,), (0,)), ((), ())),
            preferred_element_type=jnp.float32,
        )
        for o in range(2)
    ]
    picks = [
        [one_hot(same_x & (tap_y == dy) & (((row >> 2) & 1) == o)) for o in range(2)]
        for dy in range(3)
    ]
    out_row, column = iotas((6 * HALF, 4 * TALL))
    y = ((out_row >> 3) & 3) * BY + (out_row & 3)
    distance = ((column - TALL * step_index(column, TALL, 4)) >> 3) - y
    for out in range(2):
        same_z = tap_z == slice_z - out
        terms = [jnp.where(same_z, values, 0.0).astype(jnp.bfloat16) for values in wide]
        total = jnp.zeros((6 * HALF, 4 * TALL), jnp.float32)
        for dy in range(3):
            values = 0.0
            for o in range(2):
                values = values + jnp.dot(
                    picks[dy][o], terms[o], preferred_element_type=jnp.float32
                )
            total = jnp.where(distance == dy, values, total)
        t2_ref[out * 6 * HALF : (out + 1) * 6 * HALF, :] = total.astype(jnp.bfloat16)
    row, _ = iotas((2 * HALF, 2 * window))
    bias2_ref[...] = jnp.where(((row >> 2) & 1) == 0, b2_ref[0], b2_ref[1])


def edges_kernel(dims, *refs):
    count_gy, depth, rows, columns, few, count = dims
    tiles, outs = refs[:few], refs[few + 1 :]
    g = lax.axis_index("gy")
    c = lax.axis_index("col")
    height = depth * rows
    block = (1 - c) * height

    def take(i, start, size):
        start = pl.ds(pl.multiple_of(start, TILE), size)
        if few > 1:
            return tiles[i][start, :]
        return tiles[0][i, start, :]

    def pair(i):
        for k in range(2):
            at = pl.multiple_of((2 * i + k) * height, TILE)
            outs[0][pl.ds(at, height), :] = take(2 * i + k, block, height)
        low, high = [], []
        for k in range(2):
            for zz in range(depth):
                first, last = [], []
                for base in (0, height):
                    at = base + zz * rows
                    first.append(take(2 * i + k, at, TILE).astype(jnp.float32)[0:2])
                    at = at + rows - TILE
                    last.append(take(2 * i + k, at, TILE).astype(jnp.float32)[TILE - 2 :])
                low.append(jnp.concatenate(first, axis=1))
                high.append(jnp.concatenate(last, axis=1))
        at = pl.multiple_of(2 * i * 2 * depth, TILE)
        first, last = jnp.concatenate(low, axis=0), jnp.concatenate(high, axis=0)
        sends = [jnp.where(g == 0, last, first)] if count_gy == 2 else [last, first]
        for n, send in enumerate(sends):
            send = send.astype(jnp.bfloat16)
            outs[1 + n][pl.ds(at, TILE), :] = send

    if few > 1:
        for i in range(count // 2):
            pair(i)
    else:
        pl.loop(0, count // 2)(pair)


def corner_kernel(edge_ref, _, corner_ref):
    c = lax.axis_index("col")
    corner_ref[...] = jnp.where(c == 0, edge_ref[:, BX:], edge_ref[:, 0:BX])


def laplace(field, z, y):
    centre = field[z][y]
    last = lax.broadcasted_iota(jnp.int32, centre.shape, 1) == BX - 1
    ahead = jnp.where(last, 0.0, pltpu.roll(centre, BX - 1, 1) - centre)
    result = ahead - pltpu.roll(ahead, 1, 1)
    beside = [
        field[zz][yy]
        for zz, yy in ((z - 1, y), (z + 1, y), (z, y - 1), (z, y + 1))
        if 0 <= zz < len(field) and 0 <= yy < BY
    ]
    return result + (functools.reduce(jnp.add, beside) - float(len(beside)) * centre)


def uptake_of(quarter, doc, oxy):
    return quarter * doc * oxy / ((0.5 + jnp.abs(doc)) * (0.3 + jnp.abs(oxy)))


def prepare_kernel(dims, solutes_ref, biomass_ref, _, *refs):
    depth, slots = dims
    outs, (state, biomass, mass, sems) = refs[:5], refs[5:]
    size = depth * BY
    copies = []
    for group in range(slots // 8):
        for k, (source, target) in enumerate(((solutes_ref, state), (biomass_ref, biomass))):
            rows = (2 - k) * 8 * size
            at = pl.ds(group * rows, rows)
            copies.append(
                pltpu.make_async_copy(source.at[at], target.at[at], sems.at[group, k])
            )
    for copy in copies:
        copy.start()
    for group in range(slots // 8):
        copies[2 * group].wait()
        copies[2 * group + 1].wait()
        at = slice(group * 8 * size, (group + 1) * 8 * size)
        mass[at, :] = biomass[at, :].astype(jnp.float32)

        def rows_of(pitch, offset):
            return pl.ds(group * 8 * pitch + offset, 8, stride=pitch)

        grid = [(z, y) for z in range(depth) for y in range(BY)]
        carbon, oxygen = [
            [
                [state[rows_of(2 * size, k * size + z * BY + y), :] for y in range(BY)]
                for z in range(depth)
            ]
            for k in range(2)
        ]
        for z, y in grid:
            at = group * 8 * size + (z * BY + y) * 8
            at = slice(at, at + 8)
            doc, oxy = carbon[z][y], oxygen[z][y]
            quarter = 0.25 * mass[rows_of(size, z * BY + y), :]
            uptake = uptake_of(quarter, doc, oxy)
            values = (
                doc - uptake,
                oxy - uptake,
                laplace(carbon, z, y),
                laplace(oxygen, z, y),
                quarter,
            )
            for out, value in zip(outs, values):
                out[at, :] = value


def column_kernel(dims, few, *refs):
    count_gz, count_gy, depth, rows, columns, segment, slots, directions = dims
    tiles, refs = refs[:few], refs[few:]
    x_ref, refs = refs[0], refs[1:]
    top_refs, refs = refs[:2], refs[2:]
    if directions == 1:
        bottom_refs = top_refs
    else:
        bottom_refs, refs = refs[:2], refs[2:]
    t1_ref, bias_ref, t2_ref, bias2_ref, *refs = refs
    carbon_ref, oxygen_ref, carbon_around_ref, oxygen_around_ref, quarter_ref, *refs = refs
    fractions_ref, next_ref, *refs = refs
    (
        edge_rows,
        shifted,
        hidden,
        bricks,
        arrived,
        state,
        fractions,
        owner_rows,
        owner_table,
        brick_of_slot,
        sems,
        group_sems,
    ) = refs
    z_index = lax.axis_index("gz")
    g = lax.axis_index("gy")
    c = lax.axis_index("col")
    window = columns + BX
    brick_rows = HALF // BY
    brick_columns = columns // BX
    brick_count = rows // BY * brick_columns
    capacity = slots // count_gz
    single = segment == count_gz
    first_tile = z_index if few > 1 else 0
    size = depth * BY

    def tile_rows(i, start, size):
        if not isinstance(start, int):
            start = pl.multiple_of(start, TILE)
        if few > 1:
            return tiles[i][pl.ds(start, size), :]
        return tiles[0][i, pl.ds(start, size), :]

    def read_owners(i):
        row = tile_rows(i, brick_columns * depth * rows, TILE)
        owner_rows[i] = row.astype(jnp.float32)[0:8].astype(jnp.int32)

    if few > 1:
        for i in range(count_gz):
            read_owners(i)
    else:
        pl.loop(0, count_gz)(read_owners)
    table_copy = pltpu.make_async_copy(owner_rows, owner_table, sems.at[0])
    table_copy.start()

    def arrange(left, right, other):
        return jnp.concatenate(
            [
                jnp.where(c == 0, left, other),
                jnp.where(c == 0, right, left),
                jnp.where(c == 0, other, right),
            ],
            axis=1,
        )

    for k, pair in enumerate((top_refs, bottom_refs)):
        exists = (g > 0) if k == 0 else (g < count_gy - 1)
        own, other = pair[0][...].astype(jnp.float32), pair[1][...].astype(jnp.float32)
        values = arrange(own[:, 0:BX], own[:, BX:columns], other)
        edge_rows[k] = values * exists.astype(jnp.float32)

    def moved(values):
        lane = lax.broadcasted_iota(jnp.int32, values.shape, 1)
        left = jnp.where(lane == 0, 0.0, pltpu.roll(values, 1, 1))
        right = jnp.where(lane == window - 1, 0.0, pltpu.roll(values, window - 1, 1))
        return left.astype(values.dtype), values, right.astype(values.dtype)

    def edge_pair(k, at):
        if isinstance(at, int):
            return edge_rows[k, at : at + 2, :]
        group = edge_rows[k, pl.ds(pl.multiple_of(at // 8 * 8, 8), 8), :]
        return pltpu.roll(group, lax.rem(8 - at % 8, 8), 0)[0:2]

    def shifts(i, zz, slot, valid):
        z = i * depth + zz
        halves = []
        for h in range(2):
            at = zz * rows + h * HALF
            own = [tile_rows(i, k * depth * rows + at, HALF) for k in range(2)]
            at = z * rows + h * HALF
            if not isinstance(at, int):
                at = pl.multiple_of(at, TILE)
            values = arrange(*own, x_ref[pl.ds(at, HALF), :]).astype(jnp.float32)
            halves.append(values if valid is None else values * valid)
        top, bottom = edge_pair(0, 2 * z), edge_pair(1, 2 * z)
        if valid is not None:
            top, bottom = top * valid, bottom * valid
        seams = [
            jnp.concatenate([top, halves[1][0:2]], axis=0),
            jnp.concatenate([halves[0][HALF - 2 :], bottom], axis=0),
        ]
        for h in range(2):
            lanes = slice(h * window, (h + 1) * window)
            for dx, values in enumerate(moved(halves[h])):
                shifted[slot, dx * HALF : (dx + 1) * HALF, lanes] = values.astype(jnp.bfloat16)
            values = jnp.concatenate(
                [*moved(seams[h]), jnp.zeros((4, window), jnp.float32)], axis=0
            )
            shifted[slot, 3 * HALF : PART, lanes] = values.astype(jnp.bfloat16)

    def first(z, valid):
        total = jnp.dot(
            t1_ref[...],
            shifted[pl.ds(z + 1, 4)].reshape(4 * PART, 2 * window),
            preferred_element_type=jnp.float32,
        )
        for out in range(2):
            values = jnp.maximum(total[out * TALL : (out + 1) * TALL] + bias_ref[...], 0.0)
            if valid is not None:
                values = values * valid(z + out)
            hidden[z + 1 + out] = values.astype(jnp.bfloat16)

    height = 2 * HALF
    lane = lax.broadcasted_iota(jnp.int32, (height, 2 * window), 1)
    left_edge = (lane == 0) | (lane == window)
    right_edge = (lane == window - 1) | (lane == 2 * window - 1)

    def second(z, tile):
        total = jnp.dot(
            t2_ref[...],
            hidden[pl.ds(z, 4)].reshape(4 * TALL, 2 * window),
            preferred_element_type=jnp.float32,
        )
        for out in range(2):
            at = z + out
            place(total[3 * height * out : 3 * height * (out + 1)], tile + at // depth, at % depth)

    def place(total, t, zz):
        before = pltpu.roll(total[0:height], 1, 1)
        after = pltpu.roll(total[2 * height :], 2 * window - 1, 1)
        total = total[height : 2 * height] + bias2_ref[...]
        total = total + jnp.where(left_edge, 0.0, before)
        total = total + jnp.where(right_edge, 0.0, after)
        for h in range(2):
            at = h * window
            own = jnp.where(
                c == 0, total[:, at : at + columns], total[:, at + BX : at + window]
            )
            values = 0.5 + 0.5 * jnp.tanh(0.5 * own)
            values = values.astype(jnp.bfloat16).astype(jnp.float32)
            for yb in range(brick_rows):
                for xb in range(brick_columns):
                    b = (h * brick_rows + yb) * brick_columns + xb
                    bricks[t, b, zz] = values[yb * 8 : yb * 8 + 8, xb * BX : (xb + 1) * BX]

    def valid_slice(z):
        return ((z >= 0) & (z < count_gz * depth)).astype(jnp.float32)

    depths = segment * depth
    if single:
        shifted[1] = jnp.zeros((PART, 2 * window), jnp.bfloat16)
        shifted[depths + 2] = jnp.zeros((PART, 2 * window), jnp.bfloat16)
        hidden[0] = jnp.zeros((TALL, 2 * window), jnp.bfloat16)
        hidden[depths + 1] = jnp.zeros((TALL, 2 * window), jnp.bfloat16)
        for i in range(count_gz):
            tile = lax.rem(first_tile + i, count_gz)
            for zz in range(depth):
                shifts(i, zz, tile * depth + zz + 2, None)

        @pl.loop(0, depths // 2, unroll=2)
        def _(k):
            first(2 * k, None)

        @pl.loop(0, depths // 2, unroll=2)
        def _(k):
            second(2 * k, 0)

    else:

        @pl.loop(0, count_gz // segment)
        def _(q):
            @pl.loop(-2, depths + 2)
            def _(z):
                at = q * depths + z
                inside = jnp.clip(at, 0, count_gz * depth - 1)
                shifts(inside // depth, inside % depth, z + 2, valid_slice(at))

            @pl.loop(0, depths // 2 + 1)
            def _(k):
                first(2 * k - 1, lambda z: valid_slice(q * depths + z))

            @pl.loop(0, depths // 2)
            def _(k):
                second(2 * k, q * segment)

    for zz in range(depth):
        for xb in range(brick_columns):
            own = [
                bricks[z_index, yb * brick_columns + xb, zz] for yb in range(rows // BY)
            ]
            for o in range(2):
                values = jnp.concatenate([v[o * BY : o * BY + BY] for v in own], axis=0)
                fractions[o, zz, :, xb * BX : (xb + 1) * BX] = values.astype(jnp.bfloat16)
    fractions_copy = pltpu.make_async_copy(fractions, fractions_ref, sems.at[1])
    fractions_copy.start()

    table_copy.wait()
    for j in range(slots):
        brick_of_slot[j] = -1

    @pl.loop(0, count_gz)
    def _(i):
        first = lax.rem(first_tile + i, count_gz) * capacity
        rank = jnp.int32(0)
        for b in range(brick_count):
            mine = owner_table[i, 0, b] == z_index
            brick_of_slot[jnp.where(mine, first + rank, slots)] = b
            rank = rank + mine.astype(jnp.int32)

    @pl.loop(0, slots, unroll=8)
    def _(j):
        brick = brick_of_slot[j]
        values = bricks[j // capacity, jnp.maximum(brick, 0)]
        values = jnp.where(brick >= 0, values, 0.0)
        at = pl.multiple_of(j * (2 * size), 8)
        arrived[pl.ds(at, 2 * size), :] = values.reshape(2 * size, BX)

    def next_copy(group):
        at = pl.ds(pl.multiple_of(group * 16 * size, 16 * size), 16 * size)
        return pltpu.make_async_copy(state.at[at], next_ref.at[at], group_sems.at[group])

    @pl.loop(0, slots // 8)
    def _(group):
        grid = [(z, y) for z in range(depth) for y in range(BY)]

        def load(ref):
            base = group * (8 * size)
            return [
                [
                    ref[pl.ds(pl.multiple_of(base + (z * BY + y) * 8, 8), 8), :]
                    for y in range(BY)
                ]
                for z in range(depth)
            ]

        def rows_of(offset):
            return pl.ds(group * 16 * size + offset, 8, stride=2 * size)

        quarter = load(quarter_ref)
        pore = [[arrived[rows_of(z * 8 + y), :] for y in range(BY)] for z in range(depth)]
        organic = [
            [0.3 * arrived[rows_of(z * 8 + BY + y), :] for y in range(BY)] for z in range(depth)
        ]
        slow = [[0.12 * p for p in row] for row in pore]
        fast = [[0.16 * p for p in row] for row in pore]
        carbon, oxygen = load(carbon_ref), load(oxygen_ref)
        around = load(carbon_around_ref), load(oxygen_around_ref)
        for z, y in grid:
            carbon[z][y] += slow[z][y] * around[0][z][y] + organic[z][y]
            oxygen[z][y] += fast[z][y] * around[1][z][y]
        for _ in range(STEPS - 1):
            carbon_new = [[None] * BY for _ in range(depth)]
            oxygen_new = [[None] * BY for _ in range(depth)]
            for z, y in grid:
                doc, oxy = carbon[z][y], oxygen[z][y]
                uptake = uptake_of(quarter[z][y], doc, oxy)
                gain = organic[z][y] - uptake
                carbon_new[z][y] = doc + slow[z][y] * laplace(carbon, z, y) + gain
                oxygen_new[z][y] = oxy + fast[z][y] * laplace(oxygen, z, y) - uptake
            carbon, oxygen = carbon_new, oxygen_new
        for z, y in grid:
            state[rows_of(z * BY + y), :] = carbon[z][y]
            state[rows_of(size + z * BY + y), :] = oxygen[z][y]
        next_copy(group).start()

    @pl.loop(0, slots // 8)
    def _(group):
        next_copy(group).wait()

    fractions_copy.wait()


def per_device(
    sizes, density, first_kernel, first_bias, second_kernel, second_bias, owners, solutes, biomass
):
    count_gz, count_gy, count_col = sizes
    depth, rows, columns = density.shape
    slots = solutes.shape[3]
    window = columns + BX
    segment = min(count_gz, 4)
    brick_count = (rows // BY) * (columns // BX)
    height = depth * rows
    depths = count_gz * depth
    bf16, f32 = jnp.bfloat16, jnp.float32
    shape = jax.ShapeDtypeStruct

    payload = pl.pallas_call(
        pack_kernel,
        out_shape=shape((columns // BX * height + TILE, BX), bf16),
        in_specs=[HBM, HBM],
        out_specs=VMEM,
        scratch_shapes=[
            pltpu.VMEM((1, brick_count), jnp.int32),
            pltpu.SemaphoreType.DMA((columns // BX + 1,)),
        ],
        compiler_params=pltpu.CompilerParams(vmem_limit_bytes=4 * 2**20),
        name="pack",
    )(in_hbm(density.reshape(height, columns)), in_hbm(owners.reshape(1, brick_count)))

    few = count_gz if count_gz == segment else 1
    if few > 1:
        tiles = [payload] + [
            lax.ppermute(payload, "gz", [((i + s) % count_gz, i) for i in range(count_gz)])
            for s in range(1, count_gz)
        ]
    else:
        tiles = [lax.all_gather(payload, "gz", axis=0, tiled=False)]

    cells = depth * BY
    t1, bias, t2, bias2 = pl.pallas_call(
        functools.partial(banded_kernel, (window, count_gy)),
        out_shape=(
            shape((2 * TALL, 4 * PART), bf16),
            shape((TALL, 2 * window), f32),
            shape((12 * HALF, 4 * TALL), bf16),
            shape((2 * HALF, 2 * window), f32),
        ),
        in_specs=[HBM, HBM, HBM, HBM, ANY],
        out_specs=(VMEM, VMEM, VMEM, VMEM),
        scratch_shapes=[
            pltpu.VMEM((CHANNELS, 27), bf16),
            pltpu.SMEM((CHANNELS,), f32),
            pltpu.VMEM((2 * CHANNELS, 27), bf16),
            pltpu.SMEM((2,), f32),
            pltpu.SemaphoreType.DMA((4,)),
        ],
        compiler_params=pltpu.CompilerParams(vmem_limit_bytes=16 * 2**20),
        cost_estimate=pl.CostEstimate(
            flops=20 * 2**20, bytes_accessed=4 * 2**20, transcendentals=0
        ),
        name="banded",
    )(
        in_hbm(first_kernel.transpose(2, 1, 0).reshape(CHANNELS, 27)),
        in_hbm(first_bias),
        in_hbm(second_kernel.transpose(1, 2, 0).reshape(2 * CHANNELS, 27)),
        in_hbm(second_bias),
        payload,
    )

    if count_gy == 2:
        ways = [[(0, 1), (1, 0)]]
    else:
        up = [(i, i + 1) for i in range(count_gy - 1)]
        ways = [up, [(j, i) for i, j in up]]
    directions = len(ways)
    swap = [(0, 1), (1, 0)]
    near, *sent = pl.pallas_call(
        functools.partial(edges_kernel, (count_gy, depth, rows, columns, few, count_gz)),
        out_shape=[shape((depths * rows, BX), bf16)]
        + [shape((2 * depths, columns), bf16)] * directions,
        in_specs=[VMEM] * few + [ANY],
        out_specs=[VMEM] * (1 + directions),
        compiler_params=pltpu.CompilerParams(vmem_limit_bytes=16 * 2**20),
        name="edges",
    )(*tiles, bias2)
    prepared = pl.pallas_call(
        functools.partial(prepare_kernel, (depth, slots)),
        out_shape=[shape((slots * cells, BX), f32)] * 5,
        in_specs=[HBM, HBM, ANY],
        out_specs=[VMEM] * 5,
        scratch_shapes=[
            pltpu.VMEM((slots * 2 * cells, BX), f32),
            pltpu.VMEM((slots * cells, BX), bf16),
            pltpu.VMEM((slots * cells, BX), f32),
            pltpu.SemaphoreType.DMA((slots // 8, 2)),
        ],
        compiler_params=pltpu.CompilerParams(vmem_limit_bytes=12 * 2**20),
        cost_estimate=pl.CostEstimate(
            flops=60 * slots * cells * BX, bytes_accessed=2**20, transcendentals=0
        ),
        name="prepare",
    )(
        in_hbm(solutes.reshape(slots * 2 * cells, BX)),
        in_hbm(biomass.reshape(slots * cells, BX)),
        near,
    )
    edges = []
    for pairs, edge in zip(ways, sent):
        edge = lax.ppermute(edge, "gy", pairs)
        corner = pl.pallas_call(
            corner_kernel,
            out_shape=shape((2 * depths, BX), bf16),
            in_specs=[VMEM, ANY],
            out_specs=VMEM,
            compiler_params=pltpu.CompilerParams(vmem_limit_bytes=4 * 2**20),
            name="corner",
        )(edge, prepared[-1])
        edges += [edge, lax.ppermute(corner, "col", swap)]
    near = lax.ppermute(near, "col", swap)

    fractions, solutes_next = pl.pallas_call(
        functools.partial(
            column_kernel,
            (count_gz, count_gy, depth, rows, columns, segment, slots, directions),
            few,
        ),
        out_shape=(
            shape((2, depth, rows, columns), bf16),
            shape((slots * 2 * cells, BX), f32),
        ),
        in_specs=[VMEM] * (few + 1 + len(edges) + 9),
        out_specs=(HBM, HBM),
        scratch_shapes=[
            pltpu.VMEM((2, 2 * depths, window), f32),
            pltpu.VMEM((segment * depth + 4, PART, 2 * window), bf16),
            pltpu.VMEM((segment * depth + 2, TALL, 2 * window), bf16),
            pltpu.VMEM((count_gz, brick_count, depth, 8, BX), f32),
            pltpu.VMEM((slots * 2 * cells, BX), f32),
            pltpu.VMEM((slots * 2 * cells, BX), f32),
            pltpu.VMEM((2, depth, rows, columns), bf16),
            pltpu.VMEM((count_gz, 8, BX), jnp.int32),
            pltpu.SMEM((count_gz, 8, BX), jnp.int32),
            pltpu.SMEM((slots + 1,), jnp.int32),
            pltpu.SemaphoreType.DMA((2,)),
            pltpu.SemaphoreType.DMA((slots // 8,)),
        ],
        compiler_params=pltpu.CompilerParams(vmem_limit_bytes=40 * 2**20),
        cost_estimate=pl.CostEstimate(
            flops=2 * depths * 2 * window * TALL * (4 * PART + 4 * 6 * HALF),
            bytes_accessed=4 * 2**20,
            transcendentals=0,
        ),
        name="column",
    )(
        *tiles,
        near,
        *edges,
        t1,
        bias,
        t2,
        bias2,
        *prepared,
    )
    return fractions, solutes_next.reshape(solutes.shape)


def solution(mesh):
    sizes = (mesh.shape["gz"], mesh.shape["gy"], mesh.shape["col"])
    assert sizes[2] == 2
    return jax.shard_map(
        functools.partial(per_device, sizes),
        mesh=mesh,
        in_specs=(
            P(("cores", "gz"), "gy", "col"),
            P(),
            P(),
            P(),
            P(),
            P(("cores", "gz"), "gy", "col", None, None),
            P(("cores", "gz"), "gy", "col", None, None, None, None, None),
            P(("cores", "gz"), "gy", "col", None, None, None, None),
        ),
        out_specs=(
            P(None, ("cores", "gz"), "gy", "col"),
            P(("cores", "gz"), "gy", "col", None, None, None, None, None),
        ),
        check_vma=False,
    )
```

```python
import functools

import jax
import jax.numpy as jnp
from jax import lax
from jax.experimental import pallas as pl
from jax.experimental.pallas import tpu as pltpu
from jax.sharding import PartitionSpec as P

BY = 4
BX = 128
STEPS = 4
TILE = 16
HALF = 16
CHANNELS = 8
REACH = HALF + 2
PART = 3 * HALF + TILE
TALL = REACH * CHANNELS
ONE_ROW = 3 * HALF + 12
OUTSIDE = -1e30

VMEM = pl.BlockSpec(memory_space=pltpu.VMEM)
SMEM = pl.BlockSpec(memory_space=pltpu.SMEM)
ANY = pl.BlockSpec(memory_space=pl.ANY)
HBM = pl.BlockSpec(memory_space=pltpu.HBM)


def in_hbm(array):
    return pltpu.with_memory_space_constraint(array, pltpu.HBM)


def step_index(values, width, count):
    index = jnp.zeros(values.shape, jnp.int32)
    for k in range(1, count):
        index = index + (values >= k * width).astype(jnp.int32)
    return index


def one_hot(condition):
    return jnp.where(condition, 1.0, 0.0).astype(jnp.bfloat16)


def iotas(shape):
    return (
        lax.broadcasted_iota(jnp.int32, shape, 0),
        lax.broadcasted_iota(jnp.int32, shape, 1),
    )


def tap_parts(tap):
    dz = step_index(tap, 9, 3)
    dy = step_index(tap - 9 * dz, 3, 3)
    return dz, dy, tap - 9 * dz - 3 * dy


def pack_kernel(density_ref, owners_ref, payload_ref, named_ref, sems):
    height, columns = density_ref.shape
    blocks = columns // BX
    copies = [pltpu.make_async_copy(owners_ref, named_ref, sems.at[blocks])]
    for k in range(blocks):
        copies.append(
            pltpu.make_async_copy(
                density_ref.at[:, k * BX : (k + 1) * BX],
                payload_ref.at[k * height : (k + 1) * height],
                sems.at[k],
            )
        )
    for copy in copies:
        copy.start()
    copies[0].wait()
    named = named_ref[...].astype(jnp.float32)
    count = named.shape[1]
    payload_ref[blocks * height : blocks * height + TILE, :] = jnp.concatenate(
        [
            jnp.broadcast_to(named, (TILE, count)),
            jnp.zeros((TILE, BX - count), jnp.float32),
        ],
        axis=1,
    ).astype(jnp.bfloat16)
    for copy in copies[1:]:
        copy.wait()


def banded_kernel(*refs):
    sources, refs = refs[:4], refs[5:]
    t1_ref, t2_ref, bias2_ref, *local, sems = refs
    copies = [
        pltpu.make_async_copy(source, target, sems.at[k])
        for k, (source, target) in enumerate(zip(sources, local))
    ]
    for copy in copies:
        copy.start()
    for copy in copies:
        copy.wait()
    w1_ref, b1_ref, w2_ref, b2_ref = local
    row, channel = iotas((TALL, CHANNELS))
    spread = one_hot((row & (CHANNELS - 1)) == channel)
    w1 = jnp.dot(spread, w1_ref[...], preferred_element_type=jnp.float32).astype(jnp.bfloat16)
    tap, column = iotas((27, 4 * PART))
    dz = column >> 6
    place = column & (PART - 1)
    dx = jnp.where(place < 3 * HALF, place >> 4, (place - 3 * HALF) >> 2)
    base = 9 * dz + dx
    row, column = iotas((TALL, 4 * PART))
    place = column & (PART - 1)
    seam = (place - 3 * HALF) & 3
    seam_row = jnp.where(seam < 2, seam - 2, seam + HALF - 2)
    input_row = jnp.where(place < 3 * HALF, place & (HALF - 1), seam_row)
    distance = jnp.where(place < 3 * HALF + 12, input_row - (row >> 3) + 2, -1)
    bias = jnp.zeros((TALL, 4 * PART), jnp.float32)
    for k in range(CHANNELS):
        bias = jnp.where((row & (CHANNELS - 1)) == k, b1_ref[k], bias)
    high = bias.astype(jnp.bfloat16).astype(jnp.float32)
    middle = (bias - high).astype(jnp.bfloat16).astype(jnp.float32)
    constant = jnp.where(column == PART + ONE_ROW, high, 0.0)
    constant = jnp.where(column == 2 * PART + ONE_ROW, middle, constant)
    constant = jnp.where(column == 2 * PART - 1, bias - high - middle, constant)
    outside = ((column == PART + ONE_ROW + 1) & (row < CHANNELS)) | (
        (column == PART + ONE_ROW + 2) & (row >= TALL - CHANNELS)
    )
    constant = jnp.where(outside, OUTSIDE, constant)
    for out in range(2):
        total = constant
        for dy in range(3):
            pick = one_hot(tap == base - 9 * out + 3 * dy)
            values = jnp.dot(w1, pick, preferred_element_type=jnp.float32)
            total = jnp.where(distance == dy, values, total)
        t1_ref[out * TALL : (out + 1) * TALL, :] = total.astype(jnp.bfloat16)
    channel, column = iotas((CHANNELS, 4 * TALL))
    spread = one_hot((column & (CHANNELS - 1)) == channel)
    tap, column = iotas((27, 4 * TALL))
    tap_z, slice_z = tap_parts(tap)[0], step_index(column, TALL, 4)
    row, tap = iotas((6 * HALF, 27))
    _, tap_y, tap_x = tap_parts(tap)
    same_x = (row >> 5) == tap_x
    wide = [
        lax.dot_general(
            w2_ref[o * CHANNELS : (o + 1) * CHANNELS, :],
            spread,
            (((0,), (0,)), ((), ())),
            preferred_element_type=jnp.float32,
        )
        for o in range(2)
    ]
    picks = [
        [one_hot(same_x & (tap_y == dy) & (((row >> 2) & 1) == o)) for o in range(2)]
        for dy in range(3)
    ]
    out_row, column = iotas((6 * HALF, 4 * TALL))
    y = ((out_row >> 3) & 3) * BY + (out_row & 3)
    distance = ((column - TALL * step_index(column, TALL, 4)) >> 3) - y
    for out in range(2):
        same_z = tap_z == slice_z - out
        terms = [jnp.where(same_z, values, 0.0).astype(jnp.bfloat16) for values in wide]
        total = jnp.zeros((6 * HALF, 4 * TALL), jnp.float32)
        for dy in range(3):
            values = 0.0
            for o in range(2):
                values = values + jnp.dot(
                    picks[dy][o], terms[o], preferred_element_type=jnp.float32
                )
            total = jnp.where(distance == dy, values, total)
        t2_ref[out * 6 * HALF : (out + 1) * 6 * HALF, :] = (0.5 * total).astype(jnp.bfloat16)
    row, _ = iotas((2 * HALF, BX))
    bias2_ref[...] = 0.5 * jnp.where(((row >> 2) & 1) == 0, b2_ref[0], b2_ref[1])


def edges_kernel(dims, *refs):
    count_gy, depth, rows, columns, few, count = dims
    tiles, outs = refs[:few], refs[few + 1 :]
    g = lax.axis_index("gy")
    c = lax.axis_index("col")
    height = depth * rows
    block = (1 - c) * height

    def take(i, start, size):
        start = pl.ds(pl.multiple_of(start, TILE), size)
        if few > 1:
            return tiles[i][start, :]
        return tiles[0][i, start, :]

    def pair(i):
        for k in range(2):
            at = pl.multiple_of((2 * i + k) * height, TILE)
            outs[0][pl.ds(at, height), :] = take(2 * i + k, block, height)
        low, high = [], []
        for k in range(2):
            for zz in range(depth):
                first, last = [], []
                for base in (0, height):
                    at = base + zz * rows
                    first.append(take(2 * i + k, at, TILE).astype(jnp.float32)[0:2])
                    at = at + rows - TILE
                    last.append(take(2 * i + k, at, TILE).astype(jnp.float32)[TILE - 2 :])
                low.append(jnp.concatenate(first, axis=1))
                high.append(jnp.concatenate(last, axis=1))
        at = pl.multiple_of(2 * i * 2 * depth, TILE)
        first, last = jnp.concatenate(low, axis=0), jnp.concatenate(high, axis=0)
        sends = [jnp.where(g == 0, last, first)] if count_gy == 2 else [last, first]
        for n, send in enumerate(sends):
            send = send.astype(jnp.bfloat16)
            outs[1 + n][pl.ds(at, TILE), :] = send

    if few > 1:
        for i in range(count // 2):
            pair(i)
    else:
        pl.loop(0, count // 2)(pair)


def corner_kernel(edge_ref, _, corner_ref):
    c = lax.axis_index("col")
    corner_ref[...] = jnp.where(c == 0, edge_ref[:, BX:], edge_ref[:, 0:BX])


def laplace(field, z, y):
    centre = field[z][y]
    last = lax.broadcasted_iota(jnp.int32, centre.shape, 1) == BX - 1
    ahead = jnp.where(last, 0.0, pltpu.roll(centre, BX - 1, 1) - centre)
    result = ahead - pltpu.roll(ahead, 1, 1)
    beside = [
        field[zz][yy]
        for zz, yy in ((z - 1, y), (z + 1, y), (z, y - 1), (z, y + 1))
        if 0 <= zz < len(field) and 0 <= yy < BY
    ]
    return result + (functools.reduce(jnp.add, beside) - float(len(beside)) * centre)


def uptake_of(quarter, doc, oxy):
    return quarter * doc * oxy / ((0.5 + jnp.abs(doc)) * (0.3 + jnp.abs(oxy)))


def prepare_kernel(dims, solutes_ref, biomass_ref, _, *refs):
    depth, slots = dims
    outs, (state, biomass, mass, sems) = refs[:5], refs[5:]
    size = depth * BY
    copies = []
    for group in range(slots // 8):
        for k, (source, target) in enumerate(((solutes_ref, state), (biomass_ref, biomass))):
            rows = (2 - k) * 8 * size
            at = pl.ds(group * rows, rows)
            copies.append(
                pltpu.make_async_copy(source.at[at], target.at[at], sems.at[group, k])
            )
    for copy in copies:
        copy.start()
    for group in range(slots // 8):
        copies[2 * group].wait()
        copies[2 * group + 1].wait()
        at = slice(group * 8 * size, (group + 1) * 8 * size)
        mass[at, :] = biomass[at, :].astype(jnp.float32)

        def rows_of(pitch, offset):
            return pl.ds(group * 8 * pitch + offset, 8, stride=pitch)

        grid = [(z, y) for z in range(depth) for y in range(BY)]
        carbon, oxygen = [
            [
                [state[rows_of(2 * size, k * size + z * BY + y), :] for y in range(BY)]
                for z in range(depth)
            ]
            for k in range(2)
        ]
        for z, y in grid:
            at = group * 8 * size + (z * BY + y) * 8
            at = slice(at, at + 8)
            doc, oxy = carbon[z][y], oxygen[z][y]
            quarter = 0.25 * mass[rows_of(size, z * BY + y), :]
            uptake = uptake_of(quarter, doc, oxy)
            values = (
                doc - uptake,
                oxy - uptake,
                laplace(carbon, z, y),
                laplace(oxygen, z, y),
                quarter,
            )
            for out, value in zip(outs, values):
                out[at, :] = value


def column_kernel(dims, few, *refs):
    count_gz, count_gy, depth, rows, columns, segment, slots, directions = dims
    tiles, refs = refs[:few], refs[few:]
    x_ref, refs = refs[0], refs[1:]
    top_refs, refs = refs[:2], refs[2:]
    if directions == 1:
        bottom_refs = top_refs
    else:
        bottom_refs, refs = refs[:2], refs[2:]
    t1_ref, t2_ref, bias2_ref, *refs = refs
    carbon_ref, oxygen_ref, carbon_around_ref, oxygen_around_ref, quarter_ref, *refs = refs
    fractions_ref, next_ref, *refs = refs
    (
        edge_rows,
        shifted,
        hidden,
        bricks,
        arrived,
        state,
        fractions,
        owner_rows,
        owner_table,
        brick_of_slot,
        sems,
        group_sems,
    ) = refs
    z_index = lax.axis_index("gz")
    g = lax.axis_index("gy")
    c = lax.axis_index("col")
    window = columns + BX
    brick_rows = HALF // BY
    brick_columns = columns // BX
    brick_count = rows // BY * brick_columns
    capacity = slots // count_gz
    single = segment == count_gz
    first_tile = z_index if few > 1 else 0
    size = depth * BY

    def tile_rows(i, start, size):
        if not isinstance(start, int):
            start = pl.multiple_of(start, TILE)
        if few > 1:
            return tiles[i][pl.ds(start, size), :]
        return tiles[0][i, pl.ds(start, size), :]

    def read_owners(i):
        row = tile_rows(i, brick_columns * depth * rows, TILE)
        owner_rows[i] = row.astype(jnp.float32)[0:8].astype(jnp.int32)

    if few > 1:
        for i in range(count_gz):
            read_owners(i)
    else:
        pl.loop(0, count_gz)(read_owners)
    table_copy = pltpu.make_async_copy(owner_rows, owner_table, sems.at[0])
    table_copy.start()

    def arrange(left, right, other):
        return jnp.concatenate(
            [
                jnp.where(c == 0, left, other),
                jnp.where(c == 0, right, left),
                jnp.where(c == 0, other, right),
            ],
            axis=1,
        )

    for k, pair in enumerate((top_refs, bottom_refs)):
        exists = (g > 0) if k == 0 else (g < count_gy - 1)
        own, other = pair[0][...].astype(jnp.float32), pair[1][...].astype(jnp.float32)
        values = arrange(own[:, 0:BX], own[:, BX:columns], other)
        edge_rows[k] = values * exists.astype(jnp.float32)

    def moved(values):
        lane = lax.broadcasted_iota(jnp.int32, values.shape, 1)
        left = jnp.where(lane == 0, 0.0, pltpu.roll(values, 1, 1))
        right = jnp.where(lane == window - 1, 0.0, pltpu.roll(values, window - 1, 1))
        return left.astype(values.dtype), values, right.astype(values.dtype)

    def edge_pair(k, at):
        if isinstance(at, int):
            return edge_rows[k, at : at + 2, :]
        group = edge_rows[k, pl.ds(pl.multiple_of(at // 8 * 8, 8), 8), :]
        return pltpu.roll(group, lax.rem(8 - at % 8, 8), 0)[0:2]

    row, _ = iotas((4, window))
    constants = [
        jnp.where((row == 0) | (row == 3), 1.0, jnp.where((row == 1 + h) & beyond, 1.0, 0.0))
        for h, beyond in enumerate((g == 0, g == count_gy - 1))
    ]

    def shifts(i, zz, slot, valid):
        z = i * depth + zz
        halves = []
        for h in range(2):
            at = zz * rows + h * HALF
            own = [tile_rows(i, k * depth * rows + at, HALF) for k in range(2)]
            at = z * rows + h * HALF
            if not isinstance(at, int):
                at = pl.multiple_of(at, TILE)
            values = arrange(*own, x_ref[pl.ds(at, HALF), :]).astype(jnp.float32)
            halves.append(values if valid is None else values * valid)
        top, bottom = edge_pair(0, 2 * z), edge_pair(1, 2 * z)
        if valid is not None:
            top, bottom = top * valid, bottom * valid
        seams = [
            jnp.concatenate([top, halves[1][0:2]], axis=0),
            jnp.concatenate([halves[0][HALF - 2 :], bottom], axis=0),
        ]
        for h in range(2):
            lanes = slice(h * window, (h + 1) * window)
            for dx, values in enumerate(moved(halves[h])):
                shifted[slot, dx * HALF : (dx + 1) * HALF, lanes] = values.astype(jnp.bfloat16)
            values = jnp.concatenate(
                [*moved(seams[h]), constants[h]], axis=0
            )
            shifted[slot, 3 * HALF : PART, lanes] = values.astype(jnp.bfloat16)

    def first(z, valid):
        total = jnp.dot(
            t1_ref[...],
            shifted[pl.ds(z + 1, 4)].reshape(4 * PART, 2 * window),
            preferred_element_type=jnp.float32,
        )
        for out in range(2):
            values = jnp.maximum(total[out * TALL : (out + 1) * TALL], 0.0)
            if valid is not None:
                values = values * valid(z + out)
            hidden[z + 1 + out] = values.astype(jnp.bfloat16)

    height = 2 * HALF
    _, lane = iotas((height, BX))

    def second(z, tile):
        total = jnp.dot(
            t2_ref[...],
            hidden[pl.ds(z, 4)].reshape(4 * TALL, 2 * window),
            preferred_element_type=jnp.float32,
        )
        for out in range(2):
            at = z + out
            place(total[3 * height * out : 3 * height * (out + 1)], tile + at // depth, at % depth)

    def place(total, t, zz):
        blocks = window // BX
        for h in range(2):
            part = [total[:, k * BX : (k + 1) * BX] for k in range(h * blocks, (h + 1) * blocks)]
            left = [0.0] + [pltpu.roll(block[0:height], 1, 1) for block in part]
            right = [pltpu.roll(block[2 * height :], BX - 1, 1) for block in part] + [0.0]
            sums = [
                part[k][height : 2 * height]
                + (
                    jnp.where(lane == 0, left[k], left[k + 1])
                    + jnp.where(lane == BX - 1, right[k + 1], right[k])
                )
                for k in range(blocks)
            ]
            for xb in range(brick_columns):
                own = jnp.where(c == 0, sums[xb], sums[xb + 1]) + bias2_ref[...]
                values = 0.5 + 0.5 * jnp.tanh(own)
                for yb in range(brick_rows):
                    b = (h * brick_rows + yb) * brick_columns + xb
                    bricks[t, b, zz] = values[yb * 8 : yb * 8 + 8]

    def valid_slice(z):
        return ((z >= 0) & (z < count_gz * depth)).astype(jnp.float32)

    depths = segment * depth
    if single:
        shifted[1] = jnp.zeros((PART, 2 * window), jnp.bfloat16)
        shifted[depths + 2] = jnp.zeros((PART, 2 * window), jnp.bfloat16)
        hidden[0] = jnp.zeros((TALL, 2 * window), jnp.bfloat16)
        hidden[depths + 1] = jnp.zeros((TALL, 2 * window), jnp.bfloat16)
        for i in range(count_gz):
            tile = lax.rem(first_tile + i, count_gz)
            for zz in range(depth):
                shifts(i, zz, tile * depth + zz + 2, None)

        @pl.loop(0, depths // 2, unroll=2)
        def _(k):
            first(2 * k, None)

        @pl.loop(0, depths // 2, unroll=2)
        def _(k):
            second(2 * k, 0)

    else:

        @pl.loop(0, count_gz // segment)
        def _(q):
            @pl.loop(-2, depths + 2)
            def _(z):
                at = q * depths + z
                inside = jnp.clip(at, 0, count_gz * depth - 1)
                shifts(inside // depth, inside % depth, z + 2, valid_slice(at))

            @pl.loop(0, depths // 2 + 1)
            def _(k):
                first(2 * k - 1, lambda z: valid_slice(q * depths + z))

            @pl.loop(0, depths // 2)
            def _(k):
                second(2 * k, q * segment)

    for zz in range(depth):
        for xb in range(brick_columns):
            own = [
                bricks[z_index, yb * brick_columns + xb, zz] for yb in range(rows // BY)
            ]
            for o in range(2):
                values = jnp.concatenate([v[o * BY : o * BY + BY] for v in own], axis=0)
                fractions[o, zz, :, xb * BX : (xb + 1) * BX] = values.astype(jnp.bfloat16)
    fractions_copy = pltpu.make_async_copy(fractions, fractions_ref, sems.at[1])
    fractions_copy.start()

    table_copy.wait()
    for j in range(slots):
        brick_of_slot[j] = -1

    @pl.loop(0, count_gz)
    def _(i):
        first = lax.rem(first_tile + i, count_gz) * capacity
        rank = jnp.int32(0)
        for b in range(brick_count):
            mine = owner_table[i, 0, b] == z_index
            brick_of_slot[jnp.where(mine, first + rank, slots)] = b
            rank = rank + mine.astype(jnp.int32)

    @pl.loop(0, slots, unroll=8)
    def _(j):
        brick = brick_of_slot[j]
        values = bricks[j // capacity, jnp.maximum(brick, 0)]
        values = jnp.where(brick >= 0, values, 0.0).astype(jnp.bfloat16).astype(jnp.float32)
        at = pl.multiple_of(j * (2 * size), 8)
        arrived[pl.ds(at, 2 * size), :] = values.reshape(2 * size, BX)

    def next_copy(group):
        at = pl.ds(pl.multiple_of(group * 16 * size, 16 * size), 16 * size)
        return pltpu.make_async_copy(state.at[at], next_ref.at[at], group_sems.at[group])

    @pl.loop(0, slots // 8)
    def _(group):
        grid = [(z, y) for z in range(depth) for y in range(BY)]

        def load(ref):
            base = group * (8 * size)
            return [
                [
                    ref[pl.ds(pl.multiple_of(base + (z * BY + y) * 8, 8), 8), :]
                    for y in range(BY)
                ]
                for z in range(depth)
            ]

        def rows_of(offset):
            return pl.ds(group * 16 * size + offset, 8, stride=2 * size)

        quarter = load(quarter_ref)
        pore = [[arrived[rows_of(z * 8 + y), :] for y in range(BY)] for z in range(depth)]
        organic = [
            [0.3 * arrived[rows_of(z * 8 + BY + y), :] for y in range(BY)] for z in range(depth)
        ]
        slow = [[0.12 * p for p in row] for row in pore]
        fast = [[0.16 * p for p in row] for row in pore]
        carbon, oxygen = load(carbon_ref), load(oxygen_ref)
        around = load(carbon_around_ref), load(oxygen_around_ref)
        for z, y in grid:
            carbon[z][y] += slow[z][y] * around[0][z][y] + organic[z][y]
            oxygen[z][y] += fast[z][y] * around[1][z][y]
        for _ in range(STEPS - 1):
            carbon_new = [[None] * BY for _ in range(depth)]
            oxygen_new = [[None] * BY for _ in range(depth)]
            for z, y in grid:
                doc, oxy = carbon[z][y], oxygen[z][y]
                uptake = uptake_of(quarter[z][y], doc, oxy)
                gain = organic[z][y] - uptake
                carbon_new[z][y] = doc + slow[z][y] * laplace(carbon, z, y) + gain
                oxygen_new[z][y] = oxy + fast[z][y] * laplace(oxygen, z, y) - uptake
            carbon, oxygen = carbon_new, oxygen_new
        for z, y in grid:
            state[rows_of(z * BY + y), :] = carbon[z][y]
            state[rows_of(size + z * BY + y), :] = oxygen[z][y]
        next_copy(group).start()

    @pl.loop(0, slots // 8)
    def _(group):
        next_copy(group).wait()

    fractions_copy.wait()


def per_device(
    sizes, density, first_kernel, first_bias, second_kernel, second_bias, owners, solutes, biomass
):
    count_gz, count_gy, count_col = sizes
    depth, rows, columns = density.shape
    slots = solutes.shape[3]
    window = columns + BX
    segment = min(count_gz, 4)
    brick_count = (rows // BY) * (columns // BX)
    height = depth * rows
    depths = count_gz * depth
    bf16, f32 = jnp.bfloat16, jnp.float32
    shape = jax.ShapeDtypeStruct

    payload = pl.pallas_call(
        pack_kernel,
        out_shape=shape((columns // BX * height + TILE, BX), bf16),
        in_specs=[HBM, HBM],
        out_specs=VMEM,
        scratch_shapes=[
            pltpu.VMEM((1, brick_count), jnp.int32),
            pltpu.SemaphoreType.DMA((columns // BX + 1,)),
        ],
        compiler_params=pltpu.CompilerParams(vmem_limit_bytes=4 * 2**20),
        name="pack",
    )(in_hbm(density.reshape(height, columns)), in_hbm(owners.reshape(1, brick_count)))

    few = count_gz if count_gz == segment else 1
    if few > 1:
        tiles = [payload] + [
            lax.ppermute(payload, "gz", [((i + s) % count_gz, i) for i in range(count_gz)])
            for s in range(1, count_gz)
        ]
    else:
        tiles = [lax.all_gather(payload, "gz", axis=0, tiled=False)]

    cells = depth * BY
    t1, t2, bias2 = pl.pallas_call(
        banded_kernel,
        out_shape=(
            shape((2 * TALL, 4 * PART), bf16),
            shape((12 * HALF, 4 * TALL), bf16),
            shape((2 * HALF, BX), f32),
        ),
        in_specs=[HBM, HBM, HBM, HBM, ANY],
        out_specs=(VMEM, VMEM, VMEM),
        scratch_shapes=[
            pltpu.VMEM((CHANNELS, 27), bf16),
            pltpu.SMEM((CHANNELS,), f32),
            pltpu.VMEM((2 * CHANNELS, 27), bf16),
            pltpu.SMEM((2,), f32),
            pltpu.SemaphoreType.DMA((4,)),
        ],
        compiler_params=pltpu.CompilerParams(vmem_limit_bytes=16 * 2**20),
        cost_estimate=pl.CostEstimate(
            flops=20 * 2**20, bytes_accessed=4 * 2**20, transcendentals=0
        ),
        name="banded",
    )(
        in_hbm(first_kernel.transpose(2, 1, 0).reshape(CHANNELS, 27)),
        in_hbm(first_bias),
        in_hbm(second_kernel.transpose(1, 2, 0).reshape(2 * CHANNELS, 27)),
        in_hbm(second_bias),
        payload,
    )

    if count_gy == 2:
        ways = [[(0, 1), (1, 0)]]
    else:
        up = [(i, i + 1) for i in range(count_gy - 1)]
        ways = [up, [(j, i) for i, j in up]]
    directions = len(ways)
    swap = [(0, 1), (1, 0)]
    near, *sent = pl.pallas_call(
        functools.partial(edges_kernel, (count_gy, depth, rows, columns, few, count_gz)),
        out_shape=[shape((depths * rows, BX), bf16)]
        + [shape((2 * depths, columns), bf16)] * directions,
        in_specs=[VMEM] * few + [ANY],
        out_specs=[VMEM] * (1 + directions),
        compiler_params=pltpu.CompilerParams(vmem_limit_bytes=16 * 2**20),
        name="edges",
    )(*tiles, bias2)
    prepared = pl.pallas_call(
        functools.partial(prepare_kernel, (depth, slots)),
        out_shape=[shape((slots * cells, BX), f32)] * 5,
        in_specs=[HBM, HBM, ANY],
        out_specs=[VMEM] * 5,
        scratch_shapes=[
            pltpu.VMEM((slots * 2 * cells, BX), f32),
            pltpu.VMEM((slots * cells, BX), bf16),
            pltpu.VMEM((slots * cells, BX), f32),
            pltpu.SemaphoreType.DMA((slots // 8, 2)),
        ],
        compiler_params=pltpu.CompilerParams(vmem_limit_bytes=12 * 2**20),
        cost_estimate=pl.CostEstimate(
            flops=60 * slots * cells * BX, bytes_accessed=2**20, transcendentals=0
        ),
        name="prepare",
    )(
        in_hbm(solutes.reshape(slots * 2 * cells, BX)),
        in_hbm(biomass.reshape(slots * cells, BX)),
        near,
    )
    edges = []
    for pairs, edge in zip(ways, sent):
        edge = lax.ppermute(edge, "gy", pairs)
        corner = pl.pallas_call(
            corner_kernel,
            out_shape=shape((2 * depths, BX), bf16),
            in_specs=[VMEM, ANY],
            out_specs=VMEM,
            compiler_params=pltpu.CompilerParams(vmem_limit_bytes=4 * 2**20),
            name="corner",
        )(edge, prepared[-1])
        edges += [edge, lax.ppermute(corner, "col", swap)]
    near = lax.ppermute(near, "col", swap)

    fractions, solutes_next = pl.pallas_call(
        functools.partial(
            column_kernel,
            (count_gz, count_gy, depth, rows, columns, segment, slots, directions),
            few,
        ),
        out_shape=(
            shape((2, depth, rows, columns), bf16),
            shape((slots * 2 * cells, BX), f32),
        ),
        in_specs=[VMEM] * (few + 1 + len(edges) + 8),
        out_specs=(HBM, HBM),
        scratch_shapes=[
            pltpu.VMEM((2, 2 * depths, window), f32),
            pltpu.VMEM((segment * depth + 4, PART, 2 * window), bf16),
            pltpu.VMEM((segment * depth + 2, TALL, 2 * window), bf16),
            pltpu.VMEM((count_gz, brick_count, depth, 8, BX), f32),
            pltpu.VMEM((slots * 2 * cells, BX), f32),
            pltpu.VMEM((slots * 2 * cells, BX), f32),
            pltpu.VMEM((2, depth, rows, columns), bf16),
            pltpu.VMEM((count_gz, 8, BX), jnp.int32),
            pltpu.SMEM((count_gz, 8, BX), jnp.int32),
            pltpu.SMEM((slots + 1,), jnp.int32),
            pltpu.SemaphoreType.DMA((2,)),
            pltpu.SemaphoreType.DMA((slots // 8,)),
        ],
        compiler_params=pltpu.CompilerParams(vmem_limit_bytes=40 * 2**20),
        cost_estimate=pl.CostEstimate(
            flops=2 * depths * 2 * window * TALL * (4 * PART + 4 * 6 * HALF),
            bytes_accessed=4 * 2**20,
            transcendentals=0,
        ),
        name="column",
    )(
        *tiles,
        near,
        *edges,
        t1,
        t2,
        bias2,
        *prepared,
    )
    return fractions, solutes_next.reshape(solutes.shape)


def solution(mesh):
    sizes = (mesh.shape["gz"], mesh.shape["gy"], mesh.shape["col"])
    assert sizes[2] == 2
    return jax.shard_map(
        functools.partial(per_device, sizes),
        mesh=mesh,
        in_specs=(
            P(("cores", "gz"), "gy", "col"),
            P(),
            P(),
            P(),
            P(),
            P(("cores", "gz"), "gy", "col", None, None),
            P(("cores", "gz"), "gy", "col", None, None, None, None, None),
            P(("cores", "gz"), "gy", "col", None, None, None, None),
        ),
        out_specs=(
            P(None, ("cores", "gz"), "gy", "col"),
            P(("cores", "gz"), "gy", "col", None, None, None, None, None),
        ),
        check_vma=False,
    )
```

```python
import functools

import jax
import jax.numpy as jnp
from jax import lax
from jax.experimental import pallas as pl
from jax.experimental.pallas import tpu as pltpu
from jax.sharding import PartitionSpec as P

BY = 4
BX = 128
STEPS = 4
TILE = 16
HALF = 16
CHANNELS = 8
REACH = HALF + 2
PART = 3 * HALF + TILE
TALL = REACH * CHANNELS
ONE_ROW = 3 * HALF + 12
OUTSIDE = -1e30

VMEM = pl.BlockSpec(memory_space=pltpu.VMEM)
SMEM = pl.BlockSpec(memory_space=pltpu.SMEM)
ANY = pl.BlockSpec(memory_space=pl.ANY)
HBM = pl.BlockSpec(memory_space=pltpu.HBM)


def in_hbm(array):
    return pltpu.with_memory_space_constraint(array, pltpu.HBM)


def step_index(values, width, count):
    index = jnp.zeros(values.shape, jnp.int32)
    for k in range(1, count):
        index = index + (values >= k * width).astype(jnp.int32)
    return index


def one_hot(condition):
    return jnp.where(condition, 1.0, 0.0).astype(jnp.bfloat16)


def iotas(shape):
    return (
        lax.broadcasted_iota(jnp.int32, shape, 0),
        lax.broadcasted_iota(jnp.int32, shape, 1),
    )


def tap_parts(tap):
    dz = step_index(tap, 9, 3)
    dy = step_index(tap - 9 * dz, 3, 3)
    return dz, dy, tap - 9 * dz - 3 * dy


def pack_kernel(density_ref, owners_ref, payload_ref, named_ref, sems):
    height, columns = density_ref.shape
    blocks = columns // BX
    copies = [pltpu.make_async_copy(owners_ref, named_ref, sems.at[blocks])]
    for k in range(blocks):
        copies.append(
            pltpu.make_async_copy(
                density_ref.at[:, k * BX : (k + 1) * BX],
                payload_ref.at[k * height : (k + 1) * height],
                sems.at[k],
            )
        )
    for copy in copies:
        copy.start()
    copies[0].wait()
    named = named_ref[...].astype(jnp.float32)
    count = named.shape[1]
    payload_ref[blocks * height : blocks * height + TILE, :] = jnp.concatenate(
        [
            jnp.broadcast_to(named, (TILE, count)),
            jnp.zeros((TILE, BX - count), jnp.float32),
        ],
        axis=1,
    ).astype(jnp.bfloat16)
    for copy in copies[1:]:
        copy.wait()


def banded_kernel(*refs):
    sources, refs = refs[:4], refs[5:]
    t1_ref, t2_ref, bias2_ref, *local, sems = refs
    copies = [
        pltpu.make_async_copy(source, target, sems.at[k])
        for k, (source, target) in enumerate(zip(sources, local))
    ]
    for copy in copies:
        copy.start()
    for copy in copies:
        copy.wait()
    w1_ref, b1_ref, w2_ref, b2_ref = local
    row, channel = iotas((TALL, CHANNELS))
    spread = one_hot((row & (CHANNELS - 1)) == channel)
    w1 = jnp.dot(spread, w1_ref[...], preferred_element_type=jnp.float32).astype(jnp.bfloat16)
    tap, column = iotas((27, 4 * PART))
    dz = column >> 6
    place = column & (PART - 1)
    dx = jnp.where(place < 3 * HALF, place >> 4, (place - 3 * HALF) >> 2)
    base = 9 * dz + dx
    row, column = iotas((TALL, 4 * PART))
    place = column & (PART - 1)
    seam = (place - 3 * HALF) & 3
    seam_row = jnp.where(seam < 2, seam - 2, seam + HALF - 2)
    input_row = jnp.where(place < 3 * HALF, place & (HALF - 1), seam_row)
    distance = jnp.where(place < 3 * HALF + 12, input_row - (row >> 3) + 2, -1)
    bias = jnp.zeros((TALL, 4 * PART), jnp.float32)
    for k in range(CHANNELS):
        bias = jnp.where((row & (CHANNELS - 1)) == k, b1_ref[k], bias)
    high = bias.astype(jnp.bfloat16).astype(jnp.float32)
    middle = (bias - high).astype(jnp.bfloat16).astype(jnp.float32)
    constant = jnp.where(column == PART + ONE_ROW, high, 0.0)
    constant = jnp.where(column == 2 * PART + ONE_ROW, middle, constant)
    constant = jnp.where(column == 2 * PART - 1, bias - high - middle, constant)
    outside = ((column == PART + ONE_ROW + 1) & (row < CHANNELS)) | (
        (column == PART + ONE_ROW + 2) & (row >= TALL - CHANNELS)
    )
    constant = jnp.where(outside, OUTSIDE, constant)
    for out in range(2):
        total = constant
        for dy in range(3):
            pick = one_hot(tap == base - 9 * out + 3 * dy)
            values = jnp.dot(w1, pick, preferred_element_type=jnp.float32)
            total = jnp.where(distance == dy, values, total)
        t1_ref[out * TALL : (out + 1) * TALL, :] = total.astype(jnp.bfloat16)
    channel, column = iotas((CHANNELS, 4 * TALL))
    spread = one_hot((column & (CHANNELS - 1)) == channel)
    tap, column = iotas((27, 4 * TALL))
    tap_z, slice_z = tap_parts(tap)[0], step_index(column, TALL, 4)
    row, tap = iotas((6 * HALF, 27))
    _, tap_y, tap_x = tap_parts(tap)
    same_x = (row >> 5) == tap_x
    wide = [
        lax.dot_general(
            w2_ref[o * CHANNELS : (o + 1) * CHANNELS, :],
            spread,
            (((0,), (0,)), ((), ())),
            preferred_element_type=jnp.float32,
        )
        for o in range(2)
    ]
    picks = [
        [one_hot(same_x & (tap_y == dy) & (((row >> 2) & 1) == o)) for o in range(2)]
        for dy in range(3)
    ]
    out_row, column = iotas((6 * HALF, 4 * TALL))
    y = ((out_row >> 3) & 3) * BY + (out_row & 3)
    distance = ((column - TALL * step_index(column, TALL, 4)) >> 3) - y
    for out in range(2):
        same_z = tap_z == slice_z - out
        terms = [jnp.where(same_z, values, 0.0).astype(jnp.bfloat16) for values in wide]
        total = jnp.zeros((6 * HALF, 4 * TALL), jnp.float32)
        for dy in range(3):
            values = 0.0
            for o in range(2):
                values = values + jnp.dot(
                    picks[dy][o], terms[o], preferred_element_type=jnp.float32
                )
            total = jnp.where(distance == dy, values, total)
        t2_ref[out * 6 * HALF : (out + 1) * 6 * HALF, :] = (0.5 * total).astype(jnp.bfloat16)
    row, _ = iotas((2 * HALF, BX))
    bias2_ref[...] = 0.5 * jnp.where(((row >> 2) & 1) == 0, b2_ref[0], b2_ref[1])


def edges_kernel(dims, *refs):
    count_gy, depth, rows, columns, few, count = dims
    tiles, outs = refs[:few], refs[few + 1 :]
    g = lax.axis_index("gy")
    c = lax.axis_index("col")
    height = depth * rows
    block = (1 - c) * height

    def take(i, start, size):
        start = pl.ds(pl.multiple_of(start, TILE), size)
        if few > 1:
            return tiles[i][start, :]
        return tiles[0][i, start, :]

    def pair(i):
        for k in range(2):
            at = pl.multiple_of((2 * i + k) * height, TILE)
            outs[0][pl.ds(at, height), :] = take(2 * i + k, block, height)
        low, high = [], []
        for k in range(2):
            for zz in range(depth):
                first, last = [], []
                for base in (0, height):
                    at = base + zz * rows
                    first.append(take(2 * i + k, at, TILE).astype(jnp.float32)[0:2])
                    at = at + rows - TILE
                    last.append(take(2 * i + k, at, TILE).astype(jnp.float32)[TILE - 2 :])
                low.append(jnp.concatenate(first, axis=1))
                high.append(jnp.concatenate(last, axis=1))
        at = pl.multiple_of(2 * i * 2 * depth, TILE)
        first, last = jnp.concatenate(low, axis=0), jnp.concatenate(high, axis=0)
        sends = [jnp.where(g == 0, last, first)] if count_gy == 2 else [last, first]
        for n, send in enumerate(sends):
            send = send.astype(jnp.bfloat16)
            outs[1 + n][pl.ds(at, TILE), :] = send

    if few > 1:
        for i in range(count // 2):
            pair(i)
    else:
        pl.loop(0, count // 2)(pair)


def corner_kernel(edge_ref, _, corner_ref):
    c = lax.axis_index("col")
    corner_ref[...] = jnp.where(c == 0, edge_ref[:, BX:], edge_ref[:, 0:BX])


def laplace(field, z, y):
    centre = field[z][y]
    last = lax.broadcasted_iota(jnp.int32, centre.shape, 1) == BX - 1
    ahead = jnp.where(last, 0.0, pltpu.roll(centre, BX - 1, 1) - centre)
    result = ahead - pltpu.roll(ahead, 1, 1)
    beside = [
        field[zz][yy]
        for zz, yy in ((z - 1, y), (z + 1, y), (z, y - 1), (z, y + 1))
        if 0 <= zz < len(field) and 0 <= yy < BY
    ]
    return result + (functools.reduce(jnp.add, beside) - float(len(beside)) * centre)


def uptake_of(quarter, doc, oxy):
    return quarter * doc * oxy / ((0.5 + jnp.abs(doc)) * (0.3 + jnp.abs(oxy)))


def prepare_kernel(dims, solutes_ref, biomass_ref, _, *refs):
    depth, slots = dims
    outs, (state, biomass, mass, sems) = refs[:5], refs[5:]
    size = depth * BY
    copies = []
    for group in range(slots // 8):
        for k, (source, target) in enumerate(((solutes_ref, state), (biomass_ref, biomass))):
            rows = (2 - k) * 8 * size
            at = pl.ds(group * rows, rows)
            copies.append(
                pltpu.make_async_copy(source.at[at], target.at[at], sems.at[group, k])
            )
    for copy in copies:
        copy.start()
    for group in range(slots // 8):
        copies[2 * group].wait()
        copies[2 * group + 1].wait()
        at = slice(group * 8 * size, (group + 1) * 8 * size)
        mass[at, :] = biomass[at, :].astype(jnp.float32)

        def rows_of(pitch, offset):
            return pl.ds(group * 8 * pitch + offset, 8, stride=pitch)

        grid = [(z, y) for z in range(depth) for y in range(BY)]
        carbon, oxygen = [
            [
                [state[rows_of(2 * size, k * size + z * BY + y), :] for y in range(BY)]
                for z in range(depth)
            ]
            for k in range(2)
        ]
        for z, y in grid:
            at = group * 8 * size + (z * BY + y) * 8
            at = slice(at, at + 8)
            doc, oxy = carbon[z][y], oxygen[z][y]
            quarter = 0.25 * mass[rows_of(size, z * BY + y), :]
            uptake = uptake_of(quarter, doc, oxy)
            values = (
                doc - uptake,
                oxy - uptake,
                laplace(carbon, z, y),
                laplace(oxygen, z, y),
                quarter,
            )
            for out, value in zip(outs, values):
                out[at, :] = value


def column_kernel(dims, few, *refs):
    count_gz, count_gy, depth, rows, columns, segment, slots, directions = dims
    tiles, refs = refs[:few], refs[few:]
    x_ref, refs = refs[0], refs[1:]
    top_refs, refs = refs[:2], refs[2:]
    if directions == 1:
        bottom_refs = top_refs
    else:
        bottom_refs, refs = refs[:2], refs[2:]
    t1_ref, t2_ref, bias2_ref, *refs = refs
    carbon_ref, oxygen_ref, carbon_around_ref, oxygen_around_ref, quarter_ref, *refs = refs
    fractions_ref, next_ref, *refs = refs
    (
        edge_rows,
        shifted,
        hidden,
        bricks,
        arrived,
        state,
        fractions,
        owner_rows,
        owner_table,
        brick_of_slot,
        sems,
        group_sems,
    ) = refs
    z_index = lax.axis_index("gz")
    g = lax.axis_index("gy")
    c = lax.axis_index("col")
    window = columns + BX
    brick_rows = HALF // BY
    brick_columns = columns // BX
    brick_count = rows // BY * brick_columns
    capacity = slots // count_gz
    single = segment == count_gz

    def tile_of(i):
        return jnp.bitwise_xor(z_index, i) if few > 1 else i

    size = depth * BY

    def tile_rows(i, start, size):
        if not isinstance(start, int):
            start = pl.multiple_of(start, TILE)
        if few > 1:
            return tiles[i][pl.ds(start, size), :]
        return tiles[0][i, pl.ds(start, size), :]

    def read_owners(i):
        row = tile_rows(i, brick_columns * depth * rows, TILE)
        owner_rows[i] = row.astype(jnp.float32)[0:8].astype(jnp.int32)

    if few > 1:
        for i in range(count_gz):
            read_owners(i)
    else:
        pl.loop(0, count_gz)(read_owners)
    table_copy = pltpu.make_async_copy(owner_rows, owner_table, sems.at[0])
    table_copy.start()

    def arrange(left, right, other):
        return jnp.concatenate(
            [
                jnp.where(c == 0, left, other),
                jnp.where(c == 0, right, left),
                jnp.where(c == 0, other, right),
            ],
            axis=1,
        )

    for k, pair in enumerate((top_refs, bottom_refs)):
        exists = (g > 0) if k == 0 else (g < count_gy - 1)
        own, other = pair[0][...].astype(jnp.float32), pair[1][...].astype(jnp.float32)
        values = arrange(own[:, 0:BX], own[:, BX:columns], other)
        edge_rows[k] = values * exists.astype(jnp.float32)

    def moved(values):
        lane = lax.broadcasted_iota(jnp.int32, values.shape, 1)
        left = jnp.where(lane == 0, 0.0, pltpu.roll(values, 1, 1))
        right = jnp.where(lane == window - 1, 0.0, pltpu.roll(values, window - 1, 1))
        return left.astype(values.dtype), values, right.astype(values.dtype)

    def edge_pair(k, at):
        if isinstance(at, int):
            return edge_rows[k, at : at + 2, :]
        group = edge_rows[k, pl.ds(pl.multiple_of(at // 8 * 8, 8), 8), :]
        return pltpu.roll(group, lax.rem(8 - at % 8, 8), 0)[0:2]

    row, _ = iotas((4, window))
    constants = [
        jnp.where((row == 0) | (row == 3), 1.0, jnp.where((row == 1 + h) & beyond, 1.0, 0.0))
        for h, beyond in enumerate((g == 0, g == count_gy - 1))
    ]

    def shifts(i, zz, slot, valid):
        z = i * depth + zz
        halves = []
        for h in range(2):
            at = zz * rows + h * HALF
            own = [tile_rows(i, k * depth * rows + at, HALF) for k in range(2)]
            at = z * rows + h * HALF
            if not isinstance(at, int):
                at = pl.multiple_of(at, TILE)
            values = arrange(*own, x_ref[pl.ds(at, HALF), :]).astype(jnp.float32)
            halves.append(values if valid is None else values * valid)
        top, bottom = edge_pair(0, 2 * z), edge_pair(1, 2 * z)
        if valid is not None:
            top, bottom = top * valid, bottom * valid
        seams = [
            jnp.concatenate([top, halves[1][0:2]], axis=0),
            jnp.concatenate([halves[0][HALF - 2 :], bottom], axis=0),
        ]
        for h in range(2):
            lanes = slice(h * window, (h + 1) * window)
            for dx, values in enumerate(moved(halves[h])):
                shifted[slot, dx * HALF : (dx + 1) * HALF, lanes] = values.astype(jnp.bfloat16)
            values = jnp.concatenate(
                [*moved(seams[h]), constants[h]], axis=0
            )
            shifted[slot, 3 * HALF : PART, lanes] = values.astype(jnp.bfloat16)

    def first(z, valid):
        total = jnp.dot(
            t1_ref[...],
            shifted[pl.ds(z + 1, 4)].reshape(4 * PART, 2 * window),
            preferred_element_type=jnp.float32,
        )
        for out in range(2):
            values = jnp.maximum(total[out * TALL : (out + 1) * TALL], 0.0)
            if valid is not None:
                values = values * valid(z + out)
            hidden[z + 1 + out] = values.astype(jnp.bfloat16)

    height = 2 * HALF
    _, lane = iotas((height, BX))

    def second(z, tile):
        total = jnp.dot(
            t2_ref[...],
            hidden[pl.ds(z, 4)].reshape(4 * TALL, 2 * window),
            preferred_element_type=jnp.float32,
        )
        for out in range(2):
            at = z + out
            place(total[3 * height * out : 3 * height * (out + 1)], tile + at // depth, at % depth)

    def place(total, t, zz):
        blocks = window // BX
        for h in range(2):
            part = [total[:, k * BX : (k + 1) * BX] for k in range(h * blocks, (h + 1) * blocks)]
            left = [0.0] + [pltpu.roll(block[0:height], 1, 1) for block in part]
            right = [pltpu.roll(block[2 * height :], BX - 1, 1) for block in part] + [0.0]
            sums = [
                part[k][height : 2 * height]
                + (
                    jnp.where(lane == 0, left[k], left[k + 1])
                    + jnp.where(lane == BX - 1, right[k + 1], right[k])
                )
                for k in range(blocks)
            ]
            for xb in range(brick_columns):
                own = jnp.where(c == 0, sums[xb], sums[xb + 1]) + bias2_ref[...]
                values = 0.5 + 0.5 * jnp.tanh(own)
                for yb in range(brick_rows):
                    b = (h * brick_rows + yb) * brick_columns + xb
                    bricks[t, b, zz] = values[yb * 8 : yb * 8 + 8]

    def valid_slice(z):
        return ((z >= 0) & (z < count_gz * depth)).astype(jnp.float32)

    depths = segment * depth
    if single:
        shifted[1] = jnp.zeros((PART, 2 * window), jnp.bfloat16)
        shifted[depths + 2] = jnp.zeros((PART, 2 * window), jnp.bfloat16)
        hidden[0] = jnp.zeros((TALL, 2 * window), jnp.bfloat16)
        hidden[depths + 1] = jnp.zeros((TALL, 2 * window), jnp.bfloat16)
        for i in range(count_gz):
            tile = tile_of(i)
            for zz in range(depth):
                shifts(i, zz, tile * depth + zz + 2, None)

        @pl.loop(0, depths // 2, unroll=4)
        def _(k):
            first(2 * k, None)

        @pl.loop(0, depths // 2, unroll=4)
        def _(k):
            second(2 * k, 0)

    else:

        @pl.loop(0, count_gz // segment)
        def _(q):
            @pl.loop(-2, depths + 2)
            def _(z):
                at = q * depths + z
                inside = jnp.clip(at, 0, count_gz * depth - 1)
                shifts(inside // depth, inside % depth, z + 2, valid_slice(at))

            @pl.loop(0, depths // 2 + 1)
            def _(k):
                first(2 * k - 1, lambda z: valid_slice(q * depths + z))

            @pl.loop(0, depths // 2)
            def _(k):
                second(2 * k, q * segment)

    for zz in range(depth):
        for xb in range(brick_columns):
            own = [
                bricks[z_index, yb * brick_columns + xb, zz] for yb in range(rows // BY)
            ]
            for o in range(2):
                values = jnp.concatenate([v[o * BY : o * BY + BY] for v in own], axis=0)
                fractions[o, zz, :, xb * BX : (xb + 1) * BX] = values.astype(jnp.bfloat16)
    fractions_copy = pltpu.make_async_copy(fractions, fractions_ref, sems.at[1])
    fractions_copy.start()

    table_copy.wait()
    for j in range(slots):
        brick_of_slot[j] = -1

    @pl.loop(0, count_gz)
    def _(i):
        first = tile_of(i) * capacity
        rank = jnp.int32(0)
        for b in range(brick_count):
            mine = owner_table[i, 0, b] == z_index
            brick_of_slot[jnp.where(mine, first + rank, slots)] = b
            rank = rank + mine.astype(jnp.int32)

    @pl.loop(0, slots, unroll=8)
    def _(j):
        brick = brick_of_slot[j]
        values = bricks[j // capacity, jnp.maximum(brick, 0)]
        values = jnp.where(brick >= 0, values, 0.0).astype(jnp.bfloat16).astype(jnp.float32)
        at = pl.multiple_of(j * (2 * size), 8)
        arrived[pl.ds(at, 2 * size), :] = values.reshape(2 * size, BX)

    def next_copy(group):
        at = pl.ds(pl.multiple_of(group * 16 * size, 16 * size), 16 * size)
        return pltpu.make_async_copy(state.at[at], next_ref.at[at], group_sems.at[group])

    @pl.loop(0, slots // 8)
    def _(group):
        grid = [(z, y) for z in range(depth) for y in range(BY)]

        def load(ref):
            base = group * (8 * size)
            return [
                [
                    ref[pl.ds(pl.multiple_of(base + (z * BY + y) * 8, 8), 8), :]
                    for y in range(BY)
                ]
                for z in range(depth)
            ]

        def rows_of(offset):
            return pl.ds(group * 16 * size + offset, 8, stride=2 * size)

        quarter = load(quarter_ref)
        pore = [[arrived[rows_of(z * 8 + y), :] for y in range(BY)] for z in range(depth)]
        organic = [
            [0.3 * arrived[rows_of(z * 8 + BY + y), :] for y in range(BY)] for z in range(depth)
        ]
        slow = [[0.12 * p for p in row] for row in pore]
        fast = [[0.16 * p for p in row] for row in pore]
        carbon, oxygen = load(carbon_ref), load(oxygen_ref)
        around = load(carbon_around_ref), load(oxygen_around_ref)
        for z, y in grid:
            carbon[z][y] += slow[z][y] * around[0][z][y] + organic[z][y]
            oxygen[z][y] += fast[z][y] * around[1][z][y]
        for _ in range(STEPS - 1):
            carbon_new = [[None] * BY for _ in range(depth)]
            oxygen_new = [[None] * BY for _ in range(depth)]
            for z, y in grid:
                doc, oxy = carbon[z][y], oxygen[z][y]
                uptake = uptake_of(quarter[z][y], doc, oxy)
                gain = organic[z][y] - uptake
                carbon_new[z][y] = doc + slow[z][y] * laplace(carbon, z, y) + gain
                oxygen_new[z][y] = oxy + fast[z][y] * laplace(oxygen, z, y) - uptake
            carbon, oxygen = carbon_new, oxygen_new
        for z, y in grid:
            state[rows_of(z * BY + y), :] = carbon[z][y]
            state[rows_of(size + z * BY + y), :] = oxygen[z][y]
        next_copy(group).start()

    @pl.loop(0, slots // 8)
    def _(group):
        next_copy(group).wait()

    fractions_copy.wait()


def per_device(
    sizes, density, first_kernel, first_bias, second_kernel, second_bias, owners, solutes, biomass
):
    count_gz, count_gy, count_col = sizes
    depth, rows, columns = density.shape
    slots = solutes.shape[3]
    window = columns + BX
    segment = min(count_gz, 4)
    brick_count = (rows // BY) * (columns // BX)
    height = depth * rows
    depths = count_gz * depth
    bf16, f32 = jnp.bfloat16, jnp.float32
    shape = jax.ShapeDtypeStruct

    payload = pl.pallas_call(
        pack_kernel,
        out_shape=shape((columns // BX * height + TILE, BX), bf16),
        in_specs=[HBM, HBM],
        out_specs=VMEM,
        scratch_shapes=[
            pltpu.VMEM((1, brick_count), jnp.int32),
            pltpu.SemaphoreType.DMA((columns // BX + 1,)),
        ],
        compiler_params=pltpu.CompilerParams(vmem_limit_bytes=4 * 2**20),
        name="pack",
    )(in_hbm(density.reshape(height, columns)), in_hbm(owners.reshape(1, brick_count)))

    few = count_gz if count_gz in (2, 4) else 1
    if few > 1:
        tiles = [payload] + [
            lax.ppermute(payload, "gz", [(i, i ^ s) for i in range(count_gz)])
            for s in range(1, count_gz)
        ]
    else:
        tiles = [lax.all_gather(payload, "gz", axis=0, tiled=False)]

    cells = depth * BY
    t1, t2, bias2 = pl.pallas_call(
        banded_kernel,
        out_shape=(
            shape((2 * TALL, 4 * PART), bf16),
            shape((12 * HALF, 4 * TALL), bf16),
            shape((2 * HALF, BX), f32),
        ),
        in_specs=[HBM, HBM, HBM, HBM, ANY],
        out_specs=(VMEM, VMEM, VMEM),
        scratch_shapes=[
            pltpu.VMEM((CHANNELS, 27), bf16),
            pltpu.SMEM((CHANNELS,), f32),
            pltpu.VMEM((2 * CHANNELS, 27), bf16),
            pltpu.SMEM((2,), f32),
            pltpu.SemaphoreType.DMA((4,)),
        ],
        compiler_params=pltpu.CompilerParams(vmem_limit_bytes=16 * 2**20),
        cost_estimate=pl.CostEstimate(
            flops=20 * 2**20, bytes_accessed=4 * 2**20, transcendentals=0
        ),
        name="banded",
    )(
        in_hbm(first_kernel.transpose(2, 1, 0).reshape(CHANNELS, 27)),
        in_hbm(first_bias),
        in_hbm(second_kernel.transpose(1, 2, 0).reshape(2 * CHANNELS, 27)),
        in_hbm(second_bias),
        payload,
    )

    if count_gy == 2:
        ways = [[(0, 1), (1, 0)]]
    else:
        up = [(i, i + 1) for i in range(count_gy - 1)]
        ways = [up, [(j, i) for i, j in up]]
    directions = len(ways)
    swap = [(0, 1), (1, 0)]
    near, *sent = pl.pallas_call(
        functools.partial(edges_kernel, (count_gy, depth, rows, columns, few, count_gz)),
        out_shape=[shape((depths * rows, BX), bf16)]
        + [shape((2 * depths, columns), bf16)] * directions,
        in_specs=[VMEM] * few + [ANY],
        out_specs=[VMEM] * (1 + directions),
        compiler_params=pltpu.CompilerParams(vmem_limit_bytes=16 * 2**20),
        name="edges",
    )(*tiles, bias2)
    prepared = pl.pallas_call(
        functools.partial(prepare_kernel, (depth, slots)),
        out_shape=[shape((slots * cells, BX), f32)] * 5,
        in_specs=[HBM, HBM, ANY],
        out_specs=[VMEM] * 5,
        scratch_shapes=[
            pltpu.VMEM((slots * 2 * cells, BX), f32),
            pltpu.VMEM((slots * cells, BX), bf16),
            pltpu.VMEM((slots * cells, BX), f32),
            pltpu.SemaphoreType.DMA((slots // 8, 2)),
        ],
        compiler_params=pltpu.CompilerParams(vmem_limit_bytes=12 * 2**20),
        cost_estimate=pl.CostEstimate(
            flops=60 * slots * cells * BX, bytes_accessed=2**20, transcendentals=0
        ),
        name="prepare",
    )(
        in_hbm(solutes.reshape(slots * 2 * cells, BX)),
        in_hbm(biomass.reshape(slots * cells, BX)),
        near,
    )
    edges = []
    for pairs, edge in zip(ways, sent):
        edge = lax.ppermute(edge, "gy", pairs)
        corner = pl.pallas_call(
            corner_kernel,
            out_shape=shape((2 * depths, BX), bf16),
            in_specs=[VMEM, ANY],
            out_specs=VMEM,
            compiler_params=pltpu.CompilerParams(vmem_limit_bytes=4 * 2**20),
            name="corner",
        )(edge, prepared[-1])
        edges += [edge, lax.ppermute(corner, "col", swap)]
    near = lax.ppermute(near, "col", swap)

    fractions, solutes_next = pl.pallas_call(
        functools.partial(
            column_kernel,
            (count_gz, count_gy, depth, rows, columns, segment, slots, directions),
            few,
        ),
        out_shape=(
            shape((2, depth, rows, columns), bf16),
            shape((slots * 2 * cells, BX), f32),
        ),
        in_specs=[VMEM] * (few + 1 + len(edges) + 8),
        out_specs=(HBM, HBM),
        scratch_shapes=[
            pltpu.VMEM((2, 2 * depths, window), f32),
            pltpu.VMEM((segment * depth + 4, PART, 2 * window), bf16),
            pltpu.VMEM((segment * depth + 2, TALL, 2 * window), bf16),
            pltpu.VMEM((count_gz, brick_count, depth, 8, BX), f32),
            pltpu.VMEM((slots * 2 * cells, BX), f32),
            pltpu.VMEM((slots * 2 * cells, BX), f32),
            pltpu.VMEM((2, depth, rows, columns), bf16),
            pltpu.VMEM((count_gz, 8, BX), jnp.int32),
            pltpu.SMEM((count_gz, 8, BX), jnp.int32),
            pltpu.SMEM((slots + 1,), jnp.int32),
            pltpu.SemaphoreType.DMA((2,)),
            pltpu.SemaphoreType.DMA((slots // 8,)),
        ],
        compiler_params=pltpu.CompilerParams(vmem_limit_bytes=40 * 2**20),
        cost_estimate=pl.CostEstimate(
            flops=2 * depths * 2 * window * TALL * (4 * PART + 4 * 6 * HALF),
            bytes_accessed=4 * 2**20,
            transcendentals=0,
        ),
        name="column",
    )(
        *tiles,
        near,
        *edges,
        t1,
        t2,
        bias2,
        *prepared,
    )
    return fractions, solutes_next.reshape(solutes.shape)


def solution(mesh):
    sizes = (mesh.shape["gz"], mesh.shape["gy"], mesh.shape["col"])
    assert sizes[2] == 2
    return jax.shard_map(
        functools.partial(per_device, sizes),
        mesh=mesh,
        in_specs=(
            P(("cores", "gz"), "gy", "col"),
            P(),
            P(),
            P(),
            P(),
            P(("cores", "gz"), "gy", "col", None, None),
            P(("cores", "gz"), "gy", "col", None, None, None, None, None),
            P(("cores", "gz"), "gy", "col", None, None, None, None),
        ),
        out_specs=(
            P(None, ("cores", "gz"), "gy", "col"),
            P(("cores", "gz"), "gy", "col", None, None, None, None, None),
        ),
        check_vma=False,
    )
```

```python
import functools

import jax
import jax.numpy as jnp
from jax import lax
from jax.experimental import pallas as pl
from jax.experimental.pallas import tpu as pltpu
from jax.sharding import PartitionSpec as P

BY = 4
BX = 128
STEPS = 4
TILE = 16
HALF = 16
CHANNELS = 8
REACH = HALF + 2
PART = 3 * HALF + TILE
TALL = REACH * CHANNELS
ONE_ROW = 3 * HALF + 12
OUTSIDE = -1e30

VMEM = pl.BlockSpec(memory_space=pltpu.VMEM)
SMEM = pl.BlockSpec(memory_space=pltpu.SMEM)
ANY = pl.BlockSpec(memory_space=pl.ANY)
HBM = pl.BlockSpec(memory_space=pltpu.HBM)


def in_hbm(array):
    return pltpu.with_memory_space_constraint(array, pltpu.HBM)


def step_index(values, width, count):
    index = jnp.zeros(values.shape, jnp.int32)
    for k in range(1, count):
        index = index + (values >= k * width).astype(jnp.int32)
    return index


def one_hot(condition):
    return jnp.where(condition, 1.0, 0.0).astype(jnp.bfloat16)


def iotas(shape):
    return (
        lax.broadcasted_iota(jnp.int32, shape, 0),
        lax.broadcasted_iota(jnp.int32, shape, 1),
    )


def tap_parts(tap):
    dz = step_index(tap, 9, 3)
    dy = step_index(tap - 9 * dz, 3, 3)
    return dz, dy, tap - 9 * dz - 3 * dy


def pack_kernel(density_ref, owners_ref, payload_ref, named_ref, sems):
    height, columns = density_ref.shape
    blocks = columns // BX
    copies = [pltpu.make_async_copy(owners_ref, named_ref, sems.at[blocks])]
    for k in range(blocks):
        copies.append(
            pltpu.make_async_copy(
                density_ref.at[:, k * BX : (k + 1) * BX],
                payload_ref.at[k * height : (k + 1) * height],
                sems.at[k],
            )
        )
    for copy in copies:
        copy.start()
    copies[0].wait()
    named = named_ref[...].astype(jnp.float32)
    count = named.shape[1]
    payload_ref[blocks * height : blocks * height + TILE, :] = jnp.concatenate(
        [
            jnp.broadcast_to(named, (TILE, count)),
            jnp.zeros((TILE, BX - count), jnp.float32),
        ],
        axis=1,
    ).astype(jnp.bfloat16)
    for copy in copies[1:]:
        copy.wait()


def banded_kernel(*refs):
    sources, refs = refs[:4], refs[5:]
    t1_ref, t2_ref, bias2_ref, *local, sems = refs
    copies = [
        pltpu.make_async_copy(source, target, sems.at[k])
        for k, (source, target) in enumerate(zip(sources, local))
    ]
    for copy in copies:
        copy.start()
    for copy in copies:
        copy.wait()
    w1_ref, b1_ref, w2_ref, b2_ref = local
    row, channel = iotas((TALL, CHANNELS))
    spread = one_hot((row & (CHANNELS - 1)) == channel)
    w1 = jnp.dot(spread, w1_ref[...], preferred_element_type=jnp.float32).astype(jnp.bfloat16)
    tap, column = iotas((27, 4 * PART))
    dz = column >> 6
    place = column & (PART - 1)
    dx = jnp.where(place < 3 * HALF, place >> 4, (place - 3 * HALF) >> 2)
    base = 9 * dz + dx
    row, column = iotas((TALL, 4 * PART))
    place = column & (PART - 1)
    seam = (place - 3 * HALF) & 3
    seam_row = jnp.where(seam < 2, seam - 2, seam + HALF - 2)
    input_row = jnp.where(place < 3 * HALF, place & (HALF - 1), seam_row)
    distance = jnp.where(place < 3 * HALF + 12, input_row - (row >> 3) + 2, -1)
    bias = jnp.zeros((TALL, 4 * PART), jnp.float32)
    for k in range(CHANNELS):
        bias = jnp.where((row & (CHANNELS - 1)) == k, b1_ref[k], bias)
    high = bias.astype(jnp.bfloat16).astype(jnp.float32)
    middle = (bias - high).astype(jnp.bfloat16).astype(jnp.float32)
    constant = jnp.where(column == PART + ONE_ROW, high, 0.0)
    constant = jnp.where(column == 2 * PART + ONE_ROW, middle, constant)
    constant = jnp.where(column == 2 * PART - 1, bias - high - middle, constant)
    outside = ((column == PART + ONE_ROW + 1) & (row < CHANNELS)) | (
        (column == PART + ONE_ROW + 2) & (row >= TALL - CHANNELS)
    )
    constant = jnp.where(outside, OUTSIDE, constant)
    for out in range(2):
        total = constant
        for dy in range(3):
            pick = one_hot(tap == base - 9 * out + 3 * dy)
            values = jnp.dot(w1, pick, preferred_element_type=jnp.float32)
            total = jnp.where(distance == dy, values, total)
        t1_ref[out * TALL : (out + 1) * TALL, :] = total.astype(jnp.bfloat16)
    channel, column = iotas((CHANNELS, 4 * TALL))
    spread = one_hot((column & (CHANNELS - 1)) == channel)
    tap, column = iotas((27, 4 * TALL))
    tap_z, slice_z = tap_parts(tap)[0], step_index(column, TALL, 4)
    row, tap = iotas((6 * HALF, 27))
    _, tap_y, tap_x = tap_parts(tap)
    same_x = (row >> 5) == tap_x
    wide = [
        lax.dot_general(
            w2_ref[o * CHANNELS : (o + 1) * CHANNELS, :],
            spread,
            (((0,), (0,)), ((), ())),
            preferred_element_type=jnp.float32,
        )
        for o in range(2)
    ]
    picks = [
        [one_hot(same_x & (tap_y == dy) & (((row >> 2) & 1) == o)) for o in range(2)]
        for dy in range(3)
    ]
    out_row, column = iotas((6 * HALF, 4 * TALL))
    y = ((out_row >> 3) & 3) * BY + (out_row & 3)
    distance = ((column - TALL * step_index(column, TALL, 4)) >> 3) - y
    for out in range(2):
        same_z = tap_z == slice_z - out
        terms = [jnp.where(same_z, values, 0.0).astype(jnp.bfloat16) for values in wide]
        total = jnp.zeros((6 * HALF, 4 * TALL), jnp.float32)
        for dy in range(3):
            values = 0.0
            for o in range(2):
                values = values + jnp.dot(
                    picks[dy][o], terms[o], preferred_element_type=jnp.float32
                )
            total = jnp.where(distance == dy, values, total)
        t2_ref[out * 6 * HALF : (out + 1) * 6 * HALF, :] = (0.5 * total).astype(jnp.bfloat16)
    row, _ = iotas((2 * HALF, BX))
    bias2_ref[...] = 0.5 * jnp.where(((row >> 2) & 1) == 0, b2_ref[0], b2_ref[1])


def edges_kernel(dims, *refs):
    count_gy, depth, rows, columns, few, count = dims
    tiles, outs = refs[:few], refs[few + 1 :]
    g = lax.axis_index("gy")
    c = lax.axis_index("col")
    height = depth * rows
    block = (1 - c) * height

    def take(i, start, size):
        start = pl.ds(pl.multiple_of(start, TILE), size)
        if few > 1:
            return tiles[i][start, :]
        return tiles[0][i, start, :]

    def pair(i):
        for k in range(2):
            at = pl.multiple_of((2 * i + k) * height, TILE)
            outs[0][pl.ds(at, height), :] = take(2 * i + k, block, height)
        low, high = [], []
        for k in range(2):
            for zz in range(depth):
                first, last = [], []
                for base in (0, height):
                    at = base + zz * rows
                    first.append(take(2 * i + k, at, TILE).astype(jnp.float32)[0:2])
                    at = at + rows - TILE
                    last.append(take(2 * i + k, at, TILE).astype(jnp.float32)[TILE - 2 :])
                low.append(jnp.concatenate(first, axis=1))
                high.append(jnp.concatenate(last, axis=1))
        at = pl.multiple_of(2 * i * 2 * depth, TILE)
        first, last = jnp.concatenate(low, axis=0), jnp.concatenate(high, axis=0)
        sends = [jnp.where(g == 0, last, first)] if count_gy == 2 else [last, first]
        for n, send in enumerate(sends):
            send = send.astype(jnp.bfloat16)
            outs[1 + n][pl.ds(at, TILE), :] = send

    if few > 1:
        for i in range(count // 2):
            pair(i)
    else:
        pl.loop(0, count // 2)(pair)


def corner_kernel(edge_ref, _, corner_ref):
    c = lax.axis_index("col")
    corner_ref[...] = jnp.where(c == 0, edge_ref[:, BX:], edge_ref[:, 0:BX])


def laplace(field, z, y):
    centre = field[z][y]
    last = lax.broadcasted_iota(jnp.int32, centre.shape, 1) == BX - 1
    ahead = jnp.where(last, 0.0, pltpu.roll(centre, BX - 1, 1) - centre)
    result = ahead - pltpu.roll(ahead, 1, 1)
    beside = [
        field[zz][yy]
        for zz, yy in ((z - 1, y), (z + 1, y), (z, y - 1), (z, y + 1))
        if 0 <= zz < len(field) and 0 <= yy < BY
    ]
    return result + (functools.reduce(jnp.add, beside) - float(len(beside)) * centre)


def uptake_of(quarter, doc, oxy):
    return quarter * doc * oxy / ((0.5 + jnp.abs(doc)) * (0.3 + jnp.abs(oxy)))


def prepare_kernel(dims, solutes_ref, biomass_ref, _, *refs):
    depth, slots = dims
    outs, (state, biomass, mass, sems) = refs[:5], refs[5:]
    size = depth * BY
    copies = []
    for group in range(slots // 8):
        for k, (source, target) in enumerate(((solutes_ref, state), (biomass_ref, biomass))):
            rows = (2 - k) * 8 * size
            at = pl.ds(group * rows, rows)
            copies.append(
                pltpu.make_async_copy(source.at[at], target.at[at], sems.at[group, k])
            )
    for copy in copies:
        copy.start()
    for group in range(slots // 8):
        copies[2 * group].wait()
        copies[2 * group + 1].wait()
        at = slice(group * 8 * size, (group + 1) * 8 * size)
        mass[at, :] = biomass[at, :].astype(jnp.float32)

        def rows_of(pitch, offset):
            return pl.ds(group * 8 * pitch + offset, 8, stride=pitch)

        grid = [(z, y) for z in range(depth) for y in range(BY)]
        carbon, oxygen = [
            [
                [state[rows_of(2 * size, k * size + z * BY + y), :] for y in range(BY)]
                for z in range(depth)
            ]
            for k in range(2)
        ]
        for z, y in grid:
            at = group * 8 * size + (z * BY + y) * 8
            at = slice(at, at + 8)
            doc, oxy = carbon[z][y], oxygen[z][y]
            quarter = 0.25 * mass[rows_of(size, z * BY + y), :]
            uptake = uptake_of(quarter, doc, oxy)
            values = (
                doc - uptake,
                oxy - uptake,
                laplace(carbon, z, y),
                laplace(oxygen, z, y),
                quarter,
            )
            for out, value in zip(outs, values):
                out[at, :] = value


def column_kernel(dims, few, *refs):
    count_gz, count_gy, depth, rows, columns, segment, slots, directions = dims
    tiles, refs = refs[:few], refs[few:]
    x_ref, refs = refs[0], refs[1:]
    top_refs, refs = refs[:2], refs[2:]
    if directions == 1:
        bottom_refs = top_refs
    else:
        bottom_refs, refs = refs[:2], refs[2:]
    t1_ref, t2_ref, bias2_ref, *refs = refs
    carbon_ref, oxygen_ref, carbon_around_ref, oxygen_around_ref, quarter_ref, *refs = refs
    fractions_ref, next_ref, *refs = refs
    (
        edge_rows,
        shifted,
        hidden,
        bricks,
        arrived,
        state,
        fractions,
        owner_rows,
        owner_table,
        brick_of_slot,
        sems,
        group_sems,
    ) = refs
    z_index = lax.axis_index("gz")
    g = lax.axis_index("gy")
    c = lax.axis_index("col")
    window = columns + BX
    brick_rows = HALF // BY
    brick_columns = columns // BX
    brick_count = rows // BY * brick_columns
    capacity = slots // count_gz
    single = segment == count_gz

    def tile_of(i):
        return jnp.bitwise_xor(z_index, i) if few > 1 else i

    size = depth * BY

    def tile_rows(i, start, size):
        if not isinstance(start, int):
            start = pl.multiple_of(start, TILE)
        if few > 1:
            return tiles[i][pl.ds(start, size), :]
        return tiles[0][i, pl.ds(start, size), :]

    def read_owners(i):
        row = tile_rows(i, brick_columns * depth * rows, TILE)
        owner_rows[i] = row.astype(jnp.float32)[0:8].astype(jnp.int32)

    if few > 1:
        for i in range(count_gz):
            read_owners(i)
    else:
        pl.loop(0, count_gz)(read_owners)
    table_copy = pltpu.make_async_copy(owner_rows, owner_table, sems.at[0])
    table_copy.start()

    def arrange(left, right, other):
        return jnp.concatenate(
            [
                jnp.where(c == 0, left, other),
                jnp.where(c == 0, right, left),
                jnp.where(c == 0, other, right),
            ],
            axis=1,
        )

    for k, pair in enumerate((top_refs, bottom_refs)):
        exists = (g > 0) if k == 0 else (g < count_gy - 1)
        own, other = pair[0][...].astype(jnp.float32), pair[1][...].astype(jnp.float32)
        values = arrange(own[:, 0:BX], own[:, BX:columns], other)
        edge_rows[k] = values * exists.astype(jnp.float32)

    def moved(values):
        lane = lax.broadcasted_iota(jnp.int32, values.shape, 1)
        left = jnp.where(lane == 0, 0.0, pltpu.roll(values, 1, 1))
        right = jnp.where(lane == window - 1, 0.0, pltpu.roll(values, window - 1, 1))
        return left.astype(values.dtype), values, right.astype(values.dtype)

    def edge_pair(k, at):
        if isinstance(at, int):
            return edge_rows[k, at : at + 2, :]
        group = edge_rows[k, pl.ds(pl.multiple_of(at // 8 * 8, 8), 8), :]
        return pltpu.roll(group, lax.rem(8 - at % 8, 8), 0)[0:2]

    row, _ = iotas((4, window))
    constants = [
        jnp.where((row == 0) | (row == 3), 1.0, jnp.where((row == 1 + h) & beyond, 1.0, 0.0))
        for h, beyond in enumerate((g == 0, g == count_gy - 1))
    ]

    def shifts(i, zz, slot, valid):
        z = i * depth + zz
        halves = []
        for h in range(2):
            at = zz * rows + h * HALF
            own = [tile_rows(i, k * depth * rows + at, HALF) for k in range(2)]
            at = z * rows + h * HALF
            if not isinstance(at, int):
                at = pl.multiple_of(at, TILE)
            values = arrange(*own, x_ref[pl.ds(at, HALF), :]).astype(jnp.float32)
            halves.append(values if valid is None else values * valid)
        top, bottom = edge_pair(0, 2 * z), edge_pair(1, 2 * z)
        if valid is not None:
            top, bottom = top * valid, bottom * valid
        seams = [
            jnp.concatenate([top, halves[1][0:2]], axis=0),
            jnp.concatenate([halves[0][HALF - 2 :], bottom], axis=0),
        ]
        for h in range(2):
            lanes = slice(h * window, (h + 1) * window)
            for dx, values in enumerate(moved(halves[h])):
                shifted[slot, dx * HALF : (dx + 1) * HALF, lanes] = values.astype(jnp.bfloat16)
            values = jnp.concatenate(
                [*moved(seams[h]), constants[h]], axis=0
            )
            shifted[slot, 3 * HALF : PART, lanes] = values.astype(jnp.bfloat16)

    def first(z, valid):
        total = jnp.dot(
            t1_ref[...],
            shifted[pl.ds(z + 1, 4)].reshape(4 * PART, 2 * window),
            preferred_element_type=jnp.float32,
        )
        for out in range(2):
            values = jnp.maximum(total[out * TALL : (out + 1) * TALL], 0.0)
            if valid is not None:
                values = values * valid(z + out)
            hidden[z + 1 + out] = values.astype(jnp.bfloat16)

    height = 2 * HALF
    _, lane = iotas((height, BX))

    def second(z, tile):
        total = jnp.dot(
            t2_ref[...],
            hidden[pl.ds(z, 4)].reshape(4 * TALL, 2 * window),
            preferred_element_type=jnp.float32,
        )
        for out in range(2):
            at = z + out
            place(total[3 * height * out : 3 * height * (out + 1)], tile + at // depth, at % depth)

    def place(total, t, zz):
        blocks = window // BX
        for h in range(2):
            part = [total[:, k * BX : (k + 1) * BX] for k in range(h * blocks, (h + 1) * blocks)]
            left = [0.0] + [pltpu.roll(block[0:height], 1, 1) for block in part]
            right = [pltpu.roll(block[2 * height :], BX - 1, 1) for block in part] + [0.0]
            sums = [
                part[k][height : 2 * height]
                + (
                    jnp.where(lane == 0, left[k], left[k + 1])
                    + jnp.where(lane == BX - 1, right[k + 1], right[k])
                )
                for k in range(blocks)
            ]
            for xb in range(brick_columns):
                own = jnp.where(c == 0, sums[xb], sums[xb + 1]) + bias2_ref[...]
                values = 0.5 + 0.5 * jnp.tanh(own)
                for yb in range(brick_rows):
                    b = (h * brick_rows + yb) * brick_columns + xb
                    bricks[t, b, zz] = values[yb * 8 : yb * 8 + 8]

    def valid_slice(z):
        return ((z >= 0) & (z < count_gz * depth)).astype(jnp.float32)

    depths = segment * depth
    if single:
        shifted[1] = jnp.zeros((PART, 2 * window), jnp.bfloat16)
        shifted[depths + 2] = jnp.zeros((PART, 2 * window), jnp.bfloat16)
        hidden[0] = jnp.zeros((TALL, 2 * window), jnp.bfloat16)
        hidden[depths + 1] = jnp.zeros((TALL, 2 * window), jnp.bfloat16)
        for i in range(count_gz):
            tile = tile_of(i)
            for zz in range(depth):
                shifts(i, zz, tile * depth + zz + 2, None)

        @pl.loop(0, depths // 2, unroll=8)
        def _(k):
            first(2 * k, None)

        @pl.loop(0, depths // 2, unroll=8)
        def _(k):
            second(2 * k, 0)

    else:

        @pl.loop(0, count_gz // segment)
        def _(q):
            @pl.loop(-2, depths + 2)
            def _(z):
                at = q * depths + z
                inside = jnp.clip(at, 0, count_gz * depth - 1)
                shifts(inside // depth, inside % depth, z + 2, valid_slice(at))

            @pl.loop(0, depths // 2 + 1)
            def _(k):
                first(2 * k - 1, lambda z: valid_slice(q * depths + z))

            @pl.loop(0, depths // 2)
            def _(k):
                second(2 * k, q * segment)

    for zz in range(depth):
        for xb in range(brick_columns):
            own = [
                bricks[z_index, yb * brick_columns + xb, zz] for yb in range(rows // BY)
            ]
            for o in range(2):
                values = jnp.concatenate([v[o * BY : o * BY + BY] for v in own], axis=0)
                fractions[o, zz, :, xb * BX : (xb + 1) * BX] = values.astype(jnp.bfloat16)
    fractions_copy = pltpu.make_async_copy(fractions, fractions_ref, sems.at[1])
    fractions_copy.start()

    table_copy.wait()
    for j in range(slots):
        brick_of_slot[j] = -1

    @pl.loop(0, count_gz)
    def _(i):
        first = tile_of(i) * capacity
        rank = jnp.int32(0)
        for b in range(brick_count):
            mine = owner_table[i, 0, b] == z_index
            brick_of_slot[jnp.where(mine, first + rank, slots)] = b
            rank = rank + mine.astype(jnp.int32)

    @pl.loop(0, slots, unroll=8)
    def _(j):
        brick = brick_of_slot[j]
        values = bricks[j // capacity, jnp.maximum(brick, 0)]
        values = jnp.where(brick >= 0, values, 0.0).astype(jnp.bfloat16).astype(jnp.float32)
        at = pl.multiple_of(j * (2 * size), 8)
        arrived[pl.ds(at, 2 * size), :] = values.reshape(2 * size, BX)

    def next_copy(group):
        at = pl.ds(pl.multiple_of(group * 16 * size, 16 * size), 16 * size)
        return pltpu.make_async_copy(state.at[at], next_ref.at[at], group_sems.at[group])

    @pl.loop(0, slots // 8)
    def _(group):
        grid = [(z, y) for z in range(depth) for y in range(BY)]

        def load(ref):
            base = group * (8 * size)
            return [
                [
                    ref[pl.ds(pl.multiple_of(base + (z * BY + y) * 8, 8), 8), :]
                    for y in range(BY)
                ]
                for z in range(depth)
            ]

        def rows_of(offset):
            return pl.ds(group * 16 * size + offset, 8, stride=2 * size)

        quarter = load(quarter_ref)
        pore = [[arrived[rows_of(z * 8 + y), :] for y in range(BY)] for z in range(depth)]
        organic = [
            [0.3 * arrived[rows_of(z * 8 + BY + y), :] for y in range(BY)] for z in range(depth)
        ]
        slow = [[0.12 * p for p in row] for row in pore]
        fast = [[0.16 * p for p in row] for row in pore]
        carbon, oxygen = load(carbon_ref), load(oxygen_ref)
        around = load(carbon_around_ref), load(oxygen_around_ref)
        for z, y in grid:
            carbon[z][y] += slow[z][y] * around[0][z][y] + organic[z][y]
            oxygen[z][y] += fast[z][y] * around[1][z][y]
        for _ in range(STEPS - 1):
            carbon_new = [[None] * BY for _ in range(depth)]
            oxygen_new = [[None] * BY for _ in range(depth)]
            for z, y in grid:
                doc, oxy = carbon[z][y], oxygen[z][y]
                uptake = uptake_of(quarter[z][y], doc, oxy)
                gain = organic[z][y] - uptake
                carbon_new[z][y] = doc + slow[z][y] * laplace(carbon, z, y) + gain
                oxygen_new[z][y] = oxy + fast[z][y] * laplace(oxygen, z, y) - uptake
            carbon, oxygen = carbon_new, oxygen_new
        for z, y in grid:
            state[rows_of(z * BY + y), :] = carbon[z][y]
            state[rows_of(size + z * BY + y), :] = oxygen[z][y]
        next_copy(group).start()

    @pl.loop(0, slots // 8)
    def _(group):
        next_copy(group).wait()

    fractions_copy.wait()


def per_device(
    sizes, density, first_kernel, first_bias, second_kernel, second_bias, owners, solutes, biomass
):
    count_gz, count_gy, count_col = sizes
    depth, rows, columns = density.shape
    slots = solutes.shape[3]
    window = columns + BX
    segment = min(count_gz, 4)
    brick_count = (rows // BY) * (columns // BX)
    height = depth * rows
    depths = count_gz * depth
    bf16, f32 = jnp.bfloat16, jnp.float32
    shape = jax.ShapeDtypeStruct

    payload = pl.pallas_call(
        pack_kernel,
        out_shape=shape((columns // BX * height + TILE, BX), bf16),
        in_specs=[HBM, HBM],
        out_specs=VMEM,
        scratch_shapes=[
            pltpu.VMEM((1, brick_count), jnp.int32),
            pltpu.SemaphoreType.DMA((columns // BX + 1,)),
        ],
        compiler_params=pltpu.CompilerParams(vmem_limit_bytes=4 * 2**20),
        name="pack",
    )(in_hbm(density.reshape(height, columns)), in_hbm(owners.reshape(1, brick_count)))

    few = count_gz if count_gz in (2, 4) else 1
    if few > 1:
        tiles = [payload] + [
            lax.ppermute(payload, "gz", [(i, i ^ s) for i in range(count_gz)])
            for s in range(1, count_gz)
        ]
    else:
        tiles = [lax.all_gather(payload, "gz", axis=0, tiled=False)]

    cells = depth * BY
    t1, t2, bias2 = pl.pallas_call(
        banded_kernel,
        out_shape=(
            shape((2 * TALL, 4 * PART), bf16),
            shape((12 * HALF, 4 * TALL), bf16),
            shape((2 * HALF, BX), f32),
        ),
        in_specs=[HBM, HBM, HBM, HBM, ANY],
        out_specs=(VMEM, VMEM, VMEM),
        scratch_shapes=[
            pltpu.VMEM((CHANNELS, 27), bf16),
            pltpu.SMEM((CHANNELS,), f32),
            pltpu.VMEM((2 * CHANNELS, 27), bf16),
            pltpu.SMEM((2,), f32),
            pltpu.SemaphoreType.DMA((4,)),
        ],
        compiler_params=pltpu.CompilerParams(vmem_limit_bytes=16 * 2**20),
        cost_estimate=pl.CostEstimate(
            flops=20 * 2**20, bytes_accessed=4 * 2**20, transcendentals=0
        ),
        name="banded",
    )(
        in_hbm(first_kernel.transpose(2, 1, 0).reshape(CHANNELS, 27)),
        in_hbm(first_bias),
        in_hbm(second_kernel.transpose(1, 2, 0).reshape(2 * CHANNELS, 27)),
        in_hbm(second_bias),
        payload,
    )

    if count_gy == 2:
        ways = [[(0, 1), (1, 0)]]
    else:
        up = [(i, i + 1) for i in range(count_gy - 1)]
        ways = [up, [(j, i) for i, j in up]]
    directions = len(ways)
    swap = [(0, 1), (1, 0)]
    near, *sent = pl.pallas_call(
        functools.partial(edges_kernel, (count_gy, depth, rows, columns, few, count_gz)),
        out_shape=[shape((depths * rows, BX), bf16)]
        + [shape((2 * depths, columns), bf16)] * directions,
        in_specs=[VMEM] * few + [ANY],
        out_specs=[VMEM] * (1 + directions),
        compiler_params=pltpu.CompilerParams(vmem_limit_bytes=16 * 2**20),
        name="edges",
    )(*tiles, bias2)
    prepared = pl.pallas_call(
        functools.partial(prepare_kernel, (depth, slots)),
        out_shape=[shape((slots * cells, BX), f32)] * 5,
        in_specs=[HBM, HBM, ANY],
        out_specs=[VMEM] * 5,
        scratch_shapes=[
            pltpu.VMEM((slots * 2 * cells, BX), f32),
            pltpu.VMEM((slots * cells, BX), bf16),
            pltpu.VMEM((slots * cells, BX), f32),
            pltpu.SemaphoreType.DMA((slots // 8, 2)),
        ],
        compiler_params=pltpu.CompilerParams(vmem_limit_bytes=12 * 2**20),
        cost_estimate=pl.CostEstimate(
            flops=60 * slots * cells * BX, bytes_accessed=2**20, transcendentals=0
        ),
        name="prepare",
    )(
        in_hbm(solutes.reshape(slots * 2 * cells, BX)),
        in_hbm(biomass.reshape(slots * cells, BX)),
        near,
    )
    edges = []
    for pairs, edge in zip(ways, sent):
        edge = lax.ppermute(edge, "gy", pairs)
        corner = pl.pallas_call(
            corner_kernel,
            out_shape=shape((2 * depths, BX), bf16),
            in_specs=[VMEM, ANY],
            out_specs=VMEM,
            compiler_params=pltpu.CompilerParams(vmem_limit_bytes=4 * 2**20),
            name="corner",
        )(edge, prepared[-1])
        edges += [edge, lax.ppermute(corner, "col", swap)]
    near = lax.ppermute(near, "col", swap)

    fractions, solutes_next = pl.pallas_call(
        functools.partial(
            column_kernel,
            (count_gz, count_gy, depth, rows, columns, segment, slots, directions),
            few,
        ),
        out_shape=(
            shape((2, depth, rows, columns), bf16),
            shape((slots * 2 * cells, BX), f32),
        ),
        in_specs=[VMEM] * (few + 1 + len(edges) + 8),
        out_specs=(HBM, HBM),
        scratch_shapes=[
            pltpu.VMEM((2, 2 * depths, window), f32),
            pltpu.VMEM((segment * depth + 4, PART, 2 * window), bf16),
            pltpu.VMEM((segment * depth + 2, TALL, 2 * window), bf16),
            pltpu.VMEM((count_gz, brick_count, depth, 8, BX), f32),
            pltpu.VMEM((slots * 2 * cells, BX), f32),
            pltpu.VMEM((slots * 2 * cells, BX), f32),
            pltpu.VMEM((2, depth, rows, columns), bf16),
            pltpu.VMEM((count_gz, 8, BX), jnp.int32),
            pltpu.SMEM((count_gz, 8, BX), jnp.int32),
            pltpu.SMEM((slots + 1,), jnp.int32),
            pltpu.SemaphoreType.DMA((2,)),
            pltpu.SemaphoreType.DMA((slots // 8,)),
        ],
        compiler_params=pltpu.CompilerParams(vmem_limit_bytes=40 * 2**20),
        cost_estimate=pl.CostEstimate(
            flops=2 * depths * 2 * window * TALL * (4 * PART + 4 * 6 * HALF),
            bytes_accessed=4 * 2**20,
            transcendentals=0,
        ),
        name="column",
    )(
        *tiles,
        near,
        *edges,
        t1,
        t2,
        bias2,
        *prepared,
    )
    return fractions, solutes_next.reshape(solutes.shape)


def solution(mesh):
    sizes = (mesh.shape["gz"], mesh.shape["gy"], mesh.shape["col"])
    assert sizes[2] == 2
    return jax.shard_map(
        functools.partial(per_device, sizes),
        mesh=mesh,
        in_specs=(
            P(("cores", "gz"), "gy", "col"),
            P(),
            P(),
            P(),
            P(),
            P(("cores", "gz"), "gy", "col", None, None),
            P(("cores", "gz"), "gy", "col", None, None, None, None, None),
            P(("cores", "gz"), "gy", "col", None, None, None, None),
        ),
        out_specs=(
            P(None, ("cores", "gz"), "gy", "col"),
            P(("cores", "gz"), "gy", "col", None, None, None, None, None),
        ),
        check_vma=False,
    )
```

```python
import functools

import jax
import jax.numpy as jnp
from jax import lax
from jax.experimental import pallas as pl
from jax.experimental.pallas import tpu as pltpu
from jax.sharding import PartitionSpec as P

BY = 4
BX = 128
STEPS = 4
TILE = 16
HALF = 16
CHANNELS = 8
REACH = HALF + 2
PART = 3 * HALF + TILE
TALL = REACH * CHANNELS
ONE_ROW = 3 * HALF + 12
OUTSIDE = -1e30

VMEM = pl.BlockSpec(memory_space=pltpu.VMEM)
SMEM = pl.BlockSpec(memory_space=pltpu.SMEM)
ANY = pl.BlockSpec(memory_space=pl.ANY)
HBM = pl.BlockSpec(memory_space=pltpu.HBM)


def in_hbm(array):
    return pltpu.with_memory_space_constraint(array, pltpu.HBM)


def step_index(values, width, count):
    index = jnp.zeros(values.shape, jnp.int32)
    for k in range(1, count):
        index = index + (values >= k * width).astype(jnp.int32)
    return index


def one_hot(condition):
    return jnp.where(condition, 1.0, 0.0).astype(jnp.bfloat16)


def iotas(shape):
    return (
        lax.broadcasted_iota(jnp.int32, shape, 0),
        lax.broadcasted_iota(jnp.int32, shape, 1),
    )


def tap_parts(tap):
    dz = step_index(tap, 9, 3)
    dy = step_index(tap - 9 * dz, 3, 3)
    return dz, dy, tap - 9 * dz - 3 * dy


def pack_kernel(density_ref, owners_ref, payload_ref, named_ref, sems):
    height, columns = density_ref.shape
    blocks = columns // BX
    copies = [pltpu.make_async_copy(owners_ref, named_ref, sems.at[blocks])]
    for k in range(blocks):
        copies.append(
            pltpu.make_async_copy(
                density_ref.at[:, k * BX : (k + 1) * BX],
                payload_ref.at[k * height : (k + 1) * height],
                sems.at[k],
            )
        )
    for copy in copies:
        copy.start()
    copies[0].wait()
    named = named_ref[...].astype(jnp.float32)
    count = named.shape[1]
    payload_ref[blocks * height : blocks * height + TILE, :] = jnp.concatenate(
        [
            jnp.broadcast_to(named, (TILE, count)),
            jnp.zeros((TILE, BX - count), jnp.float32),
        ],
        axis=1,
    ).astype(jnp.bfloat16)
    for copy in copies[1:]:
        copy.wait()


def banded_kernel(*refs):
    sources, refs = refs[:4], refs[5:]
    t1_ref, t2_ref, bias2_ref, *local, sems = refs
    copies = [
        pltpu.make_async_copy(source, target, sems.at[k])
        for k, (source, target) in enumerate(zip(sources, local))
    ]
    for copy in copies:
        copy.start()
    for copy in copies:
        copy.wait()
    w1_ref, b1_ref, w2_ref, b2_ref = local
    row, channel = iotas((TALL, CHANNELS))
    spread = one_hot((row & (CHANNELS - 1)) == channel)
    w1 = jnp.dot(spread, w1_ref[...], preferred_element_type=jnp.float32).astype(jnp.bfloat16)
    tap, column = iotas((27, 4 * PART))
    dz = column >> 6
    place = column & (PART - 1)
    dx = jnp.where(place < 3 * HALF, place >> 4, (place - 3 * HALF) >> 2)
    base = 9 * dz + dx
    row, column = iotas((TALL, 4 * PART))
    place = column & (PART - 1)
    seam = (place - 3 * HALF) & 3
    seam_row = jnp.where(seam < 2, seam - 2, seam + HALF - 2)
    input_row = jnp.where(place < 3 * HALF, place & (HALF - 1), seam_row)
    distance = jnp.where(place < 3 * HALF + 12, input_row - (row >> 3) + 2, -1)
    bias = jnp.zeros((TALL, 4 * PART), jnp.float32)
    for k in range(CHANNELS):
        bias = jnp.where((row & (CHANNELS - 1)) == k, b1_ref[k], bias)
    high = bias.astype(jnp.bfloat16).astype(jnp.float32)
    middle = (bias - high).astype(jnp.bfloat16).astype(jnp.float32)
    constant = jnp.where(column == PART + ONE_ROW, high, 0.0)
    constant = jnp.where(column == 2 * PART + ONE_ROW, middle, constant)
    constant = jnp.where(column == 2 * PART - 1, bias - high - middle, constant)
    outside = ((column == PART + ONE_ROW + 1) & (row < CHANNELS)) | (
        (column == PART + ONE_ROW + 2) & (row >= TALL - CHANNELS)
    )
    constant = jnp.where(outside, OUTSIDE, constant)
    for out in range(2):
        total = constant
        for dy in range(3):
            pick = one_hot(tap == base - 9 * out + 3 * dy)
            values = jnp.dot(w1, pick, preferred_element_type=jnp.float32)
            total = jnp.where(distance == dy, values, total)
        t1_ref[out * TALL : (out + 1) * TALL, :] = total.astype(jnp.bfloat16)
    channel, column = iotas((CHANNELS, 4 * TALL))
    spread = one_hot((column & (CHANNELS - 1)) == channel)
    tap, column = iotas((27, 4 * TALL))
    tap_z, slice_z = tap_parts(tap)[0], step_index(column, TALL, 4)
    row, tap = iotas((6 * HALF, 27))
    _, tap_y, tap_x = tap_parts(tap)
    same_x = (row >> 5) == tap_x
    wide = [
        lax.dot_general(
            w2_ref[o * CHANNELS : (o + 1) * CHANNELS, :],
            spread,
            (((0,), (0,)), ((), ())),
            preferred_element_type=jnp.float32,
        )
        for o in range(2)
    ]
    picks = [
        [one_hot(same_x & (tap_y == dy) & (((row >> 2) & 1) == o)) for o in range(2)]
        for dy in range(3)
    ]
    out_row, column = iotas((6 * HALF, 4 * TALL))
    y = ((out_row >> 3) & 3) * BY + (out_row & 3)
    distance = ((column - TALL * step_index(column, TALL, 4)) >> 3) - y
    for out in range(2):
        same_z = tap_z == slice_z - out
        terms = [jnp.where(same_z, values, 0.0).astype(jnp.bfloat16) for values in wide]
        total = jnp.zeros((6 * HALF, 4 * TALL), jnp.float32)
        for dy in range(3):
            values = 0.0
            for o in range(2):
                values = values + jnp.dot(
                    picks[dy][o], terms[o], preferred_element_type=jnp.float32
                )
            total = jnp.where(distance == dy, values, total)
        t2_ref[out * 6 * HALF : (out + 1) * 6 * HALF, :] = (0.5 * total).astype(jnp.bfloat16)
    row, _ = iotas((2 * HALF, BX))
    bias2_ref[...] = 0.5 * jnp.where(((row >> 2) & 1) == 0, b2_ref[0], b2_ref[1])


def edges_kernel(dims, *refs):
    count_gy, depth, rows, columns, few, count = dims
    tiles, outs = refs[:few], refs[few + 2 :]
    g = lax.axis_index("gy")
    c = lax.axis_index("col")
    height = depth * rows
    block = (1 - c) * height

    def take(i, start, size):
        start = pl.ds(pl.multiple_of(start, TILE), size)
        if few > 1:
            return tiles[i][start, :]
        return tiles[0][i, start, :]

    def pair(i):
        for k in range(2):
            at = pl.multiple_of((2 * i + k) * height, TILE)
            outs[0][pl.ds(at, height), :] = take(2 * i + k, block, height)
        low, high = [], []
        for k in range(2):
            for zz in range(depth):
                first, last = [], []
                for base in (0, height):
                    at = base + zz * rows
                    first.append(take(2 * i + k, at, TILE).astype(jnp.float32)[0:2])
                    at = at + rows - TILE
                    last.append(take(2 * i + k, at, TILE).astype(jnp.float32)[TILE - 2 :])
                low.append(jnp.concatenate(first, axis=1))
                high.append(jnp.concatenate(last, axis=1))
        at = pl.multiple_of(2 * i * 2 * depth, TILE)
        first, last = jnp.concatenate(low, axis=0), jnp.concatenate(high, axis=0)
        sends = [jnp.where(g == 0, last, first)] if count_gy == 2 else [last, first]
        for n, send in enumerate(sends):
            send = send.astype(jnp.bfloat16)
            outs[1 + n][pl.ds(at, TILE), :] = send

    if few > 1:
        for i in range(count // 2):
            pair(i)
    else:
        pl.loop(0, count // 2)(pair)


def corner_kernel(edge_ref, corner_ref):
    c = lax.axis_index("col")
    corner_ref[...] = jnp.where(c == 0, edge_ref[:, BX:], edge_ref[:, 0:BX])


def laplace(field, z, y):
    centre = field[z][y]
    last = lax.broadcasted_iota(jnp.int32, centre.shape, 1) == BX - 1
    ahead = jnp.where(last, 0.0, pltpu.roll(centre, BX - 1, 1) - centre)
    result = ahead - pltpu.roll(ahead, 1, 1)
    beside = [
        field[zz][yy]
        for zz, yy in ((z - 1, y), (z + 1, y), (z, y - 1), (z, y + 1))
        if 0 <= zz < len(field) and 0 <= yy < BY
    ]
    return result + (functools.reduce(jnp.add, beside) - float(len(beside)) * centre)


def uptake_of(quarter, doc, oxy):
    return quarter * doc * oxy / ((0.5 + jnp.abs(doc)) * (0.3 + jnp.abs(oxy)))


def prepare_kernel(dims, solutes_ref, biomass_ref, _, *refs):
    depth, slots = dims
    outs, (state, biomass, mass, sems) = refs[:5], refs[5:]
    size = depth * BY
    copies = []
    for group in range(slots // 8):
        for k, (source, target) in enumerate(((solutes_ref, state), (biomass_ref, biomass))):
            rows = (2 - k) * 8 * size
            at = pl.ds(group * rows, rows)
            copies.append(
                pltpu.make_async_copy(source.at[at], target.at[at], sems.at[group, k])
            )
    for copy in copies:
        copy.start()
    for group in range(slots // 8):
        copies[2 * group].wait()
        copies[2 * group + 1].wait()
        at = slice(group * 8 * size, (group + 1) * 8 * size)
        mass[at, :] = biomass[at, :].astype(jnp.float32)

        def rows_of(pitch, offset):
            return pl.ds(group * 8 * pitch + offset, 8, stride=pitch)

        grid = [(z, y) for z in range(depth) for y in range(BY)]
        carbon, oxygen = [
            [
                [state[rows_of(2 * size, k * size + z * BY + y), :] for y in range(BY)]
                for z in range(depth)
            ]
            for k in range(2)
        ]
        for z, y in grid:
            at = group * 8 * size + (z * BY + y) * 8
            at = slice(at, at + 8)
            doc, oxy = carbon[z][y], oxygen[z][y]
            quarter = 0.25 * mass[rows_of(size, z * BY + y), :]
            uptake = uptake_of(quarter, doc, oxy)
            values = (
                doc - uptake,
                oxy - uptake,
                laplace(carbon, z, y),
                laplace(oxygen, z, y),
                quarter,
            )
            for out, value in zip(outs, values):
                out[at, :] = value


def column_kernel(dims, few, *refs):
    count_gz, count_gy, depth, rows, columns, segment, slots, directions = dims
    tiles, refs = refs[:few], refs[few:]
    x_ref, refs = refs[0], refs[1:]
    top_refs, refs = refs[:2], refs[2:]
    if directions == 1:
        bottom_refs = top_refs
    else:
        bottom_refs, refs = refs[:2], refs[2:]
    t1_ref, t2_ref, bias2_ref, *refs = refs
    carbon_ref, oxygen_ref, carbon_around_ref, oxygen_around_ref, quarter_ref, *refs = refs
    fractions_ref, next_ref, *refs = refs
    (
        edge_rows,
        shifted,
        hidden,
        bricks,
        arrived,
        state,
        fractions,
        owner_rows,
        owner_table,
        brick_of_slot,
        sems,
        group_sems,
    ) = refs
    z_index = lax.axis_index("gz")
    g = lax.axis_index("gy")
    c = lax.axis_index("col")
    window = columns + BX
    brick_rows = HALF // BY
    brick_columns = columns // BX
    brick_count = rows // BY * brick_columns
    capacity = slots // count_gz
    single = segment == count_gz

    def tile_of(i):
        return jnp.bitwise_xor(z_index, i) if few > 1 else i

    size = depth * BY

    def tile_rows(i, start, size):
        if not isinstance(start, int):
            start = pl.multiple_of(start, TILE)
        if few > 1:
            return tiles[i][pl.ds(start, size), :]
        return tiles[0][i, pl.ds(start, size), :]

    def read_owners(i):
        row = tile_rows(i, brick_columns * depth * rows, TILE)
        owner_rows[i] = row.astype(jnp.float32)[0:8].astype(jnp.int32)

    if few > 1:
        for i in range(count_gz):
            read_owners(i)
    else:
        pl.loop(0, count_gz)(read_owners)
    table_copy = pltpu.make_async_copy(owner_rows, owner_table, sems.at[0])
    table_copy.start()

    def arrange(left, right, other):
        return jnp.concatenate(
            [
                jnp.where(c == 0, left, other),
                jnp.where(c == 0, right, left),
                jnp.where(c == 0, other, right),
            ],
            axis=1,
        )

    for k, pair in enumerate((top_refs, bottom_refs)):
        exists = (g > 0) if k == 0 else (g < count_gy - 1)
        own, other = pair[0][...].astype(jnp.float32), pair[1][...].astype(jnp.float32)
        values = arrange(own[:, 0:BX], own[:, BX:columns], other)
        edge_rows[k] = values * exists.astype(jnp.float32)

    def moved(values):
        lane = lax.broadcasted_iota(jnp.int32, values.shape, 1)
        left = jnp.where(lane == 0, 0.0, pltpu.roll(values, 1, 1))
        right = jnp.where(lane == window - 1, 0.0, pltpu.roll(values, window - 1, 1))
        return left.astype(values.dtype), values, right.astype(values.dtype)

    def edge_pair(k, at):
        if isinstance(at, int):
            return edge_rows[k, at : at + 2, :]
        group = edge_rows[k, pl.ds(pl.multiple_of(at // 8 * 8, 8), 8), :]
        return pltpu.roll(group, lax.rem(8 - at % 8, 8), 0)[0:2]

    row, _ = iotas((4, window))
    constants = [
        jnp.where((row == 0) | (row == 3), 1.0, jnp.where((row == 1 + h) & beyond, 1.0, 0.0))
        for h, beyond in enumerate((g == 0, g == count_gy - 1))
    ]

    def shifts(i, zz, slot, valid):
        z = i * depth + zz
        halves = []
        for h in range(2):
            at = zz * rows + h * HALF
            own = [tile_rows(i, k * depth * rows + at, HALF) for k in range(2)]
            at = z * rows + h * HALF
            if not isinstance(at, int):
                at = pl.multiple_of(at, TILE)
            values = arrange(*own, x_ref[pl.ds(at, HALF), :]).astype(jnp.float32)
            halves.append(values if valid is None else values * valid)
        top, bottom = edge_pair(0, 2 * z), edge_pair(1, 2 * z)
        if valid is not None:
            top, bottom = top * valid, bottom * valid
        seams = [
            jnp.concatenate([top, halves[1][0:2]], axis=0),
            jnp.concatenate([halves[0][HALF - 2 :], bottom], axis=0),
        ]
        for h in range(2):
            lanes = slice(h * window, (h + 1) * window)
            for dx, values in enumerate(moved(halves[h])):
                shifted[slot, dx * HALF : (dx + 1) * HALF, lanes] = values.astype(jnp.bfloat16)
            values = jnp.concatenate(
                [*moved(seams[h]), constants[h]], axis=0
            )
            shifted[slot, 3 * HALF : PART, lanes] = values.astype(jnp.bfloat16)

    def first(z, valid):
        total = jnp.dot(
            t1_ref[...],
            shifted[pl.ds(z + 1, 4)].reshape(4 * PART, 2 * window),
            preferred_element_type=jnp.float32,
        )
        for out in range(2):
            values = jnp.maximum(total[out * TALL : (out + 1) * TALL], 0.0)
            if valid is not None:
                values = values * valid(z + out)
            hidden[z + 1 + out] = values.astype(jnp.bfloat16)

    height = 2 * HALF
    _, lane = iotas((height, BX))

    def second(z, tile):
        total = jnp.dot(
            t2_ref[...],
            hidden[pl.ds(z, 4)].reshape(4 * TALL, 2 * window),
            preferred_element_type=jnp.float32,
        )
        for out in range(2):
            at = z + out
            place(total[3 * height * out : 3 * height * (out + 1)], tile + at // depth, at % depth)

    def place(total, t, zz):
        blocks = window // BX
        for h in range(2):
            part = [total[:, k * BX : (k + 1) * BX] for k in range(h * blocks, (h + 1) * blocks)]
            left = [0.0] + [pltpu.roll(block[0:height], 1, 1) for block in part]
            right = [pltpu.roll(block[2 * height :], BX - 1, 1) for block in part] + [0.0]
            sums = [
                part[k][height : 2 * height]
                + (
                    jnp.where(lane == 0, left[k], left[k + 1])
                    + jnp.where(lane == BX - 1, right[k + 1], right[k])
                )
                for k in range(blocks)
            ]
            for xb in range(brick_columns):
                own = jnp.where(c == 0, sums[xb], sums[xb + 1]) + bias2_ref[...]
                values = 0.5 + 0.5 * jnp.tanh(own)
                for yb in range(brick_rows):
                    b = (h * brick_rows + yb) * brick_columns + xb
                    bricks[t, b, zz] = values[yb * 8 : yb * 8 + 8]

    def valid_slice(z):
        return ((z >= 0) & (z < count_gz * depth)).astype(jnp.float32)

    depths = segment * depth
    if single:
        shifted[1] = jnp.zeros((PART, 2 * window), jnp.bfloat16)
        shifted[depths + 2] = jnp.zeros((PART, 2 * window), jnp.bfloat16)
        hidden[0] = jnp.zeros((TALL, 2 * window), jnp.bfloat16)
        hidden[depths + 1] = jnp.zeros((TALL, 2 * window), jnp.bfloat16)
        for i in range(count_gz):
            tile = tile_of(i)
            for zz in range(depth):
                shifts(i, zz, tile * depth + zz + 2, None)

        @pl.loop(0, depths // 2, unroll=4)
        def _(k):
            first(2 * k, None)

        @pl.loop(0, depths // 2, unroll=4)
        def _(k):
            second(2 * k, 0)

    else:

        @pl.loop(0, count_gz // segment)
        def _(q):
            @pl.loop(-2, depths + 2)
            def _(z):
                at = q * depths + z
                inside = jnp.clip(at, 0, count_gz * depth - 1)
                shifts(inside // depth, inside % depth, z + 2, valid_slice(at))

            @pl.loop(0, depths // 2 + 1)
            def _(k):
                first(2 * k - 1, lambda z: valid_slice(q * depths + z))

            @pl.loop(0, depths // 2)
            def _(k):
                second(2 * k, q * segment)

    for zz in range(depth):
        for xb in range(brick_columns):
            own = [
                bricks[z_index, yb * brick_columns + xb, zz] for yb in range(rows // BY)
            ]
            for o in range(2):
                values = jnp.concatenate([v[o * BY : o * BY + BY] for v in own], axis=0)
                fractions[o, zz, :, xb * BX : (xb + 1) * BX] = values.astype(jnp.bfloat16)
    fractions_copy = pltpu.make_async_copy(fractions, fractions_ref, sems.at[1])
    fractions_copy.start()

    table_copy.wait()
    for j in range(slots):
        brick_of_slot[j] = -1

    @pl.loop(0, count_gz)
    def _(i):
        first = tile_of(i) * capacity
        rank = jnp.int32(0)
        for b in range(brick_count):
            mine = owner_table[i, 0, b] == z_index
            brick_of_slot[jnp.where(mine, first + rank, slots)] = b
            rank = rank + mine.astype(jnp.int32)

    @pl.loop(0, slots, unroll=8)
    def _(j):
        brick = brick_of_slot[j]
        values = bricks[j // capacity, jnp.maximum(brick, 0)]
        values = jnp.where(brick >= 0, values, 0.0).astype(jnp.bfloat16).astype(jnp.float32)
        at = pl.multiple_of(j * (2 * size), 8)
        arrived[pl.ds(at, 2 * size), :] = values.reshape(2 * size, BX)

    def next_copy(group):
        at = pl.ds(pl.multiple_of(group * 16 * size, 16 * size), 16 * size)
        return pltpu.make_async_copy(state.at[at], next_ref.at[at], group_sems.at[group])

    @pl.loop(0, slots // 8)
    def _(group):
        grid = [(z, y) for z in range(depth) for y in range(BY)]

        def load(ref):
            base = group * (8 * size)
            return [
                [
                    ref[pl.ds(pl.multiple_of(base + (z * BY + y) * 8, 8), 8), :]
                    for y in range(BY)
                ]
                for z in range(depth)
            ]

        def rows_of(offset):
            return pl.ds(group * 16 * size + offset, 8, stride=2 * size)

        quarter = load(quarter_ref)
        pore = [[arrived[rows_of(z * 8 + y), :] for y in range(BY)] for z in range(depth)]
        organic = [
            [0.3 * arrived[rows_of(z * 8 + BY + y), :] for y in range(BY)] for z in range(depth)
        ]
        slow = [[0.12 * p for p in row] for row in pore]
        fast = [[0.16 * p for p in row] for row in pore]
        carbon, oxygen = load(carbon_ref), load(oxygen_ref)
        around = load(carbon_around_ref), load(oxygen_around_ref)
        for z, y in grid:
            carbon[z][y] += slow[z][y] * around[0][z][y] + organic[z][y]
            oxygen[z][y] += fast[z][y] * around[1][z][y]
        for _ in range(STEPS - 1):
            carbon_new = [[None] * BY for _ in range(depth)]
            oxygen_new = [[None] * BY for _ in range(depth)]
            for z, y in grid:
                doc, oxy = carbon[z][y], oxygen[z][y]
                uptake = uptake_of(quarter[z][y], doc, oxy)
                gain = organic[z][y] - uptake
                carbon_new[z][y] = doc + slow[z][y] * laplace(carbon, z, y) + gain
                oxygen_new[z][y] = oxy + fast[z][y] * laplace(oxygen, z, y) - uptake
            carbon, oxygen = carbon_new, oxygen_new
        for z, y in grid:
            state[rows_of(z * BY + y), :] = carbon[z][y]
            state[rows_of(size + z * BY + y), :] = oxygen[z][y]
        next_copy(group).start()

    @pl.loop(0, slots // 8)
    def _(group):
        next_copy(group).wait()

    fractions_copy.wait()


def per_device(
    sizes, density, first_kernel, first_bias, second_kernel, second_bias, owners, solutes, biomass
):
    count_gz, count_gy, count_col = sizes
    depth, rows, columns = density.shape
    slots = solutes.shape[3]
    window = columns + BX
    segment = min(count_gz, 4)
    brick_count = (rows // BY) * (columns // BX)
    height = depth * rows
    depths = count_gz * depth
    bf16, f32 = jnp.bfloat16, jnp.float32
    shape = jax.ShapeDtypeStruct

    payload = pl.pallas_call(
        pack_kernel,
        out_shape=shape((columns // BX * height + TILE, BX), bf16),
        in_specs=[HBM, HBM],
        out_specs=VMEM,
        scratch_shapes=[
            pltpu.VMEM((1, brick_count), jnp.int32),
            pltpu.SemaphoreType.DMA((columns // BX + 1,)),
        ],
        compiler_params=pltpu.CompilerParams(vmem_limit_bytes=4 * 2**20),
        name="pack",
    )(in_hbm(density.reshape(height, columns)), in_hbm(owners.reshape(1, brick_count)))

    few = count_gz if count_gz in (2, 4) else 1
    if few > 1:
        tiles = [payload] + [
            lax.ppermute(payload, "gz", [(i, i ^ s) for i in range(count_gz)])
            for s in range(1, count_gz)
        ]
    else:
        tiles = [lax.all_gather(payload, "gz", axis=0, tiled=False)]

    cells = depth * BY
    prepared = pl.pallas_call(
        functools.partial(prepare_kernel, (depth, slots)),
        out_shape=[shape((slots * cells, BX), f32)] * 5,
        in_specs=[HBM, HBM, ANY],
        out_specs=[VMEM] * 5,
        scratch_shapes=[
            pltpu.VMEM((slots * 2 * cells, BX), f32),
            pltpu.VMEM((slots * cells, BX), bf16),
            pltpu.VMEM((slots * cells, BX), f32),
            pltpu.SemaphoreType.DMA((slots // 8, 2)),
        ],
        compiler_params=pltpu.CompilerParams(vmem_limit_bytes=12 * 2**20),
        cost_estimate=pl.CostEstimate(
            flops=60 * slots * cells * BX, bytes_accessed=2**20, transcendentals=0
        ),
        name="prepare",
    )(
        in_hbm(solutes.reshape(slots * 2 * cells, BX)),
        in_hbm(biomass.reshape(slots * cells, BX)),
        payload,
    )
    t1, t2, bias2 = pl.pallas_call(
        banded_kernel,
        out_shape=(
            shape((2 * TALL, 4 * PART), bf16),
            shape((12 * HALF, 4 * TALL), bf16),
            shape((2 * HALF, BX), f32),
        ),
        in_specs=[HBM, HBM, HBM, HBM, ANY],
        out_specs=(VMEM, VMEM, VMEM),
        scratch_shapes=[
            pltpu.VMEM((CHANNELS, 27), bf16),
            pltpu.SMEM((CHANNELS,), f32),
            pltpu.VMEM((2 * CHANNELS, 27), bf16),
            pltpu.SMEM((2,), f32),
            pltpu.SemaphoreType.DMA((4,)),
        ],
        compiler_params=pltpu.CompilerParams(vmem_limit_bytes=16 * 2**20),
        cost_estimate=pl.CostEstimate(
            flops=20 * 2**20, bytes_accessed=4 * 2**20, transcendentals=0
        ),
        name="banded",
    )(
        in_hbm(first_kernel.transpose(2, 1, 0).reshape(CHANNELS, 27)),
        in_hbm(first_bias),
        in_hbm(second_kernel.transpose(1, 2, 0).reshape(2 * CHANNELS, 27)),
        in_hbm(second_bias),
        payload,
    )

    if count_gy == 2:
        ways = [[(0, 1), (1, 0)]]
    else:
        up = [(i, i + 1) for i in range(count_gy - 1)]
        ways = [up, [(j, i) for i, j in up]]
    directions = len(ways)
    swap = [(0, 1), (1, 0)]
    near, *sent = pl.pallas_call(
        functools.partial(edges_kernel, (count_gy, depth, rows, columns, few, count_gz)),
        out_shape=[shape((depths * rows, BX), bf16)]
        + [shape((2 * depths, columns), bf16)] * directions,
        in_specs=[VMEM] * few + [ANY, ANY],
        out_specs=[VMEM] * (1 + directions),
        compiler_params=pltpu.CompilerParams(vmem_limit_bytes=16 * 2**20),
        name="edges",
    )(*tiles, bias2, prepared[-1])
    edges = []
    for pairs, edge in zip(ways, sent):
        corner = pl.pallas_call(
            corner_kernel,
            out_shape=shape((2 * depths, BX), bf16),
            in_specs=[VMEM],
            out_specs=VMEM,
            compiler_params=pltpu.CompilerParams(vmem_limit_bytes=4 * 2**20),
            name="corner",
        )(edge)
        over = [
            (gy * count_col + col, to * count_col + 1 - col)
            for gy, to in pairs
            for col in range(count_col)
        ]
        corner = lax.ppermute(corner, ("gy", "col"), over)
        edges += [lax.ppermute(edge, "gy", pairs), corner]
    near = lax.ppermute(near, "col", swap)

    fractions, solutes_next = pl.pallas_call(
        functools.partial(
            column_kernel,
            (count_gz, count_gy, depth, rows, columns, segment, slots, directions),
            few,
        ),
        out_shape=(
            shape((2, depth, rows, columns), bf16),
            shape((slots * 2 * cells, BX), f32),
        ),
        in_specs=[VMEM] * (few + 1 + len(edges) + 8),
        out_specs=(HBM, HBM),
        scratch_shapes=[
            pltpu.VMEM((2, 2 * depths, window), f32),
            pltpu.VMEM((segment * depth + 4, PART, 2 * window), bf16),
            pltpu.VMEM((segment * depth + 2, TALL, 2 * window), bf16),
            pltpu.VMEM((count_gz, brick_count, depth, 8, BX), f32),
            pltpu.VMEM((slots * 2 * cells, BX), f32),
            pltpu.VMEM((slots * 2 * cells, BX), f32),
            pltpu.VMEM((2, depth, rows, columns), bf16),
            pltpu.VMEM((count_gz, 8, BX), jnp.int32),
            pltpu.SMEM((count_gz, 8, BX), jnp.int32),
            pltpu.SMEM((slots + 1,), jnp.int32),
            pltpu.SemaphoreType.DMA((2,)),
            pltpu.SemaphoreType.DMA((slots // 8,)),
        ],
        compiler_params=pltpu.CompilerParams(vmem_limit_bytes=40 * 2**20),
        cost_estimate=pl.CostEstimate(
            flops=2 * depths * 2 * window * TALL * (4 * PART + 4 * 6 * HALF),
            bytes_accessed=4 * 2**20,
            transcendentals=0,
        ),
        name="column",
    )(
        *tiles,
        near,
        *edges,
        t1,
        t2,
        bias2,
        *prepared,
    )
    return fractions, solutes_next.reshape(solutes.shape)


def solution(mesh):
    sizes = (mesh.shape["gz"], mesh.shape["gy"], mesh.shape["col"])
    assert sizes[2] == 2
    return jax.shard_map(
        functools.partial(per_device, sizes),
        mesh=mesh,
        in_specs=(
            P(("cores", "gz"), "gy", "col"),
            P(),
            P(),
            P(),
            P(),
            P(("cores", "gz"), "gy", "col", None, None),
            P(("cores", "gz"), "gy", "col", None, None, None, None, None),
            P(("cores", "gz"), "gy", "col", None, None, None, None),
        ),
        out_specs=(
            P(None, ("cores", "gz"), "gy", "col"),
            P(("cores", "gz"), "gy", "col", None, None, None, None, None),
        ),
        check_vma=False,
    )
```

```python
import functools

import jax
import jax.numpy as jnp
from jax import lax
from jax.experimental import pallas as pl
from jax.experimental.pallas import tpu as pltpu
from jax.sharding import PartitionSpec as P

BY = 4
BX = 128
STEPS = 4
TILE = 16
HALF = 16
CHANNELS = 8
REACH = HALF + 2
PART = 3 * HALF + TILE
TALL = REACH * CHANNELS
ONE_ROW = 3 * HALF + 12
OUTSIDE = -1e30

VMEM = pl.BlockSpec(memory_space=pltpu.VMEM)
SMEM = pl.BlockSpec(memory_space=pltpu.SMEM)
ANY = pl.BlockSpec(memory_space=pl.ANY)
HBM = pl.BlockSpec(memory_space=pltpu.HBM)


def in_hbm(array):
    return pltpu.with_memory_space_constraint(array, pltpu.HBM)


def step_index(values, width, count):
    index = jnp.zeros(values.shape, jnp.int32)
    for k in range(1, count):
        index = index + (values >= k * width).astype(jnp.int32)
    return index


def one_hot(condition):
    return jnp.where(condition, 1.0, 0.0).astype(jnp.bfloat16)


def iotas(shape):
    return (
        lax.broadcasted_iota(jnp.int32, shape, 0),
        lax.broadcasted_iota(jnp.int32, shape, 1),
    )


def tap_parts(tap):
    dz = step_index(tap, 9, 3)
    dy = step_index(tap - 9 * dz, 3, 3)
    return dz, dy, tap - 9 * dz - 3 * dy


def pack_kernel(density_ref, owners_ref, payload_ref, named_ref, sems):
    height, columns = density_ref.shape
    blocks = columns // BX
    copies = [pltpu.make_async_copy(owners_ref, named_ref, sems.at[blocks])]
    for k in range(blocks):
        copies.append(
            pltpu.make_async_copy(
                density_ref.at[:, k * BX : (k + 1) * BX],
                payload_ref.at[k * height : (k + 1) * height],
                sems.at[k],
            )
        )
    for copy in copies:
        copy.start()
    copies[0].wait()
    named = named_ref[...].astype(jnp.float32)
    count = named.shape[1]
    payload_ref[blocks * height : blocks * height + TILE, :] = jnp.concatenate(
        [
            jnp.broadcast_to(named, (TILE, count)),
            jnp.zeros((TILE, BX - count), jnp.float32),
        ],
        axis=1,
    ).astype(jnp.bfloat16)
    for copy in copies[1:]:
        copy.wait()


def banded_kernel(*refs):
    sources, refs = refs[:4], refs[5:]
    t1_ref, t2_ref, bias2_ref, *local, sems = refs
    copies = [
        pltpu.make_async_copy(source, target, sems.at[k])
        for k, (source, target) in enumerate(zip(sources, local))
    ]
    for copy in copies:
        copy.start()
    for copy in copies:
        copy.wait()
    w1_ref, b1_ref, w2_ref, b2_ref = local
    row, channel = iotas((TALL, CHANNELS))
    spread = one_hot((row & (CHANNELS - 1)) == channel)
    w1 = jnp.dot(spread, w1_ref[...], preferred_element_type=jnp.float32).astype(jnp.bfloat16)
    tap, column = iotas((27, 4 * PART))
    dz = column >> 6
    place = column & (PART - 1)
    dx = jnp.where(place < 3 * HALF, place >> 4, (place - 3 * HALF) >> 2)
    base = 9 * dz + dx
    row, column = iotas((TALL, 4 * PART))
    place = column & (PART - 1)
    seam = (place - 3 * HALF) & 3
    seam_row = jnp.where(seam < 2, seam - 2, seam + HALF - 2)
    input_row = jnp.where(place < 3 * HALF, place & (HALF - 1), seam_row)
    distance = jnp.where(place < 3 * HALF + 12, input_row - (row >> 3) + 2, -1)
    bias = jnp.zeros((TALL, 4 * PART), jnp.float32)
    for k in range(CHANNELS):
        bias = jnp.where((row & (CHANNELS - 1)) == k, b1_ref[k], bias)
    high = bias.astype(jnp.bfloat16).astype(jnp.float32)
    middle = (bias - high).astype(jnp.bfloat16).astype(jnp.float32)
    constant = jnp.where(column == PART + ONE_ROW, high, 0.0)
    constant = jnp.where(column == 2 * PART + ONE_ROW, middle, constant)
    constant = jnp.where(column == 2 * PART - 1, bias - high - middle, constant)
    outside = ((column == PART + ONE_ROW + 1) & (row < CHANNELS)) | (
        (column == PART + ONE_ROW + 2) & (row >= TALL - CHANNELS)
    )
    constant = jnp.where(outside, OUTSIDE, constant)
    for out in range(2):
        total = constant
        for dy in range(3):
            pick = one_hot(tap == base - 9 * out + 3 * dy)
            values = jnp.dot(w1, pick, preferred_element_type=jnp.float32)
            total = jnp.where(distance == dy, values, total)
        t1_ref[out * TALL : (out + 1) * TALL, :] = total.astype(jnp.bfloat16)
    channel, column = iotas((CHANNELS, 4 * TALL))
    spread = one_hot((column & (CHANNELS - 1)) == channel)
    tap, column = iotas((27, 4 * TALL))
    tap_z, slice_z = tap_parts(tap)[0], step_index(column, TALL, 4)
    row, tap = iotas((6 * HALF, 27))
    _, tap_y, tap_x = tap_parts(tap)
    same_x = (row >> 5) == tap_x
    wide = [
        lax.dot_general(
            w2_ref[o * CHANNELS : (o + 1) * CHANNELS, :],
            spread,
            (((0,), (0,)), ((), ())),
            preferred_element_type=jnp.float32,
        )
        for o in range(2)
    ]
    picks = [
        [one_hot(same_x & (tap_y == dy) & (((row >> 2) & 1) == o)) for o in range(2)]
        for dy in range(3)
    ]
    out_row, column = iotas((6 * HALF, 4 * TALL))
    y = ((out_row >> 3) & 3) * BY + (out_row & 3)
    distance = ((column - TALL * step_index(column, TALL, 4)) >> 3) - y
    for out in range(2):
        same_z = tap_z == slice_z - out
        terms = [jnp.where(same_z, values, 0.0).astype(jnp.bfloat16) for values in wide]
        total = jnp.zeros((6 * HALF, 4 * TALL), jnp.float32)
        for dy in range(3):
            values = 0.0
            for o in range(2):
                values = values + jnp.dot(
                    picks[dy][o], terms[o], preferred_element_type=jnp.float32
                )
            total = jnp.where(distance == dy, values, total)
        t2_ref[out * 6 * HALF : (out + 1) * 6 * HALF, :] = (0.5 * total).astype(jnp.bfloat16)
    row, _ = iotas((2 * HALF, BX))
    bias2_ref[...] = 0.5 * jnp.where(((row >> 2) & 1) == 0, b2_ref[0], b2_ref[1])


def edges_kernel(dims, *refs):
    count_gy, depth, rows, columns, few, count = dims
    tiles, outs = refs[:few], refs[few + 2 :]
    g = lax.axis_index("gy")
    c = lax.axis_index("col")
    height = depth * rows
    block = (1 - c) * height

    def take(i, start, size):
        start = pl.ds(pl.multiple_of(start, TILE), size)
        if few > 1:
            return tiles[i][start, :]
        return tiles[0][i, start, :]

    def pair(i):
        for k in range(2):
            at = pl.multiple_of((2 * i + k) * height, TILE)
            outs[0][pl.ds(at, height), :] = take(2 * i + k, block, height)
        low, high = [], []
        for k in range(2):
            for zz in range(depth):
                first, last = [], []
                for base in (0, height):
                    at = base + zz * rows
                    first.append(take(2 * i + k, at, TILE).astype(jnp.float32)[0:2])
                    at = at + rows - TILE
                    last.append(take(2 * i + k, at, TILE).astype(jnp.float32)[TILE - 2 :])
                low.append(jnp.concatenate(first, axis=1))
                high.append(jnp.concatenate(last, axis=1))
        at = pl.multiple_of(2 * i * 2 * depth, TILE)
        first, last = jnp.concatenate(low, axis=0), jnp.concatenate(high, axis=0)
        sends = [jnp.where(g == 0, last, first)] if count_gy == 2 else [last, first]
        for n, send in enumerate(sends):
            send = send.astype(jnp.bfloat16)
            outs[1 + n][pl.ds(at, TILE), :] = send

    if few > 1:
        for i in range(count // 2):
            pair(i)
    else:
        pl.loop(0, count // 2)(pair)


def corner_kernel(edge_ref, corner_ref):
    c = lax.axis_index("col")
    corner_ref[...] = jnp.where(c == 0, edge_ref[:, BX:], edge_ref[:, 0:BX])


def laplace(field, z, y):
    centre = field[z][y]
    last = lax.broadcasted_iota(jnp.int32, centre.shape, 1) == BX - 1
    ahead = jnp.where(last, 0.0, pltpu.roll(centre, BX - 1, 1) - centre)
    result = ahead - pltpu.roll(ahead, 1, 1)
    beside = [
        field[zz][yy]
        for zz, yy in ((z - 1, y), (z + 1, y), (z, y - 1), (z, y + 1))
        if 0 <= zz < len(field) and 0 <= yy < BY
    ]
    return result + (functools.reduce(jnp.add, beside) - float(len(beside)) * centre)


def uptake_of(quarter, doc, oxy):
    return quarter * doc * oxy / ((0.5 + jnp.abs(doc)) * (0.3 + jnp.abs(oxy)))


def prepare_kernel(dims, solutes_ref, biomass_ref, _, *refs):
    depth, slots = dims
    outs, (state, biomass, mass, sems) = refs[:5], refs[5:]
    size = depth * BY
    copies = []
    for group in range(slots // 8):
        for k, (source, target) in enumerate(((solutes_ref, state), (biomass_ref, biomass))):
            rows = (2 - k) * 8 * size
            at = pl.ds(group * rows, rows)
            copies.append(
                pltpu.make_async_copy(source.at[at], target.at[at], sems.at[group, k])
            )
    for copy in copies:
        copy.start()
    for group in range(slots // 8):
        copies[2 * group].wait()
        copies[2 * group + 1].wait()
        at = slice(group * 8 * size, (group + 1) * 8 * size)
        mass[at, :] = biomass[at, :].astype(jnp.float32)

        def rows_of(pitch, offset):
            return pl.ds(group * 8 * pitch + offset, 8, stride=pitch)

        grid = [(z, y) for z in range(depth) for y in range(BY)]
        carbon, oxygen = [
            [
                [state[rows_of(2 * size, k * size + z * BY + y), :] for y in range(BY)]
                for z in range(depth)
            ]
            for k in range(2)
        ]
        for z, y in grid:
            at = group * 8 * size + (z * BY + y) * 8
            at = slice(at, at + 8)
            doc, oxy = carbon[z][y], oxygen[z][y]
            quarter = 0.25 * mass[rows_of(size, z * BY + y), :]
            uptake = uptake_of(quarter, doc, oxy)
            values = (
                doc - uptake,
                oxy - uptake,
                laplace(carbon, z, y),
                laplace(oxygen, z, y),
                quarter,
            )
            for out, value in zip(outs, values):
                out[at, :] = value


def column_kernel(dims, few, *refs):
    count_gz, count_gy, depth, rows, columns, segment, slots, directions = dims
    tiles, refs = refs[:few], refs[few:]
    x_ref, refs = refs[0], refs[1:]
    top_refs, refs = refs[:2], refs[2:]
    if directions == 1:
        bottom_refs = top_refs
    else:
        bottom_refs, refs = refs[:2], refs[2:]
    t1_ref, t2_ref, bias2_ref, *refs = refs
    carbon_ref, oxygen_ref, carbon_around_ref, oxygen_around_ref, quarter_ref, *refs = refs
    fractions_ref, next_ref, *refs = refs
    (
        edge_rows,
        shifted,
        hidden,
        bricks,
        arrived,
        state,
        fractions,
        owner_rows,
        owner_table,
        brick_of_slot,
        sems,
        group_sems,
    ) = refs
    z_index = lax.axis_index("gz")
    g = lax.axis_index("gy")
    c = lax.axis_index("col")
    window = columns + BX
    brick_rows = HALF // BY
    brick_columns = columns // BX
    brick_count = rows // BY * brick_columns
    capacity = slots // count_gz
    single = segment == count_gz

    def tile_of(i):
        return lax.rem(z_index + i, count_gz) if few > 1 else i

    size = depth * BY

    def tile_rows(i, start, size):
        if not isinstance(start, int):
            start = pl.multiple_of(start, TILE)
        if few > 1:
            return tiles[i][pl.ds(start, size), :]
        return tiles[0][i, pl.ds(start, size), :]

    def read_owners(i):
        row = tile_rows(i, brick_columns * depth * rows, TILE)
        owner_rows[i] = row.astype(jnp.float32)[0:8].astype(jnp.int32)

    if few > 1:
        for i in range(count_gz):
            read_owners(i)
    else:
        pl.loop(0, count_gz)(read_owners)
    table_copy = pltpu.make_async_copy(owner_rows, owner_table, sems.at[0])
    table_copy.start()

    def arrange(left, right, other):
        return jnp.concatenate(
            [
                jnp.where(c == 0, left, other),
                jnp.where(c == 0, right, left),
                jnp.where(c == 0, other, right),
            ],
            axis=1,
        )

    for k, pair in enumerate((top_refs, bottom_refs)):
        exists = (g > 0) if k == 0 else (g < count_gy - 1)
        own, other = pair[0][...].astype(jnp.float32), pair[1][...].astype(jnp.float32)
        values = arrange(own[:, 0:BX], own[:, BX:columns], other)
        edge_rows[k] = values * exists.astype(jnp.float32)

    def moved(values):
        lane = lax.broadcasted_iota(jnp.int32, values.shape, 1)
        left = jnp.where(lane == 0, 0.0, pltpu.roll(values, 1, 1))
        right = jnp.where(lane == window - 1, 0.0, pltpu.roll(values, window - 1, 1))
        return left.astype(values.dtype), values, right.astype(values.dtype)

    def edge_pair(k, at):
        if isinstance(at, int):
            return edge_rows[k, at : at + 2, :]
        group = edge_rows[k, pl.ds(pl.multiple_of(at // 8 * 8, 8), 8), :]
        return pltpu.roll(group, lax.rem(8 - at % 8, 8), 0)[0:2]

    row, _ = iotas((4, window))
    constants = [
        jnp.where((row == 0) | (row == 3), 1.0, jnp.where((row == 1 + h) & beyond, 1.0, 0.0))
        for h, beyond in enumerate((g == 0, g == count_gy - 1))
    ]

    def shifts(i, zz, slot, valid):
        z = i * depth + zz
        halves = []
        for h in range(2):
            at = zz * rows + h * HALF
            own = [tile_rows(i, k * depth * rows + at, HALF) for k in range(2)]
            at = z * rows + h * HALF
            if not isinstance(at, int):
                at = pl.multiple_of(at, TILE)
            values = arrange(*own, x_ref[pl.ds(at, HALF), :]).astype(jnp.float32)
            halves.append(values if valid is None else values * valid)
        top, bottom = edge_pair(0, 2 * z), edge_pair(1, 2 * z)
        if valid is not None:
            top, bottom = top * valid, bottom * valid
        seams = [
            jnp.concatenate([top, halves[1][0:2]], axis=0),
            jnp.concatenate([halves[0][HALF - 2 :], bottom], axis=0),
        ]
        for h in range(2):
            lanes = slice(h * window, (h + 1) * window)
            for dx, values in enumerate(moved(halves[h])):
                shifted[slot, dx * HALF : (dx + 1) * HALF, lanes] = values.astype(jnp.bfloat16)
            values = jnp.concatenate(
                [*moved(seams[h]), constants[h]], axis=0
            )
            shifted[slot, 3 * HALF : PART, lanes] = values.astype(jnp.bfloat16)

    def first(z, valid):
        total = jnp.dot(
            t1_ref[...],
            shifted[pl.ds(z + 1, 4)].reshape(4 * PART, 2 * window),
            preferred_element_type=jnp.float32,
        )
        for out in range(2):
            values = jnp.maximum(total[out * TALL : (out + 1) * TALL], 0.0)
            if valid is not None:
                values = values * valid(z + out)
            hidden[z + 1 + out] = values.astype(jnp.bfloat16)

    height = 2 * HALF
    _, lane = iotas((height, BX))

    def second(z, tile):
        total = jnp.dot(
            t2_ref[...],
            hidden[pl.ds(z, 4)].reshape(4 * TALL, 2 * window),
            preferred_element_type=jnp.float32,
        )
        for out in range(2):
            at = z + out
            place(total[3 * height * out : 3 * height * (out + 1)], tile + at // depth, at % depth)

    def place(total, t, zz):
        blocks = window // BX
        for h in range(2):
            part = [total[:, k * BX : (k + 1) * BX] for k in range(h * blocks, (h + 1) * blocks)]
            left = [0.0] + [pltpu.roll(block[0:height], 1, 1) for block in part]
            right = [pltpu.roll(block[2 * height :], BX - 1, 1) for block in part] + [0.0]
            sums = [
                part[k][height : 2 * height]
                + (
                    jnp.where(lane == 0, left[k], left[k + 1])
                    + jnp.where(lane == BX - 1, right[k + 1], right[k])
                )
                for k in range(blocks)
            ]
            for xb in range(brick_columns):
                own = jnp.where(c == 0, sums[xb], sums[xb + 1]) + bias2_ref[...]
                values = 0.5 + 0.5 * jnp.tanh(own)
                for yb in range(brick_rows):
                    b = (h * brick_rows + yb) * brick_columns + xb
                    bricks[t, b, zz] = values[yb * 8 : yb * 8 + 8]

    def valid_slice(z):
        return ((z >= 0) & (z < count_gz * depth)).astype(jnp.float32)

    depths = segment * depth
    if single:
        shifted[1] = jnp.zeros((PART, 2 * window), jnp.bfloat16)
        shifted[depths + 2] = jnp.zeros((PART, 2 * window), jnp.bfloat16)
        hidden[0] = jnp.zeros((TALL, 2 * window), jnp.bfloat16)
        hidden[depths + 1] = jnp.zeros((TALL, 2 * window), jnp.bfloat16)
        for i in range(count_gz):
            tile = tile_of(i)
            for zz in range(depth):
                shifts(i, zz, tile * depth + zz + 2, None)

        @pl.loop(0, depths // 2, unroll=4)
        def _(k):
            first(2 * k, None)

        @pl.loop(0, depths // 2, unroll=4)
        def _(k):
            second(2 * k, 0)

    else:

        @pl.loop(0, count_gz // segment)
        def _(q):
            @pl.loop(-2, depths + 2)
            def _(z):
                at = q * depths + z
                inside = jnp.clip(at, 0, count_gz * depth - 1)
                shifts(inside // depth, inside % depth, z + 2, valid_slice(at))

            @pl.loop(0, depths // 2 + 1)
            def _(k):
                first(2 * k - 1, lambda z: valid_slice(q * depths + z))

            @pl.loop(0, depths // 2)
            def _(k):
                second(2 * k, q * segment)

    for zz in range(depth):
        for xb in range(brick_columns):
            own = [
                bricks[z_index, yb * brick_columns + xb, zz] for yb in range(rows // BY)
            ]
            for o in range(2):
                values = jnp.concatenate([v[o * BY : o * BY + BY] for v in own], axis=0)
                fractions[o, zz, :, xb * BX : (xb + 1) * BX] = values.astype(jnp.bfloat16)
    fractions_copy = pltpu.make_async_copy(fractions, fractions_ref, sems.at[1])
    fractions_copy.start()

    table_copy.wait()
    for j in range(slots):
        brick_of_slot[j] = -1

    @pl.loop(0, count_gz)
    def _(i):
        first = tile_of(i) * capacity
        rank = jnp.int32(0)
        for b in range(brick_count):
            mine = owner_table[i, 0, b] == z_index
            brick_of_slot[jnp.where(mine, first + rank, slots)] = b
            rank = rank + mine.astype(jnp.int32)

    @pl.loop(0, slots, unroll=8)
    def _(j):
        brick = brick_of_slot[j]
        values = bricks[j // capacity, jnp.maximum(brick, 0)]
        values = jnp.where(brick >= 0, values, 0.0).astype(jnp.bfloat16).astype(jnp.float32)
        at = pl.multiple_of(j * (2 * size), 8)
        arrived[pl.ds(at, 2 * size), :] = values.reshape(2 * size, BX)

    def next_copy(group):
        at = pl.ds(pl.multiple_of(group * 16 * size, 16 * size), 16 * size)
        return pltpu.make_async_copy(state.at[at], next_ref.at[at], group_sems.at[group])

    @pl.loop(0, slots // 8)
    def _(group):
        grid = [(z, y) for z in range(depth) for y in range(BY)]

        def load(ref):
            base = group * (8 * size)
            return [
                [
                    ref[pl.ds(pl.multiple_of(base + (z * BY + y) * 8, 8), 8), :]
                    for y in range(BY)
                ]
                for z in range(depth)
            ]

        def rows_of(offset):
            return pl.ds(group * 16 * size + offset, 8, stride=2 * size)

        quarter = load(quarter_ref)
        pore = [[arrived[rows_of(z * 8 + y), :] for y in range(BY)] for z in range(depth)]
        organic = [
            [0.3 * arrived[rows_of(z * 8 + BY + y), :] for y in range(BY)] for z in range(depth)
        ]
        slow = [[0.12 * p for p in row] for row in pore]
        fast = [[0.16 * p for p in row] for row in pore]
        carbon, oxygen = load(carbon_ref), load(oxygen_ref)
        around = load(carbon_around_ref), load(oxygen_around_ref)
        for z, y in grid:
            carbon[z][y] += slow[z][y] * around[0][z][y] + organic[z][y]
            oxygen[z][y] += fast[z][y] * around[1][z][y]
        for _ in range(STEPS - 1):
            carbon_new = [[None] * BY for _ in range(depth)]
            oxygen_new = [[None] * BY for _ in range(depth)]
            for z, y in grid:
                doc, oxy = carbon[z][y], oxygen[z][y]
                uptake = uptake_of(quarter[z][y], doc, oxy)
                gain = organic[z][y] - uptake
                carbon_new[z][y] = doc + slow[z][y] * laplace(carbon, z, y) + gain
                oxygen_new[z][y] = oxy + fast[z][y] * laplace(oxygen, z, y) - uptake
            carbon, oxygen = carbon_new, oxygen_new
        for z, y in grid:
            state[rows_of(z * BY + y), :] = carbon[z][y]
            state[rows_of(size + z * BY + y), :] = oxygen[z][y]
        next_copy(group).start()

    @pl.loop(0, slots // 8)
    def _(group):
        next_copy(group).wait()

    fractions_copy.wait()


def per_device(
    sizes, density, first_kernel, first_bias, second_kernel, second_bias, owners, solutes, biomass
):
    count_gz, count_gy, count_col = sizes
    depth, rows, columns = density.shape
    slots = solutes.shape[3]
    window = columns + BX
    segment = min(count_gz, 4)
    brick_count = (rows // BY) * (columns // BX)
    height = depth * rows
    depths = count_gz * depth
    bf16, f32 = jnp.bfloat16, jnp.float32
    shape = jax.ShapeDtypeStruct

    payload = pl.pallas_call(
        pack_kernel,
        out_shape=shape((columns // BX * height + TILE, BX), bf16),
        in_specs=[HBM, HBM],
        out_specs=VMEM,
        scratch_shapes=[
            pltpu.VMEM((1, brick_count), jnp.int32),
            pltpu.SemaphoreType.DMA((columns // BX + 1,)),
        ],
        compiler_params=pltpu.CompilerParams(vmem_limit_bytes=4 * 2**20),
        name="pack",
    )(in_hbm(density.reshape(height, columns)), in_hbm(owners.reshape(1, brick_count)))

    few = count_gz if count_gz in (2, 4) else 1
    if few > 1:
        tiles = [payload] + [
            lax.ppermute(payload, "gz", [((i + s) % count_gz, i) for i in range(count_gz)])
            for s in range(1, count_gz)
        ]
    else:
        tiles = [lax.all_gather(payload, "gz", axis=0, tiled=False)]

    cells = depth * BY
    prepared = pl.pallas_call(
        functools.partial(prepare_kernel, (depth, slots)),
        out_shape=[shape((slots * cells, BX), f32)] * 5,
        in_specs=[HBM, HBM, ANY],
        out_specs=[VMEM] * 5,
        scratch_shapes=[
            pltpu.VMEM((slots * 2 * cells, BX), f32),
            pltpu.VMEM((slots * cells, BX), bf16),
            pltpu.VMEM((slots * cells, BX), f32),
            pltpu.SemaphoreType.DMA((slots // 8, 2)),
        ],
        compiler_params=pltpu.CompilerParams(vmem_limit_bytes=12 * 2**20),
        cost_estimate=pl.CostEstimate(
            flops=60 * slots * cells * BX, bytes_accessed=2**20, transcendentals=0
        ),
        name="prepare",
    )(
        in_hbm(solutes.reshape(slots * 2 * cells, BX)),
        in_hbm(biomass.reshape(slots * cells, BX)),
        payload,
    )
    t1, t2, bias2 = pl.pallas_call(
        banded_kernel,
        out_shape=(
            shape((2 * TALL, 4 * PART), bf16),
            shape((12 * HALF, 4 * TALL), bf16),
            shape((2 * HALF, BX), f32),
        ),
        in_specs=[HBM, HBM, HBM, HBM, ANY],
        out_specs=(VMEM, VMEM, VMEM),
        scratch_shapes=[
            pltpu.VMEM((CHANNELS, 27), bf16),
            pltpu.SMEM((CHANNELS,), f32),
            pltpu.VMEM((2 * CHANNELS, 27), bf16),
            pltpu.SMEM((2,), f32),
            pltpu.SemaphoreType.DMA((4,)),
        ],
        compiler_params=pltpu.CompilerParams(vmem_limit_bytes=16 * 2**20),
        cost_estimate=pl.CostEstimate(
            flops=20 * 2**20, bytes_accessed=4 * 2**20, transcendentals=0
        ),
        name="banded",
    )(
        in_hbm(first_kernel.transpose(2, 1, 0).reshape(CHANNELS, 27)),
        in_hbm(first_bias),
        in_hbm(second_kernel.transpose(1, 2, 0).reshape(2 * CHANNELS, 27)),
        in_hbm(second_bias),
        payload,
    )

    if count_gy == 2:
        ways = [[(0, 1), (1, 0)]]
    else:
        up = [(i, i + 1) for i in range(count_gy - 1)]
        ways = [up, [(j, i) for i, j in up]]
    directions = len(ways)
    swap = [(0, 1), (1, 0)]
    near, *sent = pl.pallas_call(
        functools.partial(edges_kernel, (count_gy, depth, rows, columns, few, count_gz)),
        out_shape=[shape((depths * rows, BX), bf16)]
        + [shape((2 * depths, columns), bf16)] * directions,
        in_specs=[VMEM] * few + [ANY, ANY],
        out_specs=[VMEM] * (1 + directions),
        compiler_params=pltpu.CompilerParams(vmem_limit_bytes=16 * 2**20),
        name="edges",
    )(*tiles, bias2, prepared[-1])
    edges = []
    for pairs, edge in zip(ways, sent):
        corner = pl.pallas_call(
            corner_kernel,
            out_shape=shape((2 * depths, BX), bf16),
            in_specs=[VMEM],
            out_specs=VMEM,
            compiler_params=pltpu.CompilerParams(vmem_limit_bytes=4 * 2**20),
            name="corner",
        )(edge)
        over = [
            (gy * count_col + col, to * count_col + 1 - col)
            for gy, to in pairs
            for col in range(count_col)
        ]
        corner = lax.ppermute(corner, ("gy", "col"), over)
        edges += [lax.ppermute(edge, "gy", pairs), corner]
    near = lax.ppermute(near, "col", swap)

    fractions, solutes_next = pl.pallas_call(
        functools.partial(
            column_kernel,
            (count_gz, count_gy, depth, rows, columns, segment, slots, directions),
            few,
        ),
        out_shape=(
            shape((2, depth, rows, columns), bf16),
            shape((slots * 2 * cells, BX), f32),
        ),
        in_specs=[VMEM] * (few + 1 + len(edges) + 8),
        out_specs=(HBM, HBM),
        scratch_shapes=[
            pltpu.VMEM((2, 2 * depths, window), f32),
            pltpu.VMEM((segment * depth + 4, PART, 2 * window), bf16),
            pltpu.VMEM((segment * depth + 2, TALL, 2 * window), bf16),
            pltpu.VMEM((count_gz, brick_count, depth, 8, BX), f32),
            pltpu.VMEM((slots * 2 * cells, BX), f32),
            pltpu.VMEM((slots * 2 * cells, BX), f32),
            pltpu.VMEM((2, depth, rows, columns), bf16),
            pltpu.VMEM((count_gz, 8, BX), jnp.int32),
            pltpu.SMEM((count_gz, 8, BX), jnp.int32),
            pltpu.SMEM((slots + 1,), jnp.int32),
            pltpu.SemaphoreType.DMA((2,)),
            pltpu.SemaphoreType.DMA((slots // 8,)),
        ],
        compiler_params=pltpu.CompilerParams(vmem_limit_bytes=40 * 2**20),
        cost_estimate=pl.CostEstimate(
            flops=2 * depths * 2 * window * TALL * (4 * PART + 4 * 6 * HALF),
            bytes_accessed=4 * 2**20,
            transcendentals=0,
        ),
        name="column",
    )(
        *tiles,
        near,
        *edges,
        t1,
        t2,
        bias2,
        *prepared,
    )
    return fractions, solutes_next.reshape(solutes.shape)


def solution(mesh):
    sizes = (mesh.shape["gz"], mesh.shape["gy"], mesh.shape["col"])
    assert sizes[2] == 2
    return jax.shard_map(
        functools.partial(per_device, sizes),
        mesh=mesh,
        in_specs=(
            P(("cores", "gz"), "gy", "col"),
            P(),
            P(),
            P(),
            P(),
            P(("cores", "gz"), "gy", "col", None, None),
            P(("cores", "gz"), "gy", "col", None, None, None, None, None),
            P(("cores", "gz"), "gy", "col", None, None, None, None),
        ),
        out_specs=(
            P(None, ("cores", "gz"), "gy", "col"),
            P(("cores", "gz"), "gy", "col", None, None, None, None, None),
        ),
        check_vma=False,
    )
```

```python
import functools

import jax
import jax.numpy as jnp
from jax import lax
from jax.experimental import pallas as pl
from jax.experimental.pallas import tpu as pltpu
from jax.sharding import PartitionSpec as P

BY = 4
BX = 128
STEPS = 4
TILE = 16
HALF = 16
CHANNELS = 8
REACH = HALF + 2
PART = 3 * HALF + TILE
TALL = REACH * CHANNELS
ONE_ROW = 3 * HALF + 12
OUTSIDE = -1e30

VMEM = pl.BlockSpec(memory_space=pltpu.VMEM)
SMEM = pl.BlockSpec(memory_space=pltpu.SMEM)
ANY = pl.BlockSpec(memory_space=pl.ANY)
HBM = pl.BlockSpec(memory_space=pltpu.HBM)


def in_hbm(array):
    return pltpu.with_memory_space_constraint(array, pltpu.HBM)


def step_index(values, width, count):
    index = jnp.zeros(values.shape, jnp.int32)
    for k in range(1, count):
        index = index + (values >= k * width).astype(jnp.int32)
    return index


def one_hot(condition):
    return jnp.where(condition, 1.0, 0.0).astype(jnp.bfloat16)


def iotas(shape):
    return (
        lax.broadcasted_iota(jnp.int32, shape, 0),
        lax.broadcasted_iota(jnp.int32, shape, 1),
    )


def tap_parts(tap):
    dz = step_index(tap, 9, 3)
    dy = step_index(tap - 9 * dz, 3, 3)
    return dz, dy, tap - 9 * dz - 3 * dy


def pack_kernel(density_ref, owners_ref, payload_ref, named_ref, sems):
    height, columns = density_ref.shape
    blocks = columns // BX
    copies = [pltpu.make_async_copy(owners_ref, named_ref, sems.at[blocks])]
    for k in range(blocks):
        copies.append(
            pltpu.make_async_copy(
                density_ref.at[:, k * BX : (k + 1) * BX],
                payload_ref.at[k * height : (k + 1) * height],
                sems.at[k],
            )
        )
    for copy in copies:
        copy.start()
    copies[0].wait()
    named = named_ref[...].astype(jnp.float32)
    count = named.shape[1]
    payload_ref[blocks * height : blocks * height + TILE, :] = jnp.concatenate(
        [
            jnp.broadcast_to(named, (TILE, count)),
            jnp.zeros((TILE, BX - count), jnp.float32),
        ],
        axis=1,
    ).astype(jnp.bfloat16)
    for copy in copies[1:]:
        copy.wait()


def banded_kernel(*refs):
    sources, refs = refs[:4], refs[5:]
    t1_ref, t2_ref, bias2_ref, *local, sems = refs
    copies = [
        pltpu.make_async_copy(source, target, sems.at[k])
        for k, (source, target) in enumerate(zip(sources, local))
    ]
    for copy in copies:
        copy.start()
    for copy in copies:
        copy.wait()
    w1_ref, b1_ref, w2_ref, b2_ref = local
    row, channel = iotas((TALL, CHANNELS))
    spread = one_hot((row & (CHANNELS - 1)) == channel)
    w1 = jnp.dot(spread, w1_ref[...], preferred_element_type=jnp.float32).astype(jnp.bfloat16)
    tap, column = iotas((27, 4 * PART))
    dz = column >> 6
    place = column & (PART - 1)
    dx = jnp.where(place < 3 * HALF, place >> 4, (place - 3 * HALF) >> 2)
    base = 9 * dz + dx
    row, column = iotas((TALL, 4 * PART))
    place = column & (PART - 1)
    seam = (place - 3 * HALF) & 3
    seam_row = jnp.where(seam < 2, seam - 2, seam + HALF - 2)
    input_row = jnp.where(place < 3 * HALF, place & (HALF - 1), seam_row)
    distance = jnp.where(place < 3 * HALF + 12, input_row - (row >> 3) + 2, -1)
    bias = jnp.zeros((TALL, 4 * PART), jnp.float32)
    for k in range(CHANNELS):
        bias = jnp.where((row & (CHANNELS - 1)) == k, b1_ref[k], bias)
    high = bias.astype(jnp.bfloat16).astype(jnp.float32)
    middle = (bias - high).astype(jnp.bfloat16).astype(jnp.float32)
    constant = jnp.where(column == PART + ONE_ROW, high, 0.0)
    constant = jnp.where(column == 2 * PART + ONE_ROW, middle, constant)
    constant = jnp.where(column == 2 * PART - 1, bias - high - middle, constant)
    outside = ((column == PART + ONE_ROW + 1) & (row < CHANNELS)) | (
        (column == PART + ONE_ROW + 2) & (row >= TALL - CHANNELS)
    )
    constant = jnp.where(outside, OUTSIDE, constant)
    for out in range(2):
        total = constant
        for dy in range(3):
            pick = one_hot(tap == base - 9 * out + 3 * dy)
            values = jnp.dot(w1, pick, preferred_element_type=jnp.float32)
            total = jnp.where(distance == dy, values, total)
        t1_ref[out * TALL : (out + 1) * TALL, :] = total.astype(jnp.bfloat16)
    channel, column = iotas((CHANNELS, 4 * TALL))
    spread = one_hot((column & (CHANNELS - 1)) == channel)
    tap, column = iotas((27, 4 * TALL))
    tap_z, slice_z = tap_parts(tap)[0], step_index(column, TALL, 4)
    row, tap = iotas((6 * HALF, 27))
    _, tap_y, tap_x = tap_parts(tap)
    same_x = (row >> 5) == tap_x
    wide = [
        lax.dot_general(
            w2_ref[o * CHANNELS : (o + 1) * CHANNELS, :],
            spread,
            (((0,), (0,)), ((), ())),
            preferred_element_type=jnp.float32,
        )
        for o in range(2)
    ]
    picks = [
        [one_hot(same_x & (tap_y == dy) & (((row >> 2) & 1) == o)) for o in range(2)]
        for dy in range(3)
    ]
    out_row, column = iotas((6 * HALF, 4 * TALL))
    y = ((out_row >> 3) & 3) * BY + (out_row & 3)
    distance = ((column - TALL * step_index(column, TALL, 4)) >> 3) - y
    for out in range(2):
        same_z = tap_z == slice_z - out
        terms = [jnp.where(same_z, values, 0.0).astype(jnp.bfloat16) for values in wide]
        total = jnp.zeros((6 * HALF, 4 * TALL), jnp.float32)
        for dy in range(3):
            values = 0.0
            for o in range(2):
                values = values + jnp.dot(
                    picks[dy][o], terms[o], preferred_element_type=jnp.float32
                )
            total = jnp.where(distance == dy, values, total)
        t2_ref[out * 6 * HALF : (out + 1) * 6 * HALF, :] = (0.5 * total).astype(jnp.bfloat16)
    row, _ = iotas((2 * HALF, BX))
    bias2_ref[...] = 0.5 * jnp.where(((row >> 2) & 1) == 0, b2_ref[0], b2_ref[1])


def edges_kernel(dims, *refs):
    count_gy, depth, rows, columns, few, count = dims
    tiles, outs = refs[:few], refs[few + 1 :]
    g = lax.axis_index("gy")
    c = lax.axis_index("col")
    height = depth * rows
    block = (1 - c) * height

    def take(i, start, size):
        start = pl.ds(pl.multiple_of(start, TILE), size)
        if few > 1:
            return tiles[i][start, :]
        return tiles[0][i, start, :]

    def pair(i):
        for k in range(2):
            at = pl.multiple_of((2 * i + k) * height, TILE)
            outs[0][pl.ds(at, height), :] = take(2 * i + k, block, height)
        low, high = [], []
        for k in range(2):
            for zz in range(depth):
                first, last = [], []
                for base in (0, height):
                    at = base + zz * rows
                    first.append(take(2 * i + k, at, TILE).astype(jnp.float32)[0:2])
                    at = at + rows - TILE
                    last.append(take(2 * i + k, at, TILE).astype(jnp.float32)[TILE - 2 :])
                low.append(jnp.concatenate(first, axis=1))
                high.append(jnp.concatenate(last, axis=1))
        at = pl.multiple_of(2 * i * 2 * depth, TILE)
        first, last = jnp.concatenate(low, axis=0), jnp.concatenate(high, axis=0)
        sends = [jnp.where(g == 0, last, first)] if count_gy == 2 else [last, first]
        for n, send in enumerate(sends):
            send = send.astype(jnp.bfloat16)
            outs[1 + n][pl.ds(at, TILE), :] = send

    if few > 1:
        for i in range(count // 2):
            pair(i)
    else:
        pl.loop(0, count // 2)(pair)


def corner_kernel(edge_ref, corner_ref):
    c = lax.axis_index("col")
    corner_ref[...] = jnp.where(c == 0, edge_ref[:, BX:], edge_ref[:, 0:BX])


def laplace(field, z, y):
    centre = field[z][y]
    last = lax.broadcasted_iota(jnp.int32, centre.shape, 1) == BX - 1
    ahead = jnp.where(last, 0.0, pltpu.roll(centre, BX - 1, 1) - centre)
    result = ahead - pltpu.roll(ahead, 1, 1)
    beside = [
        field[zz][yy]
        for zz, yy in ((z - 1, y), (z + 1, y), (z, y - 1), (z, y + 1))
        if 0 <= zz < len(field) and 0 <= yy < BY
    ]
    return result + (functools.reduce(jnp.add, beside) - float(len(beside)) * centre)


def uptake_of(quarter, doc, oxy):
    return quarter * doc * oxy / ((0.5 + jnp.abs(doc)) * (0.3 + jnp.abs(oxy)))


def prepare_kernel(dims, solutes_ref, biomass_ref, _, *refs):
    depth, slots = dims
    outs, (state, biomass, mass, sems) = refs[:5], refs[5:]
    size = depth * BY
    copies = []
    for group in range(slots // 8):
        for k, (source, target) in enumerate(((solutes_ref, state), (biomass_ref, biomass))):
            rows = (2 - k) * 8 * size
            at = pl.ds(group * rows, rows)
            copies.append(
                pltpu.make_async_copy(source.at[at], target.at[at], sems.at[group, k])
            )
    for copy in copies:
        copy.start()
    for group in range(slots // 8):
        copies[2 * group].wait()
        copies[2 * group + 1].wait()
        at = slice(group * 8 * size, (group + 1) * 8 * size)
        mass[at, :] = biomass[at, :].astype(jnp.float32)

        def rows_of(pitch, offset):
            return pl.ds(group * 8 * pitch + offset, 8, stride=pitch)

        grid = [(z, y) for z in range(depth) for y in range(BY)]
        carbon, oxygen = [
            [
                [state[rows_of(2 * size, k * size + z * BY + y), :] for y in range(BY)]
                for z in range(depth)
            ]
            for k in range(2)
        ]
        for z, y in grid:
            at = group * 8 * size + (z * BY + y) * 8
            at = slice(at, at + 8)
            doc, oxy = carbon[z][y], oxygen[z][y]
            quarter = 0.25 * mass[rows_of(size, z * BY + y), :]
            uptake = uptake_of(quarter, doc, oxy)
            values = (
                doc - uptake,
                oxy - uptake,
                laplace(carbon, z, y),
                laplace(oxygen, z, y),
                quarter,
            )
            for out, value in zip(outs, values):
                out[at, :] = value


def column_kernel(dims, few, *refs):
    count_gz, count_gy, depth, rows, columns, segment, slots, directions = dims
    tiles, refs = refs[:few], refs[few:]
    x_ref, refs = refs[0], refs[1:]
    top_refs, refs = refs[:2], refs[2:]
    if directions == 1:
        bottom_refs = top_refs
    else:
        bottom_refs, refs = refs[:2], refs[2:]
    t1_ref, t2_ref, bias2_ref, *refs = refs
    carbon_ref, oxygen_ref, carbon_around_ref, oxygen_around_ref, quarter_ref, *refs = refs
    fractions_ref, next_ref, *refs = refs
    (
        edge_rows,
        shifted,
        hidden,
        bricks,
        arrived,
        state,
        fractions,
        owner_rows,
        owner_table,
        brick_of_slot,
        sems,
        group_sems,
    ) = refs
    z_index = lax.axis_index("gz")
    g = lax.axis_index("gy")
    c = lax.axis_index("col")
    window = columns + BX
    brick_rows = HALF // BY
    brick_columns = columns // BX
    brick_count = rows // BY * brick_columns
    capacity = slots // count_gz
    single = segment == count_gz

    def tile_of(i):
        return lax.rem(z_index + i, count_gz) if few > 1 else i

    size = depth * BY

    def tile_rows(i, start, size):
        if not isinstance(start, int):
            start = pl.multiple_of(start, TILE)
        if few > 1:
            return tiles[i][pl.ds(start, size), :]
        return tiles[0][i, pl.ds(start, size), :]

    def read_owners(i):
        row = tile_rows(i, brick_columns * depth * rows, TILE)
        owner_rows[i] = row.astype(jnp.float32)[0:8].astype(jnp.int32)

    if few > 1:
        for i in range(count_gz):
            read_owners(i)
    else:
        pl.loop(0, count_gz)(read_owners)
    table_copy = pltpu.make_async_copy(owner_rows, owner_table, sems.at[0])
    table_copy.start()

    def arrange(left, right, other):
        return jnp.concatenate(
            [
                jnp.where(c == 0, left, other),
                jnp.where(c == 0, right, left),
                jnp.where(c == 0, other, right),
            ],
            axis=1,
        )

    for k, pair in enumerate((top_refs, bottom_refs)):
        exists = (g > 0) if k == 0 else (g < count_gy - 1)
        own, other = pair[0][...].astype(jnp.float32), pair[1][...].astype(jnp.float32)
        values = arrange(own[:, 0:BX], own[:, BX:columns], other)
        edge_rows[k] = values * exists.astype(jnp.float32)

    def moved(values):
        lane = lax.broadcasted_iota(jnp.int32, values.shape, 1)
        left = jnp.where(lane == 0, 0.0, pltpu.roll(values, 1, 1))
        right = jnp.where(lane == window - 1, 0.0, pltpu.roll(values, window - 1, 1))
        return left.astype(values.dtype), values, right.astype(values.dtype)

    def edge_pair(k, at):
        if isinstance(at, int):
            return edge_rows[k, at : at + 2, :]
        group = edge_rows[k, pl.ds(pl.multiple_of(at // 8 * 8, 8), 8), :]
        return pltpu.roll(group, lax.rem(8 - at % 8, 8), 0)[0:2]

    row, _ = iotas((4, window))
    constants = [
        jnp.where((row == 0) | (row == 3), 1.0, jnp.where((row == 1 + h) & beyond, 1.0, 0.0))
        for h, beyond in enumerate((g == 0, g == count_gy - 1))
    ]

    def shifts(i, zz, slot, valid):
        z = i * depth + zz
        halves = []
        for h in range(2):
            at = zz * rows + h * HALF
            own = [tile_rows(i, k * depth * rows + at, HALF) for k in range(2)]
            at = z * rows + h * HALF
            if not isinstance(at, int):
                at = pl.multiple_of(at, TILE)
            values = arrange(*own, x_ref[pl.ds(at, HALF), :]).astype(jnp.float32)
            halves.append(values if valid is None else values * valid)
        top, bottom = edge_pair(0, 2 * z), edge_pair(1, 2 * z)
        if valid is not None:
            top, bottom = top * valid, bottom * valid
        seams = [
            jnp.concatenate([top, halves[1][0:2]], axis=0),
            jnp.concatenate([halves[0][HALF - 2 :], bottom], axis=0),
        ]
        for h in range(2):
            lanes = slice(h * window, (h + 1) * window)
            for dx, values in enumerate(moved(halves[h])):
                shifted[slot, dx * HALF : (dx + 1) * HALF, lanes] = values.astype(jnp.bfloat16)
            values = jnp.concatenate(
                [*moved(seams[h]), constants[h]], axis=0
            )
            shifted[slot, 3 * HALF : PART, lanes] = values.astype(jnp.bfloat16)

    def first(z, valid):
        total = jnp.dot(
            t1_ref[...],
            shifted[pl.ds(z + 1, 4)].reshape(4 * PART, 2 * window),
            preferred_element_type=jnp.float32,
        )
        for out in range(2):
            values = jnp.maximum(total[out * TALL : (out + 1) * TALL], 0.0)
            if valid is not None:
                values = values * valid(z + out)
            hidden[z + 1 + out] = values.astype(jnp.bfloat16)

    height = 2 * HALF
    _, lane = iotas((height, BX))

    def second(z, tile):
        total = jnp.dot(
            t2_ref[...],
            hidden[pl.ds(z, 4)].reshape(4 * TALL, 2 * window),
            preferred_element_type=jnp.float32,
        )
        for out in range(2):
            at = z + out
            place(total[3 * height * out : 3 * height * (out + 1)], tile + at // depth, at % depth)

    def place(total, t, zz):
        blocks = window // BX
        for h in range(2):
            part = [total[:, k * BX : (k + 1) * BX] for k in range(h * blocks, (h + 1) * blocks)]
            left = [0.0] + [pltpu.roll(block[0:height], 1, 1) for block in part]
            right = [pltpu.roll(block[2 * height :], BX - 1, 1) for block in part] + [0.0]
            sums = [
                part[k][height : 2 * height]
                + (
                    jnp.where(lane == 0, left[k], left[k + 1])
                    + jnp.where(lane == BX - 1, right[k + 1], right[k])
                )
                for k in range(blocks)
            ]
            for xb in range(brick_columns):
                own = jnp.where(c == 0, sums[xb], sums[xb + 1]) + bias2_ref[...]
                values = 0.5 + 0.5 * jnp.tanh(own)
                for yb in range(brick_rows):
                    b = (h * brick_rows + yb) * brick_columns + xb
                    bricks[t, b, zz] = values[yb * 8 : yb * 8 + 8]

    def valid_slice(z):
        return ((z >= 0) & (z < count_gz * depth)).astype(jnp.float32)

    depths = segment * depth
    if single:
        shifted[1] = jnp.zeros((PART, 2 * window), jnp.bfloat16)
        shifted[depths + 2] = jnp.zeros((PART, 2 * window), jnp.bfloat16)
        hidden[0] = jnp.zeros((TALL, 2 * window), jnp.bfloat16)
        hidden[depths + 1] = jnp.zeros((TALL, 2 * window), jnp.bfloat16)
        for i in range(count_gz):
            tile = tile_of(i)
            for zz in range(depth):
                shifts(i, zz, tile * depth + zz + 2, None)

        @pl.loop(0, depths // 2, unroll=4)
        def _(k):
            first(2 * k, None)

        @pl.loop(0, depths // 2, unroll=4)
        def _(k):
            second(2 * k, 0)

    else:

        @pl.loop(0, count_gz // segment)
        def _(q):
            @pl.loop(-2, depths + 2)
            def _(z):
                at = q * depths + z
                inside = jnp.clip(at, 0, count_gz * depth - 1)
                shifts(inside // depth, inside % depth, z + 2, valid_slice(at))

            @pl.loop(0, depths // 2 + 1)
            def _(k):
                first(2 * k - 1, lambda z: valid_slice(q * depths + z))

            @pl.loop(0, depths // 2)
            def _(k):
                second(2 * k, q * segment)

    for zz in range(depth):
        for xb in range(brick_columns):
            own = [
                bricks[z_index, yb * brick_columns + xb, zz] for yb in range(rows // BY)
            ]
            for o in range(2):
                values = jnp.concatenate([v[o * BY : o * BY + BY] for v in own], axis=0)
                fractions[o, zz, :, xb * BX : (xb + 1) * BX] = values.astype(jnp.bfloat16)
    fractions_copy = pltpu.make_async_copy(fractions, fractions_ref, sems.at[1])
    fractions_copy.start()

    table_copy.wait()
    for j in range(slots):
        brick_of_slot[j] = -1

    @pl.loop(0, count_gz)
    def _(i):
        first = tile_of(i) * capacity
        rank = jnp.int32(0)
        for b in range(brick_count):
            mine = owner_table[i, 0, b] == z_index
            brick_of_slot[jnp.where(mine, first + rank, slots)] = b
            rank = rank + mine.astype(jnp.int32)

    @pl.loop(0, slots, unroll=8)
    def _(j):
        brick = brick_of_slot[j]
        values = bricks[j // capacity, jnp.maximum(brick, 0)]
        values = jnp.where(brick >= 0, values, 0.0).astype(jnp.bfloat16).astype(jnp.float32)
        at = pl.multiple_of(j * (2 * size), 8)
        arrived[pl.ds(at, 2 * size), :] = values.reshape(2 * size, BX)

    def next_copy(group):
        at = pl.ds(pl.multiple_of(group * 16 * size, 16 * size), 16 * size)
        return pltpu.make_async_copy(state.at[at], next_ref.at[at], group_sems.at[group])

    @pl.loop(0, slots // 8)
    def _(group):
        grid = [(z, y) for z in range(depth) for y in range(BY)]

        def load(ref):
            base = group * (8 * size)
            return [
                [
                    ref[pl.ds(pl.multiple_of(base + (z * BY + y) * 8, 8), 8), :]
                    for y in range(BY)
                ]
                for z in range(depth)
            ]

        def rows_of(offset):
            return pl.ds(group * 16 * size + offset, 8, stride=2 * size)

        quarter = load(quarter_ref)
        pore = [[arrived[rows_of(z * 8 + y), :] for y in range(BY)] for z in range(depth)]
        organic = [
            [0.3 * arrived[rows_of(z * 8 + BY + y), :] for y in range(BY)] for z in range(depth)
        ]
        slow = [[0.12 * p for p in row] for row in pore]
        fast = [[0.16 * p for p in row] for row in pore]
        carbon, oxygen = load(carbon_ref), load(oxygen_ref)
        around = load(carbon_around_ref), load(oxygen_around_ref)
        for z, y in grid:
            carbon[z][y] += slow[z][y] * around[0][z][y] + organic[z][y]
            oxygen[z][y] += fast[z][y] * around[1][z][y]
        for _ in range(STEPS - 1):
            carbon_new = [[None] * BY for _ in range(depth)]
            oxygen_new = [[None] * BY for _ in range(depth)]
            for z, y in grid:
                doc, oxy = carbon[z][y], oxygen[z][y]
                uptake = uptake_of(quarter[z][y], doc, oxy)
                gain = organic[z][y] - uptake
                carbon_new[z][y] = doc + slow[z][y] * laplace(carbon, z, y) + gain
                oxygen_new[z][y] = oxy + fast[z][y] * laplace(oxygen, z, y) - uptake
            carbon, oxygen = carbon_new, oxygen_new
        for z, y in grid:
            state[rows_of(z * BY + y), :] = carbon[z][y]
            state[rows_of(size + z * BY + y), :] = oxygen[z][y]
        next_copy(group).start()

    @pl.loop(0, slots // 8)
    def _(group):
        next_copy(group).wait()

    fractions_copy.wait()


def per_device(
    sizes, density, first_kernel, first_bias, second_kernel, second_bias, owners, solutes, biomass
):
    count_gz, count_gy, count_col = sizes
    depth, rows, columns = density.shape
    slots = solutes.shape[3]
    window = columns + BX
    segment = min(count_gz, 4)
    brick_count = (rows // BY) * (columns // BX)
    height = depth * rows
    depths = count_gz * depth
    bf16, f32 = jnp.bfloat16, jnp.float32
    shape = jax.ShapeDtypeStruct

    payload = pl.pallas_call(
        pack_kernel,
        out_shape=shape((columns // BX * height + TILE, BX), bf16),
        in_specs=[HBM, HBM],
        out_specs=VMEM,
        scratch_shapes=[
            pltpu.VMEM((1, brick_count), jnp.int32),
            pltpu.SemaphoreType.DMA((columns // BX + 1,)),
        ],
        compiler_params=pltpu.CompilerParams(vmem_limit_bytes=4 * 2**20),
        name="pack",
    )(in_hbm(density.reshape(height, columns)), in_hbm(owners.reshape(1, brick_count)))

    few = count_gz if count_gz in (2, 4) else 1
    if few > 1:
        tiles = [payload] + [
            lax.ppermute(payload, "gz", [((i + s) % count_gz, i) for i in range(count_gz)])
            for s in range(1, count_gz)
        ]
    else:
        tiles = [lax.all_gather(payload, "gz", axis=0, tiled=False)]

    cells = depth * BY
    prepared = pl.pallas_call(
        functools.partial(prepare_kernel, (depth, slots)),
        out_shape=[shape((slots * cells, BX), f32)] * 5,
        in_specs=[HBM, HBM, ANY],
        out_specs=[VMEM] * 5,
        scratch_shapes=[
            pltpu.VMEM((slots * 2 * cells, BX), f32),
            pltpu.VMEM((slots * cells, BX), bf16),
            pltpu.VMEM((slots * cells, BX), f32),
            pltpu.SemaphoreType.DMA((slots // 8, 2)),
        ],
        compiler_params=pltpu.CompilerParams(vmem_limit_bytes=12 * 2**20),
        cost_estimate=pl.CostEstimate(
            flops=60 * slots * cells * BX, bytes_accessed=2**20, transcendentals=0
        ),
        name="prepare",
    )(
        in_hbm(solutes.reshape(slots * 2 * cells, BX)),
        in_hbm(biomass.reshape(slots * cells, BX)),
        payload,
    )
    if count_gy == 2:
        ways = [[(0, 1), (1, 0)]]
    else:
        up = [(i, i + 1) for i in range(count_gy - 1)]
        ways = [up, [(j, i) for i, j in up]]
    directions = len(ways)
    swap = [(0, 1), (1, 0)]
    near, *sent = pl.pallas_call(
        functools.partial(edges_kernel, (count_gy, depth, rows, columns, few, count_gz)),
        out_shape=[shape((depths * rows, BX), bf16)]
        + [shape((2 * depths, columns), bf16)] * directions,
        in_specs=[VMEM] * few + [ANY],
        out_specs=[VMEM] * (1 + directions),
        compiler_params=pltpu.CompilerParams(vmem_limit_bytes=16 * 2**20),
        name="edges",
    )(*tiles, prepared[-1])
    t1, t2, bias2 = pl.pallas_call(
        banded_kernel,
        out_shape=(
            shape((2 * TALL, 4 * PART), bf16),
            shape((12 * HALF, 4 * TALL), bf16),
            shape((2 * HALF, BX), f32),
        ),
        in_specs=[HBM, HBM, HBM, HBM, ANY],
        out_specs=(VMEM, VMEM, VMEM),
        scratch_shapes=[
            pltpu.VMEM((CHANNELS, 27), bf16),
            pltpu.SMEM((CHANNELS,), f32),
            pltpu.VMEM((2 * CHANNELS, 27), bf16),
            pltpu.SMEM((2,), f32),
            pltpu.SemaphoreType.DMA((4,)),
        ],
        compiler_params=pltpu.CompilerParams(vmem_limit_bytes=16 * 2**20),
        cost_estimate=pl.CostEstimate(
            flops=20 * 2**20, bytes_accessed=4 * 2**20, transcendentals=0
        ),
        name="banded",
    )(
        in_hbm(first_kernel.transpose(2, 1, 0).reshape(CHANNELS, 27)),
        in_hbm(first_bias),
        in_hbm(second_kernel.transpose(1, 2, 0).reshape(2 * CHANNELS, 27)),
        in_hbm(second_bias),
        sent[0],
    )

    edges = []
    for pairs, edge in zip(ways, sent):
        corner = pl.pallas_call(
            corner_kernel,
            out_shape=shape((2 * depths, BX), bf16),
            in_specs=[VMEM],
            out_specs=VMEM,
            compiler_params=pltpu.CompilerParams(vmem_limit_bytes=4 * 2**20),
            name="corner",
        )(edge)
        over = [
            (gy * count_col + col, to * count_col + 1 - col)
            for gy, to in pairs
            for col in range(count_col)
        ]
        corner = lax.ppermute(corner, ("gy", "col"), over)
        edges += [lax.ppermute(edge, "gy", pairs), corner]
    near = lax.ppermute(near, "col", swap)

    fractions, solutes_next = pl.pallas_call(
        functools.partial(
            column_kernel,
            (count_gz, count_gy, depth, rows, columns, segment, slots, directions),
            few,
        ),
        out_shape=(
            shape((2, depth, rows, columns), bf16),
            shape((slots * 2 * cells, BX), f32),
        ),
        in_specs=[VMEM] * (few + 1 + len(edges) + 8),
        out_specs=(HBM, HBM),
        scratch_shapes=[
            pltpu.VMEM((2, 2 * depths, window), f32),
            pltpu.VMEM((segment * depth + 4, PART, 2 * window), bf16),
            pltpu.VMEM((segment * depth + 2, TALL, 2 * window), bf16),
            pltpu.VMEM((count_gz, brick_count, depth, 8, BX), f32),
            pltpu.VMEM((slots * 2 * cells, BX), f32),
            pltpu.VMEM((slots * 2 * cells, BX), f32),
            pltpu.VMEM((2, depth, rows, columns), bf16),
            pltpu.VMEM((count_gz, 8, BX), jnp.int32),
            pltpu.SMEM((count_gz, 8, BX), jnp.int32),
            pltpu.SMEM((slots + 1,), jnp.int32),
            pltpu.SemaphoreType.DMA((2,)),
            pltpu.SemaphoreType.DMA((slots // 8,)),
        ],
        compiler_params=pltpu.CompilerParams(vmem_limit_bytes=40 * 2**20),
        cost_estimate=pl.CostEstimate(
            flops=2 * depths * 2 * window * TALL * (4 * PART + 4 * 6 * HALF),
            bytes_accessed=4 * 2**20,
            transcendentals=0,
        ),
        name="column",
    )(
        *tiles,
        near,
        *edges,
        t1,
        t2,
        bias2,
        *prepared,
    )
    return fractions, solutes_next.reshape(solutes.shape)


def solution(mesh):
    sizes = (mesh.shape["gz"], mesh.shape["gy"], mesh.shape["col"])
    assert sizes[2] == 2
    return jax.shard_map(
        functools.partial(per_device, sizes),
        mesh=mesh,
        in_specs=(
            P(("cores", "gz"), "gy", "col"),
            P(),
            P(),
            P(),
            P(),
            P(("cores", "gz"), "gy", "col", None, None),
            P(("cores", "gz"), "gy", "col", None, None, None, None, None),
            P(("cores", "gz"), "gy", "col", None, None, None, None),
        ),
        out_specs=(
            P(None, ("cores", "gz"), "gy", "col"),
            P(("cores", "gz"), "gy", "col", None, None, None, None, None),
        ),
        check_vma=False,
    )
```

```python
import functools

import jax
import jax.numpy as jnp
from jax import lax
from jax.experimental import pallas as pl
from jax.experimental.pallas import tpu as pltpu
from jax.sharding import PartitionSpec as P

BY = 4
BX = 128
STEPS = 4
TILE = 16
HALF = 16
CHANNELS = 8
REACH = HALF + 2
PART = 3 * HALF + TILE
TALL = REACH * CHANNELS
ONE_ROW = 3 * HALF + 12
OUTSIDE = -1e30

VMEM = pl.BlockSpec(memory_space=pltpu.VMEM)
SMEM = pl.BlockSpec(memory_space=pltpu.SMEM)
ANY = pl.BlockSpec(memory_space=pl.ANY)
HBM = pl.BlockSpec(memory_space=pltpu.HBM)


def in_hbm(array):
    return pltpu.with_memory_space_constraint(array, pltpu.HBM)


def step_index(values, width, count):
    index = jnp.zeros(values.shape, jnp.int32)
    for k in range(1, count):
        index = index + (values >= k * width).astype(jnp.int32)
    return index


def one_hot(condition):
    return jnp.where(condition, 1.0, 0.0).astype(jnp.bfloat16)


def iotas(shape):
    return (
        lax.broadcasted_iota(jnp.int32, shape, 0),
        lax.broadcasted_iota(jnp.int32, shape, 1),
    )


def tap_parts(tap):
    dz = step_index(tap, 9, 3)
    dy = step_index(tap - 9 * dz, 3, 3)
    return dz, dy, tap - 9 * dz - 3 * dy


def pack_kernel(density_ref, owners_ref, payload_ref, named_ref, sems):
    height, columns = density_ref.shape
    blocks = columns // BX
    copies = [pltpu.make_async_copy(owners_ref, named_ref, sems.at[blocks])]
    for k in range(blocks):
        copies.append(
            pltpu.make_async_copy(
                density_ref.at[:, k * BX : (k + 1) * BX],
                payload_ref.at[k * height : (k + 1) * height],
                sems.at[k],
            )
        )
    for copy in copies:
        copy.start()
    copies[0].wait()
    named = named_ref[...].astype(jnp.float32)
    count = named.shape[1]
    payload_ref[blocks * height : blocks * height + TILE, :] = jnp.concatenate(
        [
            jnp.broadcast_to(named, (TILE, count)),
            jnp.zeros((TILE, BX - count), jnp.float32),
        ],
        axis=1,
    ).astype(jnp.bfloat16)
    for copy in copies[1:]:
        copy.wait()


def banded_kernel(*refs):
    sources, refs = refs[:4], refs[5:]
    t1_ref, t2_ref, bias2_ref, *local, sems = refs
    copies = [
        pltpu.make_async_copy(source, target, sems.at[k])
        for k, (source, target) in enumerate(zip(sources, local))
    ]
    for copy in copies:
        copy.start()
    for copy in copies:
        copy.wait()
    w1_ref, b1_ref, w2_ref, b2_ref = local
    row, channel = iotas((TALL, CHANNELS))
    spread = one_hot((row & (CHANNELS - 1)) == channel)
    w1 = jnp.dot(spread, w1_ref[...], preferred_element_type=jnp.float32).astype(jnp.bfloat16)
    tap, column = iotas((27, 4 * PART))
    dz = column >> 6
    place = column & (PART - 1)
    dx = jnp.where(place < 3 * HALF, place >> 4, (place - 3 * HALF) >> 2)
    base = 9 * dz + dx
    row, column = iotas((TALL, 4 * PART))
    place = column & (PART - 1)
    seam = (place - 3 * HALF) & 3
    seam_row = jnp.where(seam < 2, seam - 2, seam + HALF - 2)
    input_row = jnp.where(place < 3 * HALF, place & (HALF - 1), seam_row)
    distance = jnp.where(place < 3 * HALF + 12, input_row - (row >> 3) + 2, -1)
    bias = jnp.zeros((TALL, 4 * PART), jnp.float32)
    for k in range(CHANNELS):
        bias = jnp.where((row & (CHANNELS - 1)) == k, b1_ref[k], bias)
    high = bias.astype(jnp.bfloat16).astype(jnp.float32)
    middle = (bias - high).astype(jnp.bfloat16).astype(jnp.float32)
    constant = jnp.where(column == PART + ONE_ROW, high, 0.0)
    constant = jnp.where(column == 2 * PART + ONE_ROW, middle, constant)
    constant = jnp.where(column == 2 * PART - 1, bias - high - middle, constant)
    outside = ((column == PART + ONE_ROW + 1) & (row < CHANNELS)) | (
        (column == PART + ONE_ROW + 2) & (row >= TALL - CHANNELS)
    )
    constant = jnp.where(outside, OUTSIDE, constant)
    for out in range(2):
        total = constant
        for dy in range(3):
            pick = one_hot(tap == base - 9 * out + 3 * dy)
            values = jnp.dot(w1, pick, preferred_element_type=jnp.float32)
            total = jnp.where(distance == dy, values, total)
        t1_ref[out * TALL : (out + 1) * TALL, :] = total.astype(jnp.bfloat16)
    channel, column = iotas((CHANNELS, 4 * TALL))
    spread = one_hot((column & (CHANNELS - 1)) == channel)
    tap, column = iotas((27, 4 * TALL))
    tap_z, slice_z = tap_parts(tap)[0], step_index(column, TALL, 4)
    row, tap = iotas((6 * HALF, 27))
    _, tap_y, tap_x = tap_parts(tap)
    same_x = (row >> 5) == tap_x
    wide = [
        lax.dot_general(
            w2_ref[o * CHANNELS : (o + 1) * CHANNELS, :],
            spread,
            (((0,), (0,)), ((), ())),
            preferred_element_type=jnp.float32,
        )
        for o in range(2)
    ]
    picks = [
        [one_hot(same_x & (tap_y == dy) & (((row >> 2) & 1) == o)) for o in range(2)]
        for dy in range(3)
    ]
    out_row, column = iotas((6 * HALF, 4 * TALL))
    y = ((out_row >> 3) & 3) * BY + (out_row & 3)
    distance = ((column - TALL * step_index(column, TALL, 4)) >> 3) - y
    for out in range(2):
        same_z = tap_z == slice_z - out
        terms = [jnp.where(same_z, values, 0.0).astype(jnp.bfloat16) for values in wide]
        total = jnp.zeros((6 * HALF, 4 * TALL), jnp.float32)
        for dy in range(3):
            values = 0.0
            for o in range(2):
                values = values + jnp.dot(
                    picks[dy][o], terms[o], preferred_element_type=jnp.float32
                )
            total = jnp.where(distance == dy, values, total)
        t2_ref[out * 6 * HALF : (out + 1) * 6 * HALF, :] = (0.5 * total).astype(jnp.bfloat16)
    row, _ = iotas((2 * HALF, BX))
    bias2_ref[...] = 0.5 * jnp.where(((row >> 2) & 1) == 0, b2_ref[0], b2_ref[1])


def edges_kernel(dims, *refs):
    count_gy, depth, rows, columns, few, count = dims
    tiles, outs = refs[:few], refs[few + 1 :]
    g = lax.axis_index("gy")
    c = lax.axis_index("col")
    height = depth * rows
    block = (1 - c) * height

    def take(i, start, size):
        start = pl.ds(pl.multiple_of(start, TILE), size)
        if few > 1:
            return tiles[i][start, :]
        return tiles[0][i, start, :]

    def pair(i):
        for k in range(2):
            at = pl.multiple_of((2 * i + k) * height, TILE)
            outs[0][pl.ds(at, height), :] = take(2 * i + k, block, height)
        low, high = [], []
        for k in range(2):
            for zz in range(depth):
                first, last = [], []
                for base in (0, height):
                    at = base + zz * rows
                    first.append(take(2 * i + k, at, TILE).astype(jnp.float32)[0:2])
                    at = at + rows - TILE
                    last.append(take(2 * i + k, at, TILE).astype(jnp.float32)[TILE - 2 :])
                low.append(jnp.concatenate(first, axis=1))
                high.append(jnp.concatenate(last, axis=1))
        at = pl.multiple_of(2 * i * 2 * depth, TILE)
        first, last = jnp.concatenate(low, axis=0), jnp.concatenate(high, axis=0)
        sends = [jnp.where(g == 0, last, first)] if count_gy == 2 else [last, first]
        for n, send in enumerate(sends):
            send = send.astype(jnp.bfloat16)
            outs[1 + n][pl.ds(at, TILE), :] = send

    if few > 1:
        for i in range(count // 2):
            pair(i)
    else:
        pl.loop(0, count // 2)(pair)


def corner_kernel(edge_ref, corner_ref):
    c = lax.axis_index("col")
    corner_ref[...] = jnp.where(c == 0, edge_ref[:, BX:], edge_ref[:, 0:BX])


def laplace(field, z, y):
    centre = field[z][y]
    last = lax.broadcasted_iota(jnp.int32, centre.shape, 1) == BX - 1
    ahead = jnp.where(last, 0.0, pltpu.roll(centre, BX - 1, 1) - centre)
    result = ahead - pltpu.roll(ahead, 1, 1)
    beside = [
        field[zz][yy]
        for zz, yy in ((z - 1, y), (z + 1, y), (z, y - 1), (z, y + 1))
        if 0 <= zz < len(field) and 0 <= yy < BY
    ]
    return result + (functools.reduce(jnp.add, beside) - float(len(beside)) * centre)


def uptake_of(quarter, doc, oxy):
    return quarter * doc * oxy / ((0.5 + jnp.abs(doc)) * (0.3 + jnp.abs(oxy)))


def prepare_kernel(dims, solutes_ref, biomass_ref, _, *refs):
    depth, slots = dims
    outs, (state, biomass, mass, sems) = refs[:5], refs[5:]
    size = depth * BY
    copies = []
    for group in range(slots // 8):
        for k, (source, target) in enumerate(((solutes_ref, state), (biomass_ref, biomass))):
            rows = (2 - k) * 8 * size
            at = pl.ds(group * rows, rows)
            copies.append(
                pltpu.make_async_copy(source.at[at], target.at[at], sems.at[group, k])
            )
    for copy in copies:
        copy.start()
    for group in range(slots // 8):
        copies[2 * group].wait()
        copies[2 * group + 1].wait()
        at = slice(group * 8 * size, (group + 1) * 8 * size)
        mass[at, :] = biomass[at, :].astype(jnp.float32)

        def rows_of(pitch, offset):
            return pl.ds(group * 8 * pitch + offset, 8, stride=pitch)

        grid = [(z, y) for z in range(depth) for y in range(BY)]
        carbon, oxygen = [
            [
                [state[rows_of(2 * size, k * size + z * BY + y), :] for y in range(BY)]
                for z in range(depth)
            ]
            for k in range(2)
        ]
        for z, y in grid:
            at = group * 8 * size + (z * BY + y) * 8
            at = slice(at, at + 8)
            doc, oxy = carbon[z][y], oxygen[z][y]
            quarter = 0.25 * mass[rows_of(size, z * BY + y), :]
            uptake = uptake_of(quarter, doc, oxy)
            values = (
                doc - uptake,
                oxy - uptake,
                laplace(carbon, z, y),
                laplace(oxygen, z, y),
                quarter,
            )
            for out, value in zip(outs, values):
                out[at, :] = value


def column_kernel(dims, few, *refs):
    count_gz, count_gy, depth, rows, columns, segment, slots, directions = dims
    tiles, refs = refs[:few], refs[few:]
    x_ref, refs = refs[0], refs[1:]
    top_refs, refs = refs[:2], refs[2:]
    if directions == 1:
        bottom_refs = top_refs
    else:
        bottom_refs, refs = refs[:2], refs[2:]
    t1_ref, t2_ref, bias2_ref, *refs = refs
    carbon_ref, oxygen_ref, carbon_around_ref, oxygen_around_ref, quarter_ref, *refs = refs
    fractions_ref, next_ref, *refs = refs
    (
        edge_rows,
        shifted,
        hidden,
        bricks,
        arrived,
        state,
        fractions,
        owner_rows,
        owner_table,
        brick_of_slot,
        sems,
        group_sems,
    ) = refs
    z_index = lax.axis_index("gz")
    g = lax.axis_index("gy")
    c = lax.axis_index("col")
    window = columns + BX
    brick_rows = HALF // BY
    brick_columns = columns // BX
    brick_count = rows // BY * brick_columns
    capacity = slots // count_gz
    single = segment == count_gz

    def tile_of(i):
        return lax.rem(z_index + i, count_gz) if few > 1 else i

    size = depth * BY

    def tile_rows(i, start, size):
        if not isinstance(start, int):
            start = pl.multiple_of(start, TILE)
        if few > 1:
            return tiles[i][pl.ds(start, size), :]
        return tiles[0][i, pl.ds(start, size), :]

    def read_owners(i):
        row = tile_rows(i, brick_columns * depth * rows, TILE)
        owner_rows[i] = row.astype(jnp.float32)[0:8].astype(jnp.int32)

    if few > 1:
        for i in range(count_gz):
            read_owners(i)
    else:
        pl.loop(0, count_gz)(read_owners)
    table_copy = pltpu.make_async_copy(owner_rows, owner_table, sems.at[0])
    table_copy.start()

    def arrange(left, right, other):
        return jnp.concatenate(
            [
                jnp.where(c == 0, left, other),
                jnp.where(c == 0, right, left),
                jnp.where(c == 0, other, right),
            ],
            axis=1,
        )

    for k, pair in enumerate((top_refs, bottom_refs)):
        exists = (g > 0) if k == 0 else (g < count_gy - 1)
        own, other = pair[0][...].astype(jnp.float32), pair[1][...].astype(jnp.float32)
        values = arrange(own[:, 0:BX], own[:, BX:columns], other)
        edge_rows[k] = values * exists.astype(jnp.float32)

    def moved(values):
        lane = lax.broadcasted_iota(jnp.int32, values.shape, 1)
        left = jnp.where(lane == 0, 0.0, pltpu.roll(values, 1, 1))
        right = jnp.where(lane == window - 1, 0.0, pltpu.roll(values, window - 1, 1))
        return left.astype(values.dtype), values, right.astype(values.dtype)

    def edge_pair(k, at):
        if isinstance(at, int):
            return edge_rows[k, at : at + 2, :]
        group = edge_rows[k, pl.ds(pl.multiple_of(at // 8 * 8, 8), 8), :]
        return pltpu.roll(group, lax.rem(8 - at % 8, 8), 0)[0:2]

    row, _ = iotas((4, window))
    constants = [
        jnp.where((row == 0) | (row == 3), 1.0, jnp.where((row == 1 + h) & beyond, 1.0, 0.0))
        for h, beyond in enumerate((g == 0, g == count_gy - 1))
    ]

    def shifts(i, zz, slot, valid):
        z = i * depth + zz
        halves = []
        for h in range(2):
            at = zz * rows + h * HALF
            own = [tile_rows(i, k * depth * rows + at, HALF) for k in range(2)]
            at = z * rows + h * HALF
            if not isinstance(at, int):
                at = pl.multiple_of(at, TILE)
            values = arrange(*own, x_ref[pl.ds(at, HALF), :]).astype(jnp.float32)
            halves.append(values if valid is None else values * valid)
        top, bottom = edge_pair(0, 2 * z), edge_pair(1, 2 * z)
        if valid is not None:
            top, bottom = top * valid, bottom * valid
        seams = [
            jnp.concatenate([top, halves[1][0:2]], axis=0),
            jnp.concatenate([halves[0][HALF - 2 :], bottom], axis=0),
        ]
        for h in range(2):
            lanes = slice(h * window, (h + 1) * window)
            for dx, values in enumerate(moved(halves[h])):
                shifted[slot, dx * HALF : (dx + 1) * HALF, lanes] = values.astype(jnp.bfloat16)
            values = jnp.concatenate(
                [*moved(seams[h]), constants[h]], axis=0
            )
            shifted[slot, 3 * HALF : PART, lanes] = values.astype(jnp.bfloat16)

    def first(z, valid):
        total = jnp.dot(
            t1_ref[...],
            shifted[pl.ds(z + 1, 4)].reshape(4 * PART, 2 * window),
            preferred_element_type=jnp.float32,
        )
        for out in range(2):
            values = jnp.maximum(total[out * TALL : (out + 1) * TALL], 0.0)
            if valid is not None:
                values = values * valid(z + out)
            hidden[z + 1 + out] = values.astype(jnp.bfloat16)

    height = 2 * HALF
    _, lane = iotas((height, BX))

    def second(z, tile):
        total = jnp.dot(
            t2_ref[...],
            hidden[pl.ds(z, 4)].reshape(4 * TALL, 2 * window),
            preferred_element_type=jnp.float32,
        )
        for out in range(2):
            at = z + out
            place(total[3 * height * out : 3 * height * (out + 1)], tile + at // depth, at % depth)

    def place(total, t, zz):
        blocks = window // BX
        for h in range(2):
            part = [total[:, k * BX : (k + 1) * BX] for k in range(h * blocks, (h + 1) * blocks)]
            left = [0.0] + [pltpu.roll(block[0:height], 1, 1) for block in part]
            right = [pltpu.roll(block[2 * height :], BX - 1, 1) for block in part] + [0.0]
            sums = [
                part[k][height : 2 * height]
                + (
                    jnp.where(lane == 0, left[k], left[k + 1])
                    + jnp.where(lane == BX - 1, right[k + 1], right[k])
                )
                for k in range(blocks)
            ]
            for xb in range(brick_columns):
                own = jnp.where(c == 0, sums[xb], sums[xb + 1]) + bias2_ref[...]
                values = 0.5 + 0.5 * jnp.tanh(own)
                for yb in range(brick_rows):
                    b = (h * brick_rows + yb) * brick_columns + xb
                    bricks[t, b, zz] = values[yb * 8 : yb * 8 + 8]

    def valid_slice(z):
        return ((z >= 0) & (z < count_gz * depth)).astype(jnp.float32)

    depths = segment * depth
    if single:
        shifted[1] = jnp.zeros((PART, 2 * window), jnp.bfloat16)
        shifted[depths + 2] = jnp.zeros((PART, 2 * window), jnp.bfloat16)
        hidden[0] = jnp.zeros((TALL, 2 * window), jnp.bfloat16)
        hidden[depths + 1] = jnp.zeros((TALL, 2 * window), jnp.bfloat16)
        for i in range(count_gz):
            tile = tile_of(i)
            for zz in range(depth):
                shifts(i, zz, tile * depth + zz + 2, None)

        @pl.loop(0, depths // 2, unroll=4)
        def _(k):
            first(2 * k, None)

        @pl.loop(0, depths // 2, unroll=4)
        def _(k):
            second(2 * k, 0)

    else:

        @pl.loop(0, count_gz // segment)
        def _(q):
            @pl.loop(-2, depths + 2)
            def _(z):
                at = q * depths + z
                inside = jnp.clip(at, 0, count_gz * depth - 1)
                shifts(inside // depth, inside % depth, z + 2, valid_slice(at))

            @pl.loop(0, depths // 2 + 1)
            def _(k):
                first(2 * k - 1, lambda z: valid_slice(q * depths + z))

            @pl.loop(0, depths // 2)
            def _(k):
                second(2 * k, q * segment)

    for zz in range(depth):
        for xb in range(brick_columns):
            own = [
                bricks[z_index, yb * brick_columns + xb, zz] for yb in range(rows // BY)
            ]
            for o in range(2):
                values = jnp.concatenate([v[o * BY : o * BY + BY] for v in own], axis=0)
                fractions[o, zz, :, xb * BX : (xb + 1) * BX] = values.astype(jnp.bfloat16)
    fractions_copy = pltpu.make_async_copy(fractions, fractions_ref, sems.at[1])
    fractions_copy.start()

    table_copy.wait()
    for j in range(slots):
        brick_of_slot[j] = -1

    @pl.loop(0, count_gz)
    def _(i):
        first = tile_of(i) * capacity
        rank = jnp.int32(0)
        for b in range(brick_count):
            mine = owner_table[i, 0, b] == z_index
            brick_of_slot[jnp.where(mine, first + rank, slots)] = b
            rank = rank + mine.astype(jnp.int32)

    @pl.loop(0, slots, unroll=8)
    def _(j):
        brick = brick_of_slot[j]
        values = bricks[j // capacity, jnp.maximum(brick, 0)]
        values = jnp.where(brick >= 0, values, 0.0).astype(jnp.bfloat16).astype(jnp.float32)
        at = pl.multiple_of(j * (2 * size), 8)
        arrived[pl.ds(at, 2 * size), :] = values.reshape(2 * size, BX)

    def next_copy(group):
        at = pl.ds(pl.multiple_of(group * 16 * size, 16 * size), 16 * size)
        return pltpu.make_async_copy(state.at[at], next_ref.at[at], group_sems.at[group])

    @pl.loop(0, slots // 8, unroll=2)
    def _(group):
        grid = [(z, y) for z in range(depth) for y in range(BY)]

        def load(ref):
            base = group * (8 * size)
            return [
                [
                    ref[pl.ds(pl.multiple_of(base + (z * BY + y) * 8, 8), 8), :]
                    for y in range(BY)
                ]
                for z in range(depth)
            ]

        def rows_of(offset):
            return pl.ds(group * 16 * size + offset, 8, stride=2 * size)

        quarter = load(quarter_ref)
        pore = [[arrived[rows_of(z * 8 + y), :] for y in range(BY)] for z in range(depth)]
        organic = [
            [0.3 * arrived[rows_of(z * 8 + BY + y), :] for y in range(BY)] for z in range(depth)
        ]
        slow = [[0.12 * p for p in row] for row in pore]
        fast = [[0.16 * p for p in row] for row in pore]
        carbon, oxygen = load(carbon_ref), load(oxygen_ref)
        around = load(carbon_around_ref), load(oxygen_around_ref)
        for z, y in grid:
            carbon[z][y] += slow[z][y] * around[0][z][y] + organic[z][y]
            oxygen[z][y] += fast[z][y] * around[1][z][y]
        for _ in range(STEPS - 1):
            carbon_new = [[None] * BY for _ in range(depth)]
            oxygen_new = [[None] * BY for _ in range(depth)]
            for z, y in grid:
                doc, oxy = carbon[z][y], oxygen[z][y]
                uptake = uptake_of(quarter[z][y], doc, oxy)
                gain = organic[z][y] - uptake
                carbon_new[z][y] = doc + slow[z][y] * laplace(carbon, z, y) + gain
                oxygen_new[z][y] = oxy + fast[z][y] * laplace(oxygen, z, y) - uptake
            carbon, oxygen = carbon_new, oxygen_new
        for z, y in grid:
            state[rows_of(z * BY + y), :] = carbon[z][y]
            state[rows_of(size + z * BY + y), :] = oxygen[z][y]
        next_copy(group).start()

    @pl.loop(0, slots // 8)
    def _(group):
        next_copy(group).wait()

    fractions_copy.wait()


def per_device(
    sizes, density, first_kernel, first_bias, second_kernel, second_bias, owners, solutes, biomass
):
    count_gz, count_gy, count_col = sizes
    depth, rows, columns = density.shape
    slots = solutes.shape[3]
    window = columns + BX
    segment = min(count_gz, 4)
    brick_count = (rows // BY) * (columns // BX)
    height = depth * rows
    depths = count_gz * depth
    bf16, f32 = jnp.bfloat16, jnp.float32
    shape = jax.ShapeDtypeStruct

    payload = pl.pallas_call(
        pack_kernel,
        out_shape=shape((columns // BX * height + TILE, BX), bf16),
        in_specs=[HBM, HBM],
        out_specs=VMEM,
        scratch_shapes=[
            pltpu.VMEM((1, brick_count), jnp.int32),
            pltpu.SemaphoreType.DMA((columns // BX + 1,)),
        ],
        compiler_params=pltpu.CompilerParams(vmem_limit_bytes=4 * 2**20),
        name="pack",
    )(in_hbm(density.reshape(height, columns)), in_hbm(owners.reshape(1, brick_count)))

    few = count_gz if count_gz in (2, 4) else 1
    if few > 1:
        tiles = [payload] + [
            lax.ppermute(payload, "gz", [((i + s) % count_gz, i) for i in range(count_gz)])
            for s in range(1, count_gz)
        ]
    else:
        tiles = [lax.all_gather(payload, "gz", axis=0, tiled=False)]

    cells = depth * BY
    prepared = pl.pallas_call(
        functools.partial(prepare_kernel, (depth, slots)),
        out_shape=[shape((slots * cells, BX), f32)] * 5,
        in_specs=[HBM, HBM, ANY],
        out_specs=[VMEM] * 5,
        scratch_shapes=[
            pltpu.VMEM((slots * 2 * cells, BX), f32),
            pltpu.VMEM((slots * cells, BX), bf16),
            pltpu.VMEM((slots * cells, BX), f32),
            pltpu.SemaphoreType.DMA((slots // 8, 2)),
        ],
        compiler_params=pltpu.CompilerParams(vmem_limit_bytes=12 * 2**20),
        cost_estimate=pl.CostEstimate(
            flops=60 * slots * cells * BX, bytes_accessed=2**20, transcendentals=0
        ),
        name="prepare",
    )(
        in_hbm(solutes.reshape(slots * 2 * cells, BX)),
        in_hbm(biomass.reshape(slots * cells, BX)),
        payload,
    )
    if count_gy == 2:
        ways = [[(0, 1), (1, 0)]]
    else:
        up = [(i, i + 1) for i in range(count_gy - 1)]
        ways = [up, [(j, i) for i, j in up]]
    directions = len(ways)
    swap = [(0, 1), (1, 0)]
    near, *sent = pl.pallas_call(
        functools.partial(edges_kernel, (count_gy, depth, rows, columns, few, count_gz)),
        out_shape=[shape((depths * rows, BX), bf16)]
        + [shape((2 * depths, columns), bf16)] * directions,
        in_specs=[VMEM] * few + [ANY],
        out_specs=[VMEM] * (1 + directions),
        compiler_params=pltpu.CompilerParams(vmem_limit_bytes=16 * 2**20),
        name="edges",
    )(*tiles, prepared[-1])
    t1, t2, bias2 = pl.pallas_call(
        banded_kernel,
        out_shape=(
            shape((2 * TALL, 4 * PART), bf16),
            shape((12 * HALF, 4 * TALL), bf16),
            shape((2 * HALF, BX), f32),
        ),
        in_specs=[HBM, HBM, HBM, HBM, ANY],
        out_specs=(VMEM, VMEM, VMEM),
        scratch_shapes=[
            pltpu.VMEM((CHANNELS, 27), bf16),
            pltpu.SMEM((CHANNELS,), f32),
            pltpu.VMEM((2 * CHANNELS, 27), bf16),
            pltpu.SMEM((2,), f32),
            pltpu.SemaphoreType.DMA((4,)),
        ],
        compiler_params=pltpu.CompilerParams(vmem_limit_bytes=16 * 2**20),
        cost_estimate=pl.CostEstimate(
            flops=20 * 2**20, bytes_accessed=4 * 2**20, transcendentals=0
        ),
        name="banded",
    )(
        in_hbm(first_kernel.transpose(2, 1, 0).reshape(CHANNELS, 27)),
        in_hbm(first_bias),
        in_hbm(second_kernel.transpose(1, 2, 0).reshape(2 * CHANNELS, 27)),
        in_hbm(second_bias),
        sent[0],
    )

    edges = []
    for pairs, edge in zip(ways, sent):
        corner = pl.pallas_call(
            corner_kernel,
            out_shape=shape((2 * depths, BX), bf16),
            in_specs=[VMEM],
            out_specs=VMEM,
            compiler_params=pltpu.CompilerParams(vmem_limit_bytes=4 * 2**20),
            name="corner",
        )(edge)
        over = [
            (gy * count_col + col, to * count_col + 1 - col)
            for gy, to in pairs
            for col in range(count_col)
        ]
        corner = lax.ppermute(corner, ("gy", "col"), over)
        edges += [lax.ppermute(edge, "gy", pairs), corner]
    near = lax.ppermute(near, "col", swap)

    fractions, solutes_next = pl.pallas_call(
        functools.partial(
            column_kernel,
            (count_gz, count_gy, depth, rows, columns, segment, slots, directions),
            few,
        ),
        out_shape=(
            shape((2, depth, rows, columns), bf16),
            shape((slots * 2 * cells, BX), f32),
        ),
        in_specs=[VMEM] * (few + 1 + len(edges) + 8),
        out_specs=(HBM, HBM),
        scratch_shapes=[
            pltpu.VMEM((2, 2 * depths, window), f32),
            pltpu.VMEM((segment * depth + 4, PART, 2 * window), bf16),
            pltpu.VMEM((segment * depth + 2, TALL, 2 * window), bf16),
            pltpu.VMEM((count_gz, brick_count, depth, 8, BX), f32),
            pltpu.VMEM((slots * 2 * cells, BX), f32),
            pltpu.VMEM((slots * 2 * cells, BX), f32),
            pltpu.VMEM((2, depth, rows, columns), bf16),
            pltpu.VMEM((count_gz, 8, BX), jnp.int32),
            pltpu.SMEM((count_gz, 8, BX), jnp.int32),
            pltpu.SMEM((slots + 1,), jnp.int32),
            pltpu.SemaphoreType.DMA((2,)),
            pltpu.SemaphoreType.DMA((slots // 8,)),
        ],
        compiler_params=pltpu.CompilerParams(vmem_limit_bytes=40 * 2**20),
        cost_estimate=pl.CostEstimate(
            flops=2 * depths * 2 * window * TALL * (4 * PART + 4 * 6 * HALF),
            bytes_accessed=4 * 2**20,
            transcendentals=0,
        ),
        name="column",
    )(
        *tiles,
        near,
        *edges,
        t1,
        t2,
        bias2,
        *prepared,
    )
    return fractions, solutes_next.reshape(solutes.shape)


def solution(mesh):
    sizes = (mesh.shape["gz"], mesh.shape["gy"], mesh.shape["col"])
    assert sizes[2] == 2
    return jax.shard_map(
        functools.partial(per_device, sizes),
        mesh=mesh,
        in_specs=(
            P(("cores", "gz"), "gy", "col"),
            P(),
            P(),
            P(),
            P(),
            P(("cores", "gz"), "gy", "col", None, None),
            P(("cores", "gz"), "gy", "col", None, None, None, None, None),
            P(("cores", "gz"), "gy", "col", None, None, None, None),
        ),
        out_specs=(
            P(None, ("cores", "gz"), "gy", "col"),
            P(("cores", "gz"), "gy", "col", None, None, None, None, None),
        ),
        check_vma=False,
    )
```
